32 devices in a mesh: dp: 2 (over x), row: 4 (over z), col: 4 (over y, core).
Axes of the slice: x: 2, y: 2, z: 4, core: 2. Of those that a mesh axis runs over, the one named last changes fastest.
Arguments:
- pair_state: bfloat16 [8, 256, 256, 128], P('dp', 'row', 'col'), parts along dimension 0, may hold values from -6 to 6
- cotangent: bfloat16 [8, 256, 256, 128], P('dp', 'row', 'col'), parts along dimension 0, may hold values from -6 to 6
- chain_lengths: int32 [8, 4], P('dp'), parts along dimension 0, may hold values from 1 to 224, 256 in all within a row
- tri_gain: float32 [128], replicated, may hold values from 0.5 to 1.5
- tri_shift: float32 [128], replicated, may hold values from -3 to 3
- tri_weight: bfloat16 [128, 640], replicated, may hold values from -0.5 to 0.5
- mix_gain: float32 [128], replicated, may hold values from 0.5 to 1.5
- mix_shift: float32 [128], replicated, may hold values from -3 to 3
- tri_out: bfloat16 [128, 128], replicated, may hold values from -0.5 to 0.5
- att_gain: float32 [128], replicated, may hold values from 0.5 to 1.5
- att_shift: float32 [128], replicated, may hold values from -3 to 3
- att_weight: bfloat16 [128, 512], replicated, may hold values from -0.5 to 0.5
- chain_bias: float32 [4], replicated, may hold values from -3 to 3
- att_out: bfloat16 [128, 128], replicated, may hold values from -3 to 3
- trans_gain: float32 [128], replicated, may hold values from 0.5 to 1.5
- trans_shift: float32 [128], replicated, may hold values from -3 to 3
- up_weight: bfloat16 [128, 256], replicated, may hold values from -0.5 to 0.5
- down_weight: bfloat16 [256, 128], replicated, may hold values from -0.375 to 0.375
Outputs:
- pair_out: bfloat16 [8, 256, 256, 128], P('dp', 'row', 'col'), parts along dimension 0
- grad_pair: bfloat16 [8, 256, 256, 128], P('dp', 'row', 'col'), parts along dimension 0
- grad_tri_gain: float32 [256], P('dp'), parts along dimension 0
- grad_tri_shift: float32 [256], P('dp'), parts along dimension 0
- grad_tri_weight: float32 [256, 640], P('dp'), parts along dimension 0
- grad_mix_gain: float32 [256], P('dp'), parts along dimension 0
- grad_mix_shift: float32 [256], P('dp'), parts along dimension 0
- grad_tri_out: float32 [256, 128], P('dp'), parts along dimension 0
- grad_att_gain: float32 [256], P('dp'), parts along dimension 0
- grad_att_shift: float32 [256], P('dp'), parts along dimension 0
- grad_att_weight: float32 [256, 512], P('dp'), parts along dimension 0
- grad_chain_bias: float32 [8], P('dp'), parts along dimension 0
- grad_att_out: float32 [256, 128], P('dp'), parts along dimension 0
- grad_trans_gain: float32 [256], P('dp'), parts along dimension 0
- grad_trans_shift: float32 [256], P('dp'), parts along dimension 0
- grad_up_weight: float32 [256, 256], P('dp'), parts along dimension 0
- grad_down_weight: float32 [512, 128], P('dp'), parts along dimension 0
The draws below stay inside these ranges and needn't reach their ends.
There are 2 independent parts, one for each index of `dp`. The reference program is written for one: setup_inputs(seed, part) draws one part's arguments, and reference() takes and returns one part's arrays. A program takes and returns all parts, laid end to end along the dimension named above; an argument that names none is the same for every part. Nothing has to cross between parts.
Inputs may be any that keep to these rules, and one draw needn't show every extreme that they name: `chain_lengths`: in each crop the lengths sum to 256, and the longest is exactly 224.
All inputs are finite; a program needn't handle non-finite values.
Results may differ from the reference program's by a relative error of at most 0.035.
Values may be sent and summed in bfloat16 or wider, within the bound.
No kernel may reach another device: no remote copies, remote signals or barrier semaphores. Data moves between devices by JAX's collectives and lax.ppermute only.
A program may use at most 448 MiB of HBM per device.

```python
import math
import jax
import jax.numpy as jnp
import numpy as np
from jax import lax

CROPS = 4
L = 256
C = 128
CT = 128
HEADS = 4
HD = 32
FF = 256
CHAINS = 4
MOST = 224


def level_of(own_key, shape, cuts, smallest, top_value):
    def one(dim, shards_of):
        draws = jax.random.uniform(jax.random.fold_in(jax.random.fold_in(own_key, 6), dim), (shards_of,), jnp.float32, smallest / len(cuts), top_value / len(cuts))
        return jnp.repeat(jnp.exp(draws), shape[dim] // shards_of).reshape((-1,) + (1,) * (len(shape) - dim - 1))

    loudness = one(*cuts[0])
    for cut in cuts[1:]:
        loudness = loudness * one(*cut)
    return loudness


def length_profile(count, total, bound, skew):
    loads = [(1 << 20) // math.isqrt(rank ** skew) + 1 for rank in range(2, count + 1)]
    spare, counts = total - bound - (count - 1), [1] * (count - 1)
    while spare > 0:
        free = [i for i in range(count - 1) if counts[i] < bound]
        pool, left = sum([loads[i] for i in free]), spare
        for i in free:
            extra = min(bound - counts[i], max(1, left * loads[i] // pool), spare)
            counts[i] = counts[i] + extra
            spare = spare - extra
    return np.array([bound] + counts)


def uneven(stream_key, count, total, reach, skew):
    if count == 2:
        one = jax.random.randint(stream_key, (), max(1, total - reach), min(reach, total - 1) + 1)
        return jnp.stack([one, total - one])
    sizes = jnp.asarray(length_profile(count, total, reach, skew), jnp.int32)
    twos = (count - 1) // 2
    source_of, taker = sizes[1:1 + 2 * twos:2], sizes[2:2 + 2 * twos:2]
    room = jnp.minimum(source_of - 1, reach - taker)
    moved = jax.random.randint(jax.random.fold_in(stream_key, 1), (twos,), 0, 1 << 20) % (room + 1)
    sizes = sizes.at[1:1 + 2 * twos:2].set(source_of - moved).at[2:2 + 2 * twos:2].set(taker + moved)
    return sizes[jax.random.permutation(jax.random.fold_in(stream_key, 2), count)]


def scatter_about(key, extent, scale, reach, cuts=(), held_as=jnp.bfloat16):
    values = scale * jax.random.normal(key, extent, jnp.float32)
    if cuts:
        values = values * level_of(key, extent, cuts, -0.22, 0.18)
    return jnp.clip(values, -reach, reach).astype(held_as)


def setup_inputs(seed: int = 0, part: int = 0) -> dict:
    splits = jax.random.split(jax.random.key(seed), 19)
    own_keys = jax.random.split(jax.random.fold_in(splits[18], part), 19)
    return {
        "pair_state": scatter_about(own_keys[0], (CROPS, L, L, C), 1.0, 6.0, ((1, 4), (2, 4))),
        "cotangent": scatter_about(own_keys[1], (CROPS, L, L, C), 1.0, 6.0, ((1, 4), (2, 4))),
        "chain_lengths": jax.vmap(lambda own: uneven(own, CHAINS, L, MOST, 2))(jax.random.split(own_keys[2], CROPS)).reshape((CROPS, CHAINS)).astype(jnp.int32),
        "tri_gain": jnp.clip(1.0 + 0.1 * jax.random.normal(splits[3], (C,), jnp.float32), 0.5, 1.5),
        "tri_shift": scatter_about(splits[4], (C,), 0.3, 3.0, (), jnp.float32),
        "tri_weight": scatter_about(splits[5], (C, 4 * CT + C), C ** -0.5, 0.5),
        "mix_gain": jnp.clip(1.0 + 0.1 * jax.random.normal(splits[6], (CT,), jnp.float32), 0.5, 1.5),
        "mix_shift": scatter_about(splits[7], (CT,), 0.3, 3.0, (), jnp.float32),
        "tri_out": scatter_about(splits[8], (CT, C), CT ** -0.5, 0.5),
        "att_gain": jnp.clip(1.0 + 0.1 * jax.random.normal(splits[9], (C,), jnp.float32), 0.5, 1.5),
        "att_shift": scatter_about(splits[10], (C,), 0.3, 3.0, (), jnp.float32),
        "att_weight": scatter_about(splits[11], (C, 4 * C), C ** -0.5, 0.5),
        "chain_bias": scatter_about(splits[12], (HEADS,), 1.0, 3.0, (), jnp.float32),
        "att_out": scatter_about(splits[13], (C, C), (max(C // 32, 1)) ** -0.5, 3.0),
        "trans_gain": jnp.clip(1.0 + 0.1 * jax.random.normal(splits[14], (C,), jnp.float32), 0.5, 1.5),
        "trans_shift": scatter_about(splits[15], (C,), 0.3, 3.0, (), jnp.float32),
        "up_weight": scatter_about(splits[16], (C, FF), C ** -0.5, 0.5),
        "down_weight": scatter_about(splits[17], (FF, C), FF ** -0.5, 0.375),
    }


@jax.custom_vjp
def low(v):
    return lax.optimization_barrier(v.astype(jnp.bfloat16)).astype(jnp.float32)

@jax.custom_vjp
def low_back(v):
    return v

def low_keep(v):
    return (low(v), None)

def low_pass(kept, grad):
    return (grad,)

def back_keep(v):
    return (v, None)

def back_low(kept, grad):
    return (low(grad),)
low.defvjp(low_keep, low_pass)
low_back.defvjp(back_keep, back_low)
eps = 1e-05

def layer_norm(values, gain, shift):
    center = values - lax.optimization_barrier(jnp.mean(values, axis=-1, keepdims=True))
    spread = lax.optimization_barrier(jnp.mean(center * center, axis=-1, keepdims=True))
    return center * lax.rsqrt(spread + eps) * gain + shift

def matmul(values, weight):
    return jnp.einsum('...c,cd->...d', values, weight, precision=lax.Precision.HIGHEST)

def chain_index(lengths):
    chain_ends = jnp.cumsum(lengths, axis=-1).astype(jnp.int32)
    places = jnp.arange(L, dtype=jnp.int32)
    return lax.optimization_barrier(jnp.sum((places[None, :, None] >= chain_ends[:, None, :]).astype(jnp.int32), axis=-1)).astype(jnp.int32)

def crop_forward(start_pair, chain, tri_gain, tri_shift, tri_weight, mix_gain, mix_shift, tri_out, att_gain, att_shift, att_weight, chain_bias, att_out, trans_gain, trans_shift, up_weight, down_weight):
    highest = lax.Precision.HIGHEST
    normed_one = low(layer_norm(start_pair, tri_gain, tri_shift))
    tri_proj = low_back(matmul(normed_one, tri_weight))
    edge_left = low(jax.nn.sigmoid(tri_proj[..., CT:2 * CT]) * tri_proj[..., :CT])
    edge_right = low(jax.nn.sigmoid(tri_proj[..., 3 * CT:4 * CT]) * tri_proj[..., 2 * CT:3 * CT])
    out_gate = jax.nn.sigmoid(tri_proj[..., 4 * CT:])
    triangle = low_back(jnp.einsum('ikc,jkc->ijc', edge_left, edge_right, precision=highest))
    mixed_low = low(layer_norm(triangle, mix_gain, mix_shift))
    after_tri = start_pair + out_gate * low_back(matmul(mixed_low, tri_out))
    att_low = low(layer_norm(after_tri, att_gain, att_shift))
    hidden = low(low_back(matmul(att_low, att_weight)))
    query = hidden[..., :C].reshape(L, L, HEADS, HD)
    keys_all = hidden[..., C:2 * C].reshape(L, L, HEADS, HD)
    values_all = hidden[..., 2 * C:3 * C].reshape(L, L, HEADS, HD)
    gate_att = jax.nn.sigmoid(hidden[..., 3 * C:])
    same_chain = (chain[:, None] == chain[None, :]).astype(jnp.float32)
    raw_scores = low_back(jnp.einsum('ijhd,ikhd->ihjk', query, keys_all, precision=highest))
    scores = raw_scores * (1.0 / math.sqrt(HD)) + chain_bias[None, :, None, None] * same_chain[None, None]
    probs = low(jax.nn.softmax(scores, axis=-1))
    mixed = low_back(jnp.einsum('ihjk,ikhd->ijhd', probs, values_all, precision=highest)).reshape(L, L, C)
    gated = low_back(low(gate_att * mixed))
    after_att = after_tri + low_back(matmul(gated, att_out))
    trans_low = low(layer_norm(after_att, trans_gain, trans_shift))
    act_low = low(jax.nn.silu(low_back(matmul(trans_low, up_weight))))
    return after_att + low_back(matmul(act_low, down_weight))

def reference(pair_state, cotangent, chain_lengths, tri_gain, tri_shift, tri_weight, mix_gain, mix_shift, tri_out, att_gain, att_shift, att_weight, chain_bias, att_out, trans_gain, trans_shift, up_weight, down_weight):
    chain_ids = chain_index(chain_lengths)
    params = (tri_gain, tri_shift, tri_weight, mix_gain, mix_shift, tri_out, att_gain, att_shift, att_weight, chain_bias, att_out, trans_gain, trans_shift, up_weight, down_weight)
    params = tuple((item.astype(jnp.float32) for item in params))

    def forward(start_pair, *weights):
        crop_step = jax.checkpoint(lambda items: crop_forward(items[0], items[1], *weights))
        return lax.map(crop_step, (start_pair, chain_ids))
    output, pull = jax.vjp(forward, pair_state.astype(jnp.float32), *params)
    grads = pull(cotangent.astype(jnp.float32))
    return (output.astype(jnp.bfloat16), grads[0].astype(jnp.bfloat16), grads[1], grads[2], grads[3], grads[4], grads[5], grads[6], grads[7], grads[8], grads[9], grads[10], grads[11], grads[12], grads[13], grads[14], grads[15])
```

```python
import functools
import math

import jax
import jax.numpy as jnp
from jax import lax
from jax.experimental import pallas as pl
from jax.experimental.pallas import tpu as pltpu
from jax.sharding import PartitionSpec as P

HEADS = 4
EPS = 1e-05
LOG2E = math.log2(math.e)
LN2 = math.log(2.0)
VMEM_LIMIT = 56 * 1024 * 1024
BF = jnp.bfloat16
F32 = jnp.float32


def nn(left, right):
    return lax.dot_general(left, right, (((1,), (0,)), ((), ())), preferred_element_type=F32)


def nt(left, right):
    return lax.dot_general(left, right, (((1,), (1,)), ((), ())), preferred_element_type=F32)


def tn(left, right):
    return lax.dot_general(left, right, (((0,), (0,)), ((), ())), preferred_element_type=F32)


def sigmoid(values):
    return 0.5 * jnp.tanh(0.5 * values) + 0.5


def normalize(values):
    center = values - jnp.mean(values, axis=0, keepdims=True)
    spread = jnp.mean(center * center, axis=0, keepdims=True)
    scale = lax.rsqrt(spread + EPS)
    return center * scale, scale


def normalize_back(grads, gain, hat, scale):
    grad_hat = grads * gain
    first = jnp.mean(grad_hat, axis=0, keepdims=True)
    second = jnp.mean(grad_hat * hat, axis=0, keepdims=True)
    return scale * (grad_hat - first - hat * second)


def widen(column, lanes):
    return jnp.concatenate([column] * (lanes // column.shape[1]), axis=1)


def fold(values):
    parts = [values[:, at : at + 128] for at in range(0, values.shape[1], 128)]
    return functools.reduce(lambda one, two: one + two, parts)


def load_rows(ref, start, count):
    _, pieces, _, tokens, width = ref.shape
    rows = [
        ref[0, :, start + n, :, :].reshape(pieces * tokens, width).astype(F32).T
        for n in range(count)
    ]
    return jnp.concatenate(rows, axis=1)


def store_rows(ref, start, count, values):
    _, pieces, _, tokens, width = ref.shape
    length = pieces * tokens
    for n in range(count):
        flat = values[:, n * length : (n + 1) * length].T.astype(ref.dtype)
        ref[0, :, start + n, :, :] = flat.reshape(pieces, tokens, width)


def stacked(ref, start, count):
    return jnp.concatenate([ref[start + n] for n in range(count)], axis=1)


def spread_out(ref, start, count, values):
    length = values.shape[1] // count
    for n in range(count):
        ref[start + n] = values[:, n * length : (n + 1) * length].astype(ref.dtype)


def edges_kernel(x_ref, w_ref, gain_ref, shift_ref, a_ref, b_ref, xt_ref, a_scr, b_scr):
    rows = xt_ref.shape[0]
    width = xt_ref.shape[1]
    count = 2

    def step(at, carry):
        start = at * count
        x0 = load_rows(x_ref, start, count)
        spread_out(xt_ref, start, count, x0)
        hat, _ = normalize(x0)
        lanes = x0.shape[1]
        normed = (hat * widen(gain_ref[...], lanes) + widen(shift_ref[...], lanes)).astype(BF)
        proj = nn(w_ref[...], normed)
        left = sigmoid(proj[width : 2 * width]) * proj[:width]
        right = sigmoid(proj[3 * width : 4 * width]) * proj[2 * width : 3 * width]
        length = lanes // count
        for n in range(count):
            cols = slice(n * length, (n + 1) * length)
            base = pl.multiple_of((start + n) * width, width)
            for half in range(length // 128):
                part = slice(n * length + half * 128, n * length + half * 128 + 128)
                a_scr[half, pl.ds(base, width), :] = left[:, part]
                b_scr[half, pl.ds(base, width), :] = right[:, part]
        return carry

    lax.fori_loop(0, rows // count, step, 0)

    def turn(at, carry):
        for n in range(8):
            e = at * 8 + n
            for scr, out in ((a_scr, a_ref), (b_scr, b_ref)):
                halves = [scr[h, pl.ds(e, rows, stride=width), :] for h in range(scr.shape[0])]
                out[e] = jnp.concatenate(halves, axis=1).astype(BF)
        return carry

    lax.fori_loop(0, width // 8, turn, 0)


def edges(x_rows, weight, gain, shift):
    blocks, pieces, sub, tokens, width = x_rows.shape
    length = pieces * tokens
    rows = blocks * sub
    const = lambda at: (0, 0)
    return pl.pallas_call(
        edges_kernel,
        grid=(blocks,),
        in_specs=[
            pl.BlockSpec((1, pieces, sub, tokens, width), lambda at: (at, 0, 0, 0, 0)),
            pl.BlockSpec(weight.shape, const),
            pl.BlockSpec(gain.shape, const),
            pl.BlockSpec(shift.shape, const),
        ],
        out_specs=[
            pl.BlockSpec((width, sub, length), lambda at: (0, at, 0)),
            pl.BlockSpec((width, sub, length), lambda at: (0, at, 0)),
            pl.BlockSpec((sub, width, length), lambda at: (at, 0, 0)),
        ],
        out_shape=[
            jax.ShapeDtypeStruct((width, rows, length), BF),
            jax.ShapeDtypeStruct((width, rows, length), BF),
            jax.ShapeDtypeStruct((rows, width, length), BF),
        ],
        scratch_shapes=[
            pltpu.VMEM((length // 128, sub * width, 128), F32),
            pltpu.VMEM((length // 128, sub * width, 128), F32),
        ],
        compiler_params=pltpu.CompilerParams(vmem_limit_bytes=VMEM_LIMIT),
        name="edges",
    )(x_rows, weight, gain, shift)


def natural(ref, e, sub):
    pieces, _, rows, _ = ref.shape
    return jnp.concatenate(
        [ref[q, e, r * sub : (r + 1) * sub, :] for r in range(rows // sub) for q in range(pieces)],
        axis=0,
    )


def triangle_kernel(sub, a_ref, b_ref, t_ref):
    for e in range(a_ref.shape[0]):
        t_ref[:, e, :] = nt(a_ref[e], natural(b_ref, e, sub))


def triangle(left, right_all, sub):
    width, rows, length = left.shape
    pieces = right_all.shape[0]
    some = 8
    return pl.pallas_call(
        functools.partial(triangle_kernel, sub),
        grid=(width // some,),
        in_specs=[
            pl.BlockSpec((some, rows, length), lambda at: (at, 0, 0)),
            pl.BlockSpec((pieces, some, rows, length), lambda at: (0, at, 0, 0)),
        ],
        out_specs=pl.BlockSpec((rows, some, length), lambda at: (0, at, 0)),
        out_shape=jax.ShapeDtypeStruct((rows, width, length), F32),
        compiler_params=pltpu.CompilerParams(vmem_limit_bytes=VMEM_LIMIT),
        name="triangle",
    )(left, right_all)


def triangle_back_kernel(sub, dt_ref, a_ref, b_ref, da_ref, db_ref):
    pieces, _, rows, _ = db_ref.shape
    for e in range(a_ref.shape[0]):
        grad = dt_ref[:, e, :].astype(BF)
        da_ref[:, e, :] = nn(grad, natural(b_ref, e, sub))
        db = tn(grad, a_ref[e]).astype(BF)
        for r in range(rows // sub):
            for q in range(pieces):
                at = (r * pieces + q) * sub
                db_ref[q, e, r * sub : (r + 1) * sub, :] = db[at : at + sub]


def triangle_back(grad, left, right_all, sub):
    width, rows, length = left.shape
    pieces = right_all.shape[0]
    some = 8
    return pl.pallas_call(
        functools.partial(triangle_back_kernel, sub),
        grid=(width // some,),
        in_specs=[
            pl.BlockSpec((rows, some, length), lambda at: (0, at, 0)),
            pl.BlockSpec((some, rows, length), lambda at: (at, 0, 0)),
            pl.BlockSpec((pieces, some, rows, length), lambda at: (0, at, 0, 0)),
        ],
        out_specs=[
            pl.BlockSpec((rows, some, length), lambda at: (0, at, 0)),
            pl.BlockSpec((pieces, some, rows, length), lambda at: (0, at, 0, 0)),
        ],
        out_shape=[
            jax.ShapeDtypeStruct((rows, width, length), F32),
            jax.ShapeDtypeStruct((pieces, width, rows, length), BF),
        ],
        compiler_params=pltpu.CompilerParams(vmem_limit_bytes=VMEM_LIMIT),
        name="triangle_back",
    )(grad, left, right_all)


def rows_kernel(
    count,
    heads,
    t_ref,
    xt_ref,
    cot_ref,
    bias_ref,
    chain_ref,
    lane_ref,
    vec_ref,
    gate_w_ref,
    gate_wt_ref,
    tri_out_ref,
    tri_out_t_ref,
    att_t_ref,
    att_kv_ref,
    att_qg_ref,
    att_out_ref,
    att_out_t_ref,
    up_ref,
    up_t_ref,
    down_ref,
    down_t_ref,
    out_ref,
    dt_ref,
    z_ref,
    g_gate_ref,
    g_tri_out_ref,
    g_qg_ref,
    g_kv_ref,
    g_att_out_ref,
    g_up_ref,
    g_down_ref,
    g_vec_ref,
    g_bias_ref,
    e_scr,
    ds_scr,
    do_scr,
    q_scr,
):
    total_rows, width, length = t_ref.shape
    lanes = count * length
    head = width // heads
    scaling = 1.0 / math.sqrt(head)

    @pl.when(pl.program_id(0) == 0)
    def _():
        for ref in (
            g_gate_ref,
            g_tri_out_ref,
            g_qg_ref,
            g_kv_ref,
            g_att_out_ref,
            g_up_ref,
            g_down_ref,
            g_vec_ref,
            g_bias_ref,
            do_scr,
            q_scr,
        ):
            ref[...] = jnp.zeros(ref.shape, ref.dtype)

    def vec(at):
        return widen(vec_ref[at], lanes)

    def step(at, carry):
        start = at * count
        x0 = stacked(xt_ref, start, count).astype(F32)
        hat1, scale1 = normalize(x0)
        normed1 = (hat1 * vec(0) + vec(1)).astype(BF)
        gate1 = sigmoid(nn(gate_wt_ref[...], normed1))
        hat_t, scale_t = normalize(stacked(t_ref, start, count))
        mixed = (hat_t * vec(2) + vec(3)).astype(BF)
        branch = nn(tri_out_t_ref[...], mixed)
        x1 = x0 + gate1 * branch
        hat2, scale2 = normalize(x1)
        normed2 = (hat2 * vec(4) + vec(5)).astype(BF)
        hidden = nn(att_t_ref[...], normed2).astype(BF)
        query = (hidden[:width].astype(F32) * (scaling * LOG2E)).astype(BF)
        key = hidden[width : 2 * width]
        value = hidden[2 * width : 3 * width]
        gate2 = sigmoid(hidden[3 * width :].astype(F32))
        normed2_tok = normed2.T
        kv_tok = nn(normed2_tok, att_kv_ref[...]).astype(BF)
        ones = jnp.ones((16, length), BF)

        mixed_rows, inverse_rows = [], []
        for n in range(count):
            cols = slice(n * length, (n + 1) * length)
            key_tok = kv_tok[cols, :width]
            query_n = query[:, cols]
            outs, inverses = [], []
            for h in range(heads):
                mine = slice(h * head, (h + 1) * head)
                there = slice(h * length, (h + 1) * length)
                score = nn(key_tok * lane_ref[h], query_n) + bias_ref[h]
                peak = jnp.max(score, axis=0, keepdims=True)
                expon = jnp.exp2(score - peak).astype(BF)
                e_scr[n, :, there] = expon
                q_scr[n, mine, there] = query_n[mine]
                both = nn(jnp.concatenate([value[mine, cols], ones], axis=0), expon)
                inverse = 1.0 / both[head : head + 1]
                outs.append(both[:head] * inverse)
                inverses.append(inverse)
            mixed_rows.append(jnp.concatenate(outs, axis=0))
            inverse_rows.append(inverses)
        attended = jnp.concatenate(mixed_rows, axis=1)
        gated = (gate2 * attended).astype(BF)
        x2 = x1 + nn(att_out_t_ref[...], gated)
        hat3, scale3 = normalize(x2)
        normed3 = (hat3 * vec(6) + vec(7)).astype(BF)
        up = nn(up_t_ref[...], normed3)
        gate3 = sigmoid(up)
        act = (up * gate3).astype(BF)
        store_rows(out_ref, start, count, x2 + nn(down_t_ref[...], act))

        cot = load_rows(cot_ref, start, count)
        cot_low = cot.astype(BF)
        g_down_ref[...] += nt(act, cot_low)
        grad_up = (nn(down_ref[...], cot_low) * (gate3 * (1.0 + up * (1.0 - gate3)))).astype(BF)
        g_up_ref[...] += nt(normed3, grad_up)
        grad3 = nn(up_ref[...], grad_up)
        g_vec_ref[6] += fold(grad3 * hat3)
        g_vec_ref[7] += fold(grad3)
        grad_x2 = cot + normalize_back(grad3, vec(6), hat3, scale3)
        grad_x2_low = grad_x2.astype(BF)
        g_att_out_ref[...] += nt(gated, grad_x2_low)
        grad_gated = nn(att_out_ref[...], grad_x2_low).astype(BF).astype(F32)
        grad_mixed = (grad_gated * gate2).astype(BF).astype(F32)
        grad_gate2 = (grad_gated * attended * gate2 * (1.0 - gate2)).astype(BF)

        grad_query_rows, grad_key_rows, grad_value_rows = [], [], []
        for n in range(count):
            cols = slice(n * length, (n + 1) * length)
            value_tok = kv_tok[cols, width:]
            parts = []
            for h in range(heads):
                mine = slice(h * head, (h + 1) * head)
                parts.append(grad_mixed[mine, cols] * inverse_rows[n][h])
            grad_out = jnp.concatenate(parts, axis=0).astype(BF)
            product = grad_out.astype(F32) * mixed_rows[n]
            grads = []
            for h in range(heads):
                mine = slice(h * head, (h + 1) * head)
                there = slice(h * length, (h + 1) * length)
                do_scr[n, mine, there] = grad_out[mine]
                center = jnp.sum(product[mine], axis=0, keepdims=True)
                grad_prob = nn(value_tok * lane_ref[h], grad_out)
                grad_score = (e_scr[n, :, there].astype(F32) * (grad_prob - center)).astype(BF)
                ds_scr[n, :, there] = grad_score
                both = nn(jnp.concatenate([key[mine, cols], chain_ref[...]], axis=0), grad_score)
                grads.append((both[:head] * scaling).astype(BF))
                g_bias_ref[h] += both[head:]
            grad_query_rows.append(jnp.concatenate(grads, axis=0))
            grad_value_rows.append(nt(e_scr[n], do_scr[n]).astype(BF))
            grad_key_rows.append((nt(ds_scr[n], q_scr[n]) * LN2).astype(BF))
        grad_qg = jnp.concatenate([jnp.concatenate(grad_query_rows, axis=1), grad_gate2], axis=0)
        grad_kv = jnp.concatenate(
            [jnp.concatenate(grad_key_rows, axis=0), jnp.concatenate(grad_value_rows, axis=0)],
            axis=1,
        )
        g_qg_ref[...] += nt(normed2, grad_qg)
        g_kv_ref[...] += nn(normed2, grad_kv)
        grad2 = nn(att_qg_ref[...], grad_qg) + nt(att_kv_ref[...], grad_kv)
        g_vec_ref[4] += fold(grad2 * hat2)
        g_vec_ref[5] += fold(grad2)
        grad_x1 = grad_x2 + normalize_back(grad2, vec(4), hat2, scale2)
        grad_branch = (grad_x1 * gate1).astype(BF)
        g_tri_out_ref[...] += nt(mixed, grad_branch)
        grad_mix = nn(tri_out_ref[...], grad_branch)
        g_vec_ref[2] += fold(grad_mix * hat_t)
        g_vec_ref[3] += fold(grad_mix)
        spread_out(dt_ref, start, count, normalize_back(grad_mix, vec(2), hat_t, scale_t))
        grad_gate1 = (grad_x1 * branch * gate1 * (1.0 - gate1)).astype(BF)
        g_gate_ref[...] += nt(normed1, grad_gate1)
        grad1 = nn(gate_w_ref[...], grad_gate1)
        g_vec_ref[0] += fold(grad1 * hat1)
        g_vec_ref[1] += fold(grad1)
        spread_out(z_ref, start, count, grad_x1 + normalize_back(grad1, vec(0), hat1, scale1))
        return carry

    lax.fori_loop(0, total_rows // count, step, 0)


def rows_pass(t, xt, cot_rows, bias, chain, lane, vecs, weights, heads):
    rows, width, length = t.shape
    blocks, pieces, sub, tokens, _ = cot_rows.shape
    some, count = 4, 2
    inner = sub // some
    full = lambda item: pl.BlockSpec(item.shape, lambda at: (0,) * item.ndim)
    by_row = pl.BlockSpec((some, width, length), lambda at: (at, 0, 0))
    by_piece = pl.BlockSpec(
        (1, pieces, some, tokens, width), lambda at: (at // inner, 0, at % inner, 0, 0)
    )
    consts = (bias, chain, lane, vecs) + weights
    wide = weights[-1].shape[1]
    sums = [
        (width, width),
        (width, width),
        (width, 2 * width),
        (width, 2 * width),
        (width, width),
        (width, wide),
        (wide, width),
        (8, width, 128),
        (heads, 16, length),
    ]
    sum_shapes = [jax.ShapeDtypeStruct(shape, F32) for shape in sums]
    return pl.pallas_call(
        functools.partial(rows_kernel, count, heads),
        grid=(rows // some,),
        in_specs=[by_row, by_row, by_piece] + [full(item) for item in consts],
        out_specs=[by_piece, by_row, by_row] + [full(item) for item in sum_shapes],
        out_shape=[
            jax.ShapeDtypeStruct(cot_rows.shape, BF),
            jax.ShapeDtypeStruct(t.shape, F32),
            jax.ShapeDtypeStruct(t.shape, F32),
        ]
        + sum_shapes,
        scratch_shapes=[
            pltpu.VMEM((count, length, heads * length), BF),
            pltpu.VMEM((count, length, heads * length), BF),
            pltpu.VMEM((count, width, heads * length), BF),
            pltpu.VMEM((count, width, heads * length), BF),
        ],
        compiler_params=pltpu.CompilerParams(vmem_limit_bytes=VMEM_LIMIT),
        name="rows",
    )(t, xt, cot_rows, *consts)


def edges_back_kernel(
    xt_ref, z_ref, da_ref, db_ref, wt_ref, w_ref, gain_ref, shift_ref, out_ref, g_w_ref, g_vec_ref, scr
):
    rows, width, length = xt_ref.shape
    count = 2

    @pl.when(pl.program_id(0) == 0)
    def _():
        g_w_ref[...] = jnp.zeros(g_w_ref.shape, F32)
        g_vec_ref[...] = jnp.zeros(g_vec_ref.shape, F32)

    def turn(at, carry):
        for n in range(8):
            e = at * 8 + n
            block = db_ref[e].astype(F32)
            for half in range(scr.shape[0]):
                scr[half, pl.ds(pl.multiple_of(e * rows, rows), rows), :] = block[
                    :, half * 128 : half * 128 + 128
                ]
        return carry

    lax.fori_loop(0, width // 8, turn, 0)

    def step(at, carry):
        start = at * count
        x0 = stacked(xt_ref, start, count).astype(F32)
        lanes = x0.shape[1]
        gain = widen(gain_ref[...], lanes)
        hat, scale = normalize(x0)
        normed = (hat * gain + widen(shift_ref[...], lanes)).astype(BF)
        proj = nn(wt_ref[...], normed)
        pa, pag = proj[:width], proj[width : 2 * width]
        pb, pbg = proj[2 * width : 3 * width], proj[3 * width :]
        da = stacked(da_ref, start, count)
        db = jnp.concatenate(
            [
                scr[half, pl.ds(start + n, width, stride=rows), :]
                for n in range(count)
                for half in range(scr.shape[0])
            ],
            axis=1,
        )
        sa, sb = sigmoid(pag), sigmoid(pbg)
        dsa, dsb = da * sa, db * sb
        grads = jnp.concatenate(
            [
                dsa.astype(BF),
                (dsa * pa * (1.0 - sa)).astype(BF),
                dsb.astype(BF),
                (dsb * pb * (1.0 - sb)).astype(BF),
            ],
            axis=0,
        )
        g_w_ref[...] += nt(normed, grads)
        grad = nn(w_ref[...], grads)
        g_vec_ref[0] += fold(grad * hat)
        g_vec_ref[1] += fold(grad)
        z = stacked(z_ref, start, count)
        store_rows(out_ref, start, count, z + normalize_back(grad, gain, hat, scale))
        return carry

    lax.fori_loop(0, rows // count, step, 0)


def edges_back(xt, z, da, db, weight_t, weight, gain, shift, shape):
    rows, width, length = xt.shape
    blocks, pieces, sub, tokens, _ = shape
    full = lambda item: pl.BlockSpec(item.shape, lambda at: (0,) * item.ndim)
    by_row = pl.BlockSpec((sub, width, length), lambda at: (at, 0, 0))
    sum_shapes = [
        jax.ShapeDtypeStruct(weight.shape, F32),
        jax.ShapeDtypeStruct((2, width, 128), F32),
    ]
    return pl.pallas_call(
        edges_back_kernel,
        grid=(blocks,),
        in_specs=[
            by_row,
            by_row,
            by_row,
            pl.BlockSpec((width, sub, length), lambda at: (0, at, 0)),
        ]
        + [full(item) for item in (weight_t, weight, gain, shift)],
        out_specs=[pl.BlockSpec((1, pieces, sub, tokens, width), lambda at: (at, 0, 0, 0, 0))]
        + [full(item) for item in sum_shapes],
        out_shape=[jax.ShapeDtypeStruct(shape, BF)] + sum_shapes,
        scratch_shapes=[pltpu.VMEM((length // 128, width * sub, 128), F32)],
        compiler_params=pltpu.CompilerParams(vmem_limit_bytes=VMEM_LIMIT),
        name="edges_back",
    )(xt, z, da, db, weight_t, weight, gain, shift)


def shards(
    row_size,
    col_size,
    pair_state,
    cotangent,
    chain_lengths,
    tri_gain,
    tri_shift,
    tri_weight,
    mix_gain,
    mix_shift,
    tri_out,
    att_gain,
    att_shift,
    att_weight,
    chain_bias,
    att_out,
    trans_gain,
    trans_shift,
    up_weight,
    down_weight,
):
    heads = HEADS
    crops, own_rows, tokens, width = pair_state.shape
    length = col_size * tokens
    sub = own_rows // col_size
    axes = ("row", "col")
    shape = (row_size, col_size, sub, tokens, width)

    def exchange(values):
        flat = values.reshape(row_size * col_size, sub, tokens, width)
        return lax.all_to_all(flat, axes, split_axis=0, concat_axis=0, tiled=True)

    x_rows = exchange(pair_state).reshape(shape)
    cot_rows = exchange(cotangent).reshape(shape)

    wide = lambda item: jnp.broadcast_to(item[:, None], (width, 128))
    vecs = jnp.stack(
        [
            wide(item)
            for item in (
                tri_gain,
                tri_shift,
                mix_gain,
                mix_shift,
                att_gain,
                att_shift,
                trans_gain,
                trans_shift,
            )
        ]
    )
    edge_w = tri_weight[:, : 4 * width]
    edge_wt = edge_w.T
    gate_w = tri_weight[:, 4 * width :]
    lengths = lax.dynamic_index_in_dim(chain_lengths, lax.axis_index("row"), 0, keepdims=False)
    ends = jnp.cumsum(lengths)
    places = jnp.arange(length, dtype=jnp.int32)
    chain = jnp.sum((places[:, None] >= ends[None, :]).astype(jnp.int32), axis=-1)
    same = (chain[:, None] == chain[None, :]).astype(F32)
    bias = (LOG2E * chain_bias)[:, None, None] * same[None]
    which = (jnp.arange(16, dtype=jnp.int32)[:, None] == chain[None, :]).astype(F32)
    head_of = jnp.arange(width, dtype=jnp.int32) // (width // heads)
    lane = (jnp.arange(heads, dtype=jnp.int32)[:, None] == head_of[None, :]).astype(BF)
    lane = jnp.broadcast_to(lane[:, None, :], (heads, length, width))

    left, right, xt = edges(x_rows, edge_wt, vecs[0], vecs[1])
    right_all = lax.all_gather(right, "col", axis=0, tiled=False)
    t = triangle(left, right_all, sub)
    weights = (
        gate_w,
        gate_w.T,
        tri_out,
        tri_out.T,
        att_weight.T,
        att_weight[:, width : 3 * width],
        jnp.concatenate([att_weight[:, :width], att_weight[:, 3 * width :]], axis=1),
        att_out,
        att_out.T,
        up_weight,
        up_weight.T,
        down_weight,
        down_weight.T,
    )
    (
        out_rows,
        dt,
        z,
        g_gate,
        g_tri_out,
        g_qg,
        g_kv,
        g_att_out,
        g_up,
        g_down,
        g_vec,
        g_bias,
    ) = rows_pass(t, xt, cot_rows, bias, which.astype(BF), lane, vecs, weights, heads)
    back = (crops, own_rows, tokens, width)
    pair_out = exchange(out_rows).reshape(back)
    da, db_parts = triangle_back(dt, left, right_all, sub)
    db = lax.psum_scatter(db_parts, "col", scatter_dimension=0, tiled=False)
    grad_rows, g_edge, g_vec_edge = edges_back(
        xt, z, da, db, edge_wt, edge_w, vecs[0], vecs[1], shape
    )
    grad_pair = exchange(grad_rows).reshape(back)

    g_vec = jnp.sum(g_vec, axis=-1)
    g_vec_edge = jnp.sum(g_vec_edge, axis=-1)
    grad_chain_bias = jnp.sum(g_bias * which[None], axis=(1, 2))
    total = lambda item: lax.psum(item.astype(BF), axes).astype(F32)
    total_gate = total(g_gate)
    total_edge = total(g_edge)
    total_qg = total(g_qg)
    small = lax.psum(
        jnp.concatenate(
            [g_vec[0] + g_vec_edge[0], g_vec[1] + g_vec_edge[1], g_vec[2:].reshape(-1), grad_chain_bias]
        ),
        axes,
    )
    piece = lambda at: small[at * width : (at + 1) * width]
    return (
        pair_out,
        grad_pair,
        piece(0),
        piece(1),
        jnp.concatenate([total_edge, total_gate], axis=1),
        piece(2),
        piece(3),
        total(g_tri_out),
        piece(4),
        piece(5),
        jnp.concatenate([total_qg[:, :width], total(g_kv), total_qg[:, width:]], axis=1),
        small[8 * width :],
        total(g_att_out),
        piece(6),
        piece(7),
        total(g_up),
        total(g_down),
    )


def solution(mesh):
    pair = P("dp", "row", "col", None)
    vector, matrix = P("dp"), P("dp", None)
    return jax.shard_map(
        functools.partial(shards, mesh.shape["row"], mesh.shape["col"]),
        mesh=mesh,
        in_specs=(pair, pair, P("dp", None)) + (P(),) * 15,
        out_specs=(
            pair,
            pair,
            vector,
            vector,
            matrix,
            vector,
            vector,
            matrix,
            vector,
            vector,
            matrix,
            vector,
            matrix,
            vector,
            vector,
            matrix,
            matrix,
        ),
        check_vma=False,
    )
```

```python
import functools
import math

import jax
import jax.numpy as jnp
from jax import lax
from jax.experimental import pallas as pl
from jax.experimental.pallas import tpu as pltpu
from jax.sharding import PartitionSpec as P

HEADS = 4
EPS = 1e-05
LOG2E = math.log2(math.e)
LN2 = math.log(2.0)
CHUNKS = 2
VMEM_LIMIT = 56 * 1024 * 1024
BF = jnp.bfloat16
F32 = jnp.float32


def nn(left, right):
    return lax.dot_general(left, right, (((1,), (0,)), ((), ())), preferred_element_type=F32)


def nt(left, right):
    return lax.dot_general(left, right, (((1,), (1,)), ((), ())), preferred_element_type=F32)


def tn(left, right):
    return lax.dot_general(left, right, (((0,), (0,)), ((), ())), preferred_element_type=F32)


def sigmoid(values):
    return 0.5 * jnp.tanh(0.5 * values) + 0.5


def normalize(values):
    center = values - jnp.mean(values, axis=0, keepdims=True)
    spread = jnp.mean(center * center, axis=0, keepdims=True)
    scale = lax.rsqrt(spread + EPS)
    return center * scale, scale


def normalize_back(grads, gain, hat, scale):
    grad_hat = grads * gain
    first = jnp.mean(grad_hat, axis=0, keepdims=True)
    second = jnp.mean(grad_hat * hat, axis=0, keepdims=True)
    return scale * (grad_hat - first - hat * second)


def widen(column, lanes):
    return jnp.concatenate([column] * (lanes // column.shape[1]), axis=1)


def fold(values):
    parts = [values[:, at : at + 128] for at in range(0, values.shape[1], 128)]
    return functools.reduce(lambda one, two: one + two, parts)


def load_tokens(ref, row, order):
    _, pieces, some, tokens, width = ref.shape
    flat = ref[row // some, :, row % some, :, :].astype(F32)
    flat = flat.reshape(order + (flat.shape[0] * tokens // math.prod(order), width))
    return flat.transpose(2, 1, 0, 3, 4).reshape(pieces * tokens, width)


def store_tokens(ref, row, order, values):
    _, pieces, some, tokens, width = ref.shape
    back = order[::-1]
    flat = values.reshape(back + (pieces * tokens // math.prod(order), width))
    flat = flat.transpose(2, 1, 0, 3, 4).reshape(pieces, tokens, width)
    ref[row // some, :, row % some, :, :] = flat.astype(ref.dtype)


def stacked(ref, start, count):
    return jnp.concatenate([ref[start + n] for n in range(count)], axis=1)


def spread_out(ref, start, count, values):
    length = values.shape[1] // count
    for n in range(count):
        ref[start + n] = values[:, n * length : (n + 1) * length].astype(ref.dtype)


def edges_kernel(order, x_ref, w_ref, gain_ref, shift_ref, a_ref, b_ref, xt_ref, a_scr, b_scr):
    rows, width, length = xt_ref.shape
    count = 2

    def step(at, carry):
        start = at * count
        tokens = [load_tokens(x_ref, start + n, order).astype(BF) for n in range(count)]
        x0 = jnp.concatenate([item.T for item in tokens], axis=1)
        spread_out(xt_ref, start, count, x0)
        hat, _ = normalize(x0.astype(F32))
        lanes = x0.shape[1]
        normed = (hat * widen(gain_ref[...], lanes) + widen(shift_ref[...], lanes)).astype(BF)
        proj = nn(w_ref[...], normed)
        left = sigmoid(proj[width : 2 * width]) * proj[:width]
        right = sigmoid(proj[3 * width : 4 * width]) * proj[2 * width : 3 * width]
        for n in range(count):
            base = pl.multiple_of((start + n) * width, width)
            for half in range(length // 128):
                part = slice(n * length + half * 128, n * length + half * 128 + 128)
                a_scr[half, pl.ds(base, width), :] = left[:, part]
                b_scr[half, pl.ds(base, width), :] = right[:, part]
        return carry

    lax.fori_loop(0, rows // count, step, 0)

    def turn(at, carry):
        for n in range(8):
            e = at * 8 + n
            for scr, out in ((a_scr, a_ref), (b_scr, b_ref)):
                halves = [scr[h, pl.ds(e, rows, stride=width), :] for h in range(scr.shape[0])]
                out[e] = jnp.concatenate(halves, axis=1).astype(BF)
        return carry

    lax.fori_loop(0, width // 8, turn, 0)


def edges(x_rows, order, weight, gain, shift):
    blocks, pieces, some, tokens, width = x_rows.shape
    length = pieces * tokens
    rows = blocks * some
    step = 16 // some
    const = lambda at: (0, 0)
    return pl.pallas_call(
        functools.partial(edges_kernel, order),
        grid=(blocks // step,),
        in_specs=[
            pl.BlockSpec((step, pieces, some, tokens, width), lambda at: (at, 0, 0, 0, 0)),
            pl.BlockSpec(weight.shape, const),
            pl.BlockSpec(gain.shape, const),
            pl.BlockSpec(shift.shape, const),
        ],
        out_specs=[
            pl.BlockSpec((width, 16, length), lambda at: (0, at, 0)),
            pl.BlockSpec((width, 16, length), lambda at: (0, at, 0)),
            pl.BlockSpec((16, width, length), lambda at: (at, 0, 0)),
        ],
        out_shape=[
            jax.ShapeDtypeStruct((width, rows, length), BF),
            jax.ShapeDtypeStruct((width, rows, length), BF),
            jax.ShapeDtypeStruct((rows, width, length), BF),
        ],
        scratch_shapes=[
            pltpu.VMEM((length // 128, 16 * width, 128), F32),
            pltpu.VMEM((length // 128, 16 * width, 128), F32),
        ],
        compiler_params=pltpu.CompilerParams(vmem_limit_bytes=VMEM_LIMIT),
        name="edges",
    )(x_rows, weight, gain, shift)


def gather_pieces(place_ref, chunks, e, scr):
    for c, pieces in enumerate(chunks):
        rows = pieces[0].shape[1]
        for m, piece in enumerate(pieces):
            at = pl.multiple_of(c * rows * len(pieces) + place_ref[m], rows)
            scr[e, pl.ds(at, rows), :] = piece[e]


def triangle_kernel(chunks, pieces, place_ref, *refs):
    lefts, refs = refs[:chunks], refs[chunks:]
    rights, refs = refs[: chunks * pieces], refs[chunks * pieces :]
    outs, scr = refs[:chunks], refs[chunks]
    rights = [rights[c * pieces : (c + 1) * pieces] for c in range(chunks)]
    for e in range(scr.shape[0]):
        gather_pieces(place_ref, rights, e, scr)
        t = nt(jnp.concatenate([left[e] for left in lefts], axis=0), scr[e])
        rows = lefts[0].shape[1]
        for c, out in enumerate(outs):
            out[:, e, :] = t[c * rows : (c + 1) * rows]


def triangle(place, lefts, rights):
    width, rows, length = lefts[0].shape
    chunks, pieces = len(lefts), len(rights[0])
    some = 8
    low = pl.BlockSpec((some, rows, length), lambda at, place: (at, 0, 0))
    high = pl.BlockSpec((rows, some, length), lambda at, place: (0, at, 0))
    return pl.pallas_call(
        functools.partial(triangle_kernel, chunks, pieces),
        grid_spec=pltpu.PrefetchScalarGridSpec(
            num_scalar_prefetch=1,
            grid=(width // some,),
            in_specs=[low] * (chunks + chunks * pieces),
            out_specs=[high] * chunks,
            scratch_shapes=[pltpu.VMEM((some, length, length), BF)],
        ),
        out_shape=[jax.ShapeDtypeStruct((rows, width, length), F32)] * chunks,
        compiler_params=pltpu.CompilerParams(vmem_limit_bytes=VMEM_LIMIT),
        name="triangle",
    )(place, *lefts, *[piece for chunk in rights for piece in chunk])


def right_back_kernel(chunks, place_ref, *refs):
    grads, refs = refs[:chunks], refs[chunks:]
    lefts, refs = refs[:chunks], refs[chunks:]
    outs, scr = refs[:-1], refs[-1]
    rows = outs[0].shape[1]
    for e in range(scr.shape[0]):
        grad = jnp.concatenate([ref[:, e, :] for ref in grads], axis=0).astype(BF)
        left = jnp.concatenate([ref[e] for ref in lefts], axis=0)
        scr[e] = tn(grad, left).astype(BF)
        for m, out in enumerate(outs):
            out[e] = scr[e, pl.ds(pl.multiple_of(place_ref[m], rows), rows), :]


def right_back(place, grads, lefts, c):
    width, rows, length = lefts[0].shape
    chunks = len(lefts)
    part = length // chunks
    pieces = part // rows
    some = 8
    low = pl.BlockSpec((some, rows, length), lambda at, place: (at, 0, 0))
    return pl.pallas_call(
        functools.partial(right_back_kernel, chunks),
        grid_spec=pltpu.PrefetchScalarGridSpec(
            num_scalar_prefetch=1,
            grid=(width // some,),
            in_specs=[pl.BlockSpec((rows, some, part), lambda at, place: (0, at, c))] * chunks
            + [low] * chunks,
            out_specs=[low] * pieces,
            scratch_shapes=[pltpu.VMEM((some, part, length), BF)],
        ),
        out_shape=[jax.ShapeDtypeStruct((width, rows, length), BF)] * pieces,
        compiler_params=pltpu.CompilerParams(vmem_limit_bytes=VMEM_LIMIT),
        name="right_back",
    )(place, *grads, *lefts)


def left_back_kernel(chunks, pieces, place_ref, *refs):
    grads, refs = refs[:chunks], refs[chunks:]
    rights, refs = refs[: chunks * pieces], refs[chunks * pieces :]
    outs, scr = refs[:chunks], refs[chunks]
    rights = [rights[c * pieces : (c + 1) * pieces] for c in range(chunks)]
    rows = grads[0].shape[0]
    for e in range(scr.shape[0]):
        gather_pieces(place_ref, rights, e, scr)
        grad = jnp.concatenate([ref[:, e, :] for ref in grads], axis=0).astype(BF)
        da = nn(grad, scr[e])
        for c, out in enumerate(outs):
            out[:, e, :] = da[c * rows : (c + 1) * rows]


def left_back(place, grads, rights):
    rows, width, length = grads[0].shape
    chunks, pieces = len(grads), len(rights[0])
    some = 8
    low = pl.BlockSpec((some, rows, length), lambda at, place: (at, 0, 0))
    high = pl.BlockSpec((rows, some, length), lambda at, place: (0, at, 0))
    return pl.pallas_call(
        functools.partial(left_back_kernel, chunks, pieces),
        grid_spec=pltpu.PrefetchScalarGridSpec(
            num_scalar_prefetch=1,
            grid=(width // some,),
            in_specs=[high] * chunks + [low] * (chunks * pieces),
            out_specs=[high] * chunks,
            scratch_shapes=[pltpu.VMEM((some, length, length), BF)],
        ),
        out_shape=[jax.ShapeDtypeStruct((rows, width, length), F32)] * chunks,
        compiler_params=pltpu.CompilerParams(vmem_limit_bytes=VMEM_LIMIT),
        name="left_back",
    )(place, *grads, *[piece for chunk in rights for piece in chunk])


def rows_kernel(count, heads, order, first, *refs):
    sums = 9
    before = [] if first else refs[:sums]
    rows_body(count, heads, order, before, *refs[len(before) :])


def rows_body(
    count,
    heads,
    order,
    before,
    t_ref,
    xt_ref,
    cot_ref,
    bias_ref,
    chain_ref,
    lane_ref,
    vec_ref,
    gate_w_ref,
    gate_wt_ref,
    tri_out_ref,
    tri_out_t_ref,
    att_t_ref,
    att_qkv_ref,
    att_qg_ref,
    att_out_ref,
    att_out_t_ref,
    up_ref,
    up_t_ref,
    down_ref,
    down_t_ref,
    out_ref,
    dt_ref,
    z_ref,
    g_gate_ref,
    g_tri_out_ref,
    g_qg_ref,
    g_kv_ref,
    g_att_out_ref,
    g_up_ref,
    g_down_ref,
    g_vec_ref,
    g_bias_ref,
    e_scr,
    ds_scr,
):
    total_rows, width, length = t_ref.shape
    lanes = count * length
    head = width // heads
    scaling = 1.0 / math.sqrt(head)

    sums = (
        g_gate_ref,
        g_tri_out_ref,
        g_qg_ref,
        g_kv_ref,
        g_att_out_ref,
        g_up_ref,
        g_down_ref,
        g_vec_ref,
        g_bias_ref,
    )

    @pl.when(pl.program_id(0) == 0)
    def _():
        for n, ref in enumerate(sums):
            ref[...] = before[n][...] if before else jnp.zeros(ref.shape, ref.dtype)

    def vec(at):
        return widen(vec_ref[at], lanes)

    def step(at, carry):
        start = at * count
        x0 = stacked(xt_ref, start, count).astype(F32)
        hat1, scale1 = normalize(x0)
        normed1 = (hat1 * vec(0) + vec(1)).astype(BF)
        gate1 = sigmoid(nn(gate_wt_ref[...], normed1))
        hat_t, scale_t = normalize(stacked(t_ref, start, count))
        mixed = (hat_t * vec(2) + vec(3)).astype(BF)
        branch = nn(tri_out_t_ref[...], mixed)
        x1 = x0 + gate1 * branch
        hat2, scale2 = normalize(x1)
        normed2 = (hat2 * vec(4) + vec(5)).astype(BF)
        hidden = nn(att_t_ref[...], normed2)
        query = (hidden[:width] * (scaling * LOG2E)).astype(BF)
        hidden = hidden.astype(BF)
        key = hidden[width : 2 * width]
        value = hidden[2 * width : 3 * width]
        gate2 = sigmoid(hidden[3 * width :].astype(F32))
        normed2_tok = normed2.T
        qkv_tok = nn(normed2_tok, att_qkv_ref[...])
        query_tok = (qkv_tok[:, :width] * (scaling * LOG2E)).astype(BF)
        qkv_tok = qkv_tok.astype(BF)
        ones = jnp.ones((16, length), BF)

        mixed_rows, inverse_rows = [], []
        for n in range(count):
            cols = slice(n * length, (n + 1) * length)
            key_tok = qkv_tok[cols, width : 2 * width]
            query_n = query[:, cols]
            outs, inverses = [], []
            for h in range(heads):
                mine = slice(h * head, (h + 1) * head)
                there = slice(h * length, (h + 1) * length)
                score = nn(key_tok * lane_ref[h], query_n) + bias_ref[h]
                peak = jnp.max(score, axis=0, keepdims=True)
                expon = jnp.exp2(score - peak).astype(BF)
                e_scr[n, :, there] = expon
                both = nn(jnp.concatenate([value[mine, cols], ones], axis=0), expon)
                inverse = 1.0 / both[head : head + 1]
                outs.append(both[:head] * inverse)
                inverses.append(inverse)
            mixed_rows.append(jnp.concatenate(outs, axis=0))
            inverse_rows.append(inverses)
        attended = jnp.concatenate(mixed_rows, axis=1)
        gated = (gate2 * attended).astype(BF)
        x2 = x1 + nn(att_out_t_ref[...], gated)
        hat3, scale3 = normalize(x2)
        normed3 = (hat3 * vec(6) + vec(7)).astype(BF)
        up = nn(up_t_ref[...], normed3)
        gate3 = sigmoid(up)
        act = (up * gate3).astype(BF)
        out = (x2 + nn(down_t_ref[...], act)).astype(BF)
        for n in range(count):
            store_tokens(out_ref, start + n, order, out[:, n * length : (n + 1) * length].T.astype(F32))

        cot_tok = [load_tokens(cot_ref, start + n, order).astype(BF) for n in range(count)]
        cot_low = jnp.concatenate([item.T for item in cot_tok], axis=1)
        cot = cot_low.astype(F32)
        g_down_ref[...] += nn(act, jnp.concatenate(cot_tok, axis=0))
        grad_up = (nn(down_ref[...], cot_low) * (gate3 * (1.0 + up * (1.0 - gate3)))).astype(BF)
        g_up_ref[...] += nt(normed3, grad_up)
        grad3 = nn(up_ref[...], grad_up)
        g_vec_ref[6] += fold(grad3 * hat3)
        g_vec_ref[7] += fold(grad3)
        grad_x2 = cot + normalize_back(grad3, vec(6), hat3, scale3)
        grad_x2_low = grad_x2.astype(BF)
        g_att_out_ref[...] += nt(gated, grad_x2_low)
        grad_gated = nn(att_out_ref[...], grad_x2_low)
        grad_mixed = grad_gated * gate2
        grad_gate2 = (grad_gated * attended * gate2 * (1.0 - gate2)).astype(BF)

        grad_query_rows, grad_key_rows, grad_value_rows = [], [], []
        for n in range(count):
            cols = slice(n * length, (n + 1) * length)
            value_tok = qkv_tok[cols, 2 * width :]
            parts = []
            for h in range(heads):
                mine = slice(h * head, (h + 1) * head)
                parts.append(grad_mixed[mine, cols] * inverse_rows[n][h])
            grad_out = jnp.concatenate(parts, axis=0).astype(BF)
            product = grad_out.astype(F32) * mixed_rows[n]
            grad_out_tok = grad_out.T
            grads = []
            for h in range(heads):
                mine = slice(h * head, (h + 1) * head)
                there = slice(h * length, (h + 1) * length)
                center = jnp.sum(product[mine], axis=0, keepdims=True)
                grad_prob = nn(value_tok * lane_ref[h], grad_out)
                grad_score = (e_scr[n, :, there].astype(F32) * (grad_prob - center)).astype(BF)
                ds_scr[n, :, there] = grad_score
                both = nn(jnp.concatenate([key[mine, cols], chain_ref[...]], axis=0), grad_score)
                grads.append((both[:head] * scaling).astype(BF))
                g_bias_ref[h] += both[head:]
            grad_query_rows.append(jnp.concatenate(grads, axis=0))
            split = lambda item: jnp.concatenate([item * lane_ref[h] for h in range(heads)], axis=0)
            grad_value_rows.append(nn(e_scr[n], split(grad_out_tok)).astype(BF))
            grad_key_rows.append((nn(ds_scr[n], split(query_tok[cols])) * LN2).astype(BF))
        grad_qg = jnp.concatenate([jnp.concatenate(grad_query_rows, axis=1), grad_gate2], axis=0)
        grad_kv = jnp.concatenate(
            [jnp.concatenate(grad_key_rows, axis=0), jnp.concatenate(grad_value_rows, axis=0)],
            axis=1,
        )
        g_qg_ref[...] += nn(grad_qg, normed2_tok)
        g_kv_ref[...] += nn(normed2, grad_kv)
        grad2 = nn(att_qg_ref[...], grad_qg) + nt(att_qkv_ref[:, width:], grad_kv)
        g_vec_ref[4] += fold(grad2 * hat2)
        g_vec_ref[5] += fold(grad2)
        grad_x1 = grad_x2 + normalize_back(grad2, vec(4), hat2, scale2)
        grad_branch = (grad_x1 * gate1).astype(BF)
        g_tri_out_ref[...] += nt(mixed, grad_branch)
        grad_mix = nn(tri_out_ref[...], grad_branch)
        g_vec_ref[2] += fold(grad_mix * hat_t)
        g_vec_ref[3] += fold(grad_mix)
        spread_out(dt_ref, start, count, normalize_back(grad_mix, vec(2), hat_t, scale_t))
        grad_gate1 = (grad_x1 * branch * gate1 * (1.0 - gate1)).astype(BF)
        g_gate_ref[...] += nt(normed1, grad_gate1)
        grad1 = nn(gate_w_ref[...], grad_gate1)
        g_vec_ref[0] += fold(grad1 * hat1)
        g_vec_ref[1] += fold(grad1)
        spread_out(z_ref, start, count, grad_x1 + normalize_back(grad1, vec(0), hat1, scale1))
        return carry

    lax.fori_loop(0, total_rows // count, step, 0)


def rows_pass(before, t, xt, cot_rows, order, bias, chain, lane, vecs, weights, heads):
    rows, width, length = t.shape
    blocks, pieces, sub, tokens, _ = cot_rows.shape
    some, count = 4, 2
    inner = sub // some
    full = lambda item: pl.BlockSpec(item.shape, lambda at: (0,) * item.ndim)
    by_row = pl.BlockSpec((some, width, length), lambda at: (at, 0, 0))
    by_piece = pl.BlockSpec(
        (1, pieces, some, tokens, width), lambda at: (at // inner, 0, at % inner, 0, 0)
    )
    consts = (bias, chain, lane, vecs) + weights
    wide = weights[-1].shape[1]
    sums = [
        (width, width),
        (width, width),
        (2 * width, width),
        (width, 2 * width),
        (width, width),
        (width, wide),
        (wide, width),
        (8, width, 128),
        (heads, 16, length),
    ]
    sum_shapes = [jax.ShapeDtypeStruct(shape, F32) for shape in sums]
    return pl.pallas_call(
        functools.partial(rows_kernel, count, heads, order, not before),
        grid=(rows // some,),
        in_specs=[full(item) for item in before]
        + [by_row, by_row, by_piece]
        + [full(item) for item in consts],
        out_specs=[by_piece, by_row, by_row] + [full(item) for item in sum_shapes],
        out_shape=[
            jax.ShapeDtypeStruct(cot_rows.shape, BF),
            jax.ShapeDtypeStruct(t.shape, F32),
            jax.ShapeDtypeStruct(t.shape, F32),
        ]
        + sum_shapes,
        scratch_shapes=[
            pltpu.VMEM((count, length, heads * length), BF),
            pltpu.VMEM((count, length, heads * length), BF),
        ],
        compiler_params=pltpu.CompilerParams(vmem_limit_bytes=VMEM_LIMIT),
        name="rows",
    )(*before, t, xt, cot_rows, *consts)


def edges_back_kernel(order, terms, first, *refs):
    before, refs = (refs[:0], refs) if first else (refs[:2], refs[2:])
    xt_ref, z_ref, da_ref = refs[:3]
    db_refs, refs = refs[3 : 3 + terms], refs[3 + terms :]
    wt_ref, w_ref, gain_ref, shift_ref, out_ref, g_w_ref, g_vec_ref, scr = refs
    rows, width, length = xt_ref.shape
    count = 2

    @pl.when(pl.program_id(0) == 0)
    def _():
        for n, ref in enumerate((g_w_ref, g_vec_ref)):
            ref[...] = jnp.zeros(ref.shape, F32) if first else before[n][...]

    def turn(at, carry):
        for n in range(8):
            e = at * 8 + n
            block = sum(ref[e].astype(F32) for ref in db_refs)
            for half in range(scr.shape[0]):
                scr[half, pl.ds(pl.multiple_of(e * rows, rows), rows), :] = block[
                    :, half * 128 : half * 128 + 128
                ]
        return carry

    lax.fori_loop(0, width // 8, turn, 0)

    def step(at, carry):
        start = at * count
        x0 = stacked(xt_ref, start, count).astype(F32)
        lanes = x0.shape[1]
        gain = widen(gain_ref[...], lanes)
        hat, scale = normalize(x0)
        normed = (hat * gain + widen(shift_ref[...], lanes)).astype(BF)
        proj = nn(wt_ref[...], normed)
        pa, pag = proj[:width], proj[width : 2 * width]
        pb, pbg = proj[2 * width : 3 * width], proj[3 * width :]
        da = stacked(da_ref, start, count)
        db = jnp.concatenate(
            [
                scr[half, pl.ds(start + n, width, stride=rows), :]
                for n in range(count)
                for half in range(scr.shape[0])
            ],
            axis=1,
        )
        sa, sb = sigmoid(pag), sigmoid(pbg)
        dsa, dsb = da * sa, db * sb
        grads = jnp.concatenate(
            [
                dsa.astype(BF),
                (dsa * pa * (1.0 - sa)).astype(BF),
                dsb.astype(BF),
                (dsb * pb * (1.0 - sb)).astype(BF),
            ],
            axis=0,
        )
        g_w_ref[...] += nt(normed, grads)
        grad = nn(w_ref[...], grads)
        g_vec_ref[0] += fold(grad * hat)
        g_vec_ref[1] += fold(grad)
        out = stacked(z_ref, start, count) + normalize_back(grad, gain, hat, scale)
        out = out.astype(BF)
        for n in range(count):
            store_tokens(out_ref, start + n, order, out[:, n * length : (n + 1) * length].T.astype(F32))
        return carry

    lax.fori_loop(0, rows // count, step, 0)


def edges_back(before, xt, z, da, db_terms, order, weight_t, weight, gain, shift, shape):
    rows, width, length = xt.shape
    blocks, pieces, some, tokens, _ = shape
    step = 16 // some
    full = lambda item: pl.BlockSpec(item.shape, lambda at: (0,) * item.ndim)
    by_row = pl.BlockSpec((16, width, length), lambda at: (at, 0, 0))
    sum_shapes = [
        jax.ShapeDtypeStruct(weight.shape, F32),
        jax.ShapeDtypeStruct((2, width, 128), F32),
    ]
    return pl.pallas_call(
        functools.partial(edges_back_kernel, order, len(db_terms), not before),
        grid=(blocks // step,),
        in_specs=[full(item) for item in before]
        + [by_row, by_row, by_row]
        + [pl.BlockSpec((width, 16, length), lambda at: (0, at, 0))] * len(db_terms)
        + [full(item) for item in (weight_t, weight, gain, shift)],
        out_specs=[pl.BlockSpec((step, pieces, some, tokens, width), lambda at: (at, 0, 0, 0, 0))]
        + [full(item) for item in sum_shapes],
        out_shape=[jax.ShapeDtypeStruct(shape, BF)] + sum_shapes,
        scratch_shapes=[pltpu.VMEM((length // 128, width * 16, 128), F32)],
        compiler_params=pltpu.CompilerParams(vmem_limit_bytes=VMEM_LIMIT),
        name="edges_back",
    )(*before, xt, z, da, *db_terms, weight_t, weight, gain, shift)


def shards(
    row_size,
    col_size,
    pair_state,
    cotangent,
    chain_lengths,
    tri_gain,
    tri_shift,
    tri_weight,
    mix_gain,
    mix_shift,
    tri_out,
    att_gain,
    att_shift,
    att_weight,
    chain_bias,
    att_out,
    trans_gain,
    trans_shift,
    up_weight,
    down_weight,
):
    heads = HEADS
    crops, own_rows, tokens, width = pair_state.shape
    length = col_size * tokens
    chunks = CHUNKS
    some = own_rows // (col_size * chunks)
    axes = ("row", "col")
    group = row_size * col_size
    order = (row_size, col_size, chunks)
    shape = (row_size, col_size, some, tokens, width)

    def swap(values):
        return lax.all_to_all(values, axes, split_axis=0, concat_axis=0, tiled=True)

    def cut(values):
        parts = values.reshape(group, chunks, some, tokens, width)
        return [parts[:, c] for c in range(chunks)]

    def join(parts):
        return jnp.stack(parts, axis=1).reshape(crops, own_rows, tokens, width)

    def across(values, bit):
        return lax.ppermute(values, "col", [(q, q ^ bit) for q in range(col_size)])

    bits = [1 << n for n in range(col_size.bit_length() - 1)]

    def gather(own):
        pieces = {0: own}
        for bit in reversed(bits):
            for m in list(pieces):
                pieces[m ^ bit] = across(pieces[m], bit)
        return [pieces[m] for m in range(col_size)]

    def scatter_sum(parts):
        terms = {m: [part] for m, part in enumerate(parts)}
        for bit in bits:
            for m in [m for m in terms if m & bit]:
                items = terms.pop(m)
                sent = items[0]
                if len(items) > 1:
                    sent = sum(item.astype(F32) for item in items).astype(BF)
                terms[m ^ bit].append(across(sent, bit))
        return terms[0]

    x_rows = [swap(part).reshape(shape) for part in cut(pair_state)]
    cot_rows = [swap(part).reshape(shape) for part in cut(cotangent)]

    wide = lambda item: jnp.broadcast_to(item[:, None], (width, 128))
    vecs = jnp.stack(
        [
            wide(item)
            for item in (
                tri_gain,
                tri_shift,
                mix_gain,
                mix_shift,
                att_gain,
                att_shift,
                trans_gain,
                trans_shift,
            )
        ]
    )
    edge_w = tri_weight[:, : 4 * width]
    edge_wt = edge_w.T
    gate_w = tri_weight[:, 4 * width :]
    lengths = lax.dynamic_index_in_dim(chain_lengths, lax.axis_index("row"), 0, keepdims=False)
    ends = jnp.cumsum(lengths)
    places = jnp.arange(length, dtype=jnp.int32)
    places = places.reshape(order + (some,)).transpose(2, 1, 0, 3).reshape(length)
    chain = jnp.sum((places[:, None] >= ends[None, :]).astype(jnp.int32), axis=-1)
    same = (chain[:, None] == chain[None, :]).astype(F32)
    bias = (LOG2E * chain_bias)[:, None, None] * same[None]
    which = (jnp.arange(16, dtype=jnp.int32)[:, None] == chain[None, :]).astype(F32)
    head_of = jnp.arange(width, dtype=jnp.int32) // (width // heads)
    lane = (jnp.arange(heads, dtype=jnp.int32)[:, None] == head_of[None, :]).astype(BF)
    lane = jnp.broadcast_to(lane[:, None, :], (heads, length, width))
    place = (lax.axis_index("col") ^ jnp.arange(col_size, dtype=jnp.int32)) * (row_size * some)

    lefts, rights, xts = [], [], []
    for c in range(chunks):
        left, right, xt = edges(x_rows[c], order, edge_wt, vecs[0], vecs[1])
        lefts.append(left)
        rights.append(gather(right))
        xts.append(xt)
    ts = triangle(place, lefts, rights)
    weights = (
        gate_w,
        gate_w.T,
        tri_out,
        tri_out.T,
        att_weight.T,
        att_weight[:, : 3 * width],
        jnp.concatenate([att_weight[:, :width], att_weight[:, 3 * width :]], axis=1),
        att_out,
        att_out.T,
        up_weight,
        up_weight.T,
        down_weight,
        down_weight.T,
    )
    chain_rows = which.astype(BF)
    sums, outs, dts, zs = [], [], [], []
    for c in range(chunks):
        out, dt, z, *sums = rows_pass(
            sums, ts[c], xts[c], cot_rows[c], order, bias, chain_rows, lane, vecs, weights, heads
        )
        outs.append(swap(out.reshape(group, some, tokens, width)))
        dts.append(dt)
        zs.append(z)
    g_gate, g_tri_out, g_qg, g_kv, g_att_out, g_up, g_down, g_vec, g_bias = sums

    def whole_sum(parts):
        flat = [part.astype(BF).reshape(group, width // group, -1) for part in parts]
        mine = swap(jnp.concatenate(flat, axis=2))
        mine = jnp.sum(mine.astype(F32), axis=0, keepdims=True).astype(BF)
        every = swap(jnp.broadcast_to(mine, (group,) + mine.shape[1:]))
        every = every.astype(F32).reshape(width, -1)
        result, at = [], 0
        for part in parts:
            result.append(every[:, at : at + part.shape[1]])
            at += part.shape[1]
        return result

    ff = g_down.shape[0] // width
    row_sums = whole_sum(
        [g_gate, g_tri_out, g_qg[:width].T, g_qg[width:].T, g_kv, g_att_out, g_up]
        + [g_down[n * width : (n + 1) * width] for n in range(ff)]
    )
    t_gate, t_tri_out, t_query, t_gate2, t_kv, t_att_out, t_up = row_sums[:7]
    t_down = jnp.concatenate(row_sums[7:], axis=0)

    db_terms = [scatter_sum(right_back(place, dts, lefts, c)) for c in range(chunks)]
    das = left_back(place, dts, rights)
    edge_sums, grads = [], []
    for c in range(chunks):
        grad, *edge_sums = edges_back(
            edge_sums, xts[c], zs[c], das[c], db_terms[c], order, edge_wt, edge_w, vecs[0], vecs[1], shape
        )
        grads.append(swap(grad.reshape(group, some, tokens, width)))
    g_edge, g_vec_edge = edge_sums
    (t_edge,) = whole_sum([g_edge])

    g_vec = jnp.sum(g_vec, axis=-1)
    g_vec_edge = jnp.sum(g_vec_edge, axis=-1)
    g_chain = jnp.sum(g_bias * which[None], axis=(1, 2))
    small = jnp.concatenate(
        [g_vec[:2] + g_vec_edge, g_vec[2:], jnp.pad(g_chain, (0, width - heads))[None]], axis=0
    )
    small = jnp.sum(swap(jnp.broadcast_to(small[None], (group,) + small.shape)), axis=0)
    return (
        join(outs),
        join(grads),
        small[0],
        small[1],
        jnp.concatenate([t_edge, t_gate], axis=1),
        small[2],
        small[3],
        t_tri_out,
        small[4],
        small[5],
        jnp.concatenate([t_query, t_kv, t_gate2], axis=1),
        small[8, :heads],
        t_att_out,
        small[6],
        small[7],
        t_up,
        t_down,
    )


def solution(mesh):
    pair = P("dp", "row", "col", None)
    vector, matrix = P("dp"), P("dp", None)
    return jax.shard_map(
        functools.partial(shards, mesh.shape["row"], mesh.shape["col"]),
        mesh=mesh,
        in_specs=(pair, pair, P("dp", None)) + (P(),) * 15,
        out_specs=(
            pair,
            pair,
            vector,
            vector,
            matrix,
            vector,
            vector,
            matrix,
            vector,
            vector,
            matrix,
            vector,
            matrix,
            vector,
            vector,
            matrix,
            matrix,
        ),
        check_vma=False,
    )
```

```python
import functools
import math

import jax
import jax.numpy as jnp
from jax import lax
from jax.experimental import pallas as pl
from jax.experimental.pallas import tpu as pltpu
from jax.sharding import PartitionSpec as P

HEADS = 4
EPS = 1e-05
LOG2E = math.log2(math.e)
LN2 = math.log(2.0)
CHUNKS = 2
VMEM_LIMIT = 56 * 1024 * 1024
BF = jnp.bfloat16
F32 = jnp.float32


def nn(left, right):
    return lax.dot_general(left, right, (((1,), (0,)), ((), ())), preferred_element_type=F32)


def nt(left, right):
    return lax.dot_general(left, right, (((1,), (1,)), ((), ())), preferred_element_type=F32)


def tn(left, right):
    return lax.dot_general(left, right, (((0,), (0,)), ((), ())), preferred_element_type=F32)


def cost(flops, size=0):
    return pl.CostEstimate(flops=int(flops), bytes_accessed=int(size), transcendentals=0)


def sigmoid(values):
    return 0.5 * jnp.tanh(0.5 * values) + 0.5


def normalize(values):
    center = values - jnp.mean(values, axis=0, keepdims=True)
    spread = jnp.mean(center * center, axis=0, keepdims=True)
    scale = lax.rsqrt(spread + EPS)
    return center * scale, scale


def normalize_back(grads, gain, hat, scale):
    grad_hat = grads * gain
    first = jnp.mean(grad_hat, axis=0, keepdims=True)
    second = jnp.mean(grad_hat * hat, axis=0, keepdims=True)
    return scale * (grad_hat - first - hat * second)


def widen(column, lanes):
    return jnp.concatenate([column] * (lanes // column.shape[1]), axis=1)


def fold(values):
    parts = [values[:, at : at + 128] for at in range(0, values.shape[1], 128)]
    return functools.reduce(lambda one, two: one + two, parts)


def load_tokens(ref, row, order):
    _, pieces, some, tokens, width = ref.shape
    flat = ref[row // some, :, row % some, :, :].astype(F32)
    flat = flat.reshape(order + (flat.shape[0] * tokens // math.prod(order), width))
    return flat.transpose(1, 2, 0, 3, 4).reshape(pieces * tokens, width)


def store_tokens(ref, row, order, values):
    _, pieces, some, tokens, width = ref.shape
    back = (order[1], order[2], order[0])
    flat = values.reshape(back + (pieces * tokens // math.prod(order), width))
    flat = flat.transpose(2, 0, 1, 3, 4).reshape(pieces, tokens, width)
    ref[row // some, :, row % some, :, :] = flat.astype(ref.dtype)


def stacked(ref, start, count):
    return jnp.concatenate([ref[start + n] for n in range(count)], axis=1)


def spread_out(ref, start, count, values):
    length = values.shape[1] // count
    for n in range(count):
        ref[start + n] = values[:, n * length : (n + 1) * length].astype(ref.dtype)


def edges_kernel(order, x_ref, w_ref, gain_ref, shift_ref, a_ref, b_ref, xt_ref, a_scr, b_scr):
    rows, width, length = xt_ref.shape
    count = 2

    def step(at, carry):
        start = at * count
        tokens = [load_tokens(x_ref, start + n, order).astype(BF) for n in range(count)]
        x0 = jnp.concatenate([item.T for item in tokens], axis=1)
        spread_out(xt_ref, start, count, x0)
        hat, _ = normalize(x0.astype(F32))
        lanes = x0.shape[1]
        normed = (hat * widen(gain_ref[...], lanes) + widen(shift_ref[...], lanes)).astype(BF)
        proj = nn(w_ref[...], normed)
        left = sigmoid(proj[width : 2 * width]) * proj[:width]
        right = sigmoid(proj[3 * width : 4 * width]) * proj[2 * width : 3 * width]
        for n in range(count):
            base = pl.multiple_of((start + n) * width, width)
            for half in range(length // 128):
                part = slice(n * length + half * 128, n * length + half * 128 + 128)
                a_scr[half, pl.ds(base, width), :] = left[:, part]
                b_scr[half, pl.ds(base, width), :] = right[:, part]
        return carry

    lax.fori_loop(0, rows // count, step, 0)

    def turn(at, carry):
        for n in range(8):
            e = at * 8 + n
            for scr, out in ((a_scr, a_ref), (b_scr, b_ref)):
                halves = [scr[h, pl.ds(e, rows, stride=width), :] for h in range(scr.shape[0])]
                out[e] = jnp.concatenate(halves, axis=1).astype(BF)
        return carry

    lax.fori_loop(0, width // 8, turn, 0)


def edges(x_rows, order, weight, gain, shift):
    blocks, pieces, some, tokens, width = x_rows.shape
    length = pieces * tokens
    rows = blocks * some
    step = 16 // some
    const = lambda at: (0, 0)
    return pl.pallas_call(
        functools.partial(edges_kernel, order),
        grid=(blocks // step,),
        in_specs=[
            pl.BlockSpec((step, pieces, some, tokens, width), lambda at: (at, 0, 0, 0, 0)),
            pl.BlockSpec(weight.shape, const),
            pl.BlockSpec(gain.shape, const),
            pl.BlockSpec(shift.shape, const),
        ],
        out_specs=[
            pl.BlockSpec((width, 16, length), lambda at: (0, at, 0)),
            pl.BlockSpec((width, 16, length), lambda at: (0, at, 0)),
            pl.BlockSpec((16, width, length), lambda at: (at, 0, 0)),
        ],
        out_shape=[
            jax.ShapeDtypeStruct((width, rows, length), BF),
            jax.ShapeDtypeStruct((width, rows, length), BF),
            jax.ShapeDtypeStruct((rows, width, length), BF),
        ],
        scratch_shapes=[
            pltpu.VMEM((length // 128, 16 * width, 128), F32),
            pltpu.VMEM((length // 128, 16 * width, 128), F32),
        ],
        compiler_params=pltpu.CompilerParams(vmem_limit_bytes=VMEM_LIMIT),
        cost_estimate=cost(1.7e10),
        name="edges",
    )(x_rows, weight, gain, shift)


def gather_pieces(place_ref, chunks, e, scr):
    for c, pieces in enumerate(chunks):
        rows = pieces[0].shape[1]
        for m, piece in enumerate(pieces):
            scr[e, pl.ds(pl.multiple_of(c * rows + place_ref[m], rows), rows), :] = piece[e]


def triangle_kernel(chunks, pieces, place_ref, *refs):
    lefts, refs = refs[:chunks], refs[chunks:]
    rights, refs = refs[: chunks * pieces], refs[chunks * pieces :]
    outs, scr = refs[:chunks], refs[chunks]
    rights = [rights[c * pieces : (c + 1) * pieces] for c in range(chunks)]
    for e in range(scr.shape[0]):
        gather_pieces(place_ref, rights, e, scr)
        t = nt(jnp.concatenate([left[e] for left in lefts], axis=0), scr[e])
        rows = lefts[0].shape[1]
        for c, out in enumerate(outs):
            out[:, e, :] = t[c * rows : (c + 1) * rows]


def triangle(place, lefts, rights):
    width, rows, length = lefts[0].shape
    chunks, pieces = len(lefts), len(rights[0])
    some = 8
    low = pl.BlockSpec((some, rows, length), lambda at, place: (at, 0, 0))
    high = pl.BlockSpec((rows, some, length), lambda at, place: (0, at, 0))
    return pl.pallas_call(
        functools.partial(triangle_kernel, chunks, pieces),
        grid_spec=pltpu.PrefetchScalarGridSpec(
            num_scalar_prefetch=1,
            grid=(width // some,),
            in_specs=[low] * (chunks + chunks * pieces),
            out_specs=[high] * chunks,
            scratch_shapes=[pltpu.VMEM((some, length, length), BF)],
        ),
        out_shape=[jax.ShapeDtypeStruct((rows, width, length), F32)] * chunks,
        compiler_params=pltpu.CompilerParams(vmem_limit_bytes=VMEM_LIMIT),
        cost_estimate=cost(2.0e10),
        name="triangle",
    )(place, *lefts, *[piece for chunk in rights for piece in chunk])


def turn_kernel(half_ref, grad_ref, near_ref, far_ref):
    lanes = near_ref.shape[2]
    for ref, half in ((near_ref, half_ref[0]), (far_ref, 1 - half_ref[0])):
        at = pl.multiple_of(half * lanes, lanes)
        for e in range(ref.shape[0]):
            ref[e] = grad_ref[:, e, pl.ds(at, lanes)].astype(BF)


def turn(half, grad):
    rows, width, length = grad.shape
    some = 16
    low = pl.BlockSpec((some, rows, length // 2), lambda at, half: (at, 0, 0))
    return pl.pallas_call(
        turn_kernel,
        grid_spec=pltpu.PrefetchScalarGridSpec(
            num_scalar_prefetch=1,
            grid=(width // some,),
            in_specs=[pl.BlockSpec((rows, some, length), lambda at, half: (0, at, 0))],
            out_specs=[low, low],
        ),
        out_shape=[jax.ShapeDtypeStruct((width, rows, length // 2), BF)] * 2,
        compiler_params=pltpu.CompilerParams(vmem_limit_bytes=VMEM_LIMIT),
        cost_estimate=cost(5.0e9),
        name="turn",
    )(half, grad)


def right_back_kernel(chunks, pieces, own_ref, *refs):
    grads, refs = refs[: chunks * pieces], refs[chunks * pieces :]
    lefts, refs = refs[: chunks * pieces], refs[chunks * pieces :]
    outs, scr = refs[:-1], refs[-1]
    rows = outs[0].shape[0]
    for e in range(scr.shape[0]):
        grad = jnp.concatenate([ref[e] for ref in grads], axis=0)
        left = jnp.concatenate([ref[e] for ref in lefts], axis=0)
        scr[e] = tn(grad, left)
        for c, out in enumerate(outs):
            at = pl.multiple_of(own_ref[0] + c * rows, rows)
            out[:, e, :] = scr[e, pl.ds(at, rows), :]


def right_back(own, grads, lefts):
    width, rows, length = lefts[0][0].shape
    chunks, pieces = len(lefts), len(lefts[0])
    part = grads[0][0].shape[2]
    some = 8
    low = lambda lanes: pl.BlockSpec((some, rows, lanes), lambda at, own: (at, 0, 0))
    high = pl.BlockSpec((rows, some, length), lambda at, own: (0, at, 0))
    return pl.pallas_call(
        functools.partial(right_back_kernel, chunks, pieces),
        grid_spec=pltpu.PrefetchScalarGridSpec(
            num_scalar_prefetch=1,
            grid=(width // some,),
            in_specs=[low(part)] * (chunks * pieces) + [low(length)] * (chunks * pieces),
            out_specs=[high] * chunks,
            scratch_shapes=[pltpu.VMEM((some, part, length), F32)],
        ),
        out_shape=[jax.ShapeDtypeStruct((rows, width, length), F32)] * chunks,
        compiler_params=pltpu.CompilerParams(vmem_limit_bytes=VMEM_LIMIT),
        cost_estimate=cost(2.2e10),
        name="right_back",
    )(own, *[item for chunk in grads for item in chunk], *[item for chunk in lefts for item in chunk])


def left_back_kernel(chunks, pieces, place_ref, *refs):
    grads, refs = refs[: 2 * chunks], refs[2 * chunks :]
    rights, refs = refs[: chunks * pieces], refs[chunks * pieces :]
    outs, scr = refs[:chunks], refs[chunks]
    rights = [rights[c * pieces : (c + 1) * pieces] for c in range(chunks)]
    rows = grads[0].shape[1]
    for e in range(scr.shape[0]):
        gather_pieces(place_ref, rights, e, scr)
        grad = [jnp.concatenate([grads[c][e], grads[chunks + c][e]], axis=1) for c in range(chunks)]
        da = nn(jnp.concatenate(grad, axis=0), scr[e])
        for c, out in enumerate(outs):
            out[:, e, :] = da[c * rows : (c + 1) * rows]


def left_back(place, nears, fars, rights):
    width, rows, part = nears[0].shape
    chunks, pieces = len(nears), len(rights[0])
    length = 2 * part
    some = 8
    low = lambda lanes: pl.BlockSpec((some, rows, lanes), lambda at, place: (at, 0, 0))
    high = pl.BlockSpec((rows, some, length), lambda at, place: (0, at, 0))
    return pl.pallas_call(
        functools.partial(left_back_kernel, chunks, pieces),
        grid_spec=pltpu.PrefetchScalarGridSpec(
            num_scalar_prefetch=1,
            grid=(width // some,),
            in_specs=[low(part)] * (2 * chunks) + [low(length)] * (chunks * pieces),
            out_specs=[high] * chunks,
            scratch_shapes=[pltpu.VMEM((some, length, length), BF)],
        ),
        out_shape=[jax.ShapeDtypeStruct((rows, width, length), F32)] * chunks,
        compiler_params=pltpu.CompilerParams(vmem_limit_bytes=VMEM_LIMIT),
        cost_estimate=cost(2.0e10),
        name="left_back",
    )(place, *nears, *fars, *[piece for chunk in rights for piece in chunk])


def rows_kernel(count, heads, order, first, *refs):
    sums = 9
    before = [] if first else refs[:sums]
    rows_body(count, heads, order, before, *refs[len(before) :])


def rows_body(
    count,
    heads,
    order,
    before,
    t_ref,
    xt_ref,
    cot_ref,
    bias_ref,
    chain_ref,
    lane_ref,
    vec_ref,
    gate_w_ref,
    gate_wt_ref,
    tri_out_ref,
    tri_out_t_ref,
    att_t_ref,
    att_qkv_ref,
    att_qg_ref,
    att_out_ref,
    att_out_t_ref,
    up_ref,
    up_t_ref,
    down_ref,
    down_t_ref,
    out_ref,
    dt_ref,
    z_ref,
    g_gate_ref,
    g_tri_out_ref,
    g_qg_ref,
    g_kv_ref,
    g_att_out_ref,
    g_up_ref,
    g_down_ref,
    g_vec_ref,
    g_bias_ref,
    e_scr,
    ds_scr,
):
    total_rows, width, length = t_ref.shape
    lanes = count * length
    head = width // heads
    scaling = 1.0 / math.sqrt(head)

    sums = (
        g_gate_ref,
        g_tri_out_ref,
        g_qg_ref,
        g_kv_ref,
        g_att_out_ref,
        g_up_ref,
        g_down_ref,
        g_vec_ref,
        g_bias_ref,
    )

    @pl.when(pl.program_id(0) == 0)
    def _():
        for n, ref in enumerate(sums):
            ref[...] = before[n][...] if before else jnp.zeros(ref.shape, ref.dtype)

    def vec(at):
        return widen(vec_ref[at], lanes)

    def step(at, carry):
        start = at * count
        x0 = stacked(xt_ref, start, count).astype(F32)
        hat1, scale1 = normalize(x0)
        normed1 = (hat1 * vec(0) + vec(1)).astype(BF)
        gate1 = sigmoid(nn(gate_wt_ref[...], normed1))
        hat_t, scale_t = normalize(stacked(t_ref, start, count))
        mixed = (hat_t * vec(2) + vec(3)).astype(BF)
        branch = nn(tri_out_t_ref[...], mixed)
        x1 = x0 + gate1 * branch
        hat2, scale2 = normalize(x1)
        normed2 = (hat2 * vec(4) + vec(5)).astype(BF)
        hidden = nn(att_t_ref[...], normed2)
        query = (hidden[:width] * (scaling * LOG2E)).astype(BF)
        hidden = hidden.astype(BF)
        key = hidden[width : 2 * width]
        value = hidden[2 * width : 3 * width]
        gate2 = sigmoid(hidden[3 * width :].astype(F32))
        normed2_tok = normed2.T
        qkv_tok = nn(normed2_tok, att_qkv_ref[...])
        query_tok = (qkv_tok[:, :width] * (scaling * LOG2E)).astype(BF)
        qkv_tok = qkv_tok.astype(BF)
        ones = jnp.ones((16, length), BF)

        mixed_rows, inverse_rows = [], []
        for n in range(count):
            cols = slice(n * length, (n + 1) * length)
            key_tok = qkv_tok[cols, width : 2 * width]
            query_n = query[:, cols]
            outs, inverses = [], []
            for h in range(heads):
                mine = slice(h * head, (h + 1) * head)
                there = slice(h * length, (h + 1) * length)
                score = nn(key_tok * lane_ref[h], query_n) + bias_ref[h]
                peak = jnp.max(score, axis=0, keepdims=True)
                expon = jnp.exp2(score - peak).astype(BF)
                e_scr[n, :, there] = expon
                both = nn(jnp.concatenate([value[mine, cols], ones], axis=0), expon)
                inverse = 1.0 / both[head : head + 1]
                outs.append(both[:head] * inverse)
                inverses.append(inverse)
            mixed_rows.append(jnp.concatenate(outs, axis=0))
            inverse_rows.append(inverses)
        attended = jnp.concatenate(mixed_rows, axis=1)
        gated = (gate2 * attended).astype(BF)
        x2 = x1 + nn(att_out_t_ref[...], gated)
        hat3, scale3 = normalize(x2)
        normed3 = (hat3 * vec(6) + vec(7)).astype(BF)
        up = nn(up_t_ref[...], normed3)
        gate3 = sigmoid(up)
        act = (up * gate3).astype(BF)
        out = (x2 + nn(down_t_ref[...], act)).astype(BF)
        for n in range(count):
            store_tokens(out_ref, start + n, order, out[:, n * length : (n + 1) * length].T.astype(F32))

        cot_tok = [load_tokens(cot_ref, start + n, order).astype(BF) for n in range(count)]
        cot_low = jnp.concatenate([item.T for item in cot_tok], axis=1)
        cot = cot_low.astype(F32)
        g_down_ref[...] += nn(act, jnp.concatenate(cot_tok, axis=0))
        grad_up = (nn(down_ref[...], cot_low) * (gate3 * (1.0 + up * (1.0 - gate3)))).astype(BF)
        g_up_ref[...] += nt(normed3, grad_up)
        grad3 = nn(up_ref[...], grad_up)
        g_vec_ref[6] += fold(grad3 * hat3)
        g_vec_ref[7] += fold(grad3)
        grad_x2 = cot + normalize_back(grad3, vec(6), hat3, scale3)
        grad_x2_low = grad_x2.astype(BF)
        g_att_out_ref[...] += nt(gated, grad_x2_low)
        grad_gated = nn(att_out_ref[...], grad_x2_low)
        grad_mixed = grad_gated * gate2
        grad_gate2 = (grad_gated * attended * gate2 * (1.0 - gate2)).astype(BF)

        grad_query_rows, grad_key_rows, grad_value_rows = [], [], []
        for n in range(count):
            cols = slice(n * length, (n + 1) * length)
            value_tok = qkv_tok[cols, 2 * width :]
            parts = []
            for h in range(heads):
                mine = slice(h * head, (h + 1) * head)
                parts.append(grad_mixed[mine, cols] * inverse_rows[n][h])
            grad_out = jnp.concatenate(parts, axis=0).astype(BF)
            product = grad_out.astype(F32) * mixed_rows[n]
            grad_out_tok = grad_out.T
            grads = []
            for h in range(heads):
                mine = slice(h * head, (h + 1) * head)
                there = slice(h * length, (h + 1) * length)
                center = jnp.sum(product[mine], axis=0, keepdims=True)
                grad_prob = nn(value_tok * lane_ref[h], grad_out)
                grad_score = (e_scr[n, :, there].astype(F32) * (grad_prob - center)).astype(BF)
                ds_scr[n, :, there] = grad_score
                both = nn(jnp.concatenate([key[mine, cols], chain_ref[...]], axis=0), grad_score)
                grads.append((both[:head] * scaling).astype(BF))
                g_bias_ref[h] += both[head:]
            grad_query_rows.append(jnp.concatenate(grads, axis=0))
            split = lambda item: jnp.concatenate([item * lane_ref[h] for h in range(heads)], axis=0)
            grad_value_rows.append(nn(e_scr[n], split(grad_out_tok)).astype(BF))
            grad_key_rows.append((nn(ds_scr[n], split(query_tok[cols])) * LN2).astype(BF))
        grad_qg = jnp.concatenate([jnp.concatenate(grad_query_rows, axis=1), grad_gate2], axis=0)
        grad_kv = jnp.concatenate(
            [jnp.concatenate(grad_key_rows, axis=0), jnp.concatenate(grad_value_rows, axis=0)],
            axis=1,
        )
        g_qg_ref[...] += nn(grad_qg, normed2_tok)
        g_kv_ref[...] += nn(normed2, grad_kv)
        grad2 = nn(att_qg_ref[...], grad_qg) + nt(att_qkv_ref[:, width:], grad_kv)
        g_vec_ref[4] += fold(grad2 * hat2)
        g_vec_ref[5] += fold(grad2)
        grad_x1 = grad_x2 + normalize_back(grad2, vec(4), hat2, scale2)
        grad_branch = (grad_x1 * gate1).astype(BF)
        g_tri_out_ref[...] += nt(mixed, grad_branch)
        grad_mix = nn(tri_out_ref[...], grad_branch)
        g_vec_ref[2] += fold(grad_mix * hat_t)
        g_vec_ref[3] += fold(grad_mix)
        spread_out(dt_ref, start, count, normalize_back(grad_mix, vec(2), hat_t, scale_t))
        grad_gate1 = (grad_x1 * branch * gate1 * (1.0 - gate1)).astype(BF)
        g_gate_ref[...] += nt(normed1, grad_gate1)
        grad1 = nn(gate_w_ref[...], grad_gate1)
        g_vec_ref[0] += fold(grad1 * hat1)
        g_vec_ref[1] += fold(grad1)
        spread_out(z_ref, start, count, grad_x1 + normalize_back(grad1, vec(0), hat1, scale1))
        return carry

    lax.fori_loop(0, total_rows // count, step, 0)


def rows_pass(before, t, xt, cot_rows, order, bias, chain, lane, vecs, weights, heads):
    rows, width, length = t.shape
    blocks, pieces, sub, tokens, _ = cot_rows.shape
    some, count = 4, 4
    inner = sub // some
    full = lambda item: pl.BlockSpec(item.shape, lambda at: (0,) * item.ndim)
    by_row = pl.BlockSpec((some, width, length), lambda at: (at, 0, 0))
    by_piece = pl.BlockSpec(
        (1, pieces, some, tokens, width), lambda at: (at // inner, 0, at % inner, 0, 0)
    )
    consts = (bias, chain, lane, vecs) + weights
    wide = weights[-1].shape[1]
    sums = [
        (width, width),
        (width, width),
        (2 * width, width),
        (width, 2 * width),
        (width, width),
        (width, wide),
        (wide, width),
        (8, width, 128),
        (heads, 16, length),
    ]
    sum_shapes = [jax.ShapeDtypeStruct(shape, F32) for shape in sums]
    return pl.pallas_call(
        functools.partial(rows_kernel, count, heads, order, not before),
        grid=(rows // some,),
        in_specs=[full(item) for item in before]
        + [by_row, by_row, by_piece]
        + [full(item) for item in consts],
        out_specs=[by_piece, by_row, by_row] + [full(item) for item in sum_shapes],
        out_shape=[
            jax.ShapeDtypeStruct(cot_rows.shape, BF),
            jax.ShapeDtypeStruct(t.shape, F32),
            jax.ShapeDtypeStruct(t.shape, F32),
        ]
        + sum_shapes,
        scratch_shapes=[
            pltpu.VMEM((count, length, heads * length), BF),
            pltpu.VMEM((count, length, heads * length), BF),
        ],
        compiler_params=pltpu.CompilerParams(vmem_limit_bytes=VMEM_LIMIT),
        cost_estimate=cost(1.2e11),
        name="rows",
    )(*before, t, xt, cot_rows, *consts)


def edges_back_kernel(order, first, *refs):
    before, refs = (refs[:0], refs) if first else (refs[:2], refs[2:])
    xt_ref, z_ref, da_ref, db_ref, wt_ref, w_ref, gain_ref, shift_ref = refs[:8]
    out_ref, g_w_ref, g_vec_ref = refs[8:]
    rows, width, length = xt_ref.shape
    count = 2

    @pl.when(pl.program_id(0) == 0)
    def _():
        for n, ref in enumerate((g_w_ref, g_vec_ref)):
            ref[...] = jnp.zeros(ref.shape, F32) if first else before[n][...]

    def step(at, carry):
        start = at * count
        x0 = stacked(xt_ref, start, count).astype(F32)
        lanes = x0.shape[1]
        gain = widen(gain_ref[...], lanes)
        hat, scale = normalize(x0)
        normed = (hat * gain + widen(shift_ref[...], lanes)).astype(BF)
        proj = nn(wt_ref[...], normed)
        pa, pag = proj[:width], proj[width : 2 * width]
        pb, pbg = proj[2 * width : 3 * width], proj[3 * width :]
        da = stacked(da_ref, start, count)
        db = stacked(db_ref, start, count)
        sa, sb = sigmoid(pag), sigmoid(pbg)
        dsa, dsb = da * sa, db * sb
        grads = jnp.concatenate(
            [
                dsa.astype(BF),
                (dsa * pa * (1.0 - sa)).astype(BF),
                dsb.astype(BF),
                (dsb * pb * (1.0 - sb)).astype(BF),
            ],
            axis=0,
        )
        g_w_ref[...] += nt(normed, grads)
        grad = nn(w_ref[...], grads)
        g_vec_ref[0] += fold(grad * hat)
        g_vec_ref[1] += fold(grad)
        out = stacked(z_ref, start, count) + normalize_back(grad, gain, hat, scale)
        out = out.astype(BF)
        for n in range(count):
            store_tokens(out_ref, start + n, order, out[:, n * length : (n + 1) * length].T.astype(F32))
        return carry

    lax.fori_loop(0, rows // count, step, 0)


def edges_back(before, xt, z, da, db, order, weight_t, weight, gain, shift, shape):
    rows, width, length = xt.shape
    blocks, pieces, some, tokens, _ = shape
    step = 16 // some
    full = lambda item: pl.BlockSpec(item.shape, lambda at: (0,) * item.ndim)
    by_row = pl.BlockSpec((16, width, length), lambda at: (at, 0, 0))
    sum_shapes = [
        jax.ShapeDtypeStruct(weight.shape, F32),
        jax.ShapeDtypeStruct((2, width, 128), F32),
    ]
    return pl.pallas_call(
        functools.partial(edges_back_kernel, order, not before),
        grid=(blocks // step,),
        in_specs=[full(item) for item in before]
        + [by_row] * 4
        + [full(item) for item in (weight_t, weight, gain, shift)],
        out_specs=[pl.BlockSpec((step, pieces, some, tokens, width), lambda at: (at, 0, 0, 0, 0))]
        + [full(item) for item in sum_shapes],
        out_shape=[jax.ShapeDtypeStruct(shape, BF)] + sum_shapes,
        compiler_params=pltpu.CompilerParams(vmem_limit_bytes=VMEM_LIMIT),
        cost_estimate=cost(2.0e10),
        name="edges_back",
    )(*before, xt, z, da, db, weight_t, weight, gain, shift)


def shards(
    row_size,
    col_size,
    pair_state,
    cotangent,
    chain_lengths,
    tri_gain,
    tri_shift,
    tri_weight,
    mix_gain,
    mix_shift,
    tri_out,
    att_gain,
    att_shift,
    att_weight,
    chain_bias,
    att_out,
    trans_gain,
    trans_shift,
    up_weight,
    down_weight,
):
    heads = HEADS
    crops, own_rows, tokens, width = pair_state.shape
    length = col_size * tokens
    chunks = CHUNKS
    some = own_rows // (col_size * chunks)
    axes = ("row", "col")
    group = row_size * col_size
    order = (row_size, col_size, chunks)
    shape = (row_size, col_size, some, tokens, width)

    def swap(values):
        return lax.all_to_all(values, axes, split_axis=0, concat_axis=0, tiled=True)

    def cut(values):
        parts = values.reshape(group, chunks, some, tokens, width)
        return [parts[:, c] for c in range(chunks)]

    def join(parts):
        return jnp.stack(parts, axis=1).reshape(crops, own_rows, tokens, width)

    def across(values, bit):
        return lax.ppermute(values, "col", [(q, q ^ bit) for q in range(col_size)])

    bits = [1 << n for n in range(col_size.bit_length() - 1)]

    def gather(own):
        pieces = {0: own}
        for bit in reversed(bits):
            for m in list(pieces):
                pieces[m ^ bit] = across(pieces[m], bit)
        return [pieces[m] for m in range(col_size)]

    def after(values, *others):
        return lax.optimization_barrier((values,) + others)[0]

    x_rows = [swap(part).reshape(shape) for part in cut(pair_state)]
    cot_parts = cut(cotangent)

    wide = lambda item: jnp.broadcast_to(item[:, None], (width, 128))
    vecs = jnp.stack(
        [
            wide(item)
            for item in (
                tri_gain,
                tri_shift,
                mix_gain,
                mix_shift,
                att_gain,
                att_shift,
                trans_gain,
                trans_shift,
            )
        ]
    )
    edge_w = tri_weight[:, : 4 * width]
    edge_wt = edge_w.T
    gate_w = tri_weight[:, 4 * width :]
    lengths = lax.dynamic_index_in_dim(chain_lengths, lax.axis_index("row"), 0, keepdims=False)
    ends = jnp.cumsum(lengths)
    places = jnp.arange(length, dtype=jnp.int32)
    places = places.reshape(order + (some,)).transpose(1, 2, 0, 3).reshape(length)
    chain = jnp.sum((places[:, None] >= ends[None, :]).astype(jnp.int32), axis=-1)
    same = (chain[:, None] == chain[None, :]).astype(F32)
    bias = (LOG2E * chain_bias)[:, None, None] * same[None]
    which = (jnp.arange(16, dtype=jnp.int32)[:, None] == chain[None, :]).astype(F32)
    head_of = jnp.arange(width, dtype=jnp.int32) // (width // heads)
    lane = (jnp.arange(heads, dtype=jnp.int32)[:, None] == head_of[None, :]).astype(BF)
    lane = jnp.broadcast_to(lane[:, None, :], (heads, length, width))
    me = lax.axis_index("col")
    flips = jnp.arange(col_size, dtype=jnp.int32)
    own = own_rows
    far_bit = col_size // 2
    inside = (me ^ flips) & (far_bit - 1)
    place = (me ^ flips) * own
    place_near = (inside + (flips & far_bit)) * own
    half = (me // far_bit).reshape(1)

    lefts, rights, xts = [], [], []
    for c in range(chunks):
        left, right, xt = edges(x_rows[c], order, edge_wt, vecs[0], vecs[1])
        lefts.append(left)
        rights.append(gather(right))
        xts.append(xt)
    ts = triangle(place, lefts, rights)
    lefts_all = [gather(after(left, *ts)) for left in lefts]
    cot_rows = [swap(after(cot_parts[0], *x_rows)).reshape(shape)]
    cot_rows += [swap(after(part, *ts, cot_rows[0])).reshape(shape) for part in cot_parts[1:]]
    weights = (
        gate_w,
        gate_w.T,
        tri_out,
        tri_out.T,
        att_weight.T,
        att_weight[:, : 3 * width],
        jnp.concatenate([att_weight[:, :width], att_weight[:, 3 * width :]], axis=1),
        att_out,
        att_out.T,
        up_weight,
        up_weight.T,
        down_weight,
        down_weight.T,
    )
    chain_rows = which.astype(BF)
    sums, outs, nears, fars, grads, zs = [], [], [], [], [], []
    for c in range(chunks):
        out, dt, z, *sums = rows_pass(
            sums, ts[c], xts[c], cot_rows[c], order, bias, chain_rows, lane, vecs, weights, heads
        )
        outs.append(swap(out.reshape(group, some, tokens, width)))
        zs.append(z)
        near, far = turn(half, dt)
        nears.append(near)
        fars.append(far)
        pieces = {0: near, far_bit: across(far, far_bit)}
        for bit in reversed(bits[:-1]):
            for m in list(pieces):
                pieces[m ^ bit] = across(pieces[m], bit)
        grads.append([pieces[m] for m in range(col_size)])
    g_gate, g_tri_out, g_qg, g_kv, g_att_out, g_up, g_down, g_vec, g_bias = sums

    ff = g_down.shape[0] // width
    parts = [g_gate, g_tri_out, g_qg[:width].T, g_qg[width:].T, g_kv, g_att_out, g_up]
    parts += [g_down[n * width : (n + 1) * width] for n in range(ff)]
    whole = lax.psum(jnp.concatenate([part.astype(BF) for part in parts], axis=1), axes).astype(F32)
    row_sums, at = [], 0
    for part in parts:
        row_sums.append(whole[:, at : at + part.shape[1]])
        at += part.shape[1]
    t_gate, t_tri_out, t_query, t_gate2, t_kv, t_att_out, t_up = row_sums[:7]
    t_down = jnp.concatenate(row_sums[7:], axis=0)

    das = left_back(place_near, nears, fars, rights)
    dbs = right_back(inside[:1] * own, grads, lefts_all)
    edge_sums, backs = [], []
    for c in range(chunks):
        grad, *edge_sums = edges_back(
            edge_sums, xts[c], zs[c], das[c], dbs[c], order, edge_wt, edge_w, vecs[0], vecs[1], shape
        )
        backs.append(swap(grad.reshape(group, some, tokens, width)))
    g_edge, g_vec_edge = edge_sums

    def doubled(values, sent):
        for axis, size in (("col", col_size), ("row", row_size)):
            for bit in [1 << n for n in range(size.bit_length() - 1)]:
                low = values.astype(sent)
                other = lax.ppermute(low, axis, [(q, q ^ bit) for q in range(size)])
                values = low.astype(F32) + other.astype(F32)
        return values

    t_edge = doubled(g_edge, BF)

    g_vec = jnp.sum(g_vec, axis=-1)
    g_vec_edge = jnp.sum(g_vec_edge, axis=-1)
    g_chain = jnp.sum(g_bias * which[None], axis=(1, 2))
    small = jnp.concatenate(
        [g_vec[:2] + g_vec_edge, g_vec[2:], jnp.pad(g_chain, (0, width - heads))[None]], axis=0
    )
    small = doubled(small, F32)
    return (
        join(outs),
        join(backs),
        small[0],
        small[1],
        jnp.concatenate([t_edge, t_gate], axis=1),
        small[2],
        small[3],
        t_tri_out,
        small[4],
        small[5],
        jnp.concatenate([t_query, t_kv, t_gate2], axis=1),
        small[8, :heads],
        t_att_out,
        small[6],
        small[7],
        t_up,
        t_down,
    )


def solution(mesh):
    pair = P("dp", "row", "col", None)
    vector, matrix = P("dp"), P("dp", None)
    return jax.shard_map(
        functools.partial(shards, mesh.shape["row"], mesh.shape["col"]),
        mesh=mesh,
        in_specs=(pair, pair, P("dp", None)) + (P(),) * 15,
        out_specs=(
            pair,
            pair,
            vector,
            vector,
            matrix,
            vector,
            vector,
            matrix,
            vector,
            vector,
            matrix,
            vector,
            matrix,
            vector,
            vector,
            matrix,
            matrix,
        ),
        check_vma=False,
    )
```

```python
import functools
import math

import jax
import jax.numpy as jnp
from jax import lax
from jax.experimental import pallas as pl
from jax.experimental.pallas import tpu as pltpu
from jax.sharding import PartitionSpec as P

HEADS = 4
EPS = 1e-05
LOG2E = math.log2(math.e)
LN2 = math.log(2.0)
CHUNKS = 2
VMEM_LIMIT = 56 * 1024 * 1024
BF = jnp.bfloat16
F32 = jnp.float32


def nn(left, right):
    return lax.dot_general(left, right, (((1,), (0,)), ((), ())), preferred_element_type=F32)


def nt(left, right):
    return lax.dot_general(left, right, (((1,), (1,)), ((), ())), preferred_element_type=F32)


def tn(left, right):
    return lax.dot_general(left, right, (((0,), (0,)), ((), ())), preferred_element_type=F32)


def cost(flops, size=0):
    return pl.CostEstimate(flops=int(flops), bytes_accessed=int(size), transcendentals=0)


def sigmoid(values):
    return 0.5 * jnp.tanh(0.5 * values) + 0.5


def normalize(values):
    center = values - jnp.mean(values, axis=0, keepdims=True)
    spread = jnp.mean(center * center, axis=0, keepdims=True)
    scale = lax.rsqrt(spread + EPS)
    return center * scale, scale


def normalize_back(grads, gain, hat, scale):
    grad_hat = grads * gain
    first = jnp.mean(grad_hat, axis=0, keepdims=True)
    second = jnp.mean(grad_hat * hat, axis=0, keepdims=True)
    return scale * (grad_hat - first - hat * second)


def widen(column, lanes):
    return jnp.concatenate([column] * (lanes // column.shape[1]), axis=1)


def fold(values):
    parts = [values[:, at : at + 128] for at in range(0, values.shape[1], 128)]
    return functools.reduce(lambda one, two: one + two, parts)


def load_tokens(ref, row, order):
    _, pieces, some, tokens, width = ref.shape
    flat = ref[row // some, :, row % some, :, :].astype(F32)
    flat = flat.reshape(order + (flat.shape[0] * tokens // math.prod(order), width))
    return flat.transpose(1, 2, 0, 3, 4).reshape(pieces * tokens, width)


def store_tokens(ref, row, order, values):
    _, pieces, some, tokens, width = ref.shape
    back = (order[1], order[2], order[0])
    flat = values.reshape(back + (pieces * tokens // math.prod(order), width))
    flat = flat.transpose(2, 0, 1, 3, 4).reshape(pieces, tokens, width)
    ref[row // some, :, row % some, :, :] = flat.astype(ref.dtype)


def stacked(ref, start, count):
    return jnp.concatenate([ref[start + n] for n in range(count)], axis=1)


def spread_out(ref, start, count, values):
    length = values.shape[1] // count
    for n in range(count):
        ref[start + n] = values[:, n * length : (n + 1) * length].astype(ref.dtype)


def edges_kernel(order, x_ref, w_ref, gain_ref, shift_ref, *refs):
    a_ref, b_ref, xt_ref, a_scr, b_scr = refs[-5:]
    rows, width, length = xt_ref.shape
    count = 2

    def step(at, carry):
        start = at * count
        tokens = [load_tokens(x_ref, start + n, order).astype(BF) for n in range(count)]
        x0 = jnp.concatenate([item.T for item in tokens], axis=1)
        spread_out(xt_ref, start, count, x0)
        hat, _ = normalize(x0.astype(F32))
        lanes = x0.shape[1]
        normed = (hat * widen(gain_ref[...], lanes) + widen(shift_ref[...], lanes)).astype(BF)
        proj = nn(w_ref[...], normed)
        left = sigmoid(proj[width : 2 * width]) * proj[:width]
        right = sigmoid(proj[3 * width : 4 * width]) * proj[2 * width : 3 * width]
        for n in range(count):
            base = pl.multiple_of((start + n) * width, width)
            for half in range(length // 128):
                part = slice(n * length + half * 128, n * length + half * 128 + 128)
                a_scr[half, pl.ds(base, width), :] = left[:, part]
                b_scr[half, pl.ds(base, width), :] = right[:, part]
        return carry

    lax.fori_loop(0, rows // count, step, 0)

    def turn(at, carry):
        for n in range(8):
            e = at * 8 + n
            for scr, out in ((a_scr, a_ref), (b_scr, b_ref)):
                halves = [scr[h, pl.ds(e, rows, stride=width), :] for h in range(scr.shape[0])]
                out[e] = jnp.concatenate(halves, axis=1).astype(BF)
        return carry

    lax.fori_loop(0, width // 8, turn, 0)


def edges(c, chunks, x_rows, before, order, weight, gain, shift):
    blocks, pieces, some, tokens, width = x_rows.shape
    length = pieces * tokens
    rows = blocks * some
    step = 16 // some
    const = lambda at: (0, 0)
    return pl.pallas_call(
        functools.partial(edges_kernel, order),
        grid=(blocks // step,),
        in_specs=[
            pl.BlockSpec((step, pieces, some, tokens, width), lambda at: (at, 0, 0, 0, 0)),
            pl.BlockSpec(weight.shape, const),
            pl.BlockSpec(gain.shape, const),
            pl.BlockSpec(shift.shape, const),
        ]
        + [pl.BlockSpec(memory_space=pl.ANY)] * len(before),
        out_specs=[
            pl.BlockSpec((width, 16, length), lambda at: (0, at, 0)),
            pl.BlockSpec((width, 16, length), lambda at: (0, at, 0)),
            pl.BlockSpec((16, width, length), lambda at: (c * (blocks // step) + at, 0, 0)),
        ],
        out_shape=[
            jax.ShapeDtypeStruct((width, rows, length), BF),
            jax.ShapeDtypeStruct((width, rows, length), BF),
            jax.ShapeDtypeStruct((chunks * rows, width, length), BF),
        ],
        input_output_aliases={4: 2} if before else {},
        scratch_shapes=[
            pltpu.VMEM((length // 128, 16 * width, 128), F32),
            pltpu.VMEM((length // 128, 16 * width, 128), F32),
        ],
        compiler_params=pltpu.CompilerParams(vmem_limit_bytes=VMEM_LIMIT),
        cost_estimate=cost(1.7e10),
        name="edges",
    )(x_rows, weight, gain, shift, *before)


def gather_pieces(place_ref, chunks, e, scr):
    for c, pieces in enumerate(chunks):
        rows = pieces[0].shape[1]
        for m, piece in enumerate(pieces):
            scr[e, pl.ds(pl.multiple_of(c * rows + place_ref[m], rows), rows), :] = piece[e]


def triangle_kernel(chunks, pieces, place_ref, *refs):
    lefts, refs = refs[:chunks], refs[chunks:]
    rights, refs = refs[: chunks * pieces], refs[chunks * pieces :]
    t_ref, scr = refs
    rights = [rights[c * pieces : (c + 1) * pieces] for c in range(chunks)]
    for e in range(scr.shape[0]):
        gather_pieces(place_ref, rights, e, scr)
        t_ref[:, e, :] = nt(jnp.concatenate([left[e] for left in lefts], axis=0), scr[e])


def triangle(place, lefts, rights):
    width, rows, length = lefts[0].shape
    chunks, pieces = len(lefts), len(rights[0])
    some = 8
    low = pl.BlockSpec((some, rows, length), lambda at, place: (at, 0, 0))
    return pl.pallas_call(
        functools.partial(triangle_kernel, chunks, pieces),
        grid_spec=pltpu.PrefetchScalarGridSpec(
            num_scalar_prefetch=1,
            grid=(width // some,),
            in_specs=[low] * (chunks + chunks * pieces),
            out_specs=pl.BlockSpec((chunks * rows, some, length), lambda at, place: (0, at, 0)),
            scratch_shapes=[pltpu.VMEM((some, length, length), BF)],
        ),
        out_shape=jax.ShapeDtypeStruct((chunks * rows, width, length), F32),
        compiler_params=pltpu.CompilerParams(vmem_limit_bytes=VMEM_LIMIT),
        cost_estimate=cost(2.0e10),
        name="triangle",
    )(place, *lefts, *[piece for chunk in rights for piece in chunk])


def turn_kernel(half_ref, grad_ref, near_ref, far_ref):
    lanes = near_ref.shape[2]
    for ref, half in ((near_ref, half_ref[0]), (far_ref, 1 - half_ref[0])):
        at = pl.multiple_of(half * lanes, lanes)
        for e in range(ref.shape[0]):
            ref[e] = grad_ref[:, e, pl.ds(at, lanes)].astype(BF)


def turn(half, grad):
    rows, width, length = grad.shape
    some = 16
    low = pl.BlockSpec((some, rows, length // 2), lambda at, half: (at, 0, 0))
    return pl.pallas_call(
        turn_kernel,
        grid_spec=pltpu.PrefetchScalarGridSpec(
            num_scalar_prefetch=1,
            grid=(width // some,),
            in_specs=[pl.BlockSpec((rows, some, length), lambda at, half: (0, at, 0))],
            out_specs=[low, low],
        ),
        out_shape=[jax.ShapeDtypeStruct((width, rows, length // 2), BF)] * 2,
        compiler_params=pltpu.CompilerParams(vmem_limit_bytes=VMEM_LIMIT),
        cost_estimate=cost(5.0e9),
        name="turn",
    )(half, grad)


def right_back_kernel(chunks, pieces, own_ref, *refs):
    grads, refs = refs[: chunks * pieces], refs[chunks * pieces :]
    lefts, refs = refs[: chunks * pieces], refs[chunks * pieces :]
    db_ref, scr = refs
    rows = db_ref.shape[0]
    for e in range(scr.shape[0]):
        grad = jnp.concatenate([ref[e] for ref in grads], axis=0)
        left = jnp.concatenate([ref[e] for ref in lefts], axis=0)
        scr[e] = tn(grad, left)
        db_ref[:, e, :] = scr[e, pl.ds(pl.multiple_of(own_ref[0], rows), rows), :]


def right_back(own, grads, lefts):
    width, rows, length = lefts[0][0].shape
    chunks, pieces = len(lefts), len(lefts[0])
    part = grads[0][0].shape[2]
    some = 8
    low = lambda lanes: pl.BlockSpec((some, rows, lanes), lambda at, own: (at, 0, 0))
    return pl.pallas_call(
        functools.partial(right_back_kernel, chunks, pieces),
        grid_spec=pltpu.PrefetchScalarGridSpec(
            num_scalar_prefetch=1,
            grid=(width // some,),
            in_specs=[low(part)] * (chunks * pieces) + [low(length)] * (chunks * pieces),
            out_specs=pl.BlockSpec((chunks * rows, some, length), lambda at, own: (0, at, 0)),
            scratch_shapes=[pltpu.VMEM((some, part, length), F32)],
        ),
        out_shape=jax.ShapeDtypeStruct((chunks * rows, width, length), F32),
        compiler_params=pltpu.CompilerParams(vmem_limit_bytes=VMEM_LIMIT),
        cost_estimate=cost(2.2e10),
        name="right_back",
    )(own, *[item for chunk in grads for item in chunk], *[item for chunk in lefts for item in chunk])


def left_back_kernel(chunks, pieces, place_ref, *refs):
    grads, refs = refs[: 2 * chunks], refs[2 * chunks :]
    rights, refs = refs[: chunks * pieces], refs[chunks * pieces :]
    da_ref, scr = refs
    rights = [rights[c * pieces : (c + 1) * pieces] for c in range(chunks)]
    for e in range(scr.shape[0]):
        gather_pieces(place_ref, rights, e, scr)
        grad = [jnp.concatenate([grads[c][e], grads[chunks + c][e]], axis=1) for c in range(chunks)]
        da_ref[:, e, :] = nn(jnp.concatenate(grad, axis=0), scr[e])


def left_back(place, nears, fars, rights):
    width, rows, part = nears[0].shape
    chunks, pieces = len(nears), len(rights[0])
    length = 2 * part
    some = 8
    low = lambda lanes: pl.BlockSpec((some, rows, lanes), lambda at, place: (at, 0, 0))
    return pl.pallas_call(
        functools.partial(left_back_kernel, chunks, pieces),
        grid_spec=pltpu.PrefetchScalarGridSpec(
            num_scalar_prefetch=1,
            grid=(width // some,),
            in_specs=[low(part)] * (2 * chunks) + [low(length)] * (chunks * pieces),
            out_specs=pl.BlockSpec((chunks * rows, some, length), lambda at, place: (0, at, 0)),
            scratch_shapes=[pltpu.VMEM((some, length, length), BF)],
        ),
        out_shape=jax.ShapeDtypeStruct((chunks * rows, width, length), F32),
        compiler_params=pltpu.CompilerParams(vmem_limit_bytes=VMEM_LIMIT),
        cost_estimate=cost(2.0e10),
        name="left_back",
    )(place, *nears, *fars, *[piece for chunk in rights for piece in chunk])


def rows_kernel(count, heads, order, first, last, *refs):
    before = []
    if not first:
        before, refs = refs[:3], refs[4:]
    rows_body(count, heads, order, before, last, *refs)


def rows_body(
    count,
    heads,
    order,
    before,
    last,
    t_ref,
    xt_ref,
    cot_ref,
    bias_ref,
    chain_ref,
    lane_ref,
    vec_ref,
    gate_w_ref,
    gate_wt_ref,
    tri_out_ref,
    tri_out_t_ref,
    att_t_ref,
    att_qkv_ref,
    att_qg_ref,
    att_out_ref,
    att_out_t_ref,
    up_ref,
    up_t_ref,
    down_ref,
    down_t_ref,
    out_ref,
    dt_ref,
    z_ref,
    g_ref,
    g_vec_ref,
    g_bias_ref,
    e_scr,
):
    total_rows, width, length = t_ref.shape
    lanes = count * length
    head = width // heads
    scaling = 1.0 / math.sqrt(head)

    sums = (g_ref, g_vec_ref, g_bias_ref)
    place = {}
    for name in ("gate", "tri_out", "query", "gate2", "key", "value", "att_out"):
        place[name] = slice(len(place) * width, (len(place) + 1) * width)
    ups = slice(7 * width, 7 * width + up_ref.shape[1])
    downs = [
        slice(at, at + width) for at in range(ups.stop, ups.stop + up_ref.shape[1], width)
    ]

    @pl.when(pl.program_id(0) == 0)
    def _():
        for n, ref in enumerate(sums):
            ref[...] = before[n][...] if before else jnp.zeros(ref.shape, ref.dtype)

    def vec(at):
        return widen(vec_ref[at], lanes)

    def step(at, carry):
        start = at * count
        x0 = stacked(xt_ref, start, count).astype(F32)
        hat1, scale1 = normalize(x0)
        normed1 = (hat1 * vec(0) + vec(1)).astype(BF)
        gate1 = sigmoid(nn(gate_wt_ref[...], normed1))
        hat_t, scale_t = normalize(stacked(t_ref, start, count))
        mixed = (hat_t * vec(2) + vec(3)).astype(BF)
        branch = nn(tri_out_t_ref[...], mixed)
        x1 = x0 + gate1 * branch
        hat2, scale2 = normalize(x1)
        normed2 = (hat2 * vec(4) + vec(5)).astype(BF)
        hidden = nn(att_t_ref[...], normed2)
        query = (hidden[:width] * (scaling * LOG2E)).astype(BF)
        hidden = hidden.astype(BF)
        key = hidden[width : 2 * width]
        value = hidden[2 * width : 3 * width]
        gate2 = sigmoid(hidden[3 * width :].astype(F32))
        normed2_tok = normed2.T
        qkv_tok = nn(normed2_tok, att_qkv_ref[...])
        query_tok = (qkv_tok[:, :width] * (scaling * LOG2E)).astype(BF)
        qkv_tok = qkv_tok.astype(BF)
        ones = jnp.ones((16, length), BF)
        pairs = [(n, h) for n in range(count) for h in range(heads)]
        cols = [slice(n * length, (n + 1) * length) for n in range(count)]
        mine = [slice(h * head, (h + 1) * head) for h in range(heads)]
        there = [slice(h * length, (h + 1) * length) for h in range(heads)]

        def scores(n, h):
            return nn(qkv_tok[cols[n], width : 2 * width] * lane_ref[h], query[:, cols[n]])

        outs, inverses = {}, {}

        def mix(n, h):
            both = nn(jnp.concatenate([value[mine[h], cols[n]], ones], axis=0), e_scr[n, :, there[h]])
            inverses[n, h] = 1.0 / both[head : head + 1]
            outs[n, h] = both[:head] * inverses[n, h]

        ahead = scores(*pairs[0])
        for at_pair, (n, h) in enumerate(pairs):
            score = ahead
            if at_pair + 1 < len(pairs):
                ahead = scores(*pairs[at_pair + 1])
            score = score + bias_ref[h]
            peak = jnp.max(score, axis=0, keepdims=True)
            e_scr[n, :, there[h]] = jnp.exp2(score - peak).astype(BF)
            if at_pair:
                mix(*pairs[at_pair - 1])
        mix(*pairs[-1])
        mixed_rows = [
            jnp.concatenate([outs[n, h] for h in range(heads)], axis=0) for n in range(count)
        ]
        attended = jnp.concatenate(mixed_rows, axis=1)
        gated = (gate2 * attended).astype(BF)
        x2 = x1 + nn(att_out_t_ref[...], gated)
        hat3, scale3 = normalize(x2)
        normed3 = (hat3 * vec(6) + vec(7)).astype(BF)
        up = nn(up_t_ref[...], normed3)
        gate3 = sigmoid(up)
        act = (up * gate3).astype(BF)
        out = (x2 + nn(down_t_ref[...], act)).astype(BF)
        for n in range(count):
            store_tokens(out_ref, start + n, order, out[:, n * length : (n + 1) * length].T.astype(F32))

        cot_tok = [load_tokens(cot_ref, start + n, order).astype(BF) for n in range(count)]
        cot_low = jnp.concatenate([item.T for item in cot_tok], axis=1)
        cot = cot_low.astype(F32)
        grad_down = nn(act, jnp.concatenate(cot_tok, axis=0))
        for n, part in enumerate(downs):
            g_ref[:, part] += grad_down[n * width : (n + 1) * width]
        grad_up = (nn(down_ref[...], cot_low) * (gate3 * (1.0 + up * (1.0 - gate3)))).astype(BF)
        g_ref[:, ups] += nt(normed3, grad_up)
        grad3 = nn(up_ref[...], grad_up)
        g_vec_ref[6] += fold(grad3 * hat3)
        g_vec_ref[7] += fold(grad3)
        grad_x2 = cot + normalize_back(grad3, vec(6), hat3, scale3)
        grad_x2_low = grad_x2.astype(BF)
        g_ref[:, place["att_out"]] += nt(gated, grad_x2_low)
        grad_gated = nn(att_out_ref[...], grad_x2_low)
        grad_mixed = grad_gated * gate2
        grad_gate2 = (grad_gated * attended * gate2 * (1.0 - gate2)).astype(BF)

        grad_outs, grad_outs_tok, products = [], [], []
        for n in range(count):
            scaled = [grad_mixed[mine[h], cols[n]] * inverses[n, h] for h in range(heads)]
            grad_out = jnp.concatenate(scaled, axis=0).astype(BF)
            grad_outs.append(grad_out)
            grad_outs_tok.append(grad_out.T)
            products.append(grad_out.astype(F32) * mixed_rows[n])
        grad_queries, grad_keys, grad_values = {}, [0.0] * count, [0.0] * count

        def probs(n, h):
            return nn(qkv_tok[cols[n], 2 * width :] * lane_ref[h], grad_outs[n])

        def spread(n, h, grad_score):
            both = nn(jnp.concatenate([key[mine[h], cols[n]], chain_ref[...]], axis=0), grad_score)
            grad_queries[n, h] = (both[:head] * scaling).astype(BF)
            g_bias_ref[h] += both[head:]
            grad_keys[n] += nn(grad_score, query_tok[cols[n]] * lane_ref[h])

        ahead, behind = probs(*pairs[0]), None
        for at_pair, (n, h) in enumerate(pairs):
            grad_prob = ahead
            if at_pair + 1 < len(pairs):
                ahead = probs(*pairs[at_pair + 1])
            center = jnp.sum(products[n][mine[h]], axis=0, keepdims=True)
            expon = e_scr[n, :, there[h]]
            grad_score = (expon.astype(F32) * (grad_prob - center)).astype(BF)
            grad_values[n] += nn(expon, grad_outs_tok[n] * lane_ref[h])
            if behind is not None:
                spread(*behind)
            behind = (n, h, grad_score)
        spread(*behind)
        grad_query_rows = [
            jnp.concatenate([grad_queries[n, h] for h in range(heads)], axis=0) for n in range(count)
        ]
        grad_key_rows = [(item * LN2).astype(BF) for item in grad_keys]
        grad_value_rows = [item.astype(BF) for item in grad_values]
        grad_qg = jnp.concatenate([jnp.concatenate(grad_query_rows, axis=1), grad_gate2], axis=0)
        grad_kv = jnp.concatenate(
            [jnp.concatenate(grad_key_rows, axis=0), jnp.concatenate(grad_value_rows, axis=0)],
            axis=1,
        )
        grad_w = nn(grad_qg, normed2_tok)
        g_ref[:, place["query"]] += grad_w[:width]
        g_ref[:, place["gate2"]] += grad_w[width:]
        g_ref[:, place["key"].start : place["value"].stop] += nn(normed2, grad_kv)
        grad2 = nn(att_qg_ref[...], grad_qg) + nt(att_qkv_ref[:, width:], grad_kv)
        g_vec_ref[4] += fold(grad2 * hat2)
        g_vec_ref[5] += fold(grad2)
        grad_x1 = grad_x2 + normalize_back(grad2, vec(4), hat2, scale2)
        grad_branch = (grad_x1 * gate1).astype(BF)
        g_ref[:, place["tri_out"]] += nt(mixed, grad_branch)
        grad_mix = nn(tri_out_ref[...], grad_branch)
        g_vec_ref[2] += fold(grad_mix * hat_t)
        g_vec_ref[3] += fold(grad_mix)
        spread_out(dt_ref, start, count, normalize_back(grad_mix, vec(2), hat_t, scale_t))
        grad_gate1 = (grad_x1 * branch * gate1 * (1.0 - gate1)).astype(BF)
        g_ref[:, place["gate"]] += nt(normed1, grad_gate1)
        grad1 = nn(gate_w_ref[...], grad_gate1)
        g_vec_ref[0] += fold(grad1 * hat1)
        g_vec_ref[1] += fold(grad1)
        spread_out(z_ref, start, count, grad_x1 + normalize_back(grad1, vec(0), hat1, scale1))
        return carry

    lax.fori_loop(0, total_rows // count, step, 0)

    if last:

        @pl.when(pl.program_id(0) == pl.num_programs(0) - 1)
        def _():
            for name in ("query", "gate2"):
                g_ref[:, place[name]] = g_ref[:, place[name]].T


def rows_pass(c, chunks, before, t, xt, cot_rows, order, bias, chain, lane, vecs, weights, heads):
    _, width, length = t.shape
    blocks, pieces, sub, tokens, _ = cot_rows.shape
    rows = blocks * sub
    some, count = 4, 4
    inner = sub // some
    full = lambda item: pl.BlockSpec(item.shape, lambda at: (0,) * item.ndim)
    by_row = pl.BlockSpec((some, width, length), lambda at: (at, 0, 0))
    of_all = pl.BlockSpec((some, width, length), lambda at: (c * (rows // some) + at, 0, 0))
    by_piece = pl.BlockSpec(
        (1, pieces, some, tokens, width), lambda at: (at // inner, 0, at % inner, 0, 0)
    )
    consts = (bias, chain, lane, vecs) + weights
    wide = weights[-1].shape[1]
    sum_shapes = [
        jax.ShapeDtypeStruct(shape, F32)
        for shape in ((width, 7 * width + 2 * wide), (8, width, 128), (heads, 16, length))
    ]
    before_specs = [full(item) for item in before[:3]]
    before_specs += [pl.BlockSpec(memory_space=pl.ANY)] * len(before[3:])
    return pl.pallas_call(
        functools.partial(rows_kernel, count, heads, order, c == 0, c == chunks - 1),
        grid=(rows // some,),
        in_specs=before_specs + [of_all, of_all, by_piece] + [full(item) for item in consts],
        out_specs=[by_piece, by_row, of_all] + [full(item) for item in sum_shapes],
        out_shape=[
            jax.ShapeDtypeStruct(cot_rows.shape, BF),
            jax.ShapeDtypeStruct((rows, width, length), F32),
            jax.ShapeDtypeStruct(t.shape, F32),
        ]
        + sum_shapes,
        input_output_aliases={3: 2} if before else {},
        scratch_shapes=[
            pltpu.VMEM((count, length, heads * length), BF),
        ],
        compiler_params=pltpu.CompilerParams(vmem_limit_bytes=VMEM_LIMIT),
        cost_estimate=cost(1.2e11),
        name="rows",
    )(*before, t, xt, cot_rows, *consts)


def edges_back_kernel(
    order, xt_ref, z_ref, da_ref, db_ref, wt_ref, w_ref, gain_ref, shift_ref, out_ref, g_w_ref, g_vec_ref
):
    rows, width, length = xt_ref.shape
    count = 2

    @pl.when(pl.program_id(0) == 0)
    def _():
        g_w_ref[...] = jnp.zeros(g_w_ref.shape, F32)
        g_vec_ref[...] = jnp.zeros(g_vec_ref.shape, F32)

    def step(at, carry):
        start = at * count
        x0 = stacked(xt_ref, start, count).astype(F32)
        lanes = x0.shape[1]
        gain = widen(gain_ref[...], lanes)
        hat, scale = normalize(x0)
        normed = (hat * gain + widen(shift_ref[...], lanes)).astype(BF)
        proj = nn(wt_ref[...], normed)
        pa, pag = proj[:width], proj[width : 2 * width]
        pb, pbg = proj[2 * width : 3 * width], proj[3 * width :]
        da = stacked(da_ref, start, count)
        db = stacked(db_ref, start, count)
        sa, sb = sigmoid(pag), sigmoid(pbg)
        dsa, dsb = da * sa, db * sb
        grads = jnp.concatenate(
            [
                dsa.astype(BF),
                (dsa * pa * (1.0 - sa)).astype(BF),
                dsb.astype(BF),
                (dsb * pb * (1.0 - sb)).astype(BF),
            ],
            axis=0,
        )
        g_w_ref[...] += nt(normed, grads)
        grad = nn(w_ref[...], grads)
        g_vec_ref[0] += fold(grad * hat)
        g_vec_ref[1] += fold(grad)
        out = stacked(z_ref, start, count) + normalize_back(grad, gain, hat, scale)
        out = out.astype(BF)
        for n in range(count):
            store_tokens(out_ref, start + n, order, out[:, n * length : (n + 1) * length].T.astype(F32))
        return carry

    lax.fori_loop(0, rows // count, step, 0)


def edges_back(xt, z, da, db, order, weight_t, weight, gain, shift, shape):
    rows, width, length = xt.shape
    blocks, pieces, sub, tokens, _ = shape
    chunks = order[2]
    some = sub // chunks
    step = 16 // some
    inner = blocks // step
    full = lambda item: pl.BlockSpec(item.shape, lambda at: (0,) * item.ndim)
    by_row = pl.BlockSpec((16, width, length), lambda at: (at, 0, 0))
    sum_shapes = [
        jax.ShapeDtypeStruct(weight.shape, F32),
        jax.ShapeDtypeStruct((2, width, 128), F32),
    ]
    by_piece = pl.BlockSpec(
        (step, pieces, some, tokens, width), lambda at: (at % inner, 0, at // inner, 0, 0)
    )
    return pl.pallas_call(
        functools.partial(edges_back_kernel, order),
        grid=(chunks * inner,),
        in_specs=[by_row] * 4 + [full(item) for item in (weight_t, weight, gain, shift)],
        out_specs=[by_piece] + [full(item) for item in sum_shapes],
        out_shape=[jax.ShapeDtypeStruct(shape, BF)] + sum_shapes,
        compiler_params=pltpu.CompilerParams(vmem_limit_bytes=VMEM_LIMIT),
        cost_estimate=cost(4.0e10),
        name="edges_back",
    )(xt, z, da, db, weight_t, weight, gain, shift)


def shards(
    row_size,
    col_size,
    pair_state,
    cotangent,
    chain_lengths,
    tri_gain,
    tri_shift,
    tri_weight,
    mix_gain,
    mix_shift,
    tri_out,
    att_gain,
    att_shift,
    att_weight,
    chain_bias,
    att_out,
    trans_gain,
    trans_shift,
    up_weight,
    down_weight,
):
    heads = HEADS
    crops, own_rows, tokens, width = pair_state.shape
    length = col_size * tokens
    chunks = CHUNKS
    some = own_rows // (col_size * chunks)
    axes = ("row", "col")
    group = row_size * col_size
    order = (row_size, col_size, chunks)
    shape = (row_size, col_size, some, tokens, width)

    def swap(values):
        return lax.all_to_all(values, axes, split_axis=0, concat_axis=0, tiled=True)

    def cut(values):
        parts = values.reshape(group, chunks, some, tokens, width)
        return [parts[:, c] for c in range(chunks)]

    def join(parts):
        return jnp.stack(parts, axis=1).reshape(crops, own_rows, tokens, width)

    def across(values, bit):
        return lax.ppermute(values, "col", [(q, q ^ bit) for q in range(col_size)])

    bits = [1 << n for n in range(col_size.bit_length() - 1)]

    def after(values, *others):
        return lax.optimization_barrier((values,) + others)[0]

    def gather(own, far, *late):
        pieces = {0: own, far_bit: across(far, far_bit)}
        arrived = pieces[far_bit]
        if late:
            pieces[far_bit] = after(arrived, *late)
        for bit in reversed(bits[:-1]):
            for m in list(pieces):
                pieces[m ^ bit] = across(pieces[m], bit)
        return [pieces[m] for m in range(col_size)], arrived

    def whole_sum(values):
        for bit in bits:
            mine = (me // bit) % 2
            parts = values.reshape(2, -1, values.shape[1])
            sent = lax.dynamic_index_in_dim(parts, 1 - mine, 0, keepdims=False).astype(BF)
            kept = lax.dynamic_index_in_dim(parts, mine, 0, keepdims=False)
            values = kept + across(sent, bit).astype(F32)
        values = doubled(values, [("row", row_size)], BF).astype(BF)
        for bit in reversed(bits):
            other = across(values, bit)
            low = jnp.concatenate([values, other], axis=0)
            high = jnp.concatenate([other, values], axis=0)
            values = jnp.where((me // bit) % 2 == 0, low, high)
        return values.astype(F32)

    def doubled(values, over, sent):
        for axis, size in over:
            for bit in [1 << n for n in range(size.bit_length() - 1)]:
                low = values.astype(sent)
                other = lax.ppermute(low, axis, [(q, q ^ bit) for q in range(size)])
                values = low.astype(F32) + other.astype(F32)
        return values

    x_rows = [swap(part).reshape(shape) for part in cut(pair_state)]
    cot_parts = cut(cotangent)

    wide = lambda item: jnp.broadcast_to(item[:, None], (width, 128))
    vecs = jnp.stack(
        [
            wide(item)
            for item in (
                tri_gain,
                tri_shift,
                mix_gain,
                mix_shift,
                att_gain,
                att_shift,
                trans_gain,
                trans_shift,
            )
        ]
    )
    edge_w = tri_weight[:, : 4 * width]
    edge_wt = edge_w.T
    gate_w = tri_weight[:, 4 * width :]
    lengths = lax.dynamic_index_in_dim(chain_lengths, lax.axis_index("row"), 0, keepdims=False)
    ends = jnp.cumsum(lengths)
    places = jnp.arange(length, dtype=jnp.int32)
    places = places.reshape(order + (some,)).transpose(1, 2, 0, 3).reshape(length)
    chain = jnp.sum((places[:, None] >= ends[None, :]).astype(jnp.int32), axis=-1)
    same = (chain[:, None] == chain[None, :]).astype(F32)
    bias = (LOG2E * chain_bias)[:, None, None] * same[None]
    which = (jnp.arange(16, dtype=jnp.int32)[:, None] == chain[None, :]).astype(F32)
    head_of = jnp.arange(width, dtype=jnp.int32) // (width // heads)
    lane = (jnp.arange(heads, dtype=jnp.int32)[:, None] == head_of[None, :]).astype(BF)
    lane = jnp.broadcast_to(lane[:, None, :], (heads, length, width))
    me = lax.axis_index("col")
    flips = jnp.arange(col_size, dtype=jnp.int32)
    own = own_rows
    far_bit = col_size // 2
    inside = (me ^ flips) & (far_bit - 1)
    place = (me ^ flips) * own
    place_near = (inside + (flips & far_bit)) * own
    half = (me // far_bit).reshape(1)

    cot_rows = [swap(after(cot_parts[0], *x_rows)).reshape(shape)]
    lefts, rights, xt, arrived = [], [], [], []
    for c in range(chunks):
        left, right, *xt = edges(c, chunks, x_rows[c], xt, order, edge_wt, vecs[0], vecs[1])
        if arrived:
            right = after(right, arrived[-1], cot_rows[0])
        pieces, there = gather(right, right)
        lefts.append(left)
        rights.append(pieces)
        arrived.append(there)
    (xt,) = xt
    t = triangle(place, lefts, rights)
    for part in cot_parts[1:]:
        cot_rows.append(swap(after(part, t, cot_rows[-1])).reshape(shape))
    weights = (
        gate_w,
        gate_w.T,
        tri_out,
        tri_out.T,
        att_weight.T,
        att_weight[:, : 3 * width],
        jnp.concatenate([att_weight[:, :width], att_weight[:, 3 * width :]], axis=1),
        att_out,
        att_out.T,
        up_weight,
        up_weight.T,
        down_weight,
        down_weight.T,
    )
    chain_rows = which.astype(BF)
    state, outs, dts = [], [], []
    lefts_all, grads, nears, fars = [], [], [], []
    for c in range(chunks):
        out, dt, z, *sums = rows_pass(
            c, chunks, state, t, xt, cot_rows[c], order, bias, chain_rows, lane, vecs, weights, heads
        )
        state = sums + [z]
        outs.append(out.reshape(group, some, tokens, width))
        near, far = turn(half, dt)
        nears.append(near)
        fars.append(far)
        if c == 0:
            for left in lefts:
                held = after(left, t)
                lefts_all.append(gather(held, held, z)[0])
    da = left_back(place_near, nears, fars, rights)
    last = None
    for c in range(chunks):
        pieces, last = gather(nears[c], fars[c], z if c < chunks - 1 else da)
        grads.append(pieces)
    outs = [swap(out) for out in outs[:-1]] + [swap(after(outs[-1], last))]
    pair_out = join(outs)
    db = right_back(inside[:1] * own, grads, lefts_all)
    whole = (row_size, col_size, some * chunks, tokens, width)
    back, g_edge, g_vec_edge = edges_back(
        xt, z, da, db, order, edge_wt, edge_w, vecs[0], vecs[1], whole
    )
    grad_pair = swap(back.reshape(group, some * chunks, tokens, width))
    grad_pair = grad_pair.reshape(crops, own_rows, tokens, width)

    g_rows, g_vec, g_bias = sums
    total = whole_sum(after(jnp.concatenate([g_rows, g_edge], axis=1), pair_out))
    column = lambda at, n=1: total[:, at * width : (at + n) * width]
    ff = up_weight.shape[1] // width
    t_gate, t_tri_out, t_query, t_gate2, t_kv = column(0), column(1), column(2), column(3), column(4, 2)
    t_att_out, t_up = column(6), column(7, ff)
    t_down = jnp.concatenate([column(7 + ff + n) for n in range(ff)], axis=0)
    t_edge = column(7 + 2 * ff, 4)

    g_vec = jnp.sum(g_vec, axis=-1)
    g_vec_edge = jnp.sum(g_vec_edge, axis=-1)
    g_chain = jnp.sum(g_bias * which[None], axis=(1, 2))
    small = jnp.concatenate(
        [g_vec[:2] + g_vec_edge, g_vec[2:], jnp.pad(g_chain, (0, width - heads))[None]], axis=0
    )
    small = doubled(small, [("col", col_size), ("row", row_size)], F32)
    return (
        pair_out,
        grad_pair,
        small[0],
        small[1],
        jnp.concatenate([t_edge, t_gate], axis=1),
        small[2],
        small[3],
        t_tri_out,
        small[4],
        small[5],
        jnp.concatenate([t_query, t_kv, t_gate2], axis=1),
        small[8, :heads],
        t_att_out,
        small[6],
        small[7],
        t_up,
        t_down,
    )


def solution(mesh):
    pair = P("dp", "row", "col", None)
    vector, matrix = P("dp"), P("dp", None)
    return jax.shard_map(
        functools.partial(shards, mesh.shape["row"], mesh.shape["col"]),
        mesh=mesh,
        in_specs=(pair, pair, P("dp", None)) + (P(),) * 15,
        out_specs=(
            pair,
            pair,
            vector,
            vector,
            matrix,
            vector,
            vector,
            matrix,
            vector,
            vector,
            matrix,
            vector,
            matrix,
            vector,
            vector,
            matrix,
            matrix,
        ),
        check_vma=False,
    )
```

```python
import functools
import math

import jax
import jax.numpy as jnp
from jax import lax
from jax.experimental import pallas as pl
from jax.experimental.pallas import tpu as pltpu
from jax.sharding import PartitionSpec as P

HEADS = 4
EPS = 1e-05
LOG2E = math.log2(math.e)
LN2 = math.log(2.0)
CHUNKS = 2
VMEM_LIMIT = 56 * 1024 * 1024
BF = jnp.bfloat16
F32 = jnp.float32


def nn(left, right):
    return lax.dot_general(left, right, (((1,), (0,)), ((), ())), preferred_element_type=F32)


def nt(left, right):
    return lax.dot_general(left, right, (((1,), (1,)), ((), ())), preferred_element_type=F32)


def tn(left, right):
    return lax.dot_general(left, right, (((0,), (0,)), ((), ())), preferred_element_type=F32)


def cost(flops, size=0):
    return pl.CostEstimate(flops=int(flops), bytes_accessed=int(size), transcendentals=0)


def sigmoid(values):
    return 0.5 * jnp.tanh(0.5 * values) + 0.5


def normalize(values):
    center = values - jnp.mean(values, axis=0, keepdims=True)
    spread = jnp.mean(center * center, axis=0, keepdims=True)
    scale = lax.rsqrt(spread + EPS)
    return center * scale, scale


def normalize_back(grads, gain, hat, scale):
    grad_hat = grads * gain
    first = jnp.mean(grad_hat, axis=0, keepdims=True)
    second = jnp.mean(grad_hat * hat, axis=0, keepdims=True)
    return scale * (grad_hat - first - hat * second)


def widen(column, lanes):
    return jnp.concatenate([column] * (lanes // column.shape[1]), axis=1)


def fold(values):
    parts = [values[:, at : at + 128] for at in range(0, values.shape[1], 128)]
    return functools.reduce(lambda one, two: one + two, parts)


def load_tokens(ref, row, order):
    _, pieces, some, tokens, width = ref.shape
    flat = ref[row // some, :, row % some, :, :].astype(F32)
    flat = flat.reshape(order + (flat.shape[0] * tokens // math.prod(order), width))
    return flat.transpose(1, 2, 0, 3, 4).reshape(pieces * tokens, width)


def store_tokens(ref, row, order, values):
    _, pieces, some, tokens, width = ref.shape
    back = (order[1], order[2], order[0])
    flat = values.reshape(back + (pieces * tokens // math.prod(order), width))
    flat = flat.transpose(2, 0, 1, 3, 4).reshape(pieces, tokens, width)
    ref[row // some, :, row % some, :, :] = flat.astype(ref.dtype)


def stacked(ref, start, count):
    return jnp.concatenate([ref[start + n] for n in range(count)], axis=1)


def spread_out(ref, start, count, values):
    length = values.shape[1] // count
    for n in range(count):
        ref[start + n] = values[:, n * length : (n + 1) * length].astype(ref.dtype)


def edges_kernel(order, x_ref, w_ref, gain_ref, shift_ref, *refs):
    a_ref, b_ref, xt_ref, a_scr, b_scr = refs[-5:]
    rows, width, length = xt_ref.shape
    count = 2

    def step(at, carry):
        start = at * count
        tokens = [load_tokens(x_ref, start + n, order).astype(BF) for n in range(count)]
        x0 = jnp.concatenate([item.T for item in tokens], axis=1)
        spread_out(xt_ref, start, count, x0)
        hat, _ = normalize(x0.astype(F32))
        lanes = x0.shape[1]
        normed = (hat * widen(gain_ref[...], lanes) + widen(shift_ref[...], lanes)).astype(BF)
        proj = nn(w_ref[...], normed)
        left = sigmoid(proj[width : 2 * width]) * proj[:width]
        right = sigmoid(proj[3 * width : 4 * width]) * proj[2 * width : 3 * width]
        for n in range(count):
            base = pl.multiple_of((start + n) * width, width)
            for half in range(length // 128):
                part = slice(n * length + half * 128, n * length + half * 128 + 128)
                a_scr[half, pl.ds(base, width), :] = left[:, part]
                b_scr[half, pl.ds(base, width), :] = right[:, part]
        return carry

    lax.fori_loop(0, rows // count, step, 0)

    def turn(at, carry):
        for n in range(8):
            e = at * 8 + n
            for scr, out in ((a_scr, a_ref), (b_scr, b_ref)):
                halves = [scr[h, pl.ds(e, rows, stride=width), :] for h in range(scr.shape[0])]
                out[e] = jnp.concatenate(halves, axis=1).astype(BF)
        return carry

    lax.fori_loop(0, width // 8, turn, 0)


def edges(c, chunks, x_rows, before, order, weight, gain, shift):
    blocks, pieces, some, tokens, width = x_rows.shape
    length = pieces * tokens
    rows = blocks * some
    step = 16 // some
    const = lambda at: (0, 0)
    return pl.pallas_call(
        functools.partial(edges_kernel, order),
        grid=(blocks // step,),
        in_specs=[
            pl.BlockSpec((step, pieces, some, tokens, width), lambda at: (at, 0, 0, 0, 0)),
            pl.BlockSpec(weight.shape, const),
            pl.BlockSpec(gain.shape, const),
            pl.BlockSpec(shift.shape, const),
        ]
        + [pl.BlockSpec(memory_space=pl.ANY)] * len(before),
        out_specs=[
            pl.BlockSpec((width, 16, length), lambda at: (0, at, 0)),
            pl.BlockSpec((width, 16, length), lambda at: (0, at, 0)),
            pl.BlockSpec((16, width, length), lambda at: (c * (blocks // step) + at, 0, 0)),
        ],
        out_shape=[
            jax.ShapeDtypeStruct((width, rows, length), BF),
            jax.ShapeDtypeStruct((width, rows, length), BF),
            jax.ShapeDtypeStruct((chunks * rows, width, length), BF),
        ],
        input_output_aliases={4: 2} if before else {},
        scratch_shapes=[
            pltpu.VMEM((length // 128, 16 * width, 128), F32),
            pltpu.VMEM((length // 128, 16 * width, 128), F32),
        ],
        compiler_params=pltpu.CompilerParams(vmem_limit_bytes=VMEM_LIMIT),
        cost_estimate=cost(1.7e10),
        name="edges",
    )(x_rows, weight, gain, shift, *before)


def gather_pieces(place_ref, chunks, e, scr):
    for c, pieces in enumerate(chunks):
        rows = pieces[0].shape[1]
        for m, piece in enumerate(pieces):
            scr[e, pl.ds(pl.multiple_of(c * rows + place_ref[m], rows), rows), :] = piece[e]


def triangle_kernel(chunks, pieces, place_ref, *refs):
    lefts, refs = refs[:chunks], refs[chunks:]
    rights, refs = refs[: chunks * pieces], refs[chunks * pieces :]
    t_ref, scr = refs
    rights = [rights[c * pieces : (c + 1) * pieces] for c in range(chunks)]
    for e in range(scr.shape[0]):
        gather_pieces(place_ref, rights, e, scr)
        t_ref[:, e, :] = nt(jnp.concatenate([left[e] for left in lefts], axis=0), scr[e])


def triangle(place, lefts, rights):
    width, rows, length = lefts[0].shape
    chunks, pieces = len(lefts), len(rights[0])
    some = 8
    low = pl.BlockSpec((some, rows, length), lambda at, place: (at, 0, 0))
    return pl.pallas_call(
        functools.partial(triangle_kernel, chunks, pieces),
        grid_spec=pltpu.PrefetchScalarGridSpec(
            num_scalar_prefetch=1,
            grid=(width // some,),
            in_specs=[low] * (chunks + chunks * pieces),
            out_specs=pl.BlockSpec((chunks * rows, some, length), lambda at, place: (0, at, 0)),
            scratch_shapes=[pltpu.VMEM((some, length, length), BF)],
        ),
        out_shape=jax.ShapeDtypeStruct((chunks * rows, width, length), F32),
        compiler_params=pltpu.CompilerParams(vmem_limit_bytes=VMEM_LIMIT),
        cost_estimate=cost(2.0e10),
        name="triangle",
    )(place, *lefts, *[piece for chunk in rights for piece in chunk])


def turn_kernel(half_ref, grad_ref, near_ref, far_ref):
    lanes = near_ref.shape[2]
    for ref, half in ((near_ref, half_ref[0]), (far_ref, 1 - half_ref[0])):
        at = pl.multiple_of(half * lanes, lanes)
        for e in range(ref.shape[0]):
            ref[e] = grad_ref[:, e, pl.ds(at, lanes)].astype(BF)


def turn(half, grad):
    rows, width, length = grad.shape
    some = 16
    low = pl.BlockSpec((some, rows, length // 2), lambda at, half: (at, 0, 0))
    return pl.pallas_call(
        turn_kernel,
        grid_spec=pltpu.PrefetchScalarGridSpec(
            num_scalar_prefetch=1,
            grid=(width // some,),
            in_specs=[pl.BlockSpec((rows, some, length), lambda at, half: (0, at, 0))],
            out_specs=[low, low],
        ),
        out_shape=[jax.ShapeDtypeStruct((width, rows, length // 2), BF)] * 2,
        compiler_params=pltpu.CompilerParams(vmem_limit_bytes=VMEM_LIMIT),
        cost_estimate=cost(5.0e9),
        name="turn",
    )(half, grad)


def right_back_kernel(chunks, pieces, own_ref, *refs):
    grads, refs = refs[: chunks * pieces], refs[chunks * pieces :]
    lefts, refs = refs[: chunks * pieces], refs[chunks * pieces :]
    db_ref, scr = refs
    rows = db_ref.shape[0]
    for e in range(scr.shape[0]):
        grad = jnp.concatenate([ref[e] for ref in grads], axis=0)
        left = jnp.concatenate([ref[e] for ref in lefts], axis=0)
        scr[e] = tn(grad, left)
        db_ref[:, e, :] = scr[e, pl.ds(pl.multiple_of(own_ref[0], rows), rows), :]


def right_back(own, grads, lefts):
    width, rows, length = lefts[0][0].shape
    chunks, pieces = len(lefts), len(lefts[0])
    part = grads[0][0].shape[2]
    some = 8
    low = lambda lanes: pl.BlockSpec((some, rows, lanes), lambda at, own: (at, 0, 0))
    return pl.pallas_call(
        functools.partial(right_back_kernel, chunks, pieces),
        grid_spec=pltpu.PrefetchScalarGridSpec(
            num_scalar_prefetch=1,
            grid=(width // some,),
            in_specs=[low(part)] * (chunks * pieces) + [low(length)] * (chunks * pieces),
            out_specs=pl.BlockSpec((chunks * rows, some, length), lambda at, own: (0, at, 0)),
            scratch_shapes=[pltpu.VMEM((some, part, length), F32)],
        ),
        out_shape=jax.ShapeDtypeStruct((chunks * rows, width, length), F32),
        compiler_params=pltpu.CompilerParams(vmem_limit_bytes=VMEM_LIMIT),
        cost_estimate=cost(2.2e10),
        name="right_back",
    )(own, *[item for chunk in grads for item in chunk], *[item for chunk in lefts for item in chunk])


def left_back_kernel(chunks, pieces, place_ref, *refs):
    grads, refs = refs[: 2 * chunks], refs[2 * chunks :]
    rights, refs = refs[: chunks * pieces], refs[chunks * pieces :]
    da_ref, scr = refs
    rights = [rights[c * pieces : (c + 1) * pieces] for c in range(chunks)]
    for e in range(scr.shape[0]):
        gather_pieces(place_ref, rights, e, scr)
        grad = [jnp.concatenate([grads[c][e], grads[chunks + c][e]], axis=1) for c in range(chunks)]
        da_ref[:, e, :] = nn(jnp.concatenate(grad, axis=0), scr[e])


def left_back(place, nears, fars, rights):
    width, rows, part = nears[0].shape
    chunks, pieces = len(nears), len(rights[0])
    length = 2 * part
    some = 8
    low = lambda lanes: pl.BlockSpec((some, rows, lanes), lambda at, place: (at, 0, 0))
    return pl.pallas_call(
        functools.partial(left_back_kernel, chunks, pieces),
        grid_spec=pltpu.PrefetchScalarGridSpec(
            num_scalar_prefetch=1,
            grid=(width // some,),
            in_specs=[low(part)] * (2 * chunks) + [low(length)] * (chunks * pieces),
            out_specs=pl.BlockSpec((chunks * rows, some, length), lambda at, place: (0, at, 0)),
            scratch_shapes=[pltpu.VMEM((some, length, length), BF)],
        ),
        out_shape=jax.ShapeDtypeStruct((chunks * rows, width, length), F32),
        compiler_params=pltpu.CompilerParams(vmem_limit_bytes=VMEM_LIMIT),
        cost_estimate=cost(2.0e10),
        name="left_back",
    )(place, *nears, *fars, *[piece for chunk in rights for piece in chunk])


def rows_kernel(count, heads, order, first, last, *refs):
    before = []
    if not first:
        before, refs = refs[:3], refs[4:]
    rows_body(count, heads, order, before, last, *refs)


def rows_body(
    count,
    heads,
    order,
    before,
    last,
    t_ref,
    xt_ref,
    cot_ref,
    bias_ref,
    chain_ref,
    lane_ref,
    vec_ref,
    gate_w_ref,
    gate_wt_ref,
    tri_out_ref,
    tri_out_t_ref,
    att_t_ref,
    att_qkv_ref,
    att_qg_ref,
    att_out_ref,
    att_out_t_ref,
    up_ref,
    up_t_ref,
    down_ref,
    down_t_ref,
    out_ref,
    dt_ref,
    z_ref,
    g_ref,
    g_vec_ref,
    g_bias_ref,
    e_scr,
):
    total_rows, width, length = t_ref.shape
    head = width // heads
    scaling = 1.0 / math.sqrt(head)

    sums = (g_ref, g_vec_ref, g_bias_ref)
    place = {}
    for name in ("gate", "tri_out", "query", "gate2", "key", "value", "att_out"):
        place[name] = slice(len(place) * width, (len(place) + 1) * width)
    ups = slice(7 * width, 7 * width + up_ref.shape[1])
    downs = [
        slice(at, at + width) for at in range(ups.stop, ups.stop + up_ref.shape[1], width)
    ]

    @pl.when(pl.program_id(0) == 0)
    def _():
        for n, ref in enumerate(sums):
            ref[...] = before[n][...] if before else jnp.zeros(ref.shape, ref.dtype)

    def vec(at):
        return widen(vec_ref[at], length)

    mine = [slice(h * head, (h + 1) * head) for h in range(heads)]
    there = [slice(h * length, (h + 1) * length) for h in range(heads)]
    ones = jnp.ones((16, length), BF)

    def row_blocks(start, n, kept):
        x0 = xt_ref[start + n].astype(F32)
        hat1, scale1 = normalize(x0)
        normed1 = (hat1 * vec(0) + vec(1)).astype(BF)
        gate1 = nn(gate_wt_ref[...], normed1)
        yield
        hat_t, scale_t = normalize(t_ref[start + n])
        mixed = (hat_t * vec(2) + vec(3)).astype(BF)
        branch = nn(tri_out_t_ref[...], mixed)
        yield
        gate1 = sigmoid(gate1)
        x1 = x0 + gate1 * branch
        hat2, scale2 = normalize(x1)
        normed2 = (hat2 * vec(4) + vec(5)).astype(BF)
        hidden = nn(att_t_ref[...], normed2)
        normed2_tok = normed2.T
        hidden_tok = nn(normed2_tok, att_qkv_ref[...])
        yield
        query = (hidden[:width] * (scaling * LOG2E)).astype(BF)
        key = hidden[width : 2 * width].astype(BF)
        value = hidden[2 * width : 3 * width].astype(BF)
        gate2 = sigmoid(hidden[3 * width :].astype(BF).astype(F32))
        query_tok = (hidden_tok[:, :width] * (scaling * LOG2E)).astype(BF)
        key_tok = hidden_tok[:, width : 2 * width].astype(BF)
        value_tok = hidden_tok[:, 2 * width :].astype(BF)

        def scores(h):
            return nn(key_tok * lane_ref[h], query)

        ahead = scores(0)
        yield
        outs, inverses, both = [], [], None

        def finish(both):
            inverse = 1.0 / both[head : head + 1]
            inverses.append(inverse)
            outs.append(both[:head] * inverse)

        for h in range(heads):
            score = ahead
            if h + 1 < heads:
                ahead = scores(h + 1)
            score = score + bias_ref[h]
            peak = jnp.max(score, axis=0, keepdims=True)
            expon = jnp.exp2(score - peak).astype(BF)
            e_scr[n, :, there[h]] = expon
            if both is not None:
                finish(both)
            both = nn(jnp.concatenate([value[mine[h]], ones], axis=0), expon)
            yield
        finish(both)
        attended = jnp.concatenate(outs, axis=0)
        gated = (gate2 * attended).astype(BF)
        x2 = nn(att_out_t_ref[...], gated)
        yield
        x2 = x1 + x2
        hat3, scale3 = normalize(x2)
        normed3 = (hat3 * vec(6) + vec(7)).astype(BF)
        up = nn(up_t_ref[...], normed3)
        cot_tok = load_tokens(cot_ref, start + n, order).astype(BF)
        cot_low = cot_tok.T
        grad_act = nn(down_ref[...], cot_low)
        yield
        gate3 = sigmoid(up)
        act = (up * gate3).astype(BF)
        down = nn(down_t_ref[...], act)
        grad_up = (grad_act * (gate3 * (1.0 + up * (1.0 - gate3)))).astype(BF)
        grad3 = nn(up_ref[...], grad_up)
        yield
        store_tokens(out_ref, start + n, order, (x2 + down).astype(BF).T.astype(F32))
        g_vec_ref[6] += fold(grad3 * hat3)
        g_vec_ref[7] += fold(grad3)
        grad_x2 = cot_low.astype(F32) + normalize_back(grad3, vec(6), hat3, scale3)
        grad_x2_low = grad_x2.astype(BF)
        grad_gated = nn(att_out_ref[...], grad_x2_low)
        kept["down"].append((act, cot_tok))
        kept["up"].append((normed3, grad_up))
        kept["att_out"].append((gated, grad_x2_low))
        yield
        grad_mixed = grad_gated * gate2
        grad_gate2 = (grad_gated * attended * gate2 * (1.0 - gate2)).astype(BF)
        scaled = [grad_mixed[mine[h]] * inverses[h] for h in range(heads)]
        grad_out = jnp.concatenate(scaled, axis=0).astype(BF)
        grad_out_tok = grad_out.T
        product = grad_out.astype(F32) * attended

        def probs(h):
            return nn(value_tok * lane_ref[h], grad_out)

        ahead = probs(0)
        yield
        grad_queries, grad_key, grad_value, both = [], 0.0, 0.0, None
        more_key, more_value = None, None
        for h in range(heads):
            grad_prob = ahead
            if h + 1 < heads:
                ahead = probs(h + 1)
            center = jnp.sum(product[mine[h]], axis=0, keepdims=True)
            expon = e_scr[n, :, there[h]]
            grad_score = (expon.astype(F32) * (grad_prob - center)).astype(BF)
            if both is not None:
                grad_queries.append((both[:head] * scaling).astype(BF))
                g_bias_ref[h - 1] += both[head:]
                grad_key += more_key
                grad_value += more_value
            more_value = nn(expon, grad_out_tok * lane_ref[h])
            both = nn(jnp.concatenate([key[mine[h]], chain_ref[...]], axis=0), grad_score)
            more_key = nn(grad_score, query_tok * lane_ref[h])
            yield
        grad_queries.append((both[:head] * scaling).astype(BF))
        g_bias_ref[heads - 1] += both[head:]
        grad_key = ((grad_key + more_key) * LN2).astype(BF)
        grad_value = (grad_value + more_value).astype(BF)
        grad_qg = jnp.concatenate(grad_queries + [grad_gate2], axis=0)
        grad_kv = jnp.concatenate([grad_key, grad_value], axis=1)
        grad2 = nn(att_qg_ref[...], grad_qg) + nt(att_qkv_ref[:, width:], grad_kv)
        kept["qg"].append((grad_qg, normed2_tok))
        kept["kv"].append((normed2, grad_kv))
        yield
        g_vec_ref[4] += fold(grad2 * hat2)
        g_vec_ref[5] += fold(grad2)
        grad_x1 = grad_x2 + normalize_back(grad2, vec(4), hat2, scale2)
        grad_branch = (grad_x1 * gate1).astype(BF)
        grad_mix = nn(tri_out_ref[...], grad_branch)
        grad_gate1 = (grad_x1 * branch * gate1 * (1.0 - gate1)).astype(BF)
        grad1 = nn(gate_w_ref[...], grad_gate1)
        kept["tri_out"].append((mixed, grad_branch))
        kept["gate"].append((normed1, grad_gate1))
        yield
        g_vec_ref[2] += fold(grad_mix * hat_t)
        g_vec_ref[3] += fold(grad_mix)
        dt_ref[start + n] = normalize_back(grad_mix, vec(2), hat_t, scale_t)
        g_vec_ref[0] += fold(grad1 * hat1)
        g_vec_ref[1] += fold(grad1)
        z_ref[start + n] = grad_x1 + normalize_back(grad1, vec(0), hat1, scale1)
        yield

    def sum_blocks(kept):
        def wide_of(name, left_axis, right_axis):
            left = jnp.concatenate([pair[0] for pair in kept[name]], axis=left_axis)
            right = jnp.concatenate([pair[1] for pair in kept[name]], axis=right_axis)
            return left, right

        grad = nn(*wide_of("down", 1, 0))
        for n, part in enumerate(downs):
            g_ref[:, part] += grad[n * width : (n + 1) * width]
        yield
        g_ref[:, ups] += nt(*wide_of("up", 1, 1))
        yield
        g_ref[:, place["att_out"]] += nt(*wide_of("att_out", 1, 1))
        yield
        grad = nn(*wide_of("qg", 1, 0))
        g_ref[:, place["query"]] += grad[:width]
        g_ref[:, place["gate2"]] += grad[width:]
        yield
        g_ref[:, place["key"].start : place["value"].stop] += nn(*wide_of("kv", 1, 0))
        yield
        g_ref[:, place["tri_out"]] += nt(*wide_of("tri_out", 1, 1))
        yield
        g_ref[:, place["gate"]] += nt(*wide_of("gate", 1, 1))
        yield

    def step(at, carry):
        start = at * count
        kept = {name: [] for name in ("down", "up", "att_out", "qg", "kv", "tri_out", "gate")}
        rows = [row_blocks(start, n, kept) for n in range(count)]
        sums = sum_blocks(kept)
        total = 12 + 2 * heads
        for block in range(total):
            for n, row in enumerate(rows):
                next(row)
                if block >= total - 3 and n % 2 == 0 and (n > 0 or block > total - 3):
                    next(sums, None)
        for _ in sums:
            pass
        for row in rows:
            assert next(row, None) is None
        return carry

    lax.fori_loop(0, total_rows // count, step, 0)

    if last:

        @pl.when(pl.program_id(0) == pl.num_programs(0) - 1)
        def _():
            for name in ("query", "gate2"):
                g_ref[:, place[name]] = g_ref[:, place[name]].T


def rows_pass(c, chunks, before, t, xt, cot_rows, order, bias, chain, lane, vecs, weights, heads):
    _, width, length = t.shape
    blocks, pieces, sub, tokens, _ = cot_rows.shape
    rows = blocks * sub
    some, count = 4, 4
    inner = sub // some
    full = lambda item: pl.BlockSpec(item.shape, lambda at: (0,) * item.ndim)
    by_row = pl.BlockSpec((some, width, length), lambda at: (at, 0, 0))
    of_all = pl.BlockSpec((some, width, length), lambda at: (c * (rows // some) + at, 0, 0))
    by_piece = pl.BlockSpec(
        (1, pieces, some, tokens, width), lambda at: (at // inner, 0, at % inner, 0, 0)
    )
    consts = (bias, chain, lane, vecs) + weights
    wide = weights[-1].shape[1]
    sum_shapes = [
        jax.ShapeDtypeStruct(shape, F32)
        for shape in ((width, 7 * width + 2 * wide), (8, width, 128), (heads, 16, length))
    ]
    before_specs = [full(item) for item in before[:3]]
    before_specs += [pl.BlockSpec(memory_space=pl.ANY)] * len(before[3:])
    return pl.pallas_call(
        functools.partial(rows_kernel, count, heads, order, c == 0, c == chunks - 1),
        grid=(rows // some,),
        in_specs=before_specs + [of_all, of_all, by_piece] + [full(item) for item in consts],
        out_specs=[by_piece, by_row, of_all] + [full(item) for item in sum_shapes],
        out_shape=[
            jax.ShapeDtypeStruct(cot_rows.shape, BF),
            jax.ShapeDtypeStruct((rows, width, length), F32),
            jax.ShapeDtypeStruct(t.shape, F32),
        ]
        + sum_shapes,
        input_output_aliases={3: 2} if before else {},
        scratch_shapes=[
            pltpu.VMEM((count, length, heads * length), BF),
        ],
        compiler_params=pltpu.CompilerParams(vmem_limit_bytes=VMEM_LIMIT),
        cost_estimate=cost(1.2e11),
        name="rows",
    )(*before, t, xt, cot_rows, *consts)


def edges_back_kernel(
    order, xt_ref, z_ref, da_ref, db_ref, wt_ref, w_ref, gain_ref, shift_ref, out_ref, g_w_ref, g_vec_ref
):
    rows, width, length = xt_ref.shape
    count = 2

    @pl.when(pl.program_id(0) == 0)
    def _():
        g_w_ref[...] = jnp.zeros(g_w_ref.shape, F32)
        g_vec_ref[...] = jnp.zeros(g_vec_ref.shape, F32)

    def step(at, carry):
        start = at * count
        x0 = stacked(xt_ref, start, count).astype(F32)
        lanes = x0.shape[1]
        gain = widen(gain_ref[...], lanes)
        hat, scale = normalize(x0)
        normed = (hat * gain + widen(shift_ref[...], lanes)).astype(BF)
        proj = nn(wt_ref[...], normed)
        pa, pag = proj[:width], proj[width : 2 * width]
        pb, pbg = proj[2 * width : 3 * width], proj[3 * width :]
        da = stacked(da_ref, start, count)
        db = stacked(db_ref, start, count)
        sa, sb = sigmoid(pag), sigmoid(pbg)
        dsa, dsb = da * sa, db * sb
        grads = jnp.concatenate(
            [
                dsa.astype(BF),
                (dsa * pa * (1.0 - sa)).astype(BF),
                dsb.astype(BF),
                (dsb * pb * (1.0 - sb)).astype(BF),
            ],
            axis=0,
        )
        g_w_ref[...] += nt(normed, grads)
        grad = nn(w_ref[...], grads)
        g_vec_ref[0] += fold(grad * hat)
        g_vec_ref[1] += fold(grad)
        out = stacked(z_ref, start, count) + normalize_back(grad, gain, hat, scale)
        out = out.astype(BF)
        for n in range(count):
            store_tokens(out_ref, start + n, order, out[:, n * length : (n + 1) * length].T.astype(F32))
        return carry

    lax.fori_loop(0, rows // count, step, 0)


def edges_back(xt, z, da, db, order, weight_t, weight, gain, shift, shape):
    rows, width, length = xt.shape
    blocks, pieces, sub, tokens, _ = shape
    chunks = order[2]
    some = sub // chunks
    step = 16 // some
    inner = blocks // step
    full = lambda item: pl.BlockSpec(item.shape, lambda at: (0,) * item.ndim)
    by_row = pl.BlockSpec((16, width, length), lambda at: (at, 0, 0))
    sum_shapes = [
        jax.ShapeDtypeStruct(weight.shape, F32),
        jax.ShapeDtypeStruct((2, width, 128), F32),
    ]
    by_piece = pl.BlockSpec(
        (step, pieces, some, tokens, width), lambda at: (at % inner, 0, at // inner, 0, 0)
    )
    return pl.pallas_call(
        functools.partial(edges_back_kernel, order),
        grid=(chunks * inner,),
        in_specs=[by_row] * 4 + [full(item) for item in (weight_t, weight, gain, shift)],
        out_specs=[by_piece] + [full(item) for item in sum_shapes],
        out_shape=[jax.ShapeDtypeStruct(shape, BF)] + sum_shapes,
        compiler_params=pltpu.CompilerParams(vmem_limit_bytes=VMEM_LIMIT),
        cost_estimate=cost(4.0e10),
        name="edges_back",
    )(xt, z, da, db, weight_t, weight, gain, shift)


def shards(
    row_size,
    col_size,
    pair_state,
    cotangent,
    chain_lengths,
    tri_gain,
    tri_shift,
    tri_weight,
    mix_gain,
    mix_shift,
    tri_out,
    att_gain,
    att_shift,
    att_weight,
    chain_bias,
    att_out,
    trans_gain,
    trans_shift,
    up_weight,
    down_weight,
):
    heads = HEADS
    crops, own_rows, tokens, width = pair_state.shape
    length = col_size * tokens
    chunks = CHUNKS
    some = own_rows // (col_size * chunks)
    axes = ("row", "col")
    group = row_size * col_size
    order = (row_size, col_size, chunks)
    shape = (row_size, col_size, some, tokens, width)

    def swap(values):
        return lax.all_to_all(values, axes, split_axis=0, concat_axis=0, tiled=True)

    def cut(values):
        parts = values.reshape(group, chunks, some, tokens, width)
        return [parts[:, c] for c in range(chunks)]

    def join(parts):
        return jnp.stack(parts, axis=1).reshape(crops, own_rows, tokens, width)

    def across(values, bit):
        return lax.ppermute(values, "col", [(q, q ^ bit) for q in range(col_size)])

    bits = [1 << n for n in range(col_size.bit_length() - 1)]

    def after(values, *others):
        return lax.optimization_barrier((values,) + others)[0]

    def gather(own, far, *late):
        pieces = {0: own, far_bit: across(far, far_bit)}
        arrived = pieces[far_bit]
        if late:
            pieces[far_bit] = after(arrived, *late)
        for bit in reversed(bits[:-1]):
            for m in list(pieces):
                pieces[m ^ bit] = across(pieces[m], bit)
        return [pieces[m] for m in range(col_size)], arrived

    def whole_sum(values):
        for bit in bits:
            mine = (me // bit) % 2
            parts = values.reshape(2, -1, values.shape[1])
            sent = lax.dynamic_index_in_dim(parts, 1 - mine, 0, keepdims=False).astype(BF)
            kept = lax.dynamic_index_in_dim(parts, mine, 0, keepdims=False)
            values = kept + across(sent, bit).astype(F32)
        values = doubled(values, [("row", row_size)], BF).astype(BF)
        for bit in reversed(bits):
            other = across(values, bit)
            low = jnp.concatenate([values, other], axis=0)
            high = jnp.concatenate([other, values], axis=0)
            values = jnp.where((me // bit) % 2 == 0, low, high)
        return values.astype(F32)

    def doubled(values, over, sent):
        for axis, size in over:
            for bit in [1 << n for n in range(size.bit_length() - 1)]:
                low = values.astype(sent)
                other = lax.ppermute(low, axis, [(q, q ^ bit) for q in range(size)])
                values = low.astype(F32) + other.astype(F32)
        return values

    x_rows = [swap(part).reshape(shape) for part in cut(pair_state)]
    cot_parts = cut(cotangent)

    wide = lambda item: jnp.broadcast_to(item[:, None], (width, 128))
    vecs = jnp.stack(
        [
            wide(item)
            for item in (
                tri_gain,
                tri_shift,
                mix_gain,
                mix_shift,
                att_gain,
                att_shift,
                trans_gain,
                trans_shift,
            )
        ]
    )
    edge_w = tri_weight[:, : 4 * width]
    edge_wt = edge_w.T
    gate_w = tri_weight[:, 4 * width :]
    lengths = lax.dynamic_index_in_dim(chain_lengths, lax.axis_index("row"), 0, keepdims=False)
    ends = jnp.cumsum(lengths)
    places = jnp.arange(length, dtype=jnp.int32)
    places = places.reshape(order + (some,)).transpose(1, 2, 0, 3).reshape(length)
    chain = jnp.sum((places[:, None] >= ends[None, :]).astype(jnp.int32), axis=-1)
    same = (chain[:, None] == chain[None, :]).astype(F32)
    bias = (LOG2E * chain_bias)[:, None, None] * same[None]
    which = (jnp.arange(16, dtype=jnp.int32)[:, None] == chain[None, :]).astype(F32)
    head_of = jnp.arange(width, dtype=jnp.int32) // (width // heads)
    lane = (jnp.arange(heads, dtype=jnp.int32)[:, None] == head_of[None, :]).astype(BF)
    lane = jnp.broadcast_to(lane[:, None, :], (heads, length, width))
    me = lax.axis_index("col")
    flips = jnp.arange(col_size, dtype=jnp.int32)
    own = own_rows
    far_bit = col_size // 2
    inside = (me ^ flips) & (far_bit - 1)
    place = (me ^ flips) * own
    place_near = (inside + (flips & far_bit)) * own
    half = (me // far_bit).reshape(1)

    cot_rows = []
    lefts, rights, xt, arrived = [], [], [], []
    for c in range(chunks):
        left, right, *xt = edges(c, chunks, x_rows[c], xt, order, edge_wt, vecs[0], vecs[1])
        if arrived:
            right = after(right, arrived[-1])
        pieces, there = gather(right, right)
        lefts.append(left)
        rights.append(pieces)
        arrived.append(there)
        if c == 0:
            cot_rows.append(swap(after(cot_parts[0], left, *x_rows)).reshape(shape))
    (xt,) = xt
    t = triangle(place, lefts, rights)
    for part in cot_parts[1:]:
        cot_rows.append(swap(after(part, t, cot_rows[-1])).reshape(shape))
    weights = (
        gate_w,
        gate_w.T,
        tri_out,
        tri_out.T,
        att_weight.T,
        att_weight[:, : 3 * width],
        jnp.concatenate([att_weight[:, :width], att_weight[:, 3 * width :]], axis=1),
        att_out,
        att_out.T,
        up_weight,
        up_weight.T,
        down_weight,
        down_weight.T,
    )
    chain_rows = which.astype(BF)
    state, outs, dts = [], [], []
    lefts_all, grads, nears, fars = [], [], [], []
    for c in range(chunks):
        out, dt, z, *sums = rows_pass(
            c, chunks, state, t, xt, cot_rows[c], order, bias, chain_rows, lane, vecs, weights, heads
        )
        state = sums + [z]
        if outs:
            dt = after(dt, outs[-1])
        near, far = turn(half, dt)
        nears.append(near)
        fars.append(far)
        if c < chunks - 1:
            outs.append(swap(out.reshape(group, some, tokens, width)))
    da = left_back(place_near, nears, fars, rights)
    for left in lefts:
        held = after(left, t)
        lefts_all.append(gather(held, held, z)[0])
    for c in range(chunks):
        pieces, last = gather(nears[c], fars[c], z if c < chunks - 1 else da)
        grads.append(pieces)
    outs.append(swap(after(out, last).reshape(group, some, tokens, width)))
    pair_out = join(outs)
    db = right_back(inside[:1] * own, grads, lefts_all)
    whole = (row_size, col_size, some * chunks, tokens, width)
    back, g_edge, g_vec_edge = edges_back(
        xt, z, da, db, order, edge_wt, edge_w, vecs[0], vecs[1], whole
    )
    grad_pair = swap(back.reshape(group, some * chunks, tokens, width))
    grad_pair = grad_pair.reshape(crops, own_rows, tokens, width)

    g_rows, g_vec, g_bias = sums
    total = whole_sum(after(jnp.concatenate([g_rows, g_edge], axis=1), pair_out))
    column = lambda at, n=1: total[:, at * width : (at + n) * width]
    ff = up_weight.shape[1] // width
    t_gate, t_tri_out, t_query, t_gate2, t_kv = column(0), column(1), column(2), column(3), column(4, 2)
    t_att_out, t_up = column(6), column(7, ff)
    t_down = jnp.concatenate([column(7 + ff + n) for n in range(ff)], axis=0)
    t_edge = column(7 + 2 * ff, 4)

    g_vec = jnp.sum(g_vec, axis=-1)
    g_vec_edge = jnp.sum(g_vec_edge, axis=-1)
    g_chain = jnp.sum(g_bias * which[None], axis=(1, 2))
    small = jnp.concatenate(
        [g_vec[:2] + g_vec_edge, g_vec[2:], jnp.pad(g_chain, (0, width - heads))[None]], axis=0
    )
    small = doubled(small, [("col", col_size), ("row", row_size)], F32)
    return (
        pair_out,
        grad_pair,
        small[0],
        small[1],
        jnp.concatenate([t_edge, t_gate], axis=1),
        small[2],
        small[3],
        t_tri_out,
        small[4],
        small[5],
        jnp.concatenate([t_query, t_kv, t_gate2], axis=1),
        small[8, :heads],
        t_att_out,
        small[6],
        small[7],
        t_up,
        t_down,
    )


def solution(mesh):
    pair = P("dp", "row", "col", None)
    vector, matrix = P("dp"), P("dp", None)
    return jax.shard_map(
        functools.partial(shards, mesh.shape["row"], mesh.shape["col"]),
        mesh=mesh,
        in_specs=(pair, pair, P("dp", None)) + (P(),) * 15,
        out_specs=(
            pair,
            pair,
            vector,
            vector,
            matrix,
            vector,
            vector,
            matrix,
            vector,
            vector,
            matrix,
            vector,
            matrix,
            vector,
            vector,
            matrix,
            matrix,
        ),
        check_vma=False,
    )
```

```python
import functools
import math

import jax
import jax.numpy as jnp
from jax import lax
from jax.experimental import pallas as pl
from jax.experimental.pallas import tpu as pltpu
from jax.sharding import PartitionSpec as P

HEADS = 4
EPS = 1e-05
LOG2E = math.log2(math.e)
LN2 = math.log(2.0)
CHUNKS = 2
VMEM_LIMIT = 56 * 1024 * 1024
BF = jnp.bfloat16
F32 = jnp.float32


def nn(left, right):
    return lax.dot_general(left, right, (((1,), (0,)), ((), ())), preferred_element_type=F32)


def nt(left, right):
    return lax.dot_general(left, right, (((1,), (1,)), ((), ())), preferred_element_type=F32)


def tn(left, right):
    return lax.dot_general(left, right, (((0,), (0,)), ((), ())), preferred_element_type=F32)


def cost(flops, size=0):
    return pl.CostEstimate(flops=int(flops), bytes_accessed=int(size), transcendentals=0)


def sigmoid(values):
    return 0.5 * jnp.tanh(0.5 * values) + 0.5


def normalize(values):
    center = values - jnp.mean(values, axis=0, keepdims=True)
    spread = jnp.mean(center * center, axis=0, keepdims=True)
    scale = lax.rsqrt(spread + EPS)
    return center * scale, scale


def normalize_back(grads, gain, hat, scale):
    grad_hat = grads * gain
    first = jnp.mean(grad_hat, axis=0, keepdims=True)
    second = jnp.mean(grad_hat * hat, axis=0, keepdims=True)
    return scale * (grad_hat - first - hat * second)


def widen(column, lanes):
    return jnp.concatenate([column] * (lanes // column.shape[1]), axis=1)


def fold(values):
    parts = [values[:, at : at + 128] for at in range(0, values.shape[1], 128)]
    return functools.reduce(lambda one, two: one + two, parts)


def load_tokens(ref, row, order):
    _, pieces, some, tokens, width = ref.shape
    flat = ref[row // some, :, row % some, :, :].astype(F32)
    flat = flat.reshape(order + (flat.shape[0] * tokens // math.prod(order), width))
    return flat.transpose(1, 2, 0, 3, 4).reshape(pieces * tokens, width)


def store_tokens(ref, row, order, values):
    _, pieces, some, tokens, width = ref.shape
    back = (order[1], order[2], order[0])
    flat = values.reshape(back + (pieces * tokens // math.prod(order), width))
    flat = flat.transpose(2, 0, 1, 3, 4).reshape(pieces, tokens, width)
    ref[row // some, :, row % some, :, :] = flat.astype(ref.dtype)


def stacked(ref, start, count):
    return jnp.concatenate([ref[start + n] for n in range(count)], axis=1)


def spread_out(ref, start, count, values):
    length = values.shape[1] // count
    for n in range(count):
        ref[start + n] = values[:, n * length : (n + 1) * length].astype(ref.dtype)


def edges_kernel(order, x_ref, w_ref, gain_ref, shift_ref, *refs):
    a_ref, b_ref, xt_ref, a_scr, b_scr = refs[-5:]
    rows, width, length = xt_ref.shape
    count = 4

    def step(at, carry):
        start = at * count
        tokens = [load_tokens(x_ref, start + n, order).astype(BF) for n in range(count)]
        x0 = jnp.concatenate([item.T for item in tokens], axis=1)
        spread_out(xt_ref, start, count, x0)
        hat, _ = normalize(x0.astype(F32))
        lanes = x0.shape[1]
        normed = (hat * widen(gain_ref[...], lanes) + widen(shift_ref[...], lanes)).astype(BF)
        proj = nn(w_ref[...], normed)
        left = sigmoid(proj[width : 2 * width]) * proj[:width]
        right = sigmoid(proj[3 * width : 4 * width]) * proj[2 * width : 3 * width]
        for n in range(count):
            base = pl.multiple_of((start + n) * width, width)
            for half in range(length // 128):
                part = slice(n * length + half * 128, n * length + half * 128 + 128)
                a_scr[half, pl.ds(base, width), :] = left[:, part]
                b_scr[half, pl.ds(base, width), :] = right[:, part]
        return carry

    lax.fori_loop(0, rows // count, step, 0)

    def turn(at, carry):
        for n in range(8):
            e = at * 8 + n
            for scr, out in ((a_scr, a_ref), (b_scr, b_ref)):
                halves = [scr[h, pl.ds(e, rows, stride=width), :] for h in range(scr.shape[0])]
                out[e] = jnp.concatenate(halves, axis=1).astype(BF)
        return carry

    lax.fori_loop(0, width // 8, turn, 0)


def edges(c, chunks, x_rows, before, order, weight, gain, shift):
    blocks, pieces, some, tokens, width = x_rows.shape
    length = pieces * tokens
    rows = blocks * some
    step = 16 // some
    const = lambda at: (0, 0)
    return pl.pallas_call(
        functools.partial(edges_kernel, order),
        grid=(blocks // step,),
        in_specs=[
            pl.BlockSpec((step, pieces, some, tokens, width), lambda at: (at, 0, 0, 0, 0)),
            pl.BlockSpec(weight.shape, const),
            pl.BlockSpec(gain.shape, const),
            pl.BlockSpec(shift.shape, const),
        ]
        + [pl.BlockSpec(memory_space=pl.ANY)] * len(before),
        out_specs=[
            pl.BlockSpec((width, 16, length), lambda at: (0, at, 0)),
            pl.BlockSpec((width, 16, length), lambda at: (0, at, 0)),
            pl.BlockSpec((16, width, length), lambda at: (c * (blocks // step) + at, 0, 0)),
        ],
        out_shape=[
            jax.ShapeDtypeStruct((width, rows, length), BF),
            jax.ShapeDtypeStruct((width, rows, length), BF),
            jax.ShapeDtypeStruct((chunks * rows, width, length), BF),
        ],
        input_output_aliases={4: 2} if before else {},
        scratch_shapes=[
            pltpu.VMEM((length // 128, 16 * width, 128), F32),
            pltpu.VMEM((length // 128, 16 * width, 128), F32),
        ],
        compiler_params=pltpu.CompilerParams(vmem_limit_bytes=VMEM_LIMIT),
        cost_estimate=cost(1.7e10),
        name="edges",
    )(x_rows, weight, gain, shift, *before)


def gather_pieces(place_ref, chunks, e, scr):
    for c, pieces in enumerate(chunks):
        rows = pieces[0].shape[1]
        for m, piece in enumerate(pieces):
            scr[e, pl.ds(pl.multiple_of(c * rows + place_ref[m], rows), rows), :] = piece[e]


def triangle_kernel(chunks, pieces, place_ref, *refs):
    lefts, refs = refs[:chunks], refs[chunks:]
    rights, refs = refs[: chunks * pieces], refs[chunks * pieces :]
    t_ref, scr = refs
    rights = [rights[c * pieces : (c + 1) * pieces] for c in range(chunks)]
    for e in range(scr.shape[0]):
        gather_pieces(place_ref, rights, e, scr)
        t_ref[:, e, :] = nt(jnp.concatenate([left[e] for left in lefts], axis=0), scr[e])


def triangle(place, lefts, rights):
    width, rows, length = lefts[0].shape
    chunks, pieces = len(lefts), len(rights[0])
    some = 8
    low = pl.BlockSpec((some, rows, length), lambda at, place: (at, 0, 0))
    return pl.pallas_call(
        functools.partial(triangle_kernel, chunks, pieces),
        grid_spec=pltpu.PrefetchScalarGridSpec(
            num_scalar_prefetch=1,
            grid=(width // some,),
            in_specs=[low] * (chunks + chunks * pieces),
            out_specs=pl.BlockSpec((chunks * rows, some, length), lambda at, place: (0, at, 0)),
            scratch_shapes=[pltpu.VMEM((some, length, length), BF)],
        ),
        out_shape=jax.ShapeDtypeStruct((chunks * rows, width, length), F32),
        compiler_params=pltpu.CompilerParams(vmem_limit_bytes=VMEM_LIMIT),
        cost_estimate=cost(2.0e10),
        name="triangle",
    )(place, *lefts, *[piece for chunk in rights for piece in chunk])


def turn_kernel(half_ref, grad_ref, near_ref, far_ref):
    lanes = near_ref.shape[2]
    for ref, half in ((near_ref, half_ref[0]), (far_ref, 1 - half_ref[0])):
        at = pl.multiple_of(half * lanes, lanes)
        for e in range(ref.shape[0]):
            ref[e] = grad_ref[:, e, pl.ds(at, lanes)].astype(BF)


def turn(half, grad):
    rows, width, length = grad.shape
    some = 16
    low = pl.BlockSpec((some, rows, length // 2), lambda at, half: (at, 0, 0))
    return pl.pallas_call(
        turn_kernel,
        grid_spec=pltpu.PrefetchScalarGridSpec(
            num_scalar_prefetch=1,
            grid=(width // some,),
            in_specs=[pl.BlockSpec((rows, some, length), lambda at, half: (0, at, 0))],
            out_specs=[low, low],
        ),
        out_shape=[jax.ShapeDtypeStruct((width, rows, length // 2), BF)] * 2,
        compiler_params=pltpu.CompilerParams(vmem_limit_bytes=VMEM_LIMIT),
        cost_estimate=cost(5.0e9),
        name="turn",
    )(half, grad)


def right_back_kernel(chunks, pieces, own_ref, *refs):
    grads, refs = refs[: chunks * pieces], refs[chunks * pieces :]
    lefts, refs = refs[: chunks * pieces], refs[chunks * pieces :]
    db_ref, scr = refs
    rows = db_ref.shape[0]
    for e in range(scr.shape[0]):
        grad = jnp.concatenate([ref[e] for ref in grads], axis=0)
        left = jnp.concatenate([ref[e] for ref in lefts], axis=0)
        scr[e] = tn(grad, left)
        db_ref[:, e, :] = scr[e, pl.ds(pl.multiple_of(own_ref[0], rows), rows), :]


def right_back(own, grads, lefts):
    width, rows, length = lefts[0][0].shape
    chunks, pieces = len(lefts), len(lefts[0])
    part = grads[0][0].shape[2]
    some = 8
    low = lambda lanes: pl.BlockSpec((some, rows, lanes), lambda at, own: (at, 0, 0))
    return pl.pallas_call(
        functools.partial(right_back_kernel, chunks, pieces),
        grid_spec=pltpu.PrefetchScalarGridSpec(
            num_scalar_prefetch=1,
            grid=(width // some,),
            in_specs=[low(part)] * (chunks * pieces) + [low(length)] * (chunks * pieces),
            out_specs=pl.BlockSpec((chunks * rows, some, length), lambda at, own: (0, at, 0)),
            scratch_shapes=[pltpu.VMEM((some, part, length), F32)],
        ),
        out_shape=jax.ShapeDtypeStruct((chunks * rows, width, length), F32),
        compiler_params=pltpu.CompilerParams(vmem_limit_bytes=VMEM_LIMIT),
        cost_estimate=cost(2.2e10),
        name="right_back",
    )(own, *[item for chunk in grads for item in chunk], *[item for chunk in lefts for item in chunk])


def left_back_kernel(chunks, pieces, place_ref, *refs):
    grads, refs = refs[: 2 * chunks], refs[2 * chunks :]
    rights, refs = refs[: chunks * pieces], refs[chunks * pieces :]
    da_ref, scr = refs
    rights = [rights[c * pieces : (c + 1) * pieces] for c in range(chunks)]
    for e in range(scr.shape[0]):
        gather_pieces(place_ref, rights, e, scr)
        grad = [jnp.concatenate([grads[c][e], grads[chunks + c][e]], axis=1) for c in range(chunks)]
        da_ref[:, e, :] = nn(jnp.concatenate(grad, axis=0), scr[e])


def left_back(place, nears, fars, rights):
    width, rows, part = nears[0].shape
    chunks, pieces = len(nears), len(rights[0])
    length = 2 * part
    some = 8
    low = lambda lanes: pl.BlockSpec((some, rows, lanes), lambda at, place: (at, 0, 0))
    return pl.pallas_call(
        functools.partial(left_back_kernel, chunks, pieces),
        grid_spec=pltpu.PrefetchScalarGridSpec(
            num_scalar_prefetch=1,
            grid=(width // some,),
            in_specs=[low(part)] * (2 * chunks) + [low(length)] * (chunks * pieces),
            out_specs=pl.BlockSpec((chunks * rows, some, length), lambda at, place: (0, at, 0)),
            scratch_shapes=[pltpu.VMEM((some, length, length), BF)],
        ),
        out_shape=jax.ShapeDtypeStruct((chunks * rows, width, length), F32),
        compiler_params=pltpu.CompilerParams(vmem_limit_bytes=VMEM_LIMIT),
        cost_estimate=cost(2.0e10),
        name="left_back",
    )(place, *nears, *fars, *[piece for chunk in rights for piece in chunk])


def rows_kernel(count, heads, order, first, *refs):
    before = []
    if not first:
        before, refs = refs[:3], refs[4:]
    rows_body(count, heads, order, before, *refs)


def rows_body(
    count,
    heads,
    order,
    before,
    t_ref,
    xt_ref,
    cot_ref,
    bias_ref,
    chain_ref,
    lane_ref,
    vec_ref,
    gate_w_ref,
    gate_wt_ref,
    tri_out_ref,
    tri_out_t_ref,
    att_t_ref,
    att_kv_ref,
    att_ref,
    att_out_ref,
    att_out_t_ref,
    up_ref,
    up_t_ref,
    down_ref,
    down_t_ref,
    out_ref,
    dt_ref,
    z_ref,
    g_ref,
    g_vec_ref,
    g_bias_ref,
    e_scr,
):
    total_rows, width, length = t_ref.shape
    lanes = count * length
    head = width // heads
    scaling = 1.0 / math.sqrt(head)

    sums = (g_ref, g_vec_ref, g_bias_ref)
    place = {}
    for name in ("gate", "tri_out", "query", "key", "value", "gate2", "att_out"):
        place[name] = slice(len(place) * width, (len(place) + 1) * width)
    ups = slice(7 * width, 7 * width + up_ref.shape[1])
    downs = [
        slice(at, at + width) for at in range(ups.stop, ups.stop + up_ref.shape[1], width)
    ]

    @pl.when(pl.program_id(0) == 0)
    def _():
        for n, ref in enumerate(sums):
            ref[...] = before[n][...] if before else jnp.zeros(ref.shape, ref.dtype)

    def vec(at):
        return widen(vec_ref[at], lanes)

    def step(at, carry):
        start = at * count
        x0 = stacked(xt_ref, start, count).astype(F32)
        hat1, scale1 = normalize(x0)
        normed1 = (hat1 * vec(0) + vec(1)).astype(BF)
        gate1 = sigmoid(nn(gate_wt_ref[...], normed1))
        hat_t, scale_t = normalize(stacked(t_ref, start, count))
        mixed = (hat_t * vec(2) + vec(3)).astype(BF)
        branch = nn(tri_out_t_ref[...], mixed)
        x1 = x0 + gate1 * branch
        hat2, scale2 = normalize(x1)
        normed2 = (hat2 * vec(4) + vec(5)).astype(BF)
        hidden = nn(att_t_ref[...], normed2)
        query = (hidden[:width] * (scaling * LOG2E)).astype(BF)
        hidden = hidden.astype(BF)
        key = hidden[width : 2 * width]
        value = hidden[2 * width : 3 * width]
        gate2 = sigmoid(hidden[3 * width :].astype(F32))
        normed2_tok = normed2.T
        kv_tok = nn(normed2_tok, att_kv_ref[...]).astype(BF)
        ones = jnp.ones((16, length), BF)
        pairs = [(n, h) for n in range(count) for h in range(heads)]
        cols = [slice(n * length, (n + 1) * length) for n in range(count)]
        mine = [slice(h * head, (h + 1) * head) for h in range(heads)]
        there = [slice(h * length, (h + 1) * length) for h in range(heads)]

        def scores(n, h):
            return nn(kv_tok[cols[n], :width] * lane_ref[h], query[:, cols[n]])

        outs, inverses = {}, {}

        def mix(n, h):
            both = nn(jnp.concatenate([value[mine[h], cols[n]], ones], axis=0), e_scr[n, :, there[h]])
            inverses[n, h] = 1.0 / both[head : head + 1]
            outs[n, h] = both[:head] * inverses[n, h]

        ahead = scores(*pairs[0])
        for at_pair, (n, h) in enumerate(pairs):
            score = ahead
            if at_pair + 1 < len(pairs):
                ahead = scores(*pairs[at_pair + 1])
            score = score + bias_ref[h]
            peak = jnp.max(score, axis=0, keepdims=True)
            e_scr[n, :, there[h]] = jnp.exp2(score - peak).astype(BF)
            if at_pair:
                mix(*pairs[at_pair - 1])
        mix(*pairs[-1])
        mixed_rows = [
            jnp.concatenate([outs[n, h] for h in range(heads)], axis=0) for n in range(count)
        ]
        attended = jnp.concatenate(mixed_rows, axis=1)
        gated = (gate2 * attended).astype(BF)
        x2 = x1 + nn(att_out_t_ref[...], gated)
        hat3, scale3 = normalize(x2)
        normed3 = (hat3 * vec(6) + vec(7)).astype(BF)
        up = nn(up_t_ref[...], normed3)
        gate3 = sigmoid(up)
        act = (up * gate3).astype(BF)
        out = (x2 + nn(down_t_ref[...], act)).astype(BF)
        for n in range(count):
            store_tokens(out_ref, start + n, order, out[:, n * length : (n + 1) * length].T.astype(F32))

        cot_tok = [load_tokens(cot_ref, start + n, order).astype(BF) for n in range(count)]
        cot_low = jnp.concatenate([item.T for item in cot_tok], axis=1)
        cot = cot_low.astype(F32)
        grad_down = nn(act, jnp.concatenate(cot_tok, axis=0))
        for n, part in enumerate(downs):
            g_ref[:, part] += grad_down[n * width : (n + 1) * width]
        grad_up = (nn(down_ref[...], cot_low) * (gate3 * (1.0 + up * (1.0 - gate3)))).astype(BF)
        g_ref[:, ups] += nt(normed3, grad_up)
        grad3 = nn(up_ref[...], grad_up)
        g_vec_ref[6] += fold(grad3 * hat3)
        g_vec_ref[7] += fold(grad3)
        grad_x2 = cot + normalize_back(grad3, vec(6), hat3, scale3)
        grad_x2_low = grad_x2.astype(BF)
        g_ref[:, place["att_out"]] += nt(gated, grad_x2_low)
        grad_gated = nn(att_out_ref[...], grad_x2_low)
        grad_mixed = grad_gated * gate2
        grad_gate2 = (grad_gated * attended * gate2 * (1.0 - gate2)).astype(BF)

        grad_outs, products = [], []
        for n in range(count):
            scaled = [grad_mixed[mine[h], cols[n]] * inverses[n, h] for h in range(heads)]
            grad_out = jnp.concatenate(scaled, axis=0).astype(BF)
            grad_outs.append(grad_out)
            products.append(grad_out.astype(F32) * mixed_rows[n])
        grad_queries, grad_keys, grad_values = {}, {}, {}

        def probs(n, h):
            return nn(kv_tok[cols[n], width:] * lane_ref[h], grad_outs[n])

        def spread(n, h, grad_score):
            both = nn(jnp.concatenate([key[mine[h], cols[n]], chain_ref[...]], axis=0), grad_score)
            grad_queries[n, h] = (both[:head] * scaling).astype(BF)
            g_bias_ref[h] += both[head:]
            grad_keys[n, h] = (nt(query[mine[h], cols[n]], grad_score) * LN2).astype(BF)

        ahead, behind = probs(*pairs[0]), None
        for at_pair, (n, h) in enumerate(pairs):
            grad_prob = ahead
            if at_pair + 1 < len(pairs):
                ahead = probs(*pairs[at_pair + 1])
            center = jnp.sum(products[n][mine[h]], axis=0, keepdims=True)
            expon = e_scr[n, :, there[h]]
            grad_score = (expon.astype(F32) * (grad_prob - center)).astype(BF)
            grad_values[n, h] = nt(grad_outs[n][mine[h]], expon).astype(BF)
            if behind is not None:
                spread(*behind)
            behind = (n, h, grad_score)
        spread(*behind)

        def whole(parts):
            by_row = [
                jnp.concatenate([parts[n, h] for h in range(heads)], axis=0) for n in range(count)
            ]
            return jnp.concatenate(by_row, axis=1)

        grad_hidden = jnp.concatenate(
            [whole(grad_queries), whole(grad_keys), whole(grad_values), grad_gate2], axis=0
        )
        g_ref[:, place["query"].start : place["gate2"].stop] += nt(normed2, grad_hidden)
        grad2 = nn(att_ref[...], grad_hidden)
        g_vec_ref[4] += fold(grad2 * hat2)
        g_vec_ref[5] += fold(grad2)
        grad_x1 = grad_x2 + normalize_back(grad2, vec(4), hat2, scale2)
        grad_branch = (grad_x1 * gate1).astype(BF)
        g_ref[:, place["tri_out"]] += nt(mixed, grad_branch)
        grad_mix = nn(tri_out_ref[...], grad_branch)
        g_vec_ref[2] += fold(grad_mix * hat_t)
        g_vec_ref[3] += fold(grad_mix)
        spread_out(dt_ref, start, count, normalize_back(grad_mix, vec(2), hat_t, scale_t))
        grad_gate1 = (grad_x1 * branch * gate1 * (1.0 - gate1)).astype(BF)
        g_ref[:, place["gate"]] += nt(normed1, grad_gate1)
        grad1 = nn(gate_w_ref[...], grad_gate1)
        g_vec_ref[0] += fold(grad1 * hat1)
        g_vec_ref[1] += fold(grad1)
        spread_out(z_ref, start, count, grad_x1 + normalize_back(grad1, vec(0), hat1, scale1))
        return carry

    lax.fori_loop(0, total_rows // count, step, 0)


def rows_pass(c, chunks, before, t, xt, cot_rows, order, bias, chain, lane, vecs, weights, heads):
    _, width, length = t.shape
    blocks, pieces, sub, tokens, _ = cot_rows.shape
    rows = blocks * sub
    some, count = 4, 4
    inner = sub // some
    full = lambda item: pl.BlockSpec(item.shape, lambda at: (0,) * item.ndim)
    by_row = pl.BlockSpec((some, width, length), lambda at: (at, 0, 0))
    of_all = pl.BlockSpec((some, width, length), lambda at: (c * (rows // some) + at, 0, 0))
    by_piece = pl.BlockSpec(
        (1, pieces, some, tokens, width), lambda at: (at // inner, 0, at % inner, 0, 0)
    )
    consts = (bias, chain, lane, vecs) + weights
    wide = weights[-1].shape[1]
    sum_shapes = [
        jax.ShapeDtypeStruct(shape, F32)
        for shape in ((width, 7 * width + 2 * wide), (8, width, 128), (heads, 16, length))
    ]
    before_specs = [full(item) for item in before[:3]]
    before_specs += [pl.BlockSpec(memory_space=pl.ANY)] * len(before[3:])
    return pl.pallas_call(
        functools.partial(rows_kernel, count, heads, order, c == 0),
        grid=(rows // some,),
        in_specs=before_specs + [of_all, of_all, by_piece] + [full(item) for item in consts],
        out_specs=[by_piece, by_row, of_all] + [full(item) for item in sum_shapes],
        out_shape=[
            jax.ShapeDtypeStruct(cot_rows.shape, BF),
            jax.ShapeDtypeStruct((rows, width, length), F32),
            jax.ShapeDtypeStruct(t.shape, F32),
        ]
        + sum_shapes,
        input_output_aliases={3: 2} if before else {},
        scratch_shapes=[
            pltpu.VMEM((count, length, heads * length), BF),
        ],
        compiler_params=pltpu.CompilerParams(vmem_limit_bytes=VMEM_LIMIT),
        cost_estimate=cost(1.2e11),
        name="rows",
    )(*before, t, xt, cot_rows, *consts)


def edges_back_kernel(
    order, xt_ref, z_ref, da_ref, db_ref, wt_ref, w_ref, gain_ref, shift_ref, out_ref, g_w_ref, g_vec_ref
):
    rows, width, length = xt_ref.shape
    count = 4

    @pl.when(pl.program_id(0) == 0)
    def _():
        g_w_ref[...] = jnp.zeros(g_w_ref.shape, F32)
        g_vec_ref[...] = jnp.zeros(g_vec_ref.shape, F32)

    def step(at, carry):
        start = at * count
        x0 = stacked(xt_ref, start, count).astype(F32)
        lanes = x0.shape[1]
        gain = widen(gain_ref[...], lanes)
        hat, scale = normalize(x0)
        normed = (hat * gain + widen(shift_ref[...], lanes)).astype(BF)
        proj = nn(wt_ref[...], normed)
        pa, pag = proj[:width], proj[width : 2 * width]
        pb, pbg = proj[2 * width : 3 * width], proj[3 * width :]
        da = stacked(da_ref, start, count)
        db = stacked(db_ref, start, count)
        sa, sb = sigmoid(pag), sigmoid(pbg)
        dsa, dsb = da * sa, db * sb
        grads = jnp.concatenate(
            [
                dsa.astype(BF),
                (dsa * pa * (1.0 - sa)).astype(BF),
                dsb.astype(BF),
                (dsb * pb * (1.0 - sb)).astype(BF),
            ],
            axis=0,
        )
        g_w_ref[...] += nt(normed, grads)
        grad = nn(w_ref[...], grads)
        g_vec_ref[0] += fold(grad * hat)
        g_vec_ref[1] += fold(grad)
        out = stacked(z_ref, start, count) + normalize_back(grad, gain, hat, scale)
        out = out.astype(BF)
        for n in range(count):
            store_tokens(out_ref, start + n, order, out[:, n * length : (n + 1) * length].T.astype(F32))
        return carry

    lax.fori_loop(0, rows // count, step, 0)


def edges_back(xt, z, da, db, order, weight_t, weight, gain, shift, shape):
    rows, width, length = xt.shape
    blocks, pieces, sub, tokens, _ = shape
    chunks = order[2]
    some = sub // chunks
    step = 16 // some
    inner = blocks // step
    full = lambda item: pl.BlockSpec(item.shape, lambda at: (0,) * item.ndim)
    by_row = pl.BlockSpec((16, width, length), lambda at: (at, 0, 0))
    sum_shapes = [
        jax.ShapeDtypeStruct(weight.shape, F32),
        jax.ShapeDtypeStruct((2, width, 128), F32),
    ]
    by_piece = pl.BlockSpec(
        (step, pieces, some, tokens, width), lambda at: (at % inner, 0, at // inner, 0, 0)
    )
    return pl.pallas_call(
        functools.partial(edges_back_kernel, order),
        grid=(chunks * inner,),
        in_specs=[by_row] * 4 + [full(item) for item in (weight_t, weight, gain, shift)],
        out_specs=[by_piece] + [full(item) for item in sum_shapes],
        out_shape=[jax.ShapeDtypeStruct(shape, BF)] + sum_shapes,
        compiler_params=pltpu.CompilerParams(vmem_limit_bytes=VMEM_LIMIT),
        cost_estimate=cost(4.0e10),
        name="edges_back",
    )(xt, z, da, db, weight_t, weight, gain, shift)


def shards(
    row_size,
    col_size,
    pair_state,
    cotangent,
    chain_lengths,
    tri_gain,
    tri_shift,
    tri_weight,
    mix_gain,
    mix_shift,
    tri_out,
    att_gain,
    att_shift,
    att_weight,
    chain_bias,
    att_out,
    trans_gain,
    trans_shift,
    up_weight,
    down_weight,
):
    heads = HEADS
    crops, own_rows, tokens, width = pair_state.shape
    length = col_size * tokens
    chunks = CHUNKS
    some = own_rows // (col_size * chunks)
    axes = ("row", "col")
    group = row_size * col_size
    order = (row_size, col_size, chunks)
    shape = (row_size, col_size, some, tokens, width)

    def swap(values):
        return lax.all_to_all(values, axes, split_axis=0, concat_axis=0, tiled=True)

    def cut(values):
        parts = values.reshape(group, chunks, some, tokens, width)
        return [parts[:, c] for c in range(chunks)]

    def join(parts):
        return jnp.stack(parts, axis=1).reshape(crops, own_rows, tokens, width)

    def across(values, bit):
        return lax.ppermute(values, "col", [(q, q ^ bit) for q in range(col_size)])

    bits = [1 << n for n in range(col_size.bit_length() - 1)]

    def after(values, *others):
        return lax.optimization_barrier((values,) + others)[0]

    def gather(own, far, *late):
        pieces = {0: own, far_bit: across(far, far_bit)}
        arrived = pieces[far_bit]
        if late:
            pieces[far_bit] = after(arrived, *late)
        for bit in reversed(bits[:-1]):
            for m in list(pieces):
                pieces[m ^ bit] = across(pieces[m], bit)
        return [pieces[m] for m in range(col_size)], arrived

    def doubled(items, axis, size, bits):
        for bit in bits:
            lows = [values.astype(sent) for values, sent in items]
            others = [lax.ppermute(low, axis, [(q, q ^ bit) for q in range(size)]) for low in lows]
            others = lax.optimization_barrier(tuple(others))
            items = [
                (low.astype(F32) + other.astype(F32), sent)
                for low, other, (_, sent) in zip(lows, others, items)
            ]
        return items

    x_rows = [swap(part).reshape(shape) for part in cut(pair_state)]
    cot_parts = cut(cotangent)

    wide = lambda item: jnp.broadcast_to(item[:, None], (width, 128))
    vecs = jnp.stack(
        [
            wide(item)
            for item in (
                tri_gain,
                tri_shift,
                mix_gain,
                mix_shift,
                att_gain,
                att_shift,
                trans_gain,
                trans_shift,
            )
        ]
    )
    edge_w = tri_weight[:, : 4 * width]
    edge_wt = edge_w.T
    gate_w = tri_weight[:, 4 * width :]
    lengths = lax.dynamic_index_in_dim(chain_lengths, lax.axis_index("row"), 0, keepdims=False)
    ends = jnp.cumsum(lengths)
    places = jnp.arange(length, dtype=jnp.int32)
    places = places.reshape(order + (some,)).transpose(1, 2, 0, 3).reshape(length)
    chain = jnp.sum((places[:, None] >= ends[None, :]).astype(jnp.int32), axis=-1)
    same = (chain[:, None] == chain[None, :]).astype(F32)
    bias = (LOG2E * chain_bias)[:, None, None] * same[None]
    which = (jnp.arange(16, dtype=jnp.int32)[:, None] == chain[None, :]).astype(F32)
    head_of = jnp.arange(width, dtype=jnp.int32) // (width // heads)
    lane = (jnp.arange(heads, dtype=jnp.int32)[:, None] == head_of[None, :]).astype(BF)
    lane = jnp.broadcast_to(lane[:, None, :], (heads, length, width))
    me = lax.axis_index("col")
    flips = jnp.arange(col_size, dtype=jnp.int32)
    own = own_rows
    far_bit = col_size // 2
    inside = (me ^ flips) & (far_bit - 1)
    place = (me ^ flips) * own
    place_near = (inside + (flips & far_bit)) * own
    half = (me // far_bit).reshape(1)

    cot_rows = []
    lefts, rights, xt, arrived = [], [], [], []
    for c in range(chunks):
        left, right, *xt = edges(c, chunks, x_rows[c], xt, order, edge_wt, vecs[0], vecs[1])
        if arrived:
            right = after(right, arrived[-1], cot_rows[0])
        pieces, there = gather(right, right)
        lefts.append(left)
        rights.append(pieces)
        arrived.append(there)
        if c == 0:
            cot_rows.append(swap(after(cot_parts[0], left, *x_rows)).reshape(shape))
    (xt,) = xt
    t = triangle(place, lefts, rights)
    for part in cot_parts[1:]:
        cot_rows.append(swap(after(part, t, cot_rows[-1])).reshape(shape))
    weights = (
        gate_w,
        gate_w.T,
        tri_out,
        tri_out.T,
        att_weight.T,
        att_weight[:, width : 3 * width],
        att_weight,
        att_out,
        att_out.T,
        up_weight,
        up_weight.T,
        down_weight,
        down_weight.T,
    )
    chain_rows = which.astype(BF)
    state, outs, dts = [], [], []
    lefts_all, grads, nears, fars = [], [], [], []
    for c in range(chunks):
        out, dt, z, *sums = rows_pass(
            c, chunks, state, t, xt, cot_rows[c], order, bias, chain_rows, lane, vecs, weights, heads
        )
        state = sums + [z]
        if outs:
            dt = after(dt, outs[-1])
        near, far = turn(half, dt)
        nears.append(near)
        fars.append(far)
        if c < chunks - 1:
            outs.append(swap(out.reshape(group, some, tokens, width)))
    g_rows, g_vec, g_bias = sums
    row_bits = [1 << n for n in range(row_size.bit_length() - 1)]
    ((g_rows, _),) = doubled([(g_rows, BF)], "row", row_size, row_bits)
    da = left_back(place_near, nears[:-1] + [after(nears[-1], g_rows)], fars, rights)
    for left in lefts:
        held = after(left, t)
        lefts_all.append(gather(held, held, z)[0])
    for c in range(chunks):
        pieces, last = gather(nears[c], fars[c], z if c < chunks - 1 else da)
        grads.append(pieces)
    outs.append(swap(after(out, last).reshape(group, some, tokens, width)))
    pair_out = join(outs)
    db = right_back(inside[:1] * own, grads, lefts_all)
    whole = (row_size, col_size, some * chunks, tokens, width)
    back, g_edge, g_vec_edge = edges_back(
        xt, z, da, db, order, edge_wt, edge_w, vecs[0], vecs[1], whole
    )
    grad_pair = swap(back.reshape(group, some * chunks, tokens, width))
    grad_pair = grad_pair.reshape(crops, own_rows, tokens, width)

    g_vec = jnp.sum(g_vec, axis=-1)
    g_vec_edge = jnp.sum(g_vec_edge, axis=-1)
    g_chain = jnp.sum(g_bias * which[None], axis=(1, 2))
    small = jnp.concatenate(
        [g_vec[:2] + g_vec_edge, g_vec[2:], jnp.pad(g_chain, (0, width - heads))[None]], axis=0
    )
    items = [(after(g_edge, pair_out), BF), (small, F32)]
    items = doubled(items, "row", row_size, row_bits)
    items = doubled(items + [(g_rows, BF)], "col", col_size, bits[::-1])
    t_edge, small, total = [values for values, _ in items]
    column = lambda at, n=1: total[:, at * width : (at + n) * width]
    ff = up_weight.shape[1] // width
    t_gate, t_tri_out, t_att = column(0), column(1), column(2, 4)
    t_att_out, t_up = column(6), column(7, ff)
    t_down = jnp.concatenate([column(7 + ff + n) for n in range(ff)], axis=0)
    return (
        pair_out,
        grad_pair,
        small[0],
        small[1],
        jnp.concatenate([t_edge, t_gate], axis=1),
        small[2],
        small[3],
        t_tri_out,
        small[4],
        small[5],
        t_att,
        small[8, :heads],
        t_att_out,
        small[6],
        small[7],
        t_up,
        t_down,
    )


def solution(mesh):
    pair = P("dp", "row", "col", None)
    vector, matrix = P("dp"), P("dp", None)
    return jax.shard_map(
        functools.partial(shards, mesh.shape["row"], mesh.shape["col"]),
        mesh=mesh,
        in_specs=(pair, pair, P("dp", None)) + (P(),) * 15,
        out_specs=(
            pair,
            pair,
            vector,
            vector,
            matrix,
            vector,
            vector,
            matrix,
            vector,
            vector,
            matrix,
            vector,
            matrix,
            vector,
            vector,
            matrix,
            matrix,
        ),
        check_vma=False,
    )
```

```python
import functools
import math

import jax
import jax.numpy as jnp
from jax import lax
from jax.experimental import pallas as pl
from jax.experimental.pallas import tpu as pltpu
from jax.sharding import PartitionSpec as P

HEADS = 4
EPS = 1e-05
LOG2E = math.log2(math.e)
LN2 = math.log(2.0)
CHUNKS = 2
VMEM_LIMIT = 56 * 1024 * 1024
BF = jnp.bfloat16
F32 = jnp.float32


def nn(left, right):
    return lax.dot_general(left, right, (((1,), (0,)), ((), ())), preferred_element_type=F32)


def nt(left, right):
    return lax.dot_general(left, right, (((1,), (1,)), ((), ())), preferred_element_type=F32)


def tn(left, right):
    return lax.dot_general(left, right, (((0,), (0,)), ((), ())), preferred_element_type=F32)


def cost(flops, size=0):
    return pl.CostEstimate(flops=int(flops), bytes_accessed=int(size), transcendentals=0)


def sigmoid(values):
    return 0.5 * jnp.tanh(0.5 * values) + 0.5


def normalize(values):
    center = values - jnp.mean(values, axis=0, keepdims=True)
    spread = jnp.mean(center * center, axis=0, keepdims=True)
    scale = lax.rsqrt(spread + EPS)
    return center * scale, scale


def normalize_back(grads, gain, hat, scale):
    grad_hat = grads * gain
    first = jnp.mean(grad_hat, axis=0, keepdims=True)
    second = jnp.mean(grad_hat * hat, axis=0, keepdims=True)
    return scale * (grad_hat - first - hat * second)


def widen(column, lanes):
    return jnp.concatenate([column] * (lanes // column.shape[1]), axis=1)


def fold(values):
    parts = [values[:, at : at + 128] for at in range(0, values.shape[1], 128)]
    return functools.reduce(lambda one, two: one + two, parts)


def load_tokens(ref, row, order):
    _, pieces, some, tokens, width = ref.shape
    flat = ref[row // some, :, row % some, :, :].astype(F32)
    flat = flat.reshape(order + (flat.shape[0] * tokens // math.prod(order), width))
    return flat.transpose(1, 2, 0, 3, 4).reshape(pieces * tokens, width)


def store_tokens(ref, row, order, values):
    _, pieces, some, tokens, width = ref.shape
    back = (order[1], order[2], order[0])
    flat = values.reshape(back + (pieces * tokens // math.prod(order), width))
    flat = flat.transpose(2, 0, 1, 3, 4).reshape(pieces, tokens, width)
    ref[row // some, :, row % some, :, :] = flat.astype(ref.dtype)


def stacked(ref, start, count):
    return jnp.concatenate([ref[start + n] for n in range(count)], axis=1)


def spread_out(ref, start, count, values):
    length = values.shape[1] // count
    for n in range(count):
        ref[start + n] = values[:, n * length : (n + 1) * length].astype(ref.dtype)


def edges_kernel(order, x_ref, w_ref, gain_ref, shift_ref, *refs):
    a_ref, b_ref, xt_ref, a_scr, b_scr = refs[-5:]
    rows, width, length = xt_ref.shape
    count = 4

    def step(at, carry):
        start = at * count
        tokens = [load_tokens(x_ref, start + n, order).astype(BF) for n in range(count)]
        x0 = jnp.concatenate([item.T for item in tokens], axis=1)
        spread_out(xt_ref, start, count, x0)
        hat, _ = normalize(x0.astype(F32))
        lanes = x0.shape[1]
        normed = (hat * widen(gain_ref[...], lanes) + widen(shift_ref[...], lanes)).astype(BF)
        proj = nn(w_ref[...], normed)
        left = sigmoid(proj[width : 2 * width]) * proj[:width]
        right = sigmoid(proj[3 * width : 4 * width]) * proj[2 * width : 3 * width]
        for n in range(count):
            base = pl.multiple_of((start + n) * width, width)
            for half in range(length // 128):
                part = slice(n * length + half * 128, n * length + half * 128 + 128)
                a_scr[half, pl.ds(base, width), :] = left[:, part]
                b_scr[half, pl.ds(base, width), :] = right[:, part]
        return carry

    lax.fori_loop(0, rows // count, step, 0)

    def turn(at, carry):
        for n in range(8):
            e = at * 8 + n
            for scr, out in ((a_scr, a_ref), (b_scr, b_ref)):
                halves = [scr[h, pl.ds(e, rows, stride=width), :] for h in range(scr.shape[0])]
                out[e] = jnp.concatenate(halves, axis=1).astype(BF)
        return carry

    lax.fori_loop(0, width // 8, turn, 0)


def edges(c, x_rows, before, order, weight, gain, shift):
    blocks, pieces, sub, tokens, width = x_rows.shape
    length = pieces * tokens
    chunks = order[2]
    some = sub // chunks
    rows = blocks * some
    step = 16 // some
    const = lambda at: (0, 0)
    return pl.pallas_call(
        functools.partial(edges_kernel, order),
        grid=(blocks // step,),
        in_specs=[
            pl.BlockSpec((step, pieces, some, tokens, width), lambda at: (at, 0, c, 0, 0)),
            pl.BlockSpec(weight.shape, const),
            pl.BlockSpec(gain.shape, const),
            pl.BlockSpec(shift.shape, const),
        ]
        + [pl.BlockSpec(memory_space=pl.ANY)] * len(before),
        out_specs=[
            pl.BlockSpec((width, 16, length), lambda at: (0, at, 0)),
            pl.BlockSpec((width, 16, length), lambda at: (0, at, 0)),
            pl.BlockSpec((16, width, length), lambda at: (c * (blocks // step) + at, 0, 0)),
        ],
        out_shape=[
            jax.ShapeDtypeStruct((width, rows, length), BF),
            jax.ShapeDtypeStruct((width, rows, length), BF),
            jax.ShapeDtypeStruct((chunks * rows, width, length), BF),
        ],
        input_output_aliases={4: 2} if before else {},
        scratch_shapes=[
            pltpu.VMEM((length // 128, 16 * width, 128), F32),
            pltpu.VMEM((length // 128, 16 * width, 128), F32),
        ],
        compiler_params=pltpu.CompilerParams(vmem_limit_bytes=VMEM_LIMIT),
        cost_estimate=cost(1.7e10),
        name="edges",
    )(x_rows, weight, gain, shift, *before)


def gather_pieces(place_ref, chunks, e, scr):
    for c, pieces in enumerate(chunks):
        rows = pieces[0].shape[1]
        for m, piece in enumerate(pieces):
            scr[e, pl.ds(pl.multiple_of(c * rows + place_ref[m], rows), rows), :] = piece[e]


def by_channel(ref):
    halves, rows, some, lanes = ref.shape
    return ref.reshape(halves, rows * some, lanes)


def put_channel(ref, e, values):
    halves, rows, some, lanes = ref.shape
    flat = by_channel(ref)
    for half in range(halves):
        flat[half, pl.ds(e, rows, stride=some), :] = values[:, half * lanes : (half + 1) * lanes]


def ahead(first, count, begin, end):
    coming = begin(first)
    for e in range(first, first + count):
        here = coming
        if e + 1 < first + count:
            coming = begin(e + 1)
        end(e, here)


SOME = 16


def triangle_kernel(chunks, pieces, place_ref, *refs):
    lefts, refs = refs[:chunks], refs[chunks:]
    rights, refs = refs[: chunks * pieces], refs[chunks * pieces :]
    t_ref, scr = refs
    rights = [rights[c * pieces : (c + 1) * pieces] for c in range(chunks)]

    def begin(e):
        gather_pieces(place_ref, rights, e, scr)
        return nt(jnp.concatenate([left[e] for left in lefts], axis=0), scr[e])

    ahead(0, SOME, begin, functools.partial(put_channel, t_ref))


def high_spec(rows, length):
    return pl.BlockSpec((length // 128, rows, SOME, 128), lambda at, place: (0, 0, at, 0))


def low_spec(rows, lanes):
    return pl.BlockSpec((SOME, rows, lanes), lambda at, place: (at, 0, 0))


def by_halves(rows, width, length):
    return jax.ShapeDtypeStruct((length // 128, rows, width, 128), F32)


def channel_call(kernel, name, flops, scalar, ins, in_specs, out_specs, out_shape, scratch=()):
    return pl.pallas_call(
        kernel,
        grid_spec=pltpu.PrefetchScalarGridSpec(
            num_scalar_prefetch=1,
            grid=(ins[0].shape[0 if ins[0].ndim == 3 else 2] // SOME,),
            in_specs=in_specs,
            out_specs=out_specs,
            scratch_shapes=scratch,
        ),
        out_shape=out_shape,
        compiler_params=pltpu.CompilerParams(vmem_limit_bytes=VMEM_LIMIT),
        cost_estimate=cost(flops),
        name=name,
    )(scalar, *ins)


def triangle(place, lefts, rights):
    width, rows, length = lefts[0].shape
    chunks, pieces = len(lefts), len(rights[0])
    return channel_call(
        functools.partial(triangle_kernel, chunks, pieces),
        "triangle",
        2.0e10,
        place,
        (*lefts, *[piece for chunk in rights for piece in chunk]),
        [low_spec(rows, length)] * (chunks + chunks * pieces),
        high_spec(chunks * rows, length),
        by_halves(chunks * rows, width, length),
        [pltpu.VMEM((SOME, length, length), BF)],
    )


def turn_kernel(half_ref, grad_ref, near_ref, far_ref):
    _, rows, some, _ = grad_ref.shape
    flat = by_channel(grad_ref)
    for e in range(some):
        for ref, half in ((near_ref, half_ref[0]), (far_ref, 1 - half_ref[0])):
            ref[e] = flat[half, pl.ds(e, rows, stride=some), :].astype(BF)


def turn(half, grad):
    halves, rows, width, lanes = grad.shape
    return channel_call(
        turn_kernel,
        "turn",
        5.0e9,
        half,
        (grad,),
        [high_spec(rows, halves * lanes)],
        [low_spec(rows, lanes)] * 2,
        [jax.ShapeDtypeStruct((width, rows, lanes), BF)] * 2,
    )


def right_back_kernel(chunks, pieces, own_ref, *refs):
    grads, refs = refs[: chunks * pieces], refs[chunks * pieces :]
    lefts, refs = refs[: chunks * pieces], refs[chunks * pieces :]
    db_ref, scr = refs
    rows = db_ref.shape[1]

    def begin(e):
        grad = jnp.concatenate([ref[e] for ref in grads], axis=0)
        return tn(grad, jnp.concatenate([ref[e] for ref in lefts], axis=0))

    def end(e, db):
        scr[e] = db
        put_channel(db_ref, e, scr[e, pl.ds(pl.multiple_of(own_ref[0], rows), rows), :])

    ahead(0, SOME, begin, end)


def right_back(own, grads, lefts):
    width, rows, length = lefts[0][0].shape
    chunks, pieces = len(lefts), len(lefts[0])
    part = grads[0][0].shape[2]
    return channel_call(
        functools.partial(right_back_kernel, chunks, pieces),
        "right_back",
        2.2e10,
        own,
        [item for chunk in grads for item in chunk] + [item for chunk in lefts for item in chunk],
        [low_spec(rows, part)] * (chunks * pieces) + [low_spec(rows, length)] * (chunks * pieces),
        high_spec(chunks * rows, length),
        by_halves(chunks * rows, width, length),
        [pltpu.VMEM((SOME, part, length), F32)],
    )


def left_back_kernel(chunks, pieces, place_ref, *refs):
    grads, refs = refs[: 2 * chunks], refs[2 * chunks :]
    rights, refs = refs[: chunks * pieces], refs[chunks * pieces :]
    da_ref, scr = refs
    rights = [rights[c * pieces : (c + 1) * pieces] for c in range(chunks)]

    def begin(e):
        gather_pieces(place_ref, rights, e, scr)
        grad = [jnp.concatenate([grads[c][e], grads[chunks + c][e]], axis=1) for c in range(chunks)]
        return nn(jnp.concatenate(grad, axis=0), scr[e])

    ahead(0, SOME, begin, functools.partial(put_channel, da_ref))


def left_back(place, nears, fars, rights):
    width, rows, part = nears[0].shape
    chunks, pieces = len(nears), len(rights[0])
    length = 2 * part
    return channel_call(
        functools.partial(left_back_kernel, chunks, pieces),
        "left_back",
        2.0e10,
        place,
        (*nears, *fars, *[piece for chunk in rights for piece in chunk]),
        [low_spec(rows, part)] * (2 * chunks) + [low_spec(rows, length)] * (chunks * pieces),
        high_spec(chunks * rows, length),
        by_halves(chunks * rows, width, length),
        [pltpu.VMEM((SOME, length, length), BF)],
    )


def rows_kernel(count, heads, order, first, *refs):
    before = []
    if not first:
        before, refs = refs[:3], refs[4:]
    rows_body(count, heads, order, before, *refs)


def rows_body(
    count,
    heads,
    order,
    before,
    t_ref,
    xt_ref,
    cot_ref,
    bias_ref,
    chain_ref,
    lane_ref,
    vec_ref,
    gate_w_ref,
    gate_wt_ref,
    tri_out_ref,
    tri_out_t_ref,
    att_t_ref,
    att_kv_ref,
    att_ref,
    att_out_ref,
    att_out_t_ref,
    up_ref,
    up_t_ref,
    down_ref,
    down_t_ref,
    out_ref,
    dt_ref,
    z_ref,
    g_ref,
    g_vec_ref,
    g_bias_ref,
    e_scr,
):
    total_rows, width, length = xt_ref.shape
    head = width // heads
    scaling = 1.0 / math.sqrt(head)

    sums = (g_ref, g_vec_ref, g_bias_ref)
    place = {}
    for name in ("gate", "tri_out", "query", "key", "value", "gate2", "att_out"):
        place[name] = slice(len(place) * width, (len(place) + 1) * width)
    ups = slice(7 * width, 7 * width + up_ref.shape[1])
    downs = [
        slice(at, at + width) for at in range(ups.stop, ups.stop + up_ref.shape[1], width)
    ]

    @pl.when(pl.program_id(0) == 0)
    def _():
        for n, ref in enumerate(sums):
            ref[...] = before[n][...] if before else jnp.zeros(ref.shape, ref.dtype)

    per = length // 128
    mine = [slice(h * head, (h + 1) * head) for h in range(heads)]
    there = [slice(h * length, (h + 1) * length) for h in range(heads)]
    ones = jnp.ones((16, length), BF)
    parts = [slice(p * 128, (p + 1) * 128) for p in range(per)]

    def tiles(n, function, *items):
        results = [function(p, *[item[:, parts[p]] for item in items]) for p in range(per)]
        return [jnp.concatenate(list(column), axis=1) for column in zip(*results)]

    def step(at, carry):
        start = at * count
        rows = range(count)
        side = lambda items: jnp.concatenate(items, axis=1)
        x0, hat1, scale1, normed1, gate_raw = {}, {}, {}, {}, {}
        hat_t, scale_t, mixed, branch = {}, {}, {}, {}
        for n in rows:

            def first(p):
                tile = xt_ref[start + n, :, parts[p]].astype(F32)
                hat, scale = normalize(tile)
                return tile, hat, scale, (hat * vec_ref[0] + vec_ref[1]).astype(BF)

            x0[n], hat1[n], scale1[n], normed1[n] = tiles(n, first)
            gate_raw[n] = nn(gate_wt_ref[...], normed1[n])

            def second(p):
                hat, scale = normalize(t_ref[p, start + n])
                return hat, scale, (hat * vec_ref[2] + vec_ref[3]).astype(BF)

            hat_t[n], scale_t[n], mixed[n] = tiles(n, second)
            branch[n] = nn(tri_out_t_ref[...], mixed[n])

        gate1, x1, hat2, scale2, normed2, hidden, kv_tok = {}, {}, {}, {}, {}, {}, {}
        for n in rows:

            def join(p, before, raw, add):
                gate = sigmoid(raw)
                after = before + gate * add
                hat, scale = normalize(after)
                return gate, after, hat, scale, (hat * vec_ref[4] + vec_ref[5]).astype(BF)

            gate1[n], x1[n], hat2[n], scale2[n], normed2[n] = tiles(
                n, join, x0[n], gate_raw[n], branch[n]
            )
            hidden[n] = nn(att_t_ref[...], normed2[n])
            kv_tok[n] = nn(normed2[n].T, att_kv_ref[...])

        query, key, value, gate2 = {}, {}, {}, {}
        for n in rows:

            def split(p, tile):
                gate = sigmoid(tile[3 * width :].astype(BF).astype(F32))
                asked = (tile[:width] * (scaling * LOG2E)).astype(BF)
                return asked, tile[width : 2 * width].astype(BF), tile[2 * width : 3 * width].astype(BF), gate

            query[n], key[n], value[n], gate2[n] = tiles(n, split, hidden[n])
            kv_tok[n] = kv_tok[n].astype(BF)

        pairs = [(n, h) for n in rows for h in range(heads)]

        def scores(n, h):
            return nn(kv_tok[n][:, :width] * lane_ref[h], query[n])

        outs, inverses = {}, {}

        def mix(n, h):
            both = nn(jnp.concatenate([value[n][mine[h]], ones], axis=0), e_scr[n, :, there[h]])
            inverses[n, h] = 1.0 / both[head : head + 1]
            outs[n, h] = both[:head] * inverses[n, h]

        coming = scores(*pairs[0])
        for at_pair, (n, h) in enumerate(pairs):
            score = coming
            if at_pair + 1 < len(pairs):
                coming = scores(*pairs[at_pair + 1])
            score = score + bias_ref[h]
            peak = jnp.max(score, axis=0, keepdims=True)
            e_scr[n, :, there[h]] = jnp.exp2(score - peak).astype(BF)
            if at_pair:
                mix(*pairs[at_pair - 1])
        mix(*pairs[-1])

        attended, gated, x2 = {}, {}, {}
        for n in rows:
            attended[n] = jnp.concatenate([outs[n, h] for h in range(heads)], axis=0)
            (gated[n],) = tiles(n, lambda p, gate, out: ((gate * out).astype(BF),), gate2[n], attended[n])
            x2[n] = nn(att_out_t_ref[...], gated[n])
        hat3, scale3, normed3, up, cot_tok, cot_low, grad_act = {}, {}, {}, {}, {}, {}, {}
        for n in rows:

            def third(p, before, add):
                after = before + add
                hat, scale = normalize(after)
                return after, hat, scale, (hat * vec_ref[6] + vec_ref[7]).astype(BF)

            x2[n], hat3[n], scale3[n], normed3[n] = tiles(n, third, x1[n], x2[n])
            up[n] = nn(up_t_ref[...], normed3[n])
            cot_tok[n] = load_tokens(cot_ref, start + n, order).astype(BF)
            cot_low[n] = cot_tok[n].T
            grad_act[n] = nn(down_ref[...], cot_low[n])
        act, down, grad_up, grad3 = {}, {}, {}, {}
        for n in rows:

            def silu(p, raw, grad):
                gate = sigmoid(raw)
                return (raw * gate).astype(BF), (grad * (gate * (1.0 + raw * (1.0 - gate)))).astype(BF)

            act[n], grad_up[n] = tiles(n, silu, up[n], grad_act[n])
            down[n] = nn(down_t_ref[...], act[n])
            grad3[n] = nn(up_ref[...], grad_up[n])
        grad = nn(side([act[n] for n in rows]), jnp.concatenate([cot_tok[n] for n in rows], axis=0))
        for n, part in enumerate(downs):
            g_ref[:, part] += grad[n * width : (n + 1) * width]
        g_ref[:, ups] += nt(side([normed3[n] for n in rows]), side([grad_up[n] for n in rows]))

        grad_x2, grad_x2_low, grad_gated = {}, {}, {}
        for n in rows:

            def third_back(p, grad_out, grad, hat, scale):
                g_vec_ref[6] += grad * hat
                g_vec_ref[7] += grad
                grad = grad_out.astype(F32) + normalize_back(grad, vec_ref[6], hat, scale)
                return grad, grad.astype(BF)

            grad_x2[n], grad_x2_low[n] = tiles(n, third_back, cot_low[n], grad3[n], hat3[n], scale3[n])
            grad_gated[n] = nn(att_out_ref[...], grad_x2_low[n])
            (out,) = tiles(n, lambda p, one, two: ((one + two).astype(BF),), x2[n], down[n])
            store_tokens(out_ref, start + n, order, out.T.astype(F32))
        g_ref[:, place["att_out"]] += nt(
            side([gated[n] for n in rows]), side([grad_x2_low[n] for n in rows])
        )
        grad_gate2, grad_out, center = {}, {}, {}
        for n in rows:

            def gate_back(p, grad, gate, out):
                mixed_grad = grad * gate
                scaled = [mixed_grad[mine[h]] * inverses[n, h][:, parts[p]] for h in range(heads)]
                low = jnp.concatenate(scaled, axis=0).astype(BF)
                product = low.astype(F32) * out
                centers = [jnp.sum(product[mine[h]], axis=0, keepdims=True) for h in range(heads)]
                return ((mixed_grad * out * (1.0 - gate)).astype(BF), low, *centers)

            grad_gate2[n], grad_out[n], *centers = tiles(n, gate_back, grad_gated[n], gate2[n], attended[n])
            for h in range(heads):
                center[n, h] = centers[h]

        grad_queries, grad_keys, grad_values = {}, {}, {}

        def probs(n, h):
            return nn(kv_tok[n][:, width:] * lane_ref[h], grad_out[n])

        def spread(n, h, grad_score):
            both = nn(jnp.concatenate([key[n][mine[h]], chain_ref[...]], axis=0), grad_score)
            grad_queries[n, h] = (both[:head] * scaling).astype(BF)
            g_bias_ref[h] += both[head:]
            grad_keys[n, h] = (nt(query[n][mine[h]], grad_score) * LN2).astype(BF)

        coming, behind = probs(*pairs[0]), None
        for at_pair, (n, h) in enumerate(pairs):
            grad_prob = coming
            if at_pair + 1 < len(pairs):
                coming = probs(*pairs[at_pair + 1])
            expon = e_scr[n, :, there[h]]
            grad_score = (expon.astype(F32) * (grad_prob - center[n, h])).astype(BF)
            grad_values[n, h] = nt(grad_out[n][mine[h]], expon).astype(BF)
            if behind is not None:
                spread(*behind)
            behind = (n, h, grad_score)
        spread(*behind)

        grad_hidden, grad2 = {}, {}
        for n in rows:
            blocks = [items[n, h] for items in (grad_queries, grad_keys, grad_values) for h in range(heads)]
            grad_hidden[n] = jnp.concatenate(blocks + [grad_gate2[n]], axis=0)
            grad2[n] = nn(att_ref[...], grad_hidden[n])
        g_ref[:, place["query"].start : place["gate2"].stop] += nt(
            side([normed2[n] for n in rows]), side([grad_hidden[n] for n in rows])
        )
        grad_x1, grad_branch, grad_gate1, grad_mix, grad1 = {}, {}, {}, {}, {}
        for n in rows:

            def second_back(p, grad_after, grad, hat, scale, gate, added):
                g_vec_ref[4] += grad * hat
                g_vec_ref[5] += grad
                grad = grad_after + normalize_back(grad, vec_ref[4], hat, scale)
                gated_grad = grad * gate
                return grad, gated_grad.astype(BF), (gated_grad * added * (1.0 - gate)).astype(BF)

            grad_x1[n], grad_branch[n], grad_gate1[n] = tiles(
                n, second_back, grad_x2[n], grad2[n], hat2[n], scale2[n], gate1[n], branch[n]
            )
            grad_mix[n] = nn(tri_out_ref[...], grad_branch[n])
            grad1[n] = nn(gate_w_ref[...], grad_gate1[n])
        g_ref[:, place["tri_out"]] += nt(
            side([mixed[n] for n in rows]), side([grad_branch[n] for n in rows])
        )
        g_ref[:, place["gate"]] += nt(
            side([normed1[n] for n in rows]), side([grad_gate1[n] for n in rows])
        )
        for n in rows:
            for p, part in enumerate(parts):
                grad, hat, scale = grad_mix[n][:, part], hat_t[n][:, part], scale_t[n][:, part]
                g_vec_ref[2] += grad * hat
                g_vec_ref[3] += grad
                dt_ref[p, start + n] = normalize_back(grad, vec_ref[2], hat, scale)
                grad, hat, scale = grad1[n][:, part], hat1[n][:, part], scale1[n][:, part]
                g_vec_ref[0] += grad * hat
                g_vec_ref[1] += grad
                grad = grad_x1[n][:, part] + normalize_back(grad, vec_ref[0], hat, scale)
                z_ref[start + n, :, part] = grad
        return carry

    lax.fori_loop(0, total_rows // count, step, 0)


def rows_pass(c, chunks, before, t, xt, cot_rows, order, bias, chain, lane, vecs, weights, heads):
    _, width, length = xt.shape
    blocks, pieces, sub, tokens, _ = cot_rows.shape
    rows = blocks * sub
    some, count = 4, 4
    inner = sub // some
    full = lambda item: pl.BlockSpec(item.shape, lambda at: (0,) * item.ndim)
    of_all = pl.BlockSpec((some, width, length), lambda at: (c * (rows // some) + at, 0, 0))
    t_some = pl.BlockSpec(
        (length // 128, some, width, 128), lambda at: (0, c * (rows // some) + at, 0, 0)
    )
    dt_some = pl.BlockSpec((length // 128, some, width, 128), lambda at: (0, at, 0, 0))
    by_piece = pl.BlockSpec(
        (1, pieces, some, tokens, width), lambda at: (at // inner, 0, at % inner, 0, 0)
    )
    consts = (bias, chain, lane, vecs) + weights
    wide = weights[-1].shape[1]
    sum_shapes = [
        jax.ShapeDtypeStruct(shape, F32)
        for shape in ((width, 7 * width + 2 * wide), (8, width, 128), (heads, 16, length))
    ]
    before_specs = [full(item) for item in before[:3]]
    before_specs += [pl.BlockSpec(memory_space=pl.ANY)] * len(before[3:])
    return pl.pallas_call(
        functools.partial(rows_kernel, count, heads, order, c == 0),
        grid=(rows // some,),
        in_specs=before_specs + [t_some, of_all, by_piece] + [full(item) for item in consts],
        out_specs=[by_piece, dt_some, of_all] + [full(item) for item in sum_shapes],
        out_shape=[
            jax.ShapeDtypeStruct(cot_rows.shape, BF),
            by_halves(rows, width, length),
            jax.ShapeDtypeStruct(xt.shape, F32),
        ]
        + sum_shapes,
        input_output_aliases={3: 2} if before else {},
        scratch_shapes=[
            pltpu.VMEM((count, length, heads * length), BF),
        ],
        compiler_params=pltpu.CompilerParams(vmem_limit_bytes=VMEM_LIMIT),
        cost_estimate=cost(1.2e11),
        name="rows",
    )(*before, t, xt, cot_rows, *consts)


def edges_back_kernel(
    order, xt_ref, z_ref, da_ref, db_ref, wt_ref, w_ref, gain_ref, shift_ref, out_ref, g_w_ref, g_vec_ref
):
    rows, width, length = xt_ref.shape
    count = 4

    @pl.when(pl.program_id(0) == 0)
    def _():
        g_w_ref[...] = jnp.zeros(g_w_ref.shape, F32)
        g_vec_ref[...] = jnp.zeros(g_vec_ref.shape, F32)

    def step(at, carry):
        start = at * count
        x0 = stacked(xt_ref, start, count).astype(F32)
        lanes = x0.shape[1]
        gain = widen(gain_ref[...], lanes)
        hat, scale = normalize(x0)
        normed = (hat * gain + widen(shift_ref[...], lanes)).astype(BF)
        proj = nn(wt_ref[...], normed)
        pa, pag = proj[:width], proj[width : 2 * width]
        pb, pbg = proj[2 * width : 3 * width], proj[3 * width :]
        halves = [(n, half) for n in range(count) for half in range(da_ref.shape[0])]
        da = jnp.concatenate([da_ref[half, start + n] for n, half in halves], axis=1)
        db = jnp.concatenate([db_ref[half, start + n] for n, half in halves], axis=1)
        sa, sb = sigmoid(pag), sigmoid(pbg)
        dsa, dsb = da * sa, db * sb
        grads = jnp.concatenate(
            [
                dsa.astype(BF),
                (dsa * pa * (1.0 - sa)).astype(BF),
                dsb.astype(BF),
                (dsb * pb * (1.0 - sb)).astype(BF),
            ],
            axis=0,
        )
        g_w_ref[...] += nt(normed, grads)
        grad = nn(w_ref[...], grads)
        g_vec_ref[0] += fold(grad * hat)
        g_vec_ref[1] += fold(grad)
        out = stacked(z_ref, start, count) + normalize_back(grad, gain, hat, scale)
        out = out.astype(BF)
        for n in range(count):
            store_tokens(out_ref, start + n, order, out[:, n * length : (n + 1) * length].T.astype(F32))
        return carry

    lax.fori_loop(0, rows // count, step, 0)


def edges_back(xt, z, da, db, order, weight_t, weight, gain, shift, shape):
    rows, width, length = xt.shape
    blocks, pieces, sub, tokens, _ = shape
    chunks = order[2]
    some = sub // chunks
    step = 16 // some
    inner = blocks // step
    full = lambda item: pl.BlockSpec(item.shape, lambda at: (0,) * item.ndim)
    by_row = pl.BlockSpec((16, width, length), lambda at: (at, 0, 0))
    by_half = pl.BlockSpec((length // 128, 16, width, 128), lambda at: (0, at, 0, 0))
    sum_shapes = [
        jax.ShapeDtypeStruct(weight.shape, F32),
        jax.ShapeDtypeStruct((2, width, 128), F32),
    ]
    by_piece = pl.BlockSpec(
        (step, pieces, some, tokens, width), lambda at: (at % inner, 0, at // inner, 0, 0)
    )
    return pl.pallas_call(
        functools.partial(edges_back_kernel, order),
        grid=(chunks * inner,),
        in_specs=[by_row] * 2 + [by_half] * 2 + [full(item) for item in (weight_t, weight, gain, shift)],
        out_specs=[by_piece] + [full(item) for item in sum_shapes],
        out_shape=[jax.ShapeDtypeStruct(shape, BF)] + sum_shapes,
        compiler_params=pltpu.CompilerParams(vmem_limit_bytes=VMEM_LIMIT),
        cost_estimate=cost(4.0e10),
        name="edges_back",
    )(xt, z, da, db, weight_t, weight, gain, shift)


def shards(
    row_size,
    col_size,
    pair_state,
    cotangent,
    chain_lengths,
    tri_gain,
    tri_shift,
    tri_weight,
    mix_gain,
    mix_shift,
    tri_out,
    att_gain,
    att_shift,
    att_weight,
    chain_bias,
    att_out,
    trans_gain,
    trans_shift,
    up_weight,
    down_weight,
):
    heads = HEADS
    crops, own_rows, tokens, width = pair_state.shape
    length = col_size * tokens
    chunks = CHUNKS
    some = own_rows // (col_size * chunks)
    axes = ("row", "col")
    group = row_size * col_size
    order = (row_size, col_size, chunks)
    shape = (row_size, col_size, some, tokens, width)

    def swap(values):
        return lax.all_to_all(values, axes, split_axis=0, concat_axis=0, tiled=True)

    def cut(values):
        parts = values.reshape(group, chunks, some, tokens, width)
        return [parts[:, c] for c in range(chunks)]

    def join(parts):
        return jnp.stack(parts, axis=1).reshape(crops, own_rows, tokens, width)

    def across(values, bit):
        return lax.ppermute(values, "col", [(q, q ^ bit) for q in range(col_size)])

    bits = [1 << n for n in range(col_size.bit_length() - 1)]

    def after(values, *others):
        return lax.optimization_barrier((values,) + others)[0]

    def gather(own, far, *late):
        pieces = {0: own, far_bit: across(far, far_bit)}
        arrived = pieces[far_bit]
        if late:
            pieces[far_bit] = after(arrived, *late)
        for bit in reversed(bits[:-1]):
            for m in list(pieces):
                pieces[m ^ bit] = across(pieces[m], bit)
        return [pieces[m] for m in range(col_size)], arrived

    def doubled(items, axis, size, bits):
        for bit in bits:
            lows = [values.astype(sent) for values, sent in items]
            others = [lax.ppermute(low, axis, [(q, q ^ bit) for q in range(size)]) for low in lows]
            others = lax.optimization_barrier(tuple(others))
            items = [
                (low.astype(F32) + other.astype(F32), sent)
                for low, other, (_, sent) in zip(lows, others, items)
            ]
        return items

    whole = (row_size, col_size, some * chunks, tokens, width)
    x_rows = swap(pair_state.reshape(group, some * chunks, tokens, width)).reshape(whole)
    cot_parts = cut(cotangent)

    wide = lambda item: jnp.broadcast_to(item[:, None], (width, 128))
    vecs = jnp.stack(
        [
            wide(item)
            for item in (
                tri_gain,
                tri_shift,
                mix_gain,
                mix_shift,
                att_gain,
                att_shift,
                trans_gain,
                trans_shift,
            )
        ]
    )
    edge_w = tri_weight[:, : 4 * width]
    edge_wt = edge_w.T
    gate_w = tri_weight[:, 4 * width :]
    lengths = lax.dynamic_index_in_dim(chain_lengths, lax.axis_index("row"), 0, keepdims=False)
    ends = jnp.cumsum(lengths)
    places = jnp.arange(length, dtype=jnp.int32)
    places = places.reshape(order + (some,)).transpose(1, 2, 0, 3).reshape(length)
    chain = jnp.sum((places[:, None] >= ends[None, :]).astype(jnp.int32), axis=-1)
    same = (chain[:, None] == chain[None, :]).astype(F32)
    bias = (LOG2E * chain_bias)[:, None, None] * same[None]
    which = (jnp.arange(16, dtype=jnp.int32)[:, None] == chain[None, :]).astype(F32)
    head_of = jnp.arange(width, dtype=jnp.int32) // (width // heads)
    lane = (jnp.arange(heads, dtype=jnp.int32)[:, None] == head_of[None, :]).astype(BF)
    lane = jnp.broadcast_to(lane[:, None, :], (heads, length, width))
    me = lax.axis_index("col")
    flips = jnp.arange(col_size, dtype=jnp.int32)
    own = own_rows
    far_bit = col_size // 2
    inside = (me ^ flips) & (far_bit - 1)
    place = (me ^ flips) * own
    place_near = (inside + (flips & far_bit)) * own
    half = (me // far_bit).reshape(1)

    cot_rows = []
    lefts, rights, xt, arrived = [], [], [], []
    for c in range(chunks):
        left, right, *xt = edges(c, x_rows, xt, order, edge_wt, vecs[0], vecs[1])
        if arrived:
            right = after(right, arrived[-1], cot_rows[0])
        pieces, there = gather(right, right)
        lefts.append(left)
        rights.append(pieces)
        arrived.append(there)
        if c == 0:
            cot_rows.append(swap(after(cot_parts[0], left)).reshape(shape))
    (xt,) = xt
    t = triangle(place, lefts, rights)
    for part in cot_parts[1:]:
        cot_rows.append(swap(after(part, t, cot_rows[-1])).reshape(shape))
    weights = (
        gate_w,
        gate_w.T,
        tri_out,
        tri_out.T,
        att_weight.T,
        att_weight[:, width : 3 * width],
        att_weight,
        att_out,
        att_out.T,
        up_weight,
        up_weight.T,
        down_weight,
        down_weight.T,
    )
    chain_rows = which.astype(BF)
    state, outs, dts = [], [], []
    lefts_all, grads, nears, fars = [], [], [], []
    for c in range(chunks):
        out, dt, z, *sums = rows_pass(
            c, chunks, state, t, xt, cot_rows[c], order, bias, chain_rows, lane, vecs, weights, heads
        )
        state = sums + [z]
        if outs:
            dt = after(dt, outs[-1])
        near, far = turn(half, dt)
        nears.append(near)
        fars.append(far)
        if c < chunks - 1:
            outs.append(swap(out.reshape(group, some, tokens, width)))
    g_rows, g_vec, g_bias = sums
    row_bits = [1 << n for n in range(row_size.bit_length() - 1)]
    ((g_rows, _),) = doubled([(g_rows, BF)], "row", row_size, row_bits)
    da = left_back(place_near, nears[:-1] + [after(nears[-1], g_rows)], fars, rights)
    for left in lefts:
        held = after(left, t)
        lefts_all.append(gather(held, held, z)[0])
    for c in range(chunks):
        pieces, last = gather(nears[c], fars[c], z if c < chunks - 1 else da)
        grads.append(pieces)
    outs.append(swap(after(out, last).reshape(group, some, tokens, width)))
    pair_out = join(outs)
    db = right_back(inside[:1] * own, grads, lefts_all)
    back, g_edge, g_vec_edge = edges_back(
        xt, z, da, db, order, edge_wt, edge_w, vecs[0], vecs[1], whole
    )
    g_vec = jnp.sum(g_vec, axis=-1)
    g_vec_edge = jnp.sum(g_vec_edge, axis=-1)
    g_chain = jnp.sum(g_bias * which[None], axis=(1, 2))
    small = jnp.concatenate(
        [g_vec[:2] + g_vec_edge, g_vec[2:], jnp.pad(g_chain, (0, width - heads))[None]], axis=0
    )
    items = doubled([(g_edge, BF), (small, F32)], "row", row_size, row_bits)
    back = after(back, *[values for values, _ in items])
    grad_pair = swap(back.reshape(group, some * chunks, tokens, width))
    grad_pair = grad_pair.reshape(crops, own_rows, tokens, width)
    items = doubled(items + [(after(g_rows, pair_out), BF)], "col", col_size, bits[::-1])
    t_edge, small, total = [values for values, _ in items]
    column = lambda at, n=1: total[:, at * width : (at + n) * width]
    ff = up_weight.shape[1] // width
    t_gate, t_tri_out, t_att = column(0), column(1), column(2, 4)
    t_att_out, t_up = column(6), column(7, ff)
    t_down = jnp.concatenate([column(7 + ff + n) for n in range(ff)], axis=0)
    return (
        pair_out,
        grad_pair,
        small[0],
        small[1],
        jnp.concatenate([t_edge, t_gate], axis=1),
        small[2],
        small[3],
        t_tri_out,
        small[4],
        small[5],
        t_att,
        small[8, :heads],
        t_att_out,
        small[6],
        small[7],
        t_up,
        t_down,
    )


def solution(mesh):
    pair = P("dp", "row", "col", None)
    vector, matrix = P("dp"), P("dp", None)
    return jax.shard_map(
        functools.partial(shards, mesh.shape["row"], mesh.shape["col"]),
        mesh=mesh,
        in_specs=(pair, pair, P("dp", None)) + (P(),) * 15,
        out_specs=(
            pair,
            pair,
            vector,
            vector,
            matrix,
            vector,
            vector,
            matrix,
            vector,
            vector,
            matrix,
            vector,
            matrix,
            vector,
            vector,
            matrix,
            matrix,
        ),
        check_vma=False,
    )
```

```python
import functools
import math

import jax
import jax.numpy as jnp
from jax import lax
from jax.experimental import pallas as pl
from jax.experimental.pallas import tpu as pltpu
from jax.sharding import PartitionSpec as P

HEADS = 4
EPS = 1e-05
LOG2E = math.log2(math.e)
LN2 = math.log(2.0)
CHUNKS = 2
VMEM_LIMIT = 56 * 1024 * 1024
BF = jnp.bfloat16
F32 = jnp.float32


def nn(left, right):
    return lax.dot_general(left, right, (((1,), (0,)), ((), ())), preferred_element_type=F32)


def nt(left, right):
    return lax.dot_general(left, right, (((1,), (1,)), ((), ())), preferred_element_type=F32)


def tn(left, right):
    return lax.dot_general(left, right, (((0,), (0,)), ((), ())), preferred_element_type=F32)


def cost(flops, size=0):
    return pl.CostEstimate(flops=int(flops), bytes_accessed=int(size), transcendentals=0)


def sigmoid(values):
    return 0.5 * jnp.tanh(0.5 * values) + 0.5


def normalize(values):
    center = values - jnp.mean(values, axis=0, keepdims=True)
    spread = jnp.mean(center * center, axis=0, keepdims=True)
    scale = lax.rsqrt(spread + EPS)
    return center * scale, scale


def normalize_back(grads, gain, hat, scale):
    grad_hat = grads * gain
    first = jnp.mean(grad_hat, axis=0, keepdims=True)
    second = jnp.mean(grad_hat * hat, axis=0, keepdims=True)
    return scale * (grad_hat - first - hat * second)


def widen(column, lanes):
    return jnp.concatenate([column] * (lanes // column.shape[1]), axis=1)


def fold(values):
    parts = [values[:, at : at + 128] for at in range(0, values.shape[1], 128)]
    return functools.reduce(lambda one, two: one + two, parts)


def load_tokens(ref, row, order):
    _, pieces, some, tokens, width = ref.shape
    flat = ref[row // some, :, row % some, :, :].astype(F32)
    flat = flat.reshape(order + (flat.shape[0] * tokens // math.prod(order), width))
    return flat.transpose(1, 2, 0, 3, 4).reshape(pieces * tokens, width)


def store_tokens(ref, row, order, values):
    _, pieces, some, tokens, width = ref.shape
    back = (order[1], order[2], order[0])
    flat = values.reshape(back + (pieces * tokens // math.prod(order), width))
    flat = flat.transpose(2, 0, 1, 3, 4).reshape(pieces, tokens, width)
    ref[row // some, :, row % some, :, :] = flat.astype(ref.dtype)


def stacked(ref, start, count):
    return jnp.concatenate([ref[start + n] for n in range(count)], axis=1)


def spread_out(ref, start, count, values):
    length = values.shape[1] // count
    for n in range(count):
        ref[start + n] = values[:, n * length : (n + 1) * length].astype(ref.dtype)


def edges_kernel(order, own, x_ref, w_ref, gain_ref, shift_ref, *refs):
    a_ref, b_ref, *xt_ref, a_scr, b_scr = refs[-5:] if own else refs
    width, rows, length = a_ref.shape
    pitch = a_scr.shape[1] // rows
    count = 4

    def step(at, carry):
        start = at * count
        tokens = [load_tokens(x_ref, start + n, order).astype(BF) for n in range(count)]
        x0 = jnp.concatenate([item.T for item in tokens], axis=1)
        if own:
            spread_out(xt_ref[0], start, count, x0)
        hat, _ = normalize(x0.astype(F32))
        lanes = x0.shape[1]
        normed = (hat * widen(gain_ref[...], lanes) + widen(shift_ref[...], lanes)).astype(BF)
        proj = nn(w_ref[...], normed)
        left = sigmoid(proj[width : 2 * width]) * proj[:width]
        right = sigmoid(proj[3 * width : 4 * width]) * proj[2 * width : 3 * width]
        for n in range(count):
            base = pl.multiple_of((start + n) * pitch, 8)
            for half in range(length // 128):
                part = slice(n * length + half * 128, n * length + half * 128 + 128)
                a_scr[half, pl.ds(base, width), :] = left[:, part]
                b_scr[half, pl.ds(base, width), :] = right[:, part]
        return carry

    lax.fori_loop(0, rows // count, step, 0)

    def turn(at, carry):
        for n in range(8):
            e = at * 8 + n
            for scr, out in ((a_scr, a_ref), (b_scr, b_ref)):
                halves = [scr[h, pl.ds(e, rows, stride=pitch), :] for h in range(scr.shape[0])]
                out[e] = jnp.concatenate(halves, axis=1).astype(BF)
        return carry

    lax.fori_loop(0, width // 8, turn, 0)


def edges(half, x_rows, order, weight, gain, shift, before=None):
    blocks, pieces, sub, tokens, width = x_rows.shape
    length = pieces * tokens
    chunks = order[2]
    some = sub // chunks
    rows = blocks * some
    own = before is not None
    const = lambda at: (0, 0)
    halves = order[0] // blocks
    pitch = width + 8
    low = pl.BlockSpec((width, rows, length), lambda at: (0, at, 0))
    outs = [jax.ShapeDtypeStruct((width, chunks * rows, length), BF)] * 2
    out_specs = [low, low]
    if own:
        out_specs.append(pl.BlockSpec((rows, width, length), lambda at: (at * halves + half, 0, 0)))
        outs.append(jax.ShapeDtypeStruct((halves * chunks * rows, width, length), BF))
    return pl.pallas_call(
        functools.partial(edges_kernel, order, own),
        grid=(chunks,),
        in_specs=[
            pl.BlockSpec((blocks, pieces, some, tokens, width), lambda at: (0, 0, at, 0, 0)),
            pl.BlockSpec(weight.shape, const),
            pl.BlockSpec(gain.shape, const),
            pl.BlockSpec(shift.shape, const),
        ]
        + [pl.BlockSpec(memory_space=pl.ANY)] * len(before or ()),
        out_specs=out_specs,
        out_shape=outs,
        input_output_aliases={4: 2} if before else {},
        scratch_shapes=[
            pltpu.VMEM((length // 128, rows * pitch, 128), F32),
            pltpu.VMEM((length // 128, rows * pitch, 128), F32),
        ],
        compiler_params=pltpu.CompilerParams(vmem_limit_bytes=VMEM_LIMIT),
        cost_estimate=cost(1.7e10),
        name="edges",
    )(x_rows, weight, gain, shift, *(before or ()))


def in_order(pieces, e, chunks):
    some = pieces[0].shape[1] // chunks
    return [piece[e, c * some : (c + 1) * some, :] for c in range(chunks) for piece in pieces]


def gather_pieces(place_ref, rights, e, scr, chunks):
    for m in range(len(rights[0])):
        for n, rows in enumerate(in_order([half[m] for half in rights], e, chunks)):
            some = rows.shape[0]
            scr[e, pl.ds(pl.multiple_of(place_ref[m] + n * some, some), some), :] = rows


def by_channel(ref):
    halves, rows, some, lanes = ref.shape
    return ref.reshape(halves, rows * some, lanes)


def put_channel(ref, e, values):
    halves, rows, some, lanes = ref.shape
    flat = by_channel(ref)
    for half in range(halves):
        flat[half, pl.ds(e, rows, stride=some), :] = values[:, half * lanes : (half + 1) * lanes]


def ahead(first, count, begin, end):
    coming = begin(first)
    for e in range(first, first + count):
        here = coming
        if e + 1 < first + count:
            coming = begin(e + 1)
        end(e, here)


SOME = 16


def cut_refs(refs, *counts):
    parts = []
    for count in counts:
        parts.append(refs[:count])
        refs = refs[count:]
    return parts + list(refs)


def triangle_kernel(halves, pieces, chunks, place_ref, *refs):
    lefts, rights, t_ref, scr = cut_refs(refs, halves, halves * pieces)
    rights = [rights[n * pieces : (n + 1) * pieces] for n in range(halves)]

    def begin(e):
        gather_pieces(place_ref, rights, e, scr, chunks)
        return nt(jnp.concatenate(in_order(lefts, e, chunks), axis=0), scr[e])

    ahead(0, SOME, begin, functools.partial(put_channel, t_ref))


def high_spec(rows, length):
    return pl.BlockSpec((length // 128, rows, SOME, 128), lambda at, place: (0, 0, at, 0))


def low_spec(rows, lanes):
    return pl.BlockSpec((SOME, rows, lanes), lambda at, place: (at, 0, 0))


def by_halves(rows, width, length):
    return jax.ShapeDtypeStruct((length // 128, rows, width, 128), F32)


def channel_call(kernel, name, flops, scalar, ins, in_specs, out_specs, out_shape, scratch=()):
    return pl.pallas_call(
        kernel,
        grid_spec=pltpu.PrefetchScalarGridSpec(
            num_scalar_prefetch=1,
            grid=(ins[0].shape[0 if ins[0].ndim == 3 else 2] // SOME,),
            in_specs=in_specs,
            out_specs=out_specs,
            scratch_shapes=scratch,
        ),
        out_shape=out_shape,
        compiler_params=pltpu.CompilerParams(vmem_limit_bytes=VMEM_LIMIT),
        cost_estimate=cost(flops),
        name=name,
    )(scalar, *ins)


def triangle(place, lefts, rights, chunks):
    width, rows, length = lefts[0].shape
    halves, pieces = len(lefts), len(rights[0])
    return channel_call(
        functools.partial(triangle_kernel, halves, pieces, chunks),
        "triangle",
        2.0e10,
        place,
        (*lefts, *[piece for half in rights for piece in half]),
        [low_spec(rows, length)] * (halves + halves * pieces),
        high_spec(halves * rows, length),
        by_halves(halves * rows, width, length),
        [pltpu.VMEM((SOME, length, length), BF)],
    )


def turn_kernel(grad_ref, out_ref):
    halves, rows, some, _ = grad_ref.shape
    flat = by_channel(grad_ref)
    for e in range(some):
        for half in range(halves):
            out_ref[half, e] = flat[half, pl.ds(e, rows, stride=some), :].astype(BF)


def turn(grad):
    halves, rows, width, lanes = grad.shape
    some = 8
    return pl.pallas_call(
        turn_kernel,
        grid=(width // some,),
        in_specs=[pl.BlockSpec((halves, rows, some, lanes), lambda at: (0, 0, at, 0))],
        out_specs=pl.BlockSpec((halves, some, rows, lanes), lambda at: (0, at, 0, 0)),
        out_shape=jax.ShapeDtypeStruct((halves, width, rows, lanes), BF),
        compiler_params=pltpu.CompilerParams(vmem_limit_bytes=VMEM_LIMIT),
        cost_estimate=cost(5.0e9),
        name="turn",
    )(grad)


def right_back_kernel(chunks, halves, here_ref, *refs):
    lefts, grads, db_ref, scr = cut_refs(refs, 4 * halves, 2 * chunks)
    rows = db_ref.shape[1]
    half = here_ref[1]

    def begin(e):
        grad, left = [], []
        for m in range(4):
            source = half if m < 2 else 1 - half
            grad += [grads[2 * c + m % 2][source, e] for c in range(chunks)]
            left += in_order([lefts[n * 4 + m] for n in range(halves)], e, chunks)
        return tn(jnp.concatenate(grad, axis=0), jnp.concatenate(left, axis=0))

    def end(e, db):
        scr[e] = db
        put_channel(db_ref, e, scr[e, pl.ds(pl.multiple_of(here_ref[0], rows), rows), :])

    ahead(0, SOME, begin, end)


def right_back(here, grads, lefts):
    width, rows, length = lefts[0][0].shape
    halves, pieces = len(lefts), len(lefts[0])
    chunks = len(grads)
    _, _, some, part = grads[0][0].shape
    both = pl.BlockSpec((2, SOME, some, part), lambda at, here: (0, at, 0, 0))
    return channel_call(
        functools.partial(right_back_kernel, chunks, halves),
        "right_back",
        2.2e10,
        here,
        [item for left in lefts for item in left] + [item for chunk in grads for item in chunk],
        [low_spec(rows, length)] * (halves * pieces) + [both] * (2 * chunks),
        high_spec(halves * rows, length),
        by_halves(halves * rows, width, length),
        [pltpu.VMEM((SOME, part, length), F32)],
    )


def left_back_kernel(chunks, halves, pieces, place_ref, *refs):
    rights, grads, da_ref, scr = cut_refs(refs, halves * pieces, chunks)
    rights = [rights[n * pieces : (n + 1) * pieces] for n in range(halves)]

    def begin(e):
        gather_pieces(place_ref, rights, e, scr, chunks)
        grad = [jnp.concatenate([ref[0, e], ref[1, e]], axis=1) for ref in grads]
        return nn(jnp.concatenate(grad, axis=0), scr[e])

    ahead(0, SOME, begin, functools.partial(put_channel, da_ref))


def left_back(place, grads, rights):
    _, width, some, part = grads[0].shape
    _, rows, length = rights[0][0].shape
    halves, pieces = len(rights), len(rights[0])
    both = pl.BlockSpec((2, SOME, some, part), lambda at, place: (0, at, 0, 0))
    return channel_call(
        functools.partial(left_back_kernel, len(grads), halves, pieces),
        "left_back",
        2.0e10,
        place,
        (*[piece for half in rights for piece in half], *grads),
        [low_spec(rows, length)] * (halves * pieces) + [both] * len(grads),
        high_spec(halves * rows, length),
        by_halves(halves * rows, width, length),
        [pltpu.VMEM((SOME, length, length), BF)],
    )


def rows_kernel(count, heads, order, first, *refs):
    before = []
    if not first:
        before, refs = refs[:3], refs[4:]
    rows_body(count, heads, order, before, *refs)


def rows_body(
    count,
    heads,
    order,
    before,
    t_ref,
    xt_ref,
    cot_ref,
    bias_ref,
    chain_ref,
    lane_ref,
    vec_ref,
    gate_w_ref,
    gate_wt_ref,
    tri_out_ref,
    tri_out_t_ref,
    att_t_ref,
    att_kv_ref,
    att_ref,
    att_out_ref,
    att_out_t_ref,
    up_ref,
    up_t_ref,
    down_ref,
    down_t_ref,
    out_ref,
    dt_ref,
    z_ref,
    g_ref,
    g_vec_ref,
    g_bias_ref,
    e_scr,
):
    total_rows, width, length = xt_ref.shape
    head = width // heads
    scaling = 1.0 / math.sqrt(head)

    sums = (g_ref, g_vec_ref, g_bias_ref)
    place = {}
    for name in ("gate", "tri_out", "query", "key", "value", "gate2", "att_out"):
        place[name] = slice(len(place) * width, (len(place) + 1) * width)
    ups = slice(7 * width, 7 * width + up_ref.shape[1])
    downs = [
        slice(at, at + width) for at in range(ups.stop, ups.stop + up_ref.shape[1], width)
    ]

    @pl.when(pl.program_id(0) == 0)
    def _():
        for n, ref in enumerate(sums):
            ref[...] = before[n][...] if before else jnp.zeros(ref.shape, ref.dtype)

    per = length // 128
    mine = [slice(h * head, (h + 1) * head) for h in range(heads)]
    there = [slice(h * length, (h + 1) * length) for h in range(heads)]
    ones = jnp.ones((16, length), BF)
    parts = [slice(p * 128, (p + 1) * 128) for p in range(per)]

    def tiles(n, function, *items):
        results = [function(p, *[item[:, parts[p]] for item in items]) for p in range(per)]
        return [jnp.concatenate(list(column), axis=1) for column in zip(*results)]

    def step(at, carry):
        start = at * count
        rows = range(count)
        side = lambda items: jnp.concatenate(items, axis=1)
        x0, hat1, scale1, normed1, gate_raw = {}, {}, {}, {}, {}
        hat_t, scale_t, mixed, branch = {}, {}, {}, {}
        for n in rows:

            def first(p):
                tile = xt_ref[start + n, :, parts[p]].astype(F32)
                hat, scale = normalize(tile)
                return tile, hat, scale, (hat * vec_ref[0] + vec_ref[1]).astype(BF)

            x0[n], hat1[n], scale1[n], normed1[n] = tiles(n, first)
            gate_raw[n] = nn(gate_wt_ref[...], normed1[n])

            def second(p):
                hat, scale = normalize(t_ref[p, start + n])
                return hat, scale, (hat * vec_ref[2] + vec_ref[3]).astype(BF)

            hat_t[n], scale_t[n], mixed[n] = tiles(n, second)
            branch[n] = nn(tri_out_t_ref[...], mixed[n])

        gate1, x1, hat2, scale2, normed2, hidden, kv_tok = {}, {}, {}, {}, {}, {}, {}
        for n in rows:

            def join(p, before, raw, add):
                gate = sigmoid(raw)
                after = before + gate * add
                hat, scale = normalize(after)
                return gate, after, hat, scale, (hat * vec_ref[4] + vec_ref[5]).astype(BF)

            gate1[n], x1[n], hat2[n], scale2[n], normed2[n] = tiles(
                n, join, x0[n], gate_raw[n], branch[n]
            )
            hidden[n] = nn(att_t_ref[...], normed2[n])
            kv_tok[n] = nn(normed2[n].T, att_kv_ref[...])

        query, key, value, gate2 = {}, {}, {}, {}
        for n in rows:

            def split(p, tile):
                gate = sigmoid(tile[3 * width :].astype(BF).astype(F32))
                asked = (tile[:width] * (scaling * LOG2E)).astype(BF)
                return asked, tile[width : 2 * width].astype(BF), tile[2 * width : 3 * width].astype(BF), gate

            query[n], key[n], value[n], gate2[n] = tiles(n, split, hidden[n])
            kv_tok[n] = kv_tok[n].astype(BF)

        pairs = [(n, h) for n in rows for h in range(heads)]

        def scores(n, h):
            return nn(kv_tok[n][:, :width] * lane_ref[h], query[n])

        outs, inverses = {}, {}

        def mix(n, h):
            both = nn(jnp.concatenate([value[n][mine[h]], ones], axis=0), e_scr[n, :, there[h]])
            inverses[n, h] = 1.0 / both[head : head + 1]
            outs[n, h] = both[:head] * inverses[n, h]

        coming = scores(*pairs[0])
        for at_pair, (n, h) in enumerate(pairs):
            score = coming
            if at_pair + 1 < len(pairs):
                coming = scores(*pairs[at_pair + 1])
            score = score + bias_ref[h]
            peak = jnp.max(score, axis=0, keepdims=True)
            e_scr[n, :, there[h]] = jnp.exp2(score - peak).astype(BF)
            if at_pair:
                mix(*pairs[at_pair - 1])
        mix(*pairs[-1])

        attended, gated, x2 = {}, {}, {}
        for n in rows:
            attended[n] = jnp.concatenate([outs[n, h] for h in range(heads)], axis=0)
            (gated[n],) = tiles(n, lambda p, gate, out: ((gate * out).astype(BF),), gate2[n], attended[n])
            x2[n] = nn(att_out_t_ref[...], gated[n])
        hat3, scale3, normed3, up, cot_tok, cot_low, grad_act = {}, {}, {}, {}, {}, {}, {}
        for n in rows:

            def third(p, before, add):
                after = before + add
                hat, scale = normalize(after)
                return after, hat, scale, (hat * vec_ref[6] + vec_ref[7]).astype(BF)

            x2[n], hat3[n], scale3[n], normed3[n] = tiles(n, third, x1[n], x2[n])
            up[n] = nn(up_t_ref[...], normed3[n])
            cot_tok[n] = load_tokens(cot_ref, start + n, order).astype(BF)
            cot_low[n] = cot_tok[n].T
            grad_act[n] = nn(down_ref[...], cot_low[n])
        act, down, grad_up, grad3 = {}, {}, {}, {}
        for n in rows:

            def silu(p, raw, grad):
                gate = sigmoid(raw)
                return (raw * gate).astype(BF), (grad * (gate * (1.0 + raw * (1.0 - gate)))).astype(BF)

            act[n], grad_up[n] = tiles(n, silu, up[n], grad_act[n])
            down[n] = nn(down_t_ref[...], act[n])
            grad3[n] = nn(up_ref[...], grad_up[n])
        grad = nn(side([act[n] for n in rows]), jnp.concatenate([cot_tok[n] for n in rows], axis=0))
        for n, part in enumerate(downs):
            g_ref[:, part] += grad[n * width : (n + 1) * width]
        g_ref[:, ups] += nt(side([normed3[n] for n in rows]), side([grad_up[n] for n in rows]))

        grad_x2, grad_x2_low, grad_gated = {}, {}, {}
        for n in rows:

            def third_back(p, grad_out, grad, hat, scale):
                g_vec_ref[6] += grad * hat
                g_vec_ref[7] += grad
                grad = grad_out.astype(F32) + normalize_back(grad, vec_ref[6], hat, scale)
                return grad, grad.astype(BF)

            grad_x2[n], grad_x2_low[n] = tiles(n, third_back, cot_low[n], grad3[n], hat3[n], scale3[n])
            grad_gated[n] = nn(att_out_ref[...], grad_x2_low[n])
            (out,) = tiles(n, lambda p, one, two: ((one + two).astype(BF),), x2[n], down[n])
            store_tokens(out_ref, start + n, order, out.T.astype(F32))
        g_ref[:, place["att_out"]] += nt(
            side([gated[n] for n in rows]), side([grad_x2_low[n] for n in rows])
        )
        grad_gate2, grad_out, center = {}, {}, {}
        for n in rows:

            def gate_back(p, grad, gate, out):
                mixed_grad = grad * gate
                scaled = [mixed_grad[mine[h]] * inverses[n, h][:, parts[p]] for h in range(heads)]
                low = jnp.concatenate(scaled, axis=0).astype(BF)
                product = low.astype(F32) * out
                centers = [jnp.sum(product[mine[h]], axis=0, keepdims=True) for h in range(heads)]
                return ((mixed_grad * out * (1.0 - gate)).astype(BF), low, *centers)

            grad_gate2[n], grad_out[n], *centers = tiles(n, gate_back, grad_gated[n], gate2[n], attended[n])
            for h in range(heads):
                center[n, h] = centers[h]

        grad_queries, grad_keys, grad_values = {}, {}, {}

        def probs(n, h):
            return nn(kv_tok[n][:, width:] * lane_ref[h], grad_out[n])

        def spread(n, h, grad_score):
            both = nn(jnp.concatenate([key[n][mine[h]], chain_ref[...]], axis=0), grad_score)
            grad_queries[n, h] = (both[:head] * scaling).astype(BF)
            g_bias_ref[h] += both[head:]
            grad_keys[n, h] = (nt(query[n][mine[h]], grad_score) * LN2).astype(BF)

        coming, behind = probs(*pairs[0]), None
        for at_pair, (n, h) in enumerate(pairs):
            grad_prob = coming
            if at_pair + 1 < len(pairs):
                coming = probs(*pairs[at_pair + 1])
            expon = e_scr[n, :, there[h]]
            grad_score = (expon.astype(F32) * (grad_prob - center[n, h])).astype(BF)
            grad_values[n, h] = nt(grad_out[n][mine[h]], expon).astype(BF)
            if behind is not None:
                spread(*behind)
            behind = (n, h, grad_score)
        spread(*behind)

        grad_hidden, grad2 = {}, {}
        for n in rows:
            blocks = [items[n, h] for items in (grad_queries, grad_keys, grad_values) for h in range(heads)]
            grad_hidden[n] = jnp.concatenate(blocks + [grad_gate2[n]], axis=0)
            grad2[n] = nn(att_ref[...], grad_hidden[n])
        g_ref[:, place["query"].start : place["gate2"].stop] += nt(
            side([normed2[n] for n in rows]), side([grad_hidden[n] for n in rows])
        )
        grad_x1, grad_branch, grad_gate1, grad_mix, grad1 = {}, {}, {}, {}, {}
        for n in rows:

            def second_back(p, grad_after, grad, hat, scale, gate, added):
                g_vec_ref[4] += grad * hat
                g_vec_ref[5] += grad
                grad = grad_after + normalize_back(grad, vec_ref[4], hat, scale)
                gated_grad = grad * gate
                return grad, gated_grad.astype(BF), (gated_grad * added * (1.0 - gate)).astype(BF)

            grad_x1[n], grad_branch[n], grad_gate1[n] = tiles(
                n, second_back, grad_x2[n], grad2[n], hat2[n], scale2[n], gate1[n], branch[n]
            )
            grad_mix[n] = nn(tri_out_ref[...], grad_branch[n])
            grad1[n] = nn(gate_w_ref[...], grad_gate1[n])
        g_ref[:, place["tri_out"]] += nt(
            side([mixed[n] for n in rows]), side([grad_branch[n] for n in rows])
        )
        g_ref[:, place["gate"]] += nt(
            side([normed1[n] for n in rows]), side([grad_gate1[n] for n in rows])
        )
        for n in rows:
            for p, part in enumerate(parts):
                grad, hat, scale = grad_mix[n][:, part], hat_t[n][:, part], scale_t[n][:, part]
                g_vec_ref[2] += grad * hat
                g_vec_ref[3] += grad
                dt_ref[p, start + n] = normalize_back(grad, vec_ref[2], hat, scale)
                grad, hat, scale = grad1[n][:, part], hat1[n][:, part], scale1[n][:, part]
                g_vec_ref[0] += grad * hat
                g_vec_ref[1] += grad
                grad = grad_x1[n][:, part] + normalize_back(grad, vec_ref[0], hat, scale)
                z_ref[start + n, :, part] = grad
        return carry

    lax.fori_loop(0, total_rows // count, step, 0)


def rows_pass(c, chunks, before, t, xt, cot_rows, order, bias, chain, lane, vecs, weights, heads):
    _, width, length = xt.shape
    blocks, pieces, sub, tokens, _ = cot_rows.shape
    rows = blocks * sub
    some, count = 4, 4
    inner = sub // some
    full = lambda item: pl.BlockSpec(item.shape, lambda at: (0,) * item.ndim)
    of_all = pl.BlockSpec((some, width, length), lambda at: (c * (rows // some) + at, 0, 0))
    t_some = pl.BlockSpec(
        (length // 128, some, width, 128), lambda at: (0, c * (rows // some) + at, 0, 0)
    )
    dt_some = pl.BlockSpec((length // 128, some, width, 128), lambda at: (0, at, 0, 0))
    by_piece = pl.BlockSpec(
        (1, pieces, some, tokens, width), lambda at: (at // inner, 0, at % inner, 0, 0)
    )
    consts = (bias, chain, lane, vecs) + weights
    wide = weights[-1].shape[1]
    sum_shapes = [
        jax.ShapeDtypeStruct(shape, F32)
        for shape in ((width, 7 * width + 2 * wide), (8, width, 128), (heads, 16, length))
    ]
    before_specs = [full(item) for item in before[:3]]
    before_specs += [pl.BlockSpec(memory_space=pl.ANY)] * len(before[3:])
    return pl.pallas_call(
        functools.partial(rows_kernel, count, heads, order, c == 0),
        grid=(rows // some,),
        in_specs=before_specs + [t_some, of_all, by_piece] + [full(item) for item in consts],
        out_specs=[by_piece, dt_some, of_all] + [full(item) for item in sum_shapes],
        out_shape=[
            jax.ShapeDtypeStruct(cot_rows.shape, BF),
            by_halves(rows, width, length),
            jax.ShapeDtypeStruct(xt.shape, F32),
        ]
        + sum_shapes,
        input_output_aliases={3: 2} if before else {},
        scratch_shapes=[
            pltpu.VMEM((count, length, heads * length), BF),
        ],
        compiler_params=pltpu.CompilerParams(vmem_limit_bytes=VMEM_LIMIT),
        cost_estimate=cost(1.2e11),
        name="rows",
    )(*before, t, xt, cot_rows, *consts)


def edges_back_kernel(
    order, xt_ref, z_ref, da_ref, db_ref, wt_ref, w_ref, gain_ref, shift_ref, out_ref, g_w_ref, g_vec_ref
):
    rows, width, length = xt_ref.shape
    count = 4

    @pl.when(pl.program_id(0) == 0)
    def _():
        g_w_ref[...] = jnp.zeros(g_w_ref.shape, F32)
        g_vec_ref[...] = jnp.zeros(g_vec_ref.shape, F32)

    def step(at, carry):
        start = at * count
        x0 = stacked(xt_ref, start, count).astype(F32)
        lanes = x0.shape[1]
        gain = widen(gain_ref[...], lanes)
        hat, scale = normalize(x0)
        normed = (hat * gain + widen(shift_ref[...], lanes)).astype(BF)
        proj = nn(wt_ref[...], normed)
        pa, pag = proj[:width], proj[width : 2 * width]
        pb, pbg = proj[2 * width : 3 * width], proj[3 * width :]
        halves = [(n, half) for n in range(count) for half in range(da_ref.shape[0])]
        da = jnp.concatenate([da_ref[half, start + n] for n, half in halves], axis=1)
        db = jnp.concatenate([db_ref[half, start + n] for n, half in halves], axis=1)
        sa, sb = sigmoid(pag), sigmoid(pbg)
        dsa, dsb = da * sa, db * sb
        grads = jnp.concatenate(
            [
                dsa.astype(BF),
                (dsa * pa * (1.0 - sa)).astype(BF),
                dsb.astype(BF),
                (dsb * pb * (1.0 - sb)).astype(BF),
            ],
            axis=0,
        )
        g_w_ref[...] += nt(normed, grads)
        grad = nn(w_ref[...], grads)
        g_vec_ref[0] += fold(grad * hat)
        g_vec_ref[1] += fold(grad)
        out = stacked(z_ref, start, count) + normalize_back(grad, gain, hat, scale)
        out = out.astype(BF)
        for n in range(count):
            store_tokens(out_ref, start + n, order, out[:, n * length : (n + 1) * length].T.astype(F32))
        return carry

    lax.fori_loop(0, rows // count, step, 0)


def edges_back(xt, z, da, db, order, weight_t, weight, gain, shift, shape):
    rows, width, length = xt.shape
    blocks, pieces, sub, tokens, _ = shape
    chunks = order[2]
    some = sub // chunks
    step = 16 // some
    inner = blocks // step
    full = lambda item: pl.BlockSpec(item.shape, lambda at: (0,) * item.ndim)
    by_row = pl.BlockSpec((16, width, length), lambda at: (at, 0, 0))
    by_half = pl.BlockSpec((length // 128, 16, width, 128), lambda at: (0, at, 0, 0))
    sum_shapes = [
        jax.ShapeDtypeStruct(weight.shape, F32),
        jax.ShapeDtypeStruct((2, width, 128), F32),
    ]
    by_piece = pl.BlockSpec(
        (step, pieces, some, tokens, width), lambda at: (at % inner, 0, at // inner, 0, 0)
    )
    return pl.pallas_call(
        functools.partial(edges_back_kernel, order),
        grid=(chunks * inner,),
        in_specs=[by_row] * 2 + [by_half] * 2 + [full(item) for item in (weight_t, weight, gain, shift)],
        out_specs=[by_piece] + [full(item) for item in sum_shapes],
        out_shape=[jax.ShapeDtypeStruct(shape, BF)] + sum_shapes,
        compiler_params=pltpu.CompilerParams(vmem_limit_bytes=VMEM_LIMIT),
        cost_estimate=cost(4.0e10),
        name="edges_back",
    )(xt, z, da, db, weight_t, weight, gain, shift)


def shards(
    row_size,
    col_size,
    pair_state,
    cotangent,
    chain_lengths,
    tri_gain,
    tri_shift,
    tri_weight,
    mix_gain,
    mix_shift,
    tri_out,
    att_gain,
    att_shift,
    att_weight,
    chain_bias,
    att_out,
    trans_gain,
    trans_shift,
    up_weight,
    down_weight,
):
    heads = HEADS
    crops, own_rows, tokens, width = pair_state.shape
    length = col_size * tokens
    chunks = CHUNKS
    some = own_rows // (col_size * chunks)
    axes = ("row", "col")
    group = row_size * col_size
    order = (row_size, col_size, chunks)
    shape = (row_size, col_size, some, tokens, width)

    def swap(values):
        return lax.all_to_all(values, axes, split_axis=0, concat_axis=0, tiled=True)

    def cut(values):
        parts = values.reshape(group, chunks, some, tokens, width)
        return [parts[:, c] for c in range(chunks)]

    def join(parts):
        return jnp.stack(parts, axis=1).reshape(crops, own_rows, tokens, width)

    def across(values, bit):
        return lax.ppermute(values, "col", [(q, q ^ bit) for q in range(col_size)])

    bits = [1 << n for n in range(col_size.bit_length() - 1)]

    def after(values, *others):
        return lax.optimization_barrier((values,) + others)[0]

    def gather(own, far, *late):
        pieces = {0: own, far_bit: across(far, far_bit)}
        arrived = pieces[far_bit]
        if late:
            pieces[far_bit] = after(arrived, *late)
        for bit in reversed(bits[:-1]):
            for m in list(pieces):
                pieces[m ^ bit] = across(pieces[m], bit)
        return [pieces[m] for m in range(col_size)], arrived

    def doubled(items, axis, size, bits):
        for bit in bits:
            lows = [values.astype(sent) for values, sent in items]
            others = [lax.ppermute(low, axis, [(q, q ^ bit) for q in range(size)]) for low in lows]
            others = lax.optimization_barrier(tuple(others))
            items = [
                (low.astype(F32) + other.astype(F32), sent)
                for low, other, (_, sent) in zip(lows, others, items)
            ]
        return items

    whole = (row_size, col_size, some * chunks, tokens, width)
    x_rows = swap(pair_state.reshape(group, some * chunks, tokens, width)).reshape(whole)
    cot_parts = cut(cotangent)

    wide = lambda item: jnp.broadcast_to(item[:, None], (width, 128))
    vecs = jnp.stack(
        [
            wide(item)
            for item in (
                tri_gain,
                tri_shift,
                mix_gain,
                mix_shift,
                att_gain,
                att_shift,
                trans_gain,
                trans_shift,
            )
        ]
    )
    edge_w = tri_weight[:, : 4 * width]
    edge_wt = edge_w.T
    gate_w = tri_weight[:, 4 * width :]
    lengths = lax.dynamic_index_in_dim(chain_lengths, lax.axis_index("row"), 0, keepdims=False)
    ends = jnp.cumsum(lengths)
    places = jnp.arange(length, dtype=jnp.int32)
    places = places.reshape(order + (some,)).transpose(1, 2, 0, 3).reshape(length)
    chain = jnp.sum((places[:, None] >= ends[None, :]).astype(jnp.int32), axis=-1)
    same = (chain[:, None] == chain[None, :]).astype(F32)
    bias = (LOG2E * chain_bias)[:, None, None] * same[None]
    which = (jnp.arange(16, dtype=jnp.int32)[:, None] == chain[None, :]).astype(F32)
    head_of = jnp.arange(width, dtype=jnp.int32) // (width // heads)
    lane = (jnp.arange(heads, dtype=jnp.int32)[:, None] == head_of[None, :]).astype(BF)
    lane = jnp.broadcast_to(lane[:, None, :], (heads, length, width))
    me = lax.axis_index("col")
    flips = jnp.arange(col_size, dtype=jnp.int32)
    own = own_rows
    far_bit = col_size // 2
    place = (me ^ flips) * own
    here = jnp.stack([(me % far_bit) * own, me // far_bit])

    halves = 2
    edge_of = functools.partial(edges, order=order, weight=edge_wt, gain=vecs[0], shift=vecs[1])
    x_halves = jnp.split(x_rows, halves, axis=0)
    lefts, rights, xt, x_far, cot_rows = [], [], [], [], []
    for n, part in enumerate(x_halves):
        x_far.append(across(after(part, x_far[-1]) if x_far else part, far_bit))
        left, right, *xt = edge_of(n, part, before=xt)
        lefts.append([left, across(left, 1)])
        rights.append([right, across(right, 1)])
    cot_rows.append(swap(after(cot_parts[0], x_far[0])).reshape(shape))
    for n, part in enumerate(x_far):
        left, right = edge_of(n, after(part, cot_rows[0]) if n else part)
        lefts[n] += [left, across(left, 1)]
        rights[n] += [right, across(right, 1)]
    (xt,) = xt
    t = triangle(place, [left[0] for left in lefts], rights, chunks)
    for part in cot_parts[1:]:
        cot_rows.append(swap(after(part, t, cot_rows[-1])).reshape(shape))
    weights = (
        gate_w,
        gate_w.T,
        tri_out,
        tri_out.T,
        att_weight.T,
        att_weight[:, width : 3 * width],
        att_weight,
        att_out,
        att_out.T,
        up_weight,
        up_weight.T,
        down_weight,
        down_weight.T,
    )
    chain_rows = which.astype(BF)
    state, outs, dts, sent = [], [], [], []
    pairs = [[q, q + far_bit] for q in range(far_bit)]
    for c in range(chunks):
        out, dt, z, *sums = rows_pass(
            c, chunks, state, t, xt, cot_rows[c], order, bias, chain_rows, lane, vecs, weights, heads
        )
        state = sums + [z]
        dt = turn(dt)
        if c < chunks - 1:
            dts.append(dt)
            outs.append(swap(out.reshape(group, some, tokens, width)))
            near = lax.dynamic_index_in_dim(dt, here[1], 0, keepdims=False)
            sent.append((near, across(lax.dynamic_index_in_dim(dt, 1 - here[1], 0, keepdims=False), far_bit)))
    dt = after(dt, *outs)
    dts.append(dt)
    crossed = []
    for near, far in sent:
        near, far = after(near, z), after(far, z)
        crossed.append(jnp.where(here[1] == 0, jnp.stack([near, far]), jnp.stack([far, near])))
    crossed.append(
        lax.all_to_all(dt, "col", split_axis=0, concat_axis=0, axis_index_groups=pairs, tiled=True)
    )
    g_rows, g_vec, g_bias = sums
    row_bits = [1 << n for n in range(row_size.bit_length() - 1)]
    ((g_rows, _),) = doubled([(g_rows, BF)], "row", row_size, row_bits)
    da = left_back(place, dts, rights)
    grads = [[item, across(item, 1)] for item in crossed[:-1]]
    grads.append([crossed[-1], across(after(crossed[-1], da), 1)])
    outs.append(swap(after(out, crossed[-1]).reshape(group, some, tokens, width)))
    pair_out = join(outs)
    db = right_back(here, grads, [[item if m else after(item, g_rows) for m, item in enumerate(left)] for left in lefts])
    back, g_edge, g_vec_edge = edges_back(
        xt, z, da, db, order, edge_wt, edge_w, vecs[0], vecs[1], whole
    )
    g_vec = jnp.sum(g_vec, axis=-1)
    g_vec_edge = jnp.sum(g_vec_edge, axis=-1)
    g_chain = jnp.sum(g_bias * which[None], axis=(1, 2))
    small = jnp.concatenate(
        [g_vec[:2] + g_vec_edge, g_vec[2:], jnp.pad(g_chain, (0, width - heads))[None]], axis=0
    )
    items = doubled([(g_edge, BF), (small, F32)], "row", row_size, row_bits)
    back = after(back, *[values for values, _ in items])
    grad_pair = swap(back.reshape(group, some * chunks, tokens, width))
    grad_pair = grad_pair.reshape(crops, own_rows, tokens, width)
    items = doubled(items + [(after(g_rows, pair_out), BF)], "col", col_size, bits[::-1])
    t_edge, small, total = [values for values, _ in items]
    column = lambda at, n=1: total[:, at * width : (at + n) * width]
    ff = up_weight.shape[1] // width
    t_gate, t_tri_out, t_att = column(0), column(1), column(2, 4)
    t_att_out, t_up = column(6), column(7, ff)
    t_down = jnp.concatenate([column(7 + ff + n) for n in range(ff)], axis=0)
    return (
        pair_out,
        grad_pair,
        small[0],
        small[1],
        jnp.concatenate([t_edge, t_gate], axis=1),
        small[2],
        small[3],
        t_tri_out,
        small[4],
        small[5],
        t_att,
        small[8, :heads],
        t_att_out,
        small[6],
        small[7],
        t_up,
        t_down,
    )


def solution(mesh):
    pair = P("dp", "row", "col", None)
    vector, matrix = P("dp"), P("dp", None)
    return jax.shard_map(
        functools.partial(shards, mesh.shape["row"], mesh.shape["col"]),
        mesh=mesh,
        in_specs=(pair, pair, P("dp", None)) + (P(),) * 15,
        out_specs=(
            pair,
            pair,
            vector,
            vector,
            matrix,
            vector,
            vector,
            matrix,
            vector,
            vector,
            matrix,
            vector,
            matrix,
            vector,
            vector,
            matrix,
            matrix,
        ),
        check_vma=False,
    )
```

```python
import functools
import math

import jax
import jax.numpy as jnp
from jax import lax
from jax.experimental import pallas as pl
from jax.experimental.pallas import tpu as pltpu
from jax.sharding import PartitionSpec as P

HEADS = 4
EPS = 1e-05
LOG2E = math.log2(math.e)
LN2 = math.log(2.0)
CHUNKS = 2
VMEM_LIMIT = 56 * 1024 * 1024
BF = jnp.bfloat16
F32 = jnp.float32


def nn(left, right):
    return lax.dot_general(left, right, (((1,), (0,)), ((), ())), preferred_element_type=F32)


def nt(left, right):
    return lax.dot_general(left, right, (((1,), (1,)), ((), ())), preferred_element_type=F32)


def tn(left, right):
    return lax.dot_general(left, right, (((0,), (0,)), ((), ())), preferred_element_type=F32)


def cost(flops, size=0):
    return pl.CostEstimate(flops=int(flops), bytes_accessed=int(size), transcendentals=0)


def sigmoid(values):
    return 0.5 * jnp.tanh(0.5 * values) + 0.5


def normalize(values):
    center = values - jnp.mean(values, axis=0, keepdims=True)
    spread = jnp.mean(center * center, axis=0, keepdims=True)
    scale = lax.rsqrt(spread + EPS)
    return center * scale, scale


def normalize_back(grads, gain, hat, scale):
    grad_hat = grads * gain
    first = jnp.mean(grad_hat, axis=0, keepdims=True)
    second = jnp.mean(grad_hat * hat, axis=0, keepdims=True)
    return scale * (grad_hat - first - hat * second)


def widen(column, lanes):
    return jnp.concatenate([column] * (lanes // column.shape[1]), axis=1)


def fold(values):
    parts = [values[:, at : at + 128] for at in range(0, values.shape[1], 128)]
    return functools.reduce(lambda one, two: one + two, parts)


def to_order(flat, order):
    length, width = flat.shape
    flat = flat.reshape(order + (length // math.prod(order), width))
    return flat.transpose(1, 2, 0, 3, 4).reshape(length, width)


def load_tokens(ref, row, order):
    _, pieces, some, tokens, width = ref.shape
    flat = ref[row // some, :, row % some, :, :].astype(F32)
    return to_order(flat.reshape(pieces * tokens, width), order)


def store_tokens(ref, row, order, values):
    _, pieces, some, tokens, width = ref.shape
    back = (order[1], order[2], order[0])
    flat = values.reshape(back + (pieces * tokens // math.prod(order), width))
    flat = flat.transpose(2, 0, 1, 3, 4).reshape(pieces, tokens, width)
    ref[row // some, :, row % some, :, :] = flat.astype(ref.dtype)


def stacked(ref, start, count):
    return jnp.concatenate([ref[start + n] for n in range(count)], axis=1)


def spread_out(ref, start, count, values):
    length = values.shape[1] // count
    for n in range(count):
        ref[start + n] = values[:, n * length : (n + 1) * length].astype(ref.dtype)


def edges_kernel(order, place_ref, *refs):
    x_refs, (w_ref, gain_ref, shift_ref), rest = refs[:4], refs[4:7], refs[-6:]
    a_ref, b_ref, xt_ref, a_scr, b_scr, x_scr = rest
    width, rows, length = a_ref.shape
    pitch = a_scr.shape[1] // rows
    count = x_scr.shape[0]
    _, some, tokens, _ = x_refs[0].shape

    def step(at, carry):
        start = at * count
        turned = []
        for n in range(count):
            row = start + n
            for m, ref in enumerate(x_refs):
                there = pl.ds(pl.multiple_of(place_ref[m], tokens), tokens)
                x_scr[n, there, :] = ref[row // some, row % some].astype(F32)
            turned.append(to_order(x_scr[n], order).astype(BF).T)
        x0 = jnp.concatenate(turned, axis=1)
        for n in range(count):
            xt_ref[0, start + n] = turned[n]
        hat, _ = normalize(x0.astype(F32))
        lanes = x0.shape[1]
        normed = (hat * widen(gain_ref[...], lanes) + widen(shift_ref[...], lanes)).astype(BF)
        proj = nn(w_ref[...], normed)
        left = sigmoid(proj[width : 2 * width]) * proj[:width]
        right = sigmoid(proj[3 * width : 4 * width]) * proj[2 * width : 3 * width]
        for n in range(count):
            base = pl.multiple_of((start + n) * pitch, 8)
            for half in range(length // 128):
                part = slice(n * length + half * 128, n * length + half * 128 + 128)
                a_scr[half, pl.ds(base, width), :] = left[:, part]
                b_scr[half, pl.ds(base, width), :] = right[:, part]
        return carry

    lax.fori_loop(0, rows // count, step, 0)

    def turn(at, carry):
        for n in range(8):
            e = at * 8 + n
            for scr, out in ((a_scr, a_ref), (b_scr, b_ref)):
                halves = [scr[h, pl.ds(e, rows, stride=pitch), :] for h in range(scr.shape[0])]
                out[e] = jnp.concatenate(halves, axis=1).astype(BF)
        return carry

    lax.fori_loop(0, width // 8, turn, 0)


def edges(place, half, x_pieces, before, order, weight, gain, shift):
    blocks, rows_there, tokens, width = x_pieces[0].shape
    length = len(x_pieces) * tokens
    chunks = order[2]
    groups = order[1] // 2
    some = rows_there // (groups * chunks)
    step = 16 // some
    inner = blocks // step
    rows = blocks * some * chunks
    const = lambda at, place: (0, 0)
    pitch = width + 8
    low = pl.BlockSpec((width, 16, length), lambda at, place: (0, at, 0))
    spec = pl.BlockSpec(
        (step, some, tokens, width),
        lambda at, place: (at % inner, place[4] * chunks + at // inner, 0, 0),
    )
    return pl.pallas_call(
        functools.partial(edges_kernel, order),
        grid_spec=pltpu.PrefetchScalarGridSpec(
            num_scalar_prefetch=1,
            grid=(chunks * inner,),
            in_specs=[spec] * 4
            + [
                pl.BlockSpec(weight.shape, const),
                pl.BlockSpec(gain.shape, const),
                pl.BlockSpec(shift.shape, const),
            ]
            + [pl.BlockSpec(memory_space=pl.ANY)] * len(before),
            out_specs=[low, low, pl.BlockSpec((1, 16, width, length), lambda at, place: (half, at, 0, 0))],
            scratch_shapes=[
                pltpu.VMEM((length // 128, 16 * pitch, 128), F32),
                pltpu.VMEM((length // 128, 16 * pitch, 128), F32),
                pltpu.VMEM((4, length, width), F32),
            ],
        ),
        out_shape=[jax.ShapeDtypeStruct((width, rows, length), BF)] * 2
        + [jax.ShapeDtypeStruct((2, rows, width, length), BF)],
        input_output_aliases={8: 2} if before else {},
        compiler_params=pltpu.CompilerParams(vmem_limit_bytes=VMEM_LIMIT),
        cost_estimate=cost(3.0e9),
        name="edges",
    )(place, *x_pieces, weight, gain, shift, *before)


def gather_pieces(place_ref, rights, e, scr):
    for n, piece in enumerate(rights):
        rows = piece.shape[1]
        scr[e, pl.ds(pl.multiple_of(place_ref[n], rows), rows), :] = piece[e]


def by_channel(ref):
    halves, rows, some, lanes = ref.shape
    return ref.reshape(halves, rows * some, lanes)


def put_channel(ref, e, values):
    halves, rows, some, lanes = ref.shape
    flat = by_channel(ref)
    for half in range(halves):
        flat[half, pl.ds(e, rows, stride=some), :] = values[:, half * lanes : (half + 1) * lanes]


def ahead(first, count, begin, end):
    coming = begin(first)
    for e in range(first, first + count):
        here = coming
        if e + 1 < first + count:
            coming = begin(e + 1)
        end(e, here)


SOME = 16


def cut_refs(refs, *counts):
    parts = []
    for count in counts:
        parts.append(refs[:count])
        refs = refs[count:]
    return parts + list(refs)


def triangle_kernel(place_ref, *refs):
    lefts, rights, t_ref, scr, own_scr = cut_refs(refs, 2, 4)
    for half, left in enumerate(lefts):

        @pl.when(place_ref[4] == half)
        def _():
            own_scr[...] = left[...]

    def begin(e):
        gather_pieces(place_ref, rights, e, scr)
        return nt(own_scr[e], scr[e])

    ahead(0, SOME, begin, functools.partial(put_channel, t_ref))


def high_spec(rows, length):
    return pl.BlockSpec((length // 128, rows, SOME, 128), lambda at, place: (0, 0, at, 0))


def low_spec(rows, lanes):
    return pl.BlockSpec((SOME, rows, lanes), lambda at, place: (at, 0, 0))


def by_halves(rows, width, length):
    return jax.ShapeDtypeStruct((length // 128, rows, width, 128), F32)


def channel_call(kernel, name, flops, scalar, ins, in_specs, out_specs, out_shape, scratch=()):
    return pl.pallas_call(
        kernel,
        grid_spec=pltpu.PrefetchScalarGridSpec(
            num_scalar_prefetch=1,
            grid=(ins[0].shape[0 if ins[0].ndim == 3 else 2] // SOME,),
            in_specs=in_specs,
            out_specs=out_specs,
            scratch_shapes=scratch,
        ),
        out_shape=out_shape,
        compiler_params=pltpu.CompilerParams(vmem_limit_bytes=VMEM_LIMIT),
        cost_estimate=cost(flops),
        name=name,
    )(scalar, *ins)


def triangle(place, lefts, rights):
    width, rows, length = lefts[0].shape
    return channel_call(
        triangle_kernel,
        "triangle",
        3.0e9,
        place,
        (*lefts, *rights),
        [low_spec(rows, length)] * 6,
        high_spec(rows, length),
        by_halves(rows, width, length),
        [pltpu.VMEM((SOME, length, length), BF), pltpu.VMEM((SOME, rows, length), BF)],
    )


def turn_kernel(grad_ref, out_ref):
    halves, rows, some, _ = grad_ref.shape
    flat = by_channel(grad_ref)
    for e in range(some):
        for half in range(halves):
            out_ref[half, e] = flat[half, pl.ds(e, rows, stride=some), :].astype(BF)


def turn(grad):
    halves, rows, width, lanes = grad.shape
    some = 32
    return pl.pallas_call(
        turn_kernel,
        grid=(width // some,),
        in_specs=[pl.BlockSpec((halves, rows, some, lanes), lambda at: (0, 0, at, 0))],
        out_specs=pl.BlockSpec((halves, some, rows, lanes), lambda at: (0, at, 0, 0)),
        out_shape=jax.ShapeDtypeStruct((halves, width, rows, lanes), BF),
        compiler_params=pltpu.CompilerParams(vmem_limit_bytes=VMEM_LIMIT),
        cost_estimate=cost(1.0e9),
        name="turn",
    )(grad)


def right_back_kernel(chunks, here_ref, *refs):
    lefts, grads, db_ref, scr = cut_refs(refs, 4, 2 * chunks)
    rows = db_ref.shape[1]

    def begin(e):
        pairs = [(s, k) for s in range(2) for k in range(2)]
        grad = [grads[2 * c + k][s, e] for s, k in pairs for c in range(chunks)]
        left = [lefts[2 * s + k][e] for s, k in pairs]
        return tn(jnp.concatenate(grad, axis=0), jnp.concatenate(left, axis=0))

    def end(e, db):
        scr[e] = db
        put_channel(db_ref, e, scr[e, pl.ds(pl.multiple_of(here_ref[0], rows), rows), :])

    ahead(0, SOME, begin, end)


def right_back(here, grads, lefts):
    width, rows, length = lefts[0].shape
    chunks = len(grads)
    _, _, some, part = grads[0][0].shape
    both = pl.BlockSpec((2, SOME, some, part), lambda at, here: (0, at, 0, 0))
    return channel_call(
        functools.partial(right_back_kernel, chunks),
        "right_back",
        3.0e9,
        here,
        [*lefts] + [item for chunk in grads for item in chunk],
        [low_spec(rows, length)] * 4 + [both] * (2 * chunks),
        high_spec(rows, length),
        by_halves(rows, width, length),
        [pltpu.VMEM((SOME, part, length), F32)],
    )


def left_back_kernel(chunks, place_ref, *refs):
    rights, grads, da_ref, scr = cut_refs(refs, 4, chunks)

    def begin(e):
        gather_pieces(place_ref, rights, e, scr)
        grad = [jnp.concatenate([ref[0, e], ref[1, e]], axis=1) for ref in grads]
        return nn(jnp.concatenate(grad, axis=0), scr[e])

    ahead(0, SOME, begin, functools.partial(put_channel, da_ref))


def left_back(place, grads, rights):
    _, width, some, part = grads[0].shape
    _, rows, length = rights[0].shape
    both = pl.BlockSpec((2, SOME, some, part), lambda at, place: (0, at, 0, 0))
    return channel_call(
        functools.partial(left_back_kernel, len(grads)),
        "left_back",
        3.0e9,
        place,
        (*rights, *grads),
        [low_spec(rows, length)] * 4 + [both] * len(grads),
        high_spec(rows, length),
        by_halves(rows, width, length),
        [pltpu.VMEM((SOME, length, length), BF)],
    )


def rows_kernel(count, heads, order, first, half_ref, *refs):
    before = []
    if not first:
        before, refs = refs[:3], refs[4:]
    rows_body(count, heads, order, before, *refs)


def rows_body(
    count,
    heads,
    order,
    before,
    t_ref,
    xt_ref,
    cot_ref,
    bias_ref,
    chain_ref,
    lane_ref,
    vec_ref,
    gate_w_ref,
    gate_wt_ref,
    tri_out_ref,
    tri_out_t_ref,
    att_t_ref,
    att_kv_ref,
    att_ref,
    att_out_ref,
    att_out_t_ref,
    up_ref,
    up_t_ref,
    down_ref,
    down_t_ref,
    out_ref,
    dt_ref,
    z_ref,
    g_ref,
    g_vec_ref,
    g_bias_ref,
    e_scr,
):
    _, total_rows, width, length = xt_ref.shape
    head = width // heads
    scaling = 1.0 / math.sqrt(head)

    sums = (g_ref, g_vec_ref, g_bias_ref)
    place = {}
    for name in ("gate", "tri_out", "query", "key", "value", "gate2", "att_out"):
        place[name] = slice(len(place) * width, (len(place) + 1) * width)
    ups = slice(7 * width, 7 * width + up_ref.shape[1])
    downs = [
        slice(at, at + width) for at in range(ups.stop, ups.stop + up_ref.shape[1], width)
    ]

    @pl.when(pl.program_id(0) == 0)
    def _():
        for n, ref in enumerate(sums):
            ref[...] = before[n][...] if before else jnp.zeros(ref.shape, ref.dtype)

    per = length // 128
    mine = [slice(h * head, (h + 1) * head) for h in range(heads)]
    there = [slice(h * length, (h + 1) * length) for h in range(heads)]
    ones = jnp.ones((16, length), BF)
    parts = [slice(p * 128, (p + 1) * 128) for p in range(per)]

    def tiles(n, function, *items):
        results = [function(p, *[item[:, parts[p]] for item in items]) for p in range(per)]
        return [jnp.concatenate(list(column), axis=1) for column in zip(*results)]

    def step(at, carry):
        start = at * count
        rows = range(count)
        side = lambda items: jnp.concatenate(items, axis=1)
        x0, hat1, scale1, normed1, gate_raw = {}, {}, {}, {}, {}
        hat_t, scale_t, mixed, branch = {}, {}, {}, {}
        for n in rows:

            def first(p):
                tile = xt_ref[0, start + n, :, parts[p]].astype(F32)
                hat, scale = normalize(tile)
                return tile, hat, scale, (hat * vec_ref[0] + vec_ref[1]).astype(BF)

            x0[n], hat1[n], scale1[n], normed1[n] = tiles(n, first)
            gate_raw[n] = nn(gate_wt_ref[...], normed1[n])

            def second(p):
                hat, scale = normalize(t_ref[p, start + n])
                return hat, scale, (hat * vec_ref[2] + vec_ref[3]).astype(BF)

            hat_t[n], scale_t[n], mixed[n] = tiles(n, second)
            branch[n] = nn(tri_out_t_ref[...], mixed[n])

        gate1, x1, hat2, scale2, normed2, hidden, kv_tok = {}, {}, {}, {}, {}, {}, {}
        for n in rows:

            def join(p, before, raw, add):
                gate = sigmoid(raw)
                after = before + gate * add
                hat, scale = normalize(after)
                return gate, after, hat, scale, (hat * vec_ref[4] + vec_ref[5]).astype(BF)

            gate1[n], x1[n], hat2[n], scale2[n], normed2[n] = tiles(
                n, join, x0[n], gate_raw[n], branch[n]
            )
            hidden[n] = nn(att_t_ref[...], normed2[n])
            kv_tok[n] = nn(normed2[n].T, att_kv_ref[...])

        query, key, value, gate2 = {}, {}, {}, {}
        for n in rows:

            def split(p, tile):
                gate = sigmoid(tile[3 * width :].astype(BF).astype(F32))
                asked = (tile[:width] * (scaling * LOG2E)).astype(BF)
                return asked, tile[width : 2 * width].astype(BF), tile[2 * width : 3 * width].astype(BF), gate

            query[n], key[n], value[n], gate2[n] = tiles(n, split, hidden[n])
            kv_tok[n] = kv_tok[n].astype(BF)

        pairs = [(n, h) for n in rows for h in range(heads)]

        def scores(n, h):
            return nn(kv_tok[n][:, :width] * lane_ref[h], query[n])

        outs, inverses = {}, {}

        def mix(n, h):
            both = nn(jnp.concatenate([value[n][mine[h]], ones], axis=0), e_scr[n, :, there[h]])
            inverses[n, h] = 1.0 / both[head : head + 1]
            outs[n, h] = both[:head] * inverses[n, h]

        coming = scores(*pairs[0])
        for at_pair, (n, h) in enumerate(pairs):
            score = coming
            if at_pair + 1 < len(pairs):
                coming = scores(*pairs[at_pair + 1])
            score = score + bias_ref[h]
            peak = jnp.max(score, axis=0, keepdims=True)
            e_scr[n, :, there[h]] = jnp.exp2(score - peak).astype(BF)
            if at_pair:
                mix(*pairs[at_pair - 1])
        mix(*pairs[-1])

        attended, gated, x2 = {}, {}, {}
        for n in rows:
            attended[n] = jnp.concatenate([outs[n, h] for h in range(heads)], axis=0)
            (gated[n],) = tiles(n, lambda p, gate, out: ((gate * out).astype(BF),), gate2[n], attended[n])
            x2[n] = nn(att_out_t_ref[...], gated[n])
        hat3, scale3, normed3, up, cot_tok, cot_low, grad_act = {}, {}, {}, {}, {}, {}, {}
        for n in rows:

            def third(p, before, add):
                after = before + add
                hat, scale = normalize(after)
                return after, hat, scale, (hat * vec_ref[6] + vec_ref[7]).astype(BF)

            x2[n], hat3[n], scale3[n], normed3[n] = tiles(n, third, x1[n], x2[n])
            up[n] = nn(up_t_ref[...], normed3[n])
            cot_tok[n] = load_tokens(cot_ref, start + n, order).astype(BF)
            cot_low[n] = cot_tok[n].T
            grad_act[n] = nn(down_ref[...], cot_low[n])
        act, down, grad_up, grad3 = {}, {}, {}, {}
        for n in rows:

            def silu(p, raw, grad):
                gate = sigmoid(raw)
                return (raw * gate).astype(BF), (grad * (gate * (1.0 + raw * (1.0 - gate)))).astype(BF)

            act[n], grad_up[n] = tiles(n, silu, up[n], grad_act[n])
            down[n] = nn(down_t_ref[...], act[n])
            grad3[n] = nn(up_ref[...], grad_up[n])
        grad = nn(side([act[n] for n in rows]), jnp.concatenate([cot_tok[n] for n in rows], axis=0))
        for n, part in enumerate(downs):
            g_ref[:, part] += grad[n * width : (n + 1) * width]
        g_ref[:, ups] += nt(side([normed3[n] for n in rows]), side([grad_up[n] for n in rows]))

        grad_x2, grad_x2_low, grad_gated = {}, {}, {}
        for n in rows:

            def third_back(p, grad_out, grad, hat, scale):
                g_vec_ref[6] += grad * hat
                g_vec_ref[7] += grad
                grad = grad_out.astype(F32) + normalize_back(grad, vec_ref[6], hat, scale)
                return grad, grad.astype(BF)

            grad_x2[n], grad_x2_low[n] = tiles(n, third_back, cot_low[n], grad3[n], hat3[n], scale3[n])
            grad_gated[n] = nn(att_out_ref[...], grad_x2_low[n])
            (out,) = tiles(n, lambda p, one, two: ((one + two).astype(BF),), x2[n], down[n])
            store_tokens(out_ref, start + n, order, out.T.astype(F32))
        g_ref[:, place["att_out"]] += nt(
            side([gated[n] for n in rows]), side([grad_x2_low[n] for n in rows])
        )
        grad_gate2, grad_out, center = {}, {}, {}
        for n in rows:

            def gate_back(p, grad, gate, out):
                mixed_grad = grad * gate
                scaled = [mixed_grad[mine[h]] * inverses[n, h][:, parts[p]] for h in range(heads)]
                low = jnp.concatenate(scaled, axis=0).astype(BF)
                product = low.astype(F32) * out
                centers = [jnp.sum(product[mine[h]], axis=0, keepdims=True) for h in range(heads)]
                return ((mixed_grad * out * (1.0 - gate)).astype(BF), low, *centers)

            grad_gate2[n], grad_out[n], *centers = tiles(n, gate_back, grad_gated[n], gate2[n], attended[n])
            for h in range(heads):
                center[n, h] = centers[h]

        grad_queries, grad_keys, grad_values = {}, {}, {}

        def probs(n, h):
            return nn(kv_tok[n][:, width:] * lane_ref[h], grad_out[n])

        def spread(n, h, grad_score):
            both = nn(jnp.concatenate([key[n][mine[h]], chain_ref[...]], axis=0), grad_score)
            grad_queries[n, h] = (both[:head] * scaling).astype(BF)
            g_bias_ref[h] += both[head:]
            grad_keys[n, h] = (nt(query[n][mine[h]], grad_score) * LN2).astype(BF)

        coming, behind = probs(*pairs[0]), None
        for at_pair, (n, h) in enumerate(pairs):
            grad_prob = coming
            if at_pair + 1 < len(pairs):
                coming = probs(*pairs[at_pair + 1])
            expon = e_scr[n, :, there[h]]
            grad_score = (expon.astype(F32) * (grad_prob - center[n, h])).astype(BF)
            grad_values[n, h] = nt(grad_out[n][mine[h]], expon).astype(BF)
            if behind is not None:
                spread(*behind)
            behind = (n, h, grad_score)
        spread(*behind)

        grad_hidden, grad2 = {}, {}
        for n in rows:
            blocks = [items[n, h] for items in (grad_queries, grad_keys, grad_values) for h in range(heads)]
            grad_hidden[n] = jnp.concatenate(blocks + [grad_gate2[n]], axis=0)
            grad2[n] = nn(att_ref[...], grad_hidden[n])
        g_ref[:, place["query"].start : place["gate2"].stop] += nt(
            side([normed2[n] for n in rows]), side([grad_hidden[n] for n in rows])
        )
        grad_x1, grad_branch, grad_gate1, grad_mix, grad1 = {}, {}, {}, {}, {}
        for n in rows:

            def second_back(p, grad_after, grad, hat, scale, gate, added):
                g_vec_ref[4] += grad * hat
                g_vec_ref[5] += grad
                grad = grad_after + normalize_back(grad, vec_ref[4], hat, scale)
                gated_grad = grad * gate
                return grad, gated_grad.astype(BF), (gated_grad * added * (1.0 - gate)).astype(BF)

            grad_x1[n], grad_branch[n], grad_gate1[n] = tiles(
                n, second_back, grad_x2[n], grad2[n], hat2[n], scale2[n], gate1[n], branch[n]
            )
            grad_mix[n] = nn(tri_out_ref[...], grad_branch[n])
            grad1[n] = nn(gate_w_ref[...], grad_gate1[n])
        g_ref[:, place["tri_out"]] += nt(
            side([mixed[n] for n in rows]), side([grad_branch[n] for n in rows])
        )
        g_ref[:, place["gate"]] += nt(
            side([normed1[n] for n in rows]), side([grad_gate1[n] for n in rows])
        )
        for n in rows:
            for p, part in enumerate(parts):
                grad, hat, scale = grad_mix[n][:, part], hat_t[n][:, part], scale_t[n][:, part]
                g_vec_ref[2] += grad * hat
                g_vec_ref[3] += grad
                dt_ref[p, start + n] = normalize_back(grad, vec_ref[2], hat, scale)
                grad, hat, scale = grad1[n][:, part], hat1[n][:, part], scale1[n][:, part]
                g_vec_ref[0] += grad * hat
                g_vec_ref[1] += grad
                grad = grad_x1[n][:, part] + normalize_back(grad, vec_ref[0], hat, scale)
                z_ref[start + n, :, part] = grad
        return carry

    lax.fori_loop(0, total_rows // count, step, 0)


def rows_pass(c, chunks, half, before, t, xt, cot_rows, order, bias, chain, lane, vecs, weights, heads):
    _, all_rows, width, length = xt.shape
    blocks, pieces, sub, tokens, _ = cot_rows.shape
    rows = blocks * sub
    some, count = 4, 4
    inner = sub // some
    full = lambda item: pl.BlockSpec(item.shape, lambda at, half: (0,) * item.ndim)
    of_all = pl.BlockSpec((some, width, length), lambda at, half: (c * (rows // some) + at, 0, 0))
    xt_some = pl.BlockSpec(
        (1, some, width, length), lambda at, half: (half[0], c * (rows // some) + at, 0, 0)
    )
    t_some = pl.BlockSpec(
        (length // 128, some, width, 128), lambda at, half: (0, c * (rows // some) + at, 0, 0)
    )
    dt_some = pl.BlockSpec((length // 128, some, width, 128), lambda at, half: (0, at, 0, 0))
    by_piece = pl.BlockSpec(
        (1, pieces, some, tokens, width), lambda at, half: (at // inner, 0, at % inner, 0, 0)
    )
    consts = (bias, chain, lane, vecs) + weights
    wide = weights[-1].shape[1]
    sum_shapes = [
        jax.ShapeDtypeStruct(shape, F32)
        for shape in ((width, 7 * width + 2 * wide), (8, width, 128), (heads, 16, length))
    ]
    before_specs = [full(item) for item in before[:3]]
    before_specs += [pl.BlockSpec(memory_space=pl.ANY)] * len(before[3:])
    return pl.pallas_call(
        functools.partial(rows_kernel, count, heads, order, c == 0),
        grid_spec=pltpu.PrefetchScalarGridSpec(
            num_scalar_prefetch=1,
            grid=(rows // some,),
            in_specs=before_specs + [t_some, xt_some, by_piece] + [full(item) for item in consts],
            out_specs=[by_piece, dt_some, of_all] + [full(item) for item in sum_shapes],
            scratch_shapes=[
                pltpu.VMEM((count, length, heads * length), BF),
            ],
        ),
        out_shape=[
            jax.ShapeDtypeStruct(cot_rows.shape, BF),
            by_halves(rows, width, length),
            jax.ShapeDtypeStruct((all_rows, width, length), F32),
        ]
        + sum_shapes,
        input_output_aliases={4: 2} if before else {},
        compiler_params=pltpu.CompilerParams(vmem_limit_bytes=VMEM_LIMIT),
        cost_estimate=cost(8.0e10),
        name="rows",
    )(half, *before, t, xt, cot_rows, *consts)


def edges_back_kernel(
    order, half_ref, xt_ref, z_ref, da_ref, db_ref, wt_ref, w_ref, gain_ref, shift_ref, out_ref, g_w_ref, g_vec_ref
):
    _, rows, width, length = xt_ref.shape
    count = 4

    @pl.when(pl.program_id(0) == 0)
    def _():
        g_w_ref[...] = jnp.zeros(g_w_ref.shape, F32)
        g_vec_ref[...] = jnp.zeros(g_vec_ref.shape, F32)

    def step(at, carry):
        start = at * count
        x0 = stacked(xt_ref.at[0], start, count).astype(F32)
        lanes = x0.shape[1]
        gain = widen(gain_ref[...], lanes)
        hat, scale = normalize(x0)
        normed = (hat * gain + widen(shift_ref[...], lanes)).astype(BF)
        proj = nn(wt_ref[...], normed)
        pa, pag = proj[:width], proj[width : 2 * width]
        pb, pbg = proj[2 * width : 3 * width], proj[3 * width :]
        halves = [(n, half) for n in range(count) for half in range(da_ref.shape[0])]
        da = jnp.concatenate([da_ref[half, start + n] for n, half in halves], axis=1)
        db = jnp.concatenate([db_ref[half, start + n] for n, half in halves], axis=1)
        sa, sb = sigmoid(pag), sigmoid(pbg)
        dsa, dsb = da * sa, db * sb
        grads = jnp.concatenate(
            [
                dsa.astype(BF),
                (dsa * pa * (1.0 - sa)).astype(BF),
                dsb.astype(BF),
                (dsb * pb * (1.0 - sb)).astype(BF),
            ],
            axis=0,
        )
        g_w_ref[...] += nt(normed, grads)
        grad = nn(w_ref[...], grads)
        g_vec_ref[0] += fold(grad * hat)
        g_vec_ref[1] += fold(grad)
        out = stacked(z_ref, start, count) + normalize_back(grad, gain, hat, scale)
        out = out.astype(BF)
        for n in range(count):
            store_tokens(out_ref, start + n, order, out[:, n * length : (n + 1) * length].T.astype(F32))
        return carry

    lax.fori_loop(0, rows // count, step, 0)


def edges_back(half, xt, z, da, db, order, weight_t, weight, gain, shift, shape):
    _, rows, width, length = xt.shape
    blocks, pieces, sub, tokens, _ = shape
    chunks = order[2]
    some = sub // chunks
    step = 16 // some
    inner = blocks // step
    full = lambda item: pl.BlockSpec(item.shape, lambda at, half: (0,) * item.ndim)
    xt_row = pl.BlockSpec((1, 16, width, length), lambda at, half: (half[0], at, 0, 0))
    by_row = pl.BlockSpec((16, width, length), lambda at, half: (at, 0, 0))
    by_half = pl.BlockSpec((length // 128, 16, width, 128), lambda at, half: (0, at, 0, 0))
    sum_shapes = [
        jax.ShapeDtypeStruct(weight.shape, F32),
        jax.ShapeDtypeStruct((2, width, 128), F32),
    ]
    by_piece = pl.BlockSpec(
        (step, pieces, some, tokens, width), lambda at, half: (at % inner, 0, at // inner, 0, 0)
    )
    return pl.pallas_call(
        functools.partial(edges_back_kernel, order),
        grid_spec=pltpu.PrefetchScalarGridSpec(
            num_scalar_prefetch=1,
            grid=(chunks * inner,),
            in_specs=[xt_row, by_row] + [by_half] * 2 + [full(item) for item in (weight_t, weight, gain, shift)],
            out_specs=[by_piece] + [full(item) for item in sum_shapes],
        ),
        out_shape=[jax.ShapeDtypeStruct(shape, BF)] + sum_shapes,
        compiler_params=pltpu.CompilerParams(vmem_limit_bytes=VMEM_LIMIT),
        cost_estimate=cost(5.0e9),
        name="edges_back",
    )(half, xt, z, da, db, weight_t, weight, gain, shift)


def shards(
    row_size,
    col_size,
    pair_state,
    cotangent,
    chain_lengths,
    tri_gain,
    tri_shift,
    tri_weight,
    mix_gain,
    mix_shift,
    tri_out,
    att_gain,
    att_shift,
    att_weight,
    chain_bias,
    att_out,
    trans_gain,
    trans_shift,
    up_weight,
    down_weight,
):
    heads = HEADS
    crops, own_rows, tokens, width = pair_state.shape
    length = col_size * tokens
    chunks = CHUNKS
    some = own_rows // (col_size * chunks)
    axes = ("row", "col")
    group = row_size * col_size
    order = (row_size, col_size, chunks)
    shape = (row_size, col_size, some, tokens, width)

    def swap(values):
        return lax.all_to_all(values, axes, split_axis=0, concat_axis=0, tiled=True)

    def cut(values):
        parts = values.reshape(group, chunks, some, tokens, width)
        return [parts[:, c] for c in range(chunks)]

    def join(parts):
        return jnp.stack(parts, axis=1).reshape(crops, own_rows, tokens, width)

    def across(values, bit):
        return lax.ppermute(values, "col", [(q, q ^ bit) for q in range(col_size)])

    bits = [1 << n for n in range(col_size.bit_length() - 1)]

    def after(values, *others):
        return lax.optimization_barrier((values,) + others)[0]

    def gather(own, far, *late):
        pieces = {0: own, far_bit: across(far, far_bit)}
        arrived = pieces[far_bit]
        if late:
            pieces[far_bit] = after(arrived, *late)
        for bit in reversed(bits[:-1]):
            for m in list(pieces):
                pieces[m ^ bit] = across(pieces[m], bit)
        return [pieces[m] for m in range(col_size)], arrived

    def doubled(items, axis, size, bits):
        for bit in bits:
            lows = [values.astype(sent) for values, sent in items]
            others = [lax.ppermute(low, axis, [(q, q ^ bit) for q in range(size)]) for low in lows]
            others = lax.optimization_barrier(tuple(others))
            items = [
                (low.astype(F32) + other.astype(F32), sent)
                for low, other, (_, sent) in zip(lows, others, items)
            ]
        return items

    whole = (row_size, col_size, some * chunks, tokens, width)
    cot_parts = cut(cotangent)

    wide = lambda item: jnp.broadcast_to(item[:, None], (width, 128))
    vecs = jnp.stack(
        [
            wide(item)
            for item in (
                tri_gain,
                tri_shift,
                mix_gain,
                mix_shift,
                att_gain,
                att_shift,
                trans_gain,
                trans_shift,
            )
        ]
    )
    edge_w = tri_weight[:, : 4 * width]
    edge_wt = edge_w.T
    gate_w = tri_weight[:, 4 * width :]
    lengths = lax.dynamic_index_in_dim(chain_lengths, lax.axis_index("row"), 0, keepdims=False)
    ends = jnp.cumsum(lengths)
    places = jnp.arange(length, dtype=jnp.int32)
    places = places.reshape(order + (some,)).transpose(1, 2, 0, 3).reshape(length)
    chain = jnp.sum((places[:, None] >= ends[None, :]).astype(jnp.int32), axis=-1)
    same = (chain[:, None] == chain[None, :]).astype(F32)
    bias = (LOG2E * chain_bias)[:, None, None] * same[None]
    which = (jnp.arange(16, dtype=jnp.int32)[:, None] == chain[None, :]).astype(F32)
    head_of = jnp.arange(width, dtype=jnp.int32) // (width // heads)
    lane = (jnp.arange(heads, dtype=jnp.int32)[:, None] == head_of[None, :]).astype(BF)
    lane = jnp.broadcast_to(lane[:, None, :], (heads, length, width))
    me = lax.axis_index("col")
    own = own_rows
    far_bit = col_size // 2
    half, core = me // far_bit, me % far_bit
    token_place = jnp.stack([(me ^ m) * tokens for m in range(col_size)] + [core])
    place = [(s * far_bit + (core ^ k)) * own for s in range(2) for k in range(2)]
    place = jnp.stack(place + [half])
    here = (core * own).reshape(1)
    half_at = half.reshape(1)
    weights = (
        gate_w,
        gate_w.T,
        tri_out,
        tri_out.T,
        att_weight.T,
        att_weight[:, width : 3 * width],
        att_weight,
        att_out,
        att_out.T,
        up_weight,
        up_weight.T,
        down_weight,
        down_weight.T,
    )
    chain_rows = which.astype(BF)

    x_parts = jnp.split(pair_state, 2, axis=1)
    lefts, rights, xt, cot_rows, early = [], [], [], [], (edge_wt, vecs, bias, lane, cot_parts[0])
    x_z = []
    for part in x_parts:
        part = after(part, *x_z)
        x_z.append(lax.all_to_all(part, "row", split_axis=0, concat_axis=0, tiled=True))
        if len(x_z) == 1:
            x_z = [after(x_z[0], *early)]
    cot_rows.append(swap(after(cot_parts[0], x_z[1])).reshape(shape))
    for s, part in enumerate(x_z):
        far = across(part, far_bit)
        pieces = [part, across(part, 1), far, across(far, 1)]
        if s:
            pieces[0] = after(pieces[0], cot_rows[0])
        left, right, *xt = edges(token_place, s, pieces, xt, order, edge_wt, vecs[0], vecs[1])
        lefts.append(left)
        rights += [right, across(right, 1)]
    (xt,) = xt
    t = triangle(place, lefts, rights)
    lefts = [item for left in lefts for item in (left, across(after(left, t), 1))]
    for part in cot_parts[1:]:
        cot_rows.append(swap(after(part, t, cot_rows[-1])).reshape(shape))
    state, outs, dts, sent = [], [], [], []
    pairs = [[q, q + far_bit] for q in range(far_bit)]
    for c in range(chunks):
        out, dt, z, *sums = rows_pass(
            c, chunks, half_at, state, t, xt, cot_rows[c], order, bias, chain_rows, lane, vecs, weights, heads
        )
        state = sums + [z]
        dt = turn(dt)
        if c < chunks - 1:
            dts.append(dt)
            outs.append(swap(out.reshape(group, some, tokens, width)))
            near = lax.dynamic_index_in_dim(dt, half, 0, keepdims=False)
            sent.append((near, across(lax.dynamic_index_in_dim(dt, 1 - half, 0, keepdims=False), far_bit)))
    dt = after(dt, *outs)
    dts.append(dt)
    crossed = []
    for near, far in sent:
        near, far = after(near, z), after(far, z)
        crossed.append(jnp.where(half == 0, jnp.stack([near, far]), jnp.stack([far, near])))
    crossed.append(
        lax.all_to_all(dt, "col", split_axis=0, concat_axis=0, axis_index_groups=pairs, tiled=True)
    )
    g_rows, g_vec, g_bias = sums
    row_bits = [1 << n for n in range(row_size.bit_length() - 1)]
    ((g_rows, _),) = doubled([(g_rows, BF)], "row", row_size, row_bits)
    da = left_back(place, dts, rights)
    grads = [[item, across(item, 1)] for item in crossed[:-1]]
    grads.append([crossed[-1], across(after(crossed[-1], da), 1)])
    outs.append(swap(after(out, crossed[-1]).reshape(group, some, tokens, width)))
    pair_out = join(outs)
    db = right_back(here, grads, [after(lefts[0], g_rows)] + lefts[1:])
    back, g_edge, g_vec_edge = edges_back(
        half_at, xt, z, da, db, order, edge_wt, edge_w, vecs[0], vecs[1], whole
    )
    g_vec = jnp.sum(g_vec, axis=-1)
    g_vec_edge = jnp.sum(g_vec_edge, axis=-1)
    g_chain = jnp.sum(g_bias * which[None], axis=(1, 2))
    small = jnp.concatenate(
        [g_vec[:2] + g_vec_edge, g_vec[2:], jnp.pad(g_chain, (0, width - heads))[None]], axis=0
    )
    items = doubled([(g_edge, BF), (small, F32)], "row", row_size, row_bits)
    back = after(back, *[values for values, _ in items])
    grad_pair = swap(back.reshape(group, some * chunks, tokens, width))
    grad_pair = grad_pair.reshape(crops, own_rows, tokens, width)
    items = doubled(items + [(after(g_rows, pair_out), BF)], "col", col_size, bits[::-1])
    t_edge, small, total = [values for values, _ in items]
    column = lambda at, n=1: total[:, at * width : (at + n) * width]
    ff = up_weight.shape[1] // width
    t_gate, t_tri_out, t_att = column(0), column(1), column(2, 4)
    t_att_out, t_up = column(6), column(7, ff)
    t_down = jnp.concatenate([column(7 + ff + n) for n in range(ff)], axis=0)
    return (
        pair_out,
        grad_pair,
        small[0],
        small[1],
        jnp.concatenate([t_edge, t_gate], axis=1),
        small[2],
        small[3],
        t_tri_out,
        small[4],
        small[5],
        t_att,
        small[8, :heads],
        t_att_out,
        small[6],
        small[7],
        t_up,
        t_down,
    )


def solution(mesh):
    pair = P("dp", "row", "col", None)
    vector, matrix = P("dp"), P("dp", None)
    return jax.shard_map(
        functools.partial(shards, mesh.shape["row"], mesh.shape["col"]),
        mesh=mesh,
        in_specs=(pair, pair, P("dp", None)) + (P(),) * 15,
        out_specs=(
            pair,
            pair,
            vector,
            vector,
            matrix,
            vector,
            vector,
            matrix,
            vector,
            vector,
            matrix,
            vector,
            matrix,
            vector,
            vector,
            matrix,
            matrix,
        ),
        check_vma=False,
    )
```

```python
import functools
import math

import jax
import jax.numpy as jnp
from jax import lax
from jax.experimental import pallas as pl
from jax.experimental.pallas import tpu as pltpu
from jax.sharding import PartitionSpec as P

HEADS = 4
EPS = 1e-05
LOG2E = math.log2(math.e)
LN2 = math.log(2.0)
CHUNKS = 2
VMEM_LIMIT = 56 * 1024 * 1024
BF = jnp.bfloat16
F32 = jnp.float32


def nn(left, right):
    return lax.dot_general(left, right, (((1,), (0,)), ((), ())), preferred_element_type=F32)


def nt(left, right):
    return lax.dot_general(left, right, (((1,), (1,)), ((), ())), preferred_element_type=F32)


def tn(left, right):
    return lax.dot_general(left, right, (((0,), (0,)), ((), ())), preferred_element_type=F32)


def cost(flops, size=0):
    return pl.CostEstimate(flops=int(flops), bytes_accessed=int(size), transcendentals=0)


def sigmoid(values):
    return 0.5 * jnp.tanh(0.5 * values) + 0.5


def normalize(values):
    center = values - jnp.mean(values, axis=0, keepdims=True)
    spread = jnp.mean(center * center, axis=0, keepdims=True)
    scale = lax.rsqrt(spread + EPS)
    return center * scale, scale


def normalize_back(grads, gain, hat, scale):
    grad_hat = grads * gain
    first = jnp.mean(grad_hat, axis=0, keepdims=True)
    second = jnp.mean(grad_hat * hat, axis=0, keepdims=True)
    return scale * (grad_hat - first - hat * second)


def widen(column, lanes):
    return jnp.concatenate([column] * (lanes // column.shape[1]), axis=1)


def fold(values):
    parts = [values[:, at : at + 128] for at in range(0, values.shape[1], 128)]
    return functools.reduce(lambda one, two: one + two, parts)


def to_order(flat, order):
    length, width = flat.shape
    flat = flat.reshape(order + (length // math.prod(order), width))
    return flat.transpose(1, 2, 0, 3, 4).reshape(length, width)


def load_tokens(ref, row, order):
    _, pieces, some, tokens, width = ref.shape
    flat = ref[row // some, :, row % some, :, :].astype(F32)
    return to_order(flat.reshape(pieces * tokens, width), order)


def store_tokens(ref, row, order, values):
    _, pieces, some, tokens, width = ref.shape
    back = (order[1], order[2], order[0])
    flat = values.reshape(back + (pieces * tokens // math.prod(order), width))
    flat = flat.transpose(2, 0, 1, 3, 4).reshape(pieces, tokens, width)
    ref[row // some, :, row % some, :, :] = flat.astype(ref.dtype)


def stacked(ref, start, count):
    return jnp.concatenate([ref[start + n] for n in range(count)], axis=1)


def spread_out(ref, start, count, values):
    length = values.shape[1] // count
    for n in range(count):
        ref[start + n] = values[:, n * length : (n + 1) * length].astype(ref.dtype)


def edges_kernel(order, place_ref, *refs):
    x_refs, (w_ref, gain_ref, shift_ref), rest = refs[:4], refs[4:7], refs[-6:]
    a_ref, b_ref, xt_ref, a_scr, b_scr, x_scr = rest
    width, rows, length = a_ref.shape
    pitch = a_scr.shape[1] // rows
    count = x_scr.shape[0]
    _, some, tokens, _ = x_refs[0].shape

    def step(at, carry):
        start = at * count
        turned = []
        for n in range(count):
            row = start + n
            for m, ref in enumerate(x_refs):
                there = pl.ds(pl.multiple_of(place_ref[m], tokens), tokens)
                x_scr[n, there, :] = ref[row // some, row % some].astype(F32)
            turned.append(to_order(x_scr[n], order).astype(BF).T)
        x0 = jnp.concatenate(turned, axis=1)
        for n in range(count):
            xt_ref[0, start + n] = turned[n]
        hat, _ = normalize(x0.astype(F32))
        lanes = x0.shape[1]
        normed = (hat * widen(gain_ref[...], lanes) + widen(shift_ref[...], lanes)).astype(BF)
        proj = nn(w_ref[...], normed)
        left = sigmoid(proj[width : 2 * width]) * proj[:width]
        right = sigmoid(proj[3 * width : 4 * width]) * proj[2 * width : 3 * width]
        for n in range(count):
            base = pl.multiple_of((start + n) * pitch, 8)
            for half in range(length // 128):
                part = slice(n * length + half * 128, n * length + half * 128 + 128)
                a_scr[half, pl.ds(base, width), :] = left[:, part]
                b_scr[half, pl.ds(base, width), :] = right[:, part]
        return carry

    lax.fori_loop(0, rows // count, step, 0)

    def turn(at, carry):
        for n in range(8):
            e = at * 8 + n
            for scr, out in ((a_scr, a_ref), (b_scr, b_ref)):
                halves = [scr[h, pl.ds(e, rows, stride=pitch), :] for h in range(scr.shape[0])]
                out[e] = jnp.concatenate(halves, axis=1).astype(BF)
        return carry

    lax.fori_loop(0, width // 8, turn, 0)


def edges(place, half, x_pieces, before, order, weight, gain, shift):
    blocks, rows_there, tokens, width = x_pieces[0].shape
    length = len(x_pieces) * tokens
    chunks = order[2]
    some = rows_there // chunks
    step = 16 // some
    inner = blocks // step
    rows = blocks * some * chunks
    const = lambda at, place: (0, 0)
    pitch = width + 8
    low = pl.BlockSpec((width, 16, length), lambda at, place: (0, at, 0))
    spec = pl.BlockSpec(
        (step, some, tokens, width),
        lambda at, place: (at % inner, at // inner, 0, 0),
    )
    return pl.pallas_call(
        functools.partial(edges_kernel, order),
        grid_spec=pltpu.PrefetchScalarGridSpec(
            num_scalar_prefetch=1,
            grid=(chunks * inner,),
            in_specs=[spec] * 4
            + [
                pl.BlockSpec(weight.shape, const),
                pl.BlockSpec(gain.shape, const),
                pl.BlockSpec(shift.shape, const),
            ]
            + [pl.BlockSpec(memory_space=pl.ANY)] * len(before),
            out_specs=[low, low, pl.BlockSpec((1, 16, width, length), lambda at, place: (half, at, 0, 0))],
            scratch_shapes=[
                pltpu.VMEM((length // 128, 16 * pitch, 128), F32),
                pltpu.VMEM((length // 128, 16 * pitch, 128), F32),
                pltpu.VMEM((4, length, width), F32),
            ],
        ),
        out_shape=[jax.ShapeDtypeStruct((width, rows, length), BF)] * 2
        + [jax.ShapeDtypeStruct((2, rows, width, length), BF)],
        input_output_aliases={8: 2} if before else {},
        compiler_params=pltpu.CompilerParams(vmem_limit_bytes=VMEM_LIMIT),
        cost_estimate=cost(2.2e10),
        name="edges",
    )(place, *x_pieces, weight, gain, shift, *before)


def gather_pieces(place_ref, rights, e, scr):
    for n, piece in enumerate(rights):
        rows = piece.shape[1]
        scr[e, pl.ds(pl.multiple_of(place_ref[n], rows), rows), :] = piece[e]


def by_channel(ref):
    halves, rows, some, lanes = ref.shape
    return ref.reshape(halves, rows * some, lanes)


def put_channel(ref, e, values):
    halves, rows, some, lanes = ref.shape
    flat = by_channel(ref)
    for half in range(halves):
        flat[half, pl.ds(e, rows, stride=some), :] = values[:, half * lanes : (half + 1) * lanes]


def ahead(first, count, begin, end):
    coming = begin(first)
    for e in range(first, first + count):
        here = coming
        if e + 1 < first + count:
            coming = begin(e + 1)
        end(e, here)


SOME = 16


def cut_refs(refs, *counts):
    parts = []
    for count in counts:
        parts.append(refs[:count])
        refs = refs[count:]
    return parts + list(refs)


def triangle_kernel(place_ref, *refs):
    lefts, rights, t_ref, scr, own_scr = cut_refs(refs, 2, 4)
    for half, left in enumerate(lefts):

        @pl.when(place_ref[4] == half)
        def _():
            own_scr[...] = left[...]

    def begin(e):
        gather_pieces(place_ref, rights, e, scr)
        return nt(own_scr[e], scr[e])

    ahead(0, SOME, begin, functools.partial(put_channel, t_ref))


def high_spec(rows, length):
    return pl.BlockSpec((length // 128, rows, SOME, 128), lambda at, place: (0, 0, at, 0))


def low_spec(rows, lanes):
    return pl.BlockSpec((SOME, rows, lanes), lambda at, place: (at, 0, 0))


def by_halves(rows, width, length):
    return jax.ShapeDtypeStruct((length // 128, rows, width, 128), F32)


def channel_call(kernel, name, flops, scalar, ins, in_specs, out_specs, out_shape, scratch=()):
    return pl.pallas_call(
        kernel,
        grid_spec=pltpu.PrefetchScalarGridSpec(
            num_scalar_prefetch=1,
            grid=(ins[0].shape[0 if ins[0].ndim == 3 else 2] // SOME,),
            in_specs=in_specs,
            out_specs=out_specs,
            scratch_shapes=scratch,
        ),
        out_shape=out_shape,
        compiler_params=pltpu.CompilerParams(vmem_limit_bytes=VMEM_LIMIT),
        cost_estimate=cost(flops),
        name=name,
    )(scalar, *ins)


def triangle(place, lefts, rights):
    width, rows, length = lefts[0].shape
    return channel_call(
        triangle_kernel,
        "triangle",
        2.0e10,
        place,
        (*lefts, *rights),
        [low_spec(rows, length)] * 6,
        high_spec(rows, length),
        by_halves(rows, width, length),
        [pltpu.VMEM((SOME, length, length), BF), pltpu.VMEM((SOME, rows, length), BF)],
    )


def turn_kernel(grad_ref, out_ref):
    halves, rows, some, _ = grad_ref.shape
    flat = by_channel(grad_ref)
    for e in range(some):
        for half in range(halves):
            out_ref[half, e] = flat[half, pl.ds(e, rows, stride=some), :].astype(BF)


def turn(grad):
    halves, rows, width, lanes = grad.shape
    some = 32
    return pl.pallas_call(
        turn_kernel,
        grid=(width // some,),
        in_specs=[pl.BlockSpec((halves, rows, some, lanes), lambda at: (0, 0, at, 0))],
        out_specs=pl.BlockSpec((halves, some, rows, lanes), lambda at: (0, at, 0, 0)),
        out_shape=jax.ShapeDtypeStruct((halves, width, rows, lanes), BF),
        compiler_params=pltpu.CompilerParams(vmem_limit_bytes=VMEM_LIMIT),
        cost_estimate=cost(5.0e9),
        name="turn",
    )(grad)


def right_back_kernel(chunks, here_ref, *refs):
    lefts, grads, db_ref, scr = cut_refs(refs, 4, 2 * chunks)
    rows = db_ref.shape[1]

    def begin(e):
        pairs = [(s, k) for s in range(2) for k in range(2)]
        grad = [grads[2 * c + k][s, e] for s, k in pairs for c in range(chunks)]
        left = [lefts[2 * s + k][e] for s, k in pairs]
        return tn(jnp.concatenate(grad, axis=0), jnp.concatenate(left, axis=0))

    def end(e, db):
        scr[e] = db
        put_channel(db_ref, e, scr[e, pl.ds(pl.multiple_of(here_ref[0], rows), rows), :])

    ahead(0, SOME, begin, end)


def right_back(here, grads, lefts):
    width, rows, length = lefts[0].shape
    chunks = len(grads)
    _, _, some, part = grads[0][0].shape
    both = pl.BlockSpec((2, SOME, some, part), lambda at, here: (0, at, 0, 0))
    return channel_call(
        functools.partial(right_back_kernel, chunks),
        "right_back",
        2.2e10,
        here,
        [*lefts] + [item for chunk in grads for item in chunk],
        [low_spec(rows, length)] * 4 + [both] * (2 * chunks),
        high_spec(rows, length),
        by_halves(rows, width, length),
        [pltpu.VMEM((SOME, part, length), F32)],
    )


def left_back_kernel(chunks, place_ref, *refs):
    rights, grads, da_ref, scr = cut_refs(refs, 4, chunks)

    def begin(e):
        gather_pieces(place_ref, rights, e, scr)
        grad = [jnp.concatenate([ref[0, e], ref[1, e]], axis=1) for ref in grads]
        return nn(jnp.concatenate(grad, axis=0), scr[e])

    ahead(0, SOME, begin, functools.partial(put_channel, da_ref))


def left_back(place, grads, rights):
    _, width, some, part = grads[0].shape
    _, rows, length = rights[0].shape
    both = pl.BlockSpec((2, SOME, some, part), lambda at, place: (0, at, 0, 0))
    return channel_call(
        functools.partial(left_back_kernel, len(grads)),
        "left_back",
        2.0e10,
        place,
        (*rights, *grads),
        [low_spec(rows, length)] * 4 + [both] * len(grads),
        high_spec(rows, length),
        by_halves(rows, width, length),
        [pltpu.VMEM((SOME, length, length), BF)],
    )


def rows_kernel(count, heads, order, first, half_ref, *refs):
    before = []
    if not first:
        before, refs = refs[:3], refs[4:]
    rows_body(count, heads, order, before, *refs)


def rows_body(
    count,
    heads,
    order,
    before,
    t_ref,
    xt_ref,
    cot_ref,
    bias_ref,
    chain_ref,
    lane_ref,
    vec_ref,
    gate_w_ref,
    gate_wt_ref,
    tri_out_ref,
    tri_out_t_ref,
    att_t_ref,
    att_kv_ref,
    att_ref,
    att_out_ref,
    att_out_t_ref,
    up_ref,
    up_t_ref,
    down_ref,
    down_t_ref,
    out_ref,
    dt_ref,
    z_ref,
    g_ref,
    g_vec_ref,
    g_bias_ref,
    e_scr,
):
    _, total_rows, width, length = xt_ref.shape
    head = width // heads
    scaling = 1.0 / math.sqrt(head)

    sums = (g_ref, g_vec_ref, g_bias_ref)
    place = {}
    for name in ("gate", "tri_out", "query", "key", "value", "gate2", "att_out"):
        place[name] = slice(len(place) * width, (len(place) + 1) * width)
    ups = slice(7 * width, 7 * width + up_ref.shape[1])
    downs = [
        slice(at, at + width) for at in range(ups.stop, ups.stop + up_ref.shape[1], width)
    ]

    @pl.when(pl.program_id(0) == 0)
    def _():
        for n, ref in enumerate(sums):
            ref[...] = before[n][...] if before else jnp.zeros(ref.shape, ref.dtype)

    per = length // 128
    mine = [slice(h * head, (h + 1) * head) for h in range(heads)]
    there = [slice(h * length, (h + 1) * length) for h in range(heads)]
    ones = jnp.ones((16, length), BF)
    parts = [slice(p * 128, (p + 1) * 128) for p in range(per)]

    def tiles(n, function, *items):
        results = [function(p, *[item[:, parts[p]] for item in items]) for p in range(per)]
        return [jnp.concatenate(list(column), axis=1) for column in zip(*results)]

    def step(at, carry):
        start = at * count
        rows = range(count)
        side = lambda items: jnp.concatenate(items, axis=1)
        x0, hat1, scale1, normed1, gate_raw = {}, {}, {}, {}, {}
        hat_t, scale_t, mixed, branch = {}, {}, {}, {}
        for n in rows:

            def first(p):
                tile = xt_ref[0, start + n, :, parts[p]].astype(F32)
                hat, scale = normalize(tile)
                return tile, hat, scale, (hat * vec_ref[0] + vec_ref[1]).astype(BF)

            x0[n], hat1[n], scale1[n], normed1[n] = tiles(n, first)
            gate_raw[n] = nn(gate_wt_ref[...], normed1[n])

            def second(p):
                hat, scale = normalize(t_ref[p, start + n])
                return hat, scale, (hat * vec_ref[2] + vec_ref[3]).astype(BF)

            hat_t[n], scale_t[n], mixed[n] = tiles(n, second)
            branch[n] = nn(tri_out_t_ref[...], mixed[n])

        gate1, x1, hat2, scale2, normed2, hidden, kv_tok = {}, {}, {}, {}, {}, {}, {}
        for n in rows:

            def join(p, before, raw, add):
                gate = sigmoid(raw)
                after = before + gate * add
                hat, scale = normalize(after)
                return gate, after, hat, scale, (hat * vec_ref[4] + vec_ref[5]).astype(BF)

            gate1[n], x1[n], hat2[n], scale2[n], normed2[n] = tiles(
                n, join, x0[n], gate_raw[n], branch[n]
            )
            hidden[n] = nn(att_t_ref[...], normed2[n])
            kv_tok[n] = nn(normed2[n].T, att_kv_ref[...])

        query, key, value, gate2 = {}, {}, {}, {}
        for n in rows:

            def split(p, tile):
                gate = sigmoid(tile[3 * width :].astype(BF).astype(F32))
                asked = (tile[:width] * (scaling * LOG2E)).astype(BF)
                return asked, tile[width : 2 * width].astype(BF), tile[2 * width : 3 * width].astype(BF), gate

            query[n], key[n], value[n], gate2[n] = tiles(n, split, hidden[n])
            kv_tok[n] = kv_tok[n].astype(BF)

        pairs = [(n, h) for n in rows for h in range(heads)]

        def scores(n, h):
            return nn(kv_tok[n][:, :width] * lane_ref[h], query[n])

        outs, inverses = {}, {}

        def mix(n, h):
            both = nn(jnp.concatenate([value[n][mine[h]], ones], axis=0), e_scr[n, :, there[h]])
            inverses[n, h] = 1.0 / both[head : head + 1]
            outs[n, h] = both[:head] * inverses[n, h]

        coming = scores(*pairs[0])
        for at_pair, (n, h) in enumerate(pairs):
            score = coming
            if at_pair + 1 < len(pairs):
                coming = scores(*pairs[at_pair + 1])
            score = score + bias_ref[h]
            peak = jnp.max(score, axis=0, keepdims=True)
            e_scr[n, :, there[h]] = jnp.exp2(score - peak).astype(BF)
            if at_pair:
                mix(*pairs[at_pair - 1])
        mix(*pairs[-1])

        attended, gated, x2 = {}, {}, {}
        for n in rows:
            attended[n] = jnp.concatenate([outs[n, h] for h in range(heads)], axis=0)
            (gated[n],) = tiles(n, lambda p, gate, out: ((gate * out).astype(BF),), gate2[n], attended[n])
            x2[n] = nn(att_out_t_ref[...], gated[n])
        hat3, scale3, normed3, up, cot_tok, cot_low, grad_act = {}, {}, {}, {}, {}, {}, {}
        for n in rows:

            def third(p, before, add):
                after = before + add
                hat, scale = normalize(after)
                return after, hat, scale, (hat * vec_ref[6] + vec_ref[7]).astype(BF)

            x2[n], hat3[n], scale3[n], normed3[n] = tiles(n, third, x1[n], x2[n])
            up[n] = nn(up_t_ref[...], normed3[n])
            cot_tok[n] = load_tokens(cot_ref, start + n, order).astype(BF)
            cot_low[n] = cot_tok[n].T
            grad_act[n] = nn(down_ref[...], cot_low[n])
        act, down, grad_up, grad3 = {}, {}, {}, {}
        for n in rows:

            def silu(p, raw, grad):
                gate = sigmoid(raw)
                return (raw * gate).astype(BF), (grad * (gate * (1.0 + raw * (1.0 - gate)))).astype(BF)

            act[n], grad_up[n] = tiles(n, silu, up[n], grad_act[n])
            down[n] = nn(down_t_ref[...], act[n])
            grad3[n] = nn(up_ref[...], grad_up[n])
        grad = nn(side([act[n] for n in rows]), jnp.concatenate([cot_tok[n] for n in rows], axis=0))
        for n, part in enumerate(downs):
            g_ref[:, part] += grad[n * width : (n + 1) * width]
        g_ref[:, ups] += nt(side([normed3[n] for n in rows]), side([grad_up[n] for n in rows]))

        grad_x2, grad_x2_low, grad_gated = {}, {}, {}
        for n in rows:

            def third_back(p, grad_out, grad, hat, scale):
                g_vec_ref[6] += grad * hat
                g_vec_ref[7] += grad
                grad = grad_out.astype(F32) + normalize_back(grad, vec_ref[6], hat, scale)
                return grad, grad.astype(BF)

            grad_x2[n], grad_x2_low[n] = tiles(n, third_back, cot_low[n], grad3[n], hat3[n], scale3[n])
            grad_gated[n] = nn(att_out_ref[...], grad_x2_low[n])
            (out,) = tiles(n, lambda p, one, two: ((one + two).astype(BF),), x2[n], down[n])
            store_tokens(out_ref, start + n, order, out.T.astype(F32))
        g_ref[:, place["att_out"]] += nt(
            side([gated[n] for n in rows]), side([grad_x2_low[n] for n in rows])
        )
        grad_gate2, grad_out, center = {}, {}, {}
        for n in rows:

            def gate_back(p, grad, gate, out):
                mixed_grad = grad * gate
                scaled = [mixed_grad[mine[h]] * inverses[n, h][:, parts[p]] for h in range(heads)]
                low = jnp.concatenate(scaled, axis=0).astype(BF)
                product = low.astype(F32) * out
                centers = [jnp.sum(product[mine[h]], axis=0, keepdims=True) for h in range(heads)]
                return ((mixed_grad * out * (1.0 - gate)).astype(BF), low, *centers)

            grad_gate2[n], grad_out[n], *centers = tiles(n, gate_back, grad_gated[n], gate2[n], attended[n])
            for h in range(heads):
                center[n, h] = centers[h]

        grad_queries, grad_keys, grad_values = {}, {}, {}

        def probs(n, h):
            return nn(kv_tok[n][:, width:] * lane_ref[h], grad_out[n])

        def spread(n, h, grad_score):
            both = nn(jnp.concatenate([key[n][mine[h]], chain_ref[...]], axis=0), grad_score)
            grad_queries[n, h] = (both[:head] * scaling).astype(BF)
            g_bias_ref[h] += both[head:]
            grad_keys[n, h] = (nt(query[n][mine[h]], grad_score) * LN2).astype(BF)

        coming, behind = probs(*pairs[0]), None
        for at_pair, (n, h) in enumerate(pairs):
            grad_prob = coming
            if at_pair + 1 < len(pairs):
                coming = probs(*pairs[at_pair + 1])
            expon = e_scr[n, :, there[h]]
            grad_score = (expon.astype(F32) * (grad_prob - center[n, h])).astype(BF)
            grad_values[n, h] = nt(grad_out[n][mine[h]], expon).astype(BF)
            if behind is not None:
                spread(*behind)
            behind = (n, h, grad_score)
        spread(*behind)

        grad_hidden, grad2 = {}, {}
        for n in rows:
            blocks = [items[n, h] for items in (grad_queries, grad_keys, grad_values) for h in range(heads)]
            grad_hidden[n] = jnp.concatenate(blocks + [grad_gate2[n]], axis=0)
            grad2[n] = nn(att_ref[...], grad_hidden[n])
        g_ref[:, place["query"].start : place["gate2"].stop] += nt(
            side([normed2[n] for n in rows]), side([grad_hidden[n] for n in rows])
        )
        grad_x1, grad_branch, grad_gate1, grad_mix, grad1 = {}, {}, {}, {}, {}
        for n in rows:

            def second_back(p, grad_after, grad, hat, scale, gate, added):
                g_vec_ref[4] += grad * hat
                g_vec_ref[5] += grad
                grad = grad_after + normalize_back(grad, vec_ref[4], hat, scale)
                gated_grad = grad * gate
                return grad, gated_grad.astype(BF), (gated_grad * added * (1.0 - gate)).astype(BF)

            grad_x1[n], grad_branch[n], grad_gate1[n] = tiles(
                n, second_back, grad_x2[n], grad2[n], hat2[n], scale2[n], gate1[n], branch[n]
            )
            grad_mix[n] = nn(tri_out_ref[...], grad_branch[n])
            grad1[n] = nn(gate_w_ref[...], grad_gate1[n])
        g_ref[:, place["tri_out"]] += nt(
            side([mixed[n] for n in rows]), side([grad_branch[n] for n in rows])
        )
        g_ref[:, place["gate"]] += nt(
            side([normed1[n] for n in rows]), side([grad_gate1[n] for n in rows])
        )
        for n in rows:
            for p, part in enumerate(parts):
                grad, hat, scale = grad_mix[n][:, part], hat_t[n][:, part], scale_t[n][:, part]
                g_vec_ref[2] += grad * hat
                g_vec_ref[3] += grad
                dt_ref[p, start + n] = normalize_back(grad, vec_ref[2], hat, scale)
                grad, hat, scale = grad1[n][:, part], hat1[n][:, part], scale1[n][:, part]
                g_vec_ref[0] += grad * hat
                g_vec_ref[1] += grad
                grad = grad_x1[n][:, part] + normalize_back(grad, vec_ref[0], hat, scale)
                z_ref[start + n, :, part] = grad
        return carry

    lax.fori_loop(0, total_rows // count, step, 0)


def rows_pass(c, chunks, half, before, t, xt, cot_rows, order, bias, chain, lane, vecs, weights, heads):
    _, all_rows, width, length = xt.shape
    blocks, pieces, sub, tokens, _ = cot_rows.shape
    rows = blocks * sub
    some, count = 8, 8
    inner = sub // some
    full = lambda item: pl.BlockSpec(item.shape, lambda at, half: (0,) * item.ndim)
    of_all = pl.BlockSpec((some, width, length), lambda at, half: (c * (rows // some) + at, 0, 0))
    xt_some = pl.BlockSpec(
        (1, some, width, length), lambda at, half: (half[0], c * (rows // some) + at, 0, 0)
    )
    t_some = pl.BlockSpec(
        (length // 128, some, width, 128), lambda at, half: (0, c * (rows // some) + at, 0, 0)
    )
    dt_some = pl.BlockSpec((length // 128, some, width, 128), lambda at, half: (0, at, 0, 0))
    by_piece = pl.BlockSpec(
        (1, pieces, some, tokens, width), lambda at, half: (at // inner, 0, at % inner, 0, 0)
    )
    consts = (bias, chain, lane, vecs) + weights
    wide = weights[-1].shape[1]
    sum_shapes = [
        jax.ShapeDtypeStruct(shape, F32)
        for shape in ((width, 7 * width + 2 * wide), (8, width, 128), (heads, 16, length))
    ]
    before_specs = [full(item) for item in before[:3]]
    before_specs += [pl.BlockSpec(memory_space=pl.ANY)] * len(before[3:])
    return pl.pallas_call(
        functools.partial(rows_kernel, count, heads, order, c == 0),
        grid_spec=pltpu.PrefetchScalarGridSpec(
            num_scalar_prefetch=1,
            grid=(rows // some,),
            in_specs=before_specs + [t_some, xt_some, by_piece] + [full(item) for item in consts],
            out_specs=[by_piece, dt_some, of_all] + [full(item) for item in sum_shapes],
            scratch_shapes=[
                pltpu.VMEM((count, length, heads * length), BF),
            ],
        ),
        out_shape=[
            jax.ShapeDtypeStruct(cot_rows.shape, BF),
            by_halves(rows, width, length),
            jax.ShapeDtypeStruct((all_rows, width, length), F32),
        ]
        + sum_shapes,
        input_output_aliases={4: 2} if before else {},
        compiler_params=pltpu.CompilerParams(vmem_limit_bytes=VMEM_LIMIT),
        cost_estimate=cost(1.2e11),
        name="rows",
    )(half, *before, t, xt, cot_rows, *consts)


def edges_back_kernel(
    order, half_ref, xt_ref, z_ref, da_ref, db_ref, wt_ref, w_ref, gain_ref, shift_ref, out_ref, g_w_ref, g_vec_ref
):
    _, rows, width, length = xt_ref.shape
    count = 4

    @pl.when(pl.program_id(0) == 0)
    def _():
        g_w_ref[...] = jnp.zeros(g_w_ref.shape, F32)
        g_vec_ref[...] = jnp.zeros(g_vec_ref.shape, F32)

    def step(at, carry):
        start = at * count
        x0 = stacked(xt_ref.at[0], start, count).astype(F32)
        lanes = x0.shape[1]
        gain = widen(gain_ref[...], lanes)
        hat, scale = normalize(x0)
        normed = (hat * gain + widen(shift_ref[...], lanes)).astype(BF)
        proj = nn(wt_ref[...], normed)
        pa, pag = proj[:width], proj[width : 2 * width]
        pb, pbg = proj[2 * width : 3 * width], proj[3 * width :]
        halves = [(n, half) for n in range(count) for half in range(da_ref.shape[0])]
        da = jnp.concatenate([da_ref[half, start + n] for n, half in halves], axis=1)
        db = jnp.concatenate([db_ref[half, start + n] for n, half in halves], axis=1)
        sa, sb = sigmoid(pag), sigmoid(pbg)
        dsa, dsb = da * sa, db * sb
        grads = jnp.concatenate(
            [
                dsa.astype(BF),
                (dsa * pa * (1.0 - sa)).astype(BF),
                dsb.astype(BF),
                (dsb * pb * (1.0 - sb)).astype(BF),
            ],
            axis=0,
        )
        g_w_ref[...] += nt(normed, grads)
        grad = nn(w_ref[...], grads)
        g_vec_ref[0] += fold(grad * hat)
        g_vec_ref[1] += fold(grad)
        out = stacked(z_ref, start, count) + normalize_back(grad, gain, hat, scale)
        out = out.astype(BF)
        for n in range(count):
            store_tokens(out_ref, start + n, order, out[:, n * length : (n + 1) * length].T.astype(F32))
        return carry

    lax.fori_loop(0, rows // count, step, 0)


def edges_back(half, xt, z, da, db, order, weight_t, weight, gain, shift, shape):
    _, rows, width, length = xt.shape
    blocks, pieces, sub, tokens, _ = shape
    chunks = order[2]
    some = sub // chunks
    step = 16 // some
    inner = blocks // step
    full = lambda item: pl.BlockSpec(item.shape, lambda at, half: (0,) * item.ndim)
    xt_row = pl.BlockSpec((1, 16, width, length), lambda at, half: (half[0], at, 0, 0))
    by_row = pl.BlockSpec((16, width, length), lambda at, half: (at, 0, 0))
    by_half = pl.BlockSpec((length // 128, 16, width, 128), lambda at, half: (0, at, 0, 0))
    sum_shapes = [
        jax.ShapeDtypeStruct(weight.shape, F32),
        jax.ShapeDtypeStruct((2, width, 128), F32),
    ]
    by_piece = pl.BlockSpec(
        (step, pieces, some, tokens, width), lambda at, half: (at % inner, 0, at // inner, 0, 0)
    )
    return pl.pallas_call(
        functools.partial(edges_back_kernel, order),
        grid_spec=pltpu.PrefetchScalarGridSpec(
            num_scalar_prefetch=1,
            grid=(chunks * inner,),
            in_specs=[xt_row, by_row] + [by_half] * 2 + [full(item) for item in (weight_t, weight, gain, shift)],
            out_specs=[by_piece] + [full(item) for item in sum_shapes],
        ),
        out_shape=[jax.ShapeDtypeStruct(shape, BF)] + sum_shapes,
        compiler_params=pltpu.CompilerParams(vmem_limit_bytes=VMEM_LIMIT),
        cost_estimate=cost(4.0e10),
        name="edges_back",
    )(half, xt, z, da, db, weight_t, weight, gain, shift)


def shards(
    row_size,
    col_size,
    pair_state,
    cotangent,
    chain_lengths,
    tri_gain,
    tri_shift,
    tri_weight,
    mix_gain,
    mix_shift,
    tri_out,
    att_gain,
    att_shift,
    att_weight,
    chain_bias,
    att_out,
    trans_gain,
    trans_shift,
    up_weight,
    down_weight,
):
    heads = HEADS
    crops, own_rows, tokens, width = pair_state.shape
    length = col_size * tokens
    chunks = CHUNKS
    some = own_rows // (col_size * chunks)
    axes = ("row", "col")
    group = row_size * col_size
    order = (row_size, col_size, chunks)
    shape = (row_size, col_size, some, tokens, width)

    def swap(values):
        return lax.all_to_all(values, axes, split_axis=0, concat_axis=0, tiled=True)

    def cut(values):
        parts = values.reshape(group, chunks, some, tokens, width)
        return [parts[:, c] for c in range(chunks)]

    def join(parts):
        return jnp.stack(parts, axis=1).reshape(crops, own_rows, tokens, width)

    def across(values, bit):
        return lax.ppermute(values, "col", [(q, q ^ bit) for q in range(col_size)])

    bits = [1 << n for n in range(col_size.bit_length() - 1)]

    def after(values, *others):
        return lax.optimization_barrier((values,) + others)[0]

    def gather(own, far, *late):
        pieces = {0: own, far_bit: across(far, far_bit)}
        arrived = pieces[far_bit]
        if late:
            pieces[far_bit] = after(arrived, *late)
        for bit in reversed(bits[:-1]):
            for m in list(pieces):
                pieces[m ^ bit] = across(pieces[m], bit)
        return [pieces[m] for m in range(col_size)], arrived

    def doubled(items, axis, size, bits):
        for bit in bits:
            lows = [values.astype(sent) for values, sent in items]
            others = [lax.ppermute(low, axis, [(q, q ^ bit) for q in range(size)]) for low in lows]
            others = lax.optimization_barrier(tuple(others))
            items = [
                (low.astype(F32) + other.astype(F32), sent)
                for low, other, (_, sent) in zip(lows, others, items)
            ]
        return items

    whole = (row_size, col_size, some * chunks, tokens, width)
    cot_parts = cut(cotangent)

    wide = lambda item: jnp.broadcast_to(item[:, None], (width, 128))
    vecs = jnp.stack(
        [
            wide(item)
            for item in (
                tri_gain,
                tri_shift,
                mix_gain,
                mix_shift,
                att_gain,
                att_shift,
                trans_gain,
                trans_shift,
            )
        ]
    )
    edge_w = tri_weight[:, : 4 * width]
    edge_wt = edge_w.T
    gate_w = tri_weight[:, 4 * width :]
    lengths = lax.dynamic_index_in_dim(chain_lengths, lax.axis_index("row"), 0, keepdims=False)
    ends = jnp.cumsum(lengths)
    places = jnp.arange(length, dtype=jnp.int32)
    places = places.reshape(order + (some,)).transpose(1, 2, 0, 3).reshape(length)
    chain = jnp.sum((places[:, None] >= ends[None, :]).astype(jnp.int32), axis=-1)
    same = (chain[:, None] == chain[None, :]).astype(F32)
    bias = (LOG2E * chain_bias)[:, None, None] * same[None]
    which = (jnp.arange(16, dtype=jnp.int32)[:, None] == chain[None, :]).astype(F32)
    head_of = jnp.arange(width, dtype=jnp.int32) // (width // heads)
    lane = (jnp.arange(heads, dtype=jnp.int32)[:, None] == head_of[None, :]).astype(BF)
    lane = jnp.broadcast_to(lane[:, None, :], (heads, length, width))
    me = lax.axis_index("col")
    own = own_rows
    far_bit = col_size // 2
    half, core = me // far_bit, me % far_bit
    token_place = jnp.stack([(me ^ m) * tokens for m in range(col_size)])
    place = [(s * far_bit + (core ^ k)) * own for s in range(2) for k in range(2)]
    place = jnp.stack(place + [half])
    here = (core * own).reshape(1)
    half_at = half.reshape(1)
    weights = (
        gate_w,
        gate_w.T,
        tri_out,
        tri_out.T,
        att_weight.T,
        att_weight[:, width : 3 * width],
        att_weight,
        att_out,
        att_out.T,
        up_weight,
        up_weight.T,
        down_weight,
        down_weight.T,
    )
    chain_rows = which.astype(BF)

    groups = pair_state.reshape(crops, 2, far_bit, own_rows // col_size, tokens, width)
    early = (edge_wt, vecs, bias, lane, cot_parts[0])
    lefts, rights, xt, cot_rows, last = [], [], [], [], ()
    for s in range(2):
        pieces = []
        for k in range(2):
            part = lax.dynamic_index_in_dim(groups[:, s], core ^ k, 1, keepdims=False)
            part = lax.all_to_all(after(part, *last), "row", split_axis=0, concat_axis=0, tiled=True)
            last = (part,)
            part = part if s or k else after(part, *early)
            pieces += [across(part, far_bit ^ 1), across(part, 1)] if k else [part, across(part, far_bit)]
        if s:
            cot_rows.append(swap(after(cot_parts[0], *last)).reshape(shape))
        own_part, far, far_other, near_other = pieces
        pieces = [own_part, near_other, far, far_other]
        left, right, *xt = edges(token_place, s, pieces, xt, order, edge_wt, vecs[0], vecs[1])
        lefts.append(left)
        rights += [right, across(right, 1)]
    (xt,) = xt
    t = triangle(place, lefts, rights)
    lefts = [item for left in lefts for item in (left, across(after(left, t), 1))]
    for part in cot_parts[1:]:
        cot_rows.append(swap(after(part, t, cot_rows[-1])).reshape(shape))
    state, outs, dts, sent = [], [], [], []
    pairs = [[q, q + far_bit] for q in range(far_bit)]
    for c in range(chunks):
        out, dt, z, *sums = rows_pass(
            c, chunks, half_at, state, t, xt, cot_rows[c], order, bias, chain_rows, lane, vecs, weights, heads
        )
        state = sums + [z]
        dt = turn(dt)
        if c < chunks - 1:
            dts.append(dt)
            outs.append(swap(out.reshape(group, some, tokens, width)))
            near = lax.dynamic_index_in_dim(dt, half, 0, keepdims=False)
            sent.append((near, across(lax.dynamic_index_in_dim(dt, 1 - half, 0, keepdims=False), far_bit)))
    dt = after(dt, *outs)
    dts.append(dt)
    crossed = []
    for near, far in sent:
        near, far = after(near, z), after(far, z)
        crossed.append(jnp.where(half == 0, jnp.stack([near, far]), jnp.stack([far, near])))
    crossed.append(
        lax.all_to_all(dt, "col", split_axis=0, concat_axis=0, axis_index_groups=pairs, tiled=True)
    )
    g_rows, g_vec, g_bias = sums
    row_bits = [1 << n for n in range(row_size.bit_length() - 1)]
    ((g_rows, _),) = doubled([(g_rows, BF)], "row", row_size, row_bits)
    da = left_back(place, dts, rights)
    grads = [[item, across(item, 1)] for item in crossed[:-1]]
    grads.append([crossed[-1], across(after(crossed[-1], da), 1)])
    outs.append(swap(after(out, crossed[-1]).reshape(group, some, tokens, width)))
    pair_out = join(outs)
    db = right_back(here, grads, [after(lefts[0], g_rows)] + lefts[1:])
    back, g_edge, g_vec_edge = edges_back(
        half_at, xt, z, da, db, order, edge_wt, edge_w, vecs[0], vecs[1], whole
    )
    g_vec = jnp.sum(g_vec, axis=-1)
    g_vec_edge = jnp.sum(g_vec_edge, axis=-1)
    g_chain = jnp.sum(g_bias * which[None], axis=(1, 2))
    small = jnp.concatenate(
        [g_vec[:2] + g_vec_edge, g_vec[2:], jnp.pad(g_chain, (0, width - heads))[None]], axis=0
    )
    items = doubled([(g_edge, BF), (small, F32)], "row", row_size, row_bits)
    back = after(back, *[values for values, _ in items])
    grad_pair = swap(back.reshape(group, some * chunks, tokens, width))
    grad_pair = grad_pair.reshape(crops, own_rows, tokens, width)
    items = doubled(items + [(after(g_rows, pair_out), BF)], "col", col_size, bits[::-1])
    t_edge, small, total = [values for values, _ in items]
    column = lambda at, n=1: total[:, at * width : (at + n) * width]
    ff = up_weight.shape[1] // width
    t_gate, t_tri_out, t_att = column(0), column(1), column(2, 4)
    t_att_out, t_up = column(6), column(7, ff)
    t_down = jnp.concatenate([column(7 + ff + n) for n in range(ff)], axis=0)
    return (
        pair_out,
        grad_pair,
        small[0],
        small[1],
        jnp.concatenate([t_edge, t_gate], axis=1),
        small[2],
        small[3],
        t_tri_out,
        small[4],
        small[5],
        t_att,
        small[8, :heads],
        t_att_out,
        small[6],
        small[7],
        t_up,
        t_down,
    )


def solution(mesh):
    pair = P("dp", "row", "col", None)
    vector, matrix = P("dp"), P("dp", None)
    return jax.shard_map(
        functools.partial(shards, mesh.shape["row"], mesh.shape["col"]),
        mesh=mesh,
        in_specs=(pair, pair, P("dp", None)) + (P(),) * 15,
        out_specs=(
            pair,
            pair,
            vector,
            vector,
            matrix,
            vector,
            vector,
            matrix,
            vector,
            vector,
            matrix,
            vector,
            matrix,
            vector,
            vector,
            matrix,
            matrix,
        ),
        check_vma=False,
    )
```

```python
import functools
import math

import jax
import jax.numpy as jnp
from jax import lax
from jax.experimental import pallas as pl
from jax.experimental.pallas import tpu as pltpu
from jax.sharding import PartitionSpec as P

HEADS = 4
EPS = 1e-05
LOG2E = math.log2(math.e)
LN2 = math.log(2.0)
CHUNKS = 2
VMEM_LIMIT = 56 * 1024 * 1024
BF = jnp.bfloat16
F32 = jnp.float32


def nn(left, right):
    return lax.dot_general(left, right, (((1,), (0,)), ((), ())), preferred_element_type=F32)


def nt(left, right):
    return lax.dot_general(left, right, (((1,), (1,)), ((), ())), preferred_element_type=F32)


def tn(left, right):
    return lax.dot_general(left, right, (((0,), (0,)), ((), ())), preferred_element_type=F32)


def cost(flops, size=0):
    return pl.CostEstimate(flops=int(flops), bytes_accessed=int(size), transcendentals=0)


def sigmoid(values):
    return 0.5 * jnp.tanh(0.5 * values) + 0.5


def normalize(values):
    center = values - jnp.mean(values, axis=0, keepdims=True)
    spread = jnp.mean(center * center, axis=0, keepdims=True)
    scale = lax.rsqrt(spread + EPS)
    return center * scale, scale


def normalize_back(grads, gain, hat, scale):
    grad_hat = grads * gain
    first = jnp.mean(grad_hat, axis=0, keepdims=True)
    second = jnp.mean(grad_hat * hat, axis=0, keepdims=True)
    return scale * (grad_hat - first - hat * second)


def widen(column, lanes):
    return jnp.concatenate([column] * (lanes // column.shape[1]), axis=1)


def fold(values):
    parts = [values[:, at : at + 128] for at in range(0, values.shape[1], 128)]
    return functools.reduce(lambda one, two: one + two, parts)


def to_order(flat, order):
    length, width = flat.shape
    flat = flat.reshape(order + (length // math.prod(order), width))
    return flat.transpose(1, 2, 0, 3, 4).reshape(length, width)


def load_tokens(ref, row, order):
    _, pieces, some, tokens, width = ref.shape
    flat = ref[row // some, :, row % some, :, :].astype(F32)
    return to_order(flat.reshape(pieces * tokens, width), order)


def store_tokens(ref, row, order, values):
    _, pieces, some, tokens, width = ref.shape
    back = (order[1], order[2], order[0])
    flat = values.reshape(back + (pieces * tokens // math.prod(order), width))
    flat = flat.transpose(2, 0, 1, 3, 4).reshape(pieces, tokens, width)
    ref[row // some, :, row % some, :, :] = flat.astype(ref.dtype)


def stacked(ref, start, count):
    return jnp.concatenate([ref[start + n] for n in range(count)], axis=1)


def spread_out(ref, start, count, values):
    length = values.shape[1] // count
    for n in range(count):
        ref[start + n] = values[:, n * length : (n + 1) * length].astype(ref.dtype)


def no_op(*refs):
    pass


def tip(values):
    return values[(0,) * (values.ndim - 2)][:16, :128]


def after(values, *others):
    others = [tip(item) for item in others]
    anywhere = pl.BlockSpec(memory_space=pltpu.HBM)
    return pl.pallas_call(
        no_op,
        in_specs=[anywhere] * (1 + len(others)),
        out_specs=anywhere,
        out_shape=jax.ShapeDtypeStruct(values.shape, values.dtype),
        input_output_aliases={0: 0},
        cost_estimate=cost(0),
        name="after",
    )(values, *others)


def edges_kernel(order, place_ref, *refs):
    x_refs, (w_ref, gain_ref, shift_ref), rest = refs[:4], refs[4:7], refs[-6:]
    a_ref, b_ref, xt_ref, a_scr, b_scr, x_scr = rest
    width, rows, length = a_ref.shape
    pitch = a_scr.shape[1] // rows
    count = x_scr.shape[0]
    _, some, tokens, _ = x_refs[0].shape

    def step(at, carry):
        start = at * count
        turned = []
        for n in range(count):
            row = start + n
            for m, ref in enumerate(x_refs):
                there = pl.ds(pl.multiple_of(place_ref[m], tokens), tokens)
                x_scr[n, there, :] = ref[row // some, row % some].astype(F32)
            turned.append(to_order(x_scr[n], order).astype(BF).T)
        x0 = jnp.concatenate(turned, axis=1)
        for n in range(count):
            xt_ref[0, start + n] = turned[n]
        hat, _ = normalize(x0.astype(F32))
        lanes = x0.shape[1]
        normed = (hat * widen(gain_ref[...], lanes) + widen(shift_ref[...], lanes)).astype(BF)
        proj = nn(w_ref[...], normed)
        left = sigmoid(proj[width : 2 * width]) * proj[:width]
        right = sigmoid(proj[3 * width : 4 * width]) * proj[2 * width : 3 * width]
        for n in range(count):
            base = pl.multiple_of((start + n) * pitch, 8)
            for half in range(length // 128):
                part = slice(n * length + half * 128, n * length + half * 128 + 128)
                a_scr[half, pl.ds(base, width), :] = left[:, part]
                b_scr[half, pl.ds(base, width), :] = right[:, part]
        return carry

    lax.fori_loop(0, rows // count, step, 0)

    def turn(at, carry):
        for n in range(8):
            e = at * 8 + n
            for scr, out in ((a_scr, a_ref), (b_scr, b_ref)):
                halves = [scr[h, pl.ds(e, rows, stride=pitch), :] for h in range(scr.shape[0])]
                out[e] = jnp.concatenate(halves, axis=1).astype(BF)
        return carry

    lax.fori_loop(0, width // 8, turn, 0)


def edges(place, half, x_pieces, before, order, weight, gain, shift):
    blocks, rows_there, tokens, width = x_pieces[0].shape
    length = len(x_pieces) * tokens
    chunks = order[2]
    some = rows_there // chunks
    step = 16 // some
    inner = blocks // step
    rows = blocks * some * chunks
    const = lambda at, place: (0, 0)
    pitch = width + 8
    low = pl.BlockSpec((width, 16, length), lambda at, place: (0, at, 0))
    spec = pl.BlockSpec(
        (step, some, tokens, width),
        lambda at, place: (at % inner, at // inner, 0, 0),
    )
    return pl.pallas_call(
        functools.partial(edges_kernel, order),
        grid_spec=pltpu.PrefetchScalarGridSpec(
            num_scalar_prefetch=1,
            grid=(chunks * inner,),
            in_specs=[spec] * 4
            + [
                pl.BlockSpec(weight.shape, const),
                pl.BlockSpec(gain.shape, const),
                pl.BlockSpec(shift.shape, const),
            ]
            + [pl.BlockSpec(memory_space=pl.ANY)] * len(before),
            out_specs=[low, low, pl.BlockSpec((1, 16, width, length), lambda at, place: (half, at, 0, 0))],
            scratch_shapes=[
                pltpu.VMEM((length // 128, 16 * pitch, 128), F32),
                pltpu.VMEM((length // 128, 16 * pitch, 128), F32),
                pltpu.VMEM((4, length, width), F32),
            ],
        ),
        out_shape=[jax.ShapeDtypeStruct((width, rows, length), BF)] * 2
        + [jax.ShapeDtypeStruct((2, rows, width, length), BF)],
        input_output_aliases={8: 2} if before else {},
        compiler_params=pltpu.CompilerParams(vmem_limit_bytes=VMEM_LIMIT),
        cost_estimate=cost(3.0e9),
        name="edges",
    )(place, *x_pieces, weight, gain, shift, *before)


def gather_pieces(place_ref, rights, e, scr):
    for n, piece in enumerate(rights):
        rows = piece.shape[1]
        scr[e, pl.ds(pl.multiple_of(place_ref[n], rows), rows), :] = piece[e]


def by_channel(ref):
    halves, rows, some, lanes = ref.shape
    return ref.reshape(halves, rows * some, lanes)


def put_channel(ref, e, values):
    halves, rows, some, lanes = ref.shape
    flat = by_channel(ref)
    for half in range(halves):
        flat[half, pl.ds(e, rows, stride=some), :] = values[:, half * lanes : (half + 1) * lanes]


def ahead(first, count, begin, end):
    coming = begin(first)
    for e in range(first, first + count):
        here = coming
        if e + 1 < first + count:
            coming = begin(e + 1)
        end(e, here)


SOME = 16


def cut_refs(refs, *counts):
    parts = []
    for count in counts:
        parts.append(refs[:count])
        refs = refs[count:]
    return parts + list(refs)


def triangle_kernel(place_ref, *refs):
    lefts, rights, t_ref, scr, own_scr = cut_refs(refs, 2, 4)
    for half, left in enumerate(lefts):

        @pl.when(place_ref[4] == half)
        def _():
            own_scr[...] = left[...]

    def begin(e):
        gather_pieces(place_ref, rights, e, scr)
        return nt(own_scr[e], scr[e])

    ahead(0, SOME, begin, functools.partial(put_channel, t_ref))


def high_spec(rows, length):
    return pl.BlockSpec((length // 128, rows, SOME, 128), lambda at, place: (0, 0, at, 0))


def low_spec(rows, lanes):
    return pl.BlockSpec((SOME, rows, lanes), lambda at, place: (at, 0, 0))


def by_halves(rows, width, length):
    return jax.ShapeDtypeStruct((length // 128, rows, width, 128), F32)


def channel_call(kernel, name, flops, scalar, ins, in_specs, out_specs, out_shape, scratch=()):
    return pl.pallas_call(
        kernel,
        grid_spec=pltpu.PrefetchScalarGridSpec(
            num_scalar_prefetch=1,
            grid=(ins[0].shape[0 if ins[0].ndim == 3 else 2] // SOME,),
            in_specs=in_specs,
            out_specs=out_specs,
            scratch_shapes=scratch,
        ),
        out_shape=out_shape,
        compiler_params=pltpu.CompilerParams(vmem_limit_bytes=VMEM_LIMIT),
        cost_estimate=cost(flops),
        name=name,
    )(scalar, *ins)


def triangle(place, lefts, rights):
    width, rows, length = lefts[0].shape
    return channel_call(
        triangle_kernel,
        "triangle",
        3.0e9,
        place,
        (*lefts, *rights),
        [low_spec(rows, length)] * 6,
        high_spec(rows, length),
        by_halves(rows, width, length),
        [pltpu.VMEM((SOME, length, length), BF), pltpu.VMEM((SOME, rows, length), BF)],
    )


def turn_kernel(grad_ref, *refs):
    out_ref = refs[-1]
    halves, rows, some, _ = grad_ref.shape
    flat = by_channel(grad_ref)
    for e in range(some):
        for half in range(halves):
            out_ref[half, e] = flat[half, pl.ds(e, rows, stride=some), :].astype(BF)


def turn(grad, others):
    halves, rows, width, lanes = grad.shape
    some = 32
    return pl.pallas_call(
        turn_kernel,
        grid=(width // some,),
        in_specs=[pl.BlockSpec((halves, rows, some, lanes), lambda at: (0, 0, at, 0))]
        + [pl.BlockSpec(memory_space=pltpu.HBM)] * len(others),
        out_specs=pl.BlockSpec((halves, some, rows, lanes), lambda at: (0, at, 0, 0)),
        out_shape=jax.ShapeDtypeStruct((halves, width, rows, lanes), BF),
        compiler_params=pltpu.CompilerParams(vmem_limit_bytes=VMEM_LIMIT),
        cost_estimate=cost(5.0e9),
        name="turn",
    )(grad, *[tip(item) for item in others])


def right_back_kernel(chunks, here_ref, *refs):
    lefts, grads, _, db_ref, scr = cut_refs(refs, 4, 2 * chunks, 1)
    rows = db_ref.shape[1]

    def begin(e):
        pairs = [(s, k) for s in range(2) for k in range(2)]
        grad = [grads[2 * c + k][s, e] for s, k in pairs for c in range(chunks)]
        left = [lefts[2 * s + k][e] for s, k in pairs]
        return tn(jnp.concatenate(grad, axis=0), jnp.concatenate(left, axis=0))

    def end(e, db):
        scr[e] = db
        put_channel(db_ref, e, scr[e, pl.ds(pl.multiple_of(here_ref[0], rows), rows), :])

    ahead(0, SOME, begin, end)


def right_back(here, grads, lefts, other):
    width, rows, length = lefts[0].shape
    chunks = len(grads)
    _, _, some, part = grads[0][0].shape
    both = pl.BlockSpec((2, SOME, some, part), lambda at, here: (0, at, 0, 0))
    return channel_call(
        functools.partial(right_back_kernel, chunks),
        "right_back",
        2.2e10,
        here,
        [*lefts] + [item for chunk in grads for item in chunk] + [tip(other)],
        [low_spec(rows, length)] * 4 + [both] * (2 * chunks) + [pl.BlockSpec(memory_space=pltpu.HBM)],
        high_spec(rows, length),
        by_halves(rows, width, length),
        [pltpu.VMEM((SOME, part, length), F32)],
    )


def left_back_kernel(chunks, place_ref, *refs):
    rights, grads, _, da_ref, scr = cut_refs(refs, 4, chunks, 1)

    def begin(e):
        gather_pieces(place_ref, rights, e, scr)
        grad = [jnp.concatenate([ref[0, e], ref[1, e]], axis=1) for ref in grads]
        return nn(jnp.concatenate(grad, axis=0), scr[e])

    ahead(0, SOME, begin, functools.partial(put_channel, da_ref))


def left_back(place, grads, rights, other):
    _, width, some, part = grads[0].shape
    _, rows, length = rights[0].shape
    both = pl.BlockSpec((2, SOME, some, part), lambda at, place: (0, at, 0, 0))
    return channel_call(
        functools.partial(left_back_kernel, len(grads)),
        "left_back",
        2.0e10,
        place,
        (*rights, *grads, tip(other)),
        [low_spec(rows, length)] * 4 + [both] * len(grads) + [pl.BlockSpec(memory_space=pltpu.HBM)],
        high_spec(rows, length),
        by_halves(rows, width, length),
        [pltpu.VMEM((SOME, length, length), BF)],
    )


def rows_kernel(count, heads, order, first, half_ref, *refs):
    before = []
    if not first:
        before, refs = refs[:3], refs[4:]
    rows_body(count, heads, order, before, *refs)


def rows_body(
    count,
    heads,
    order,
    before,
    t_ref,
    xt_ref,
    cot_ref,
    bias_ref,
    chain_ref,
    lane_ref,
    vec_ref,
    gate_w_ref,
    gate_wt_ref,
    tri_out_ref,
    tri_out_t_ref,
    att_t_ref,
    att_kv_ref,
    att_ref,
    att_out_ref,
    att_out_t_ref,
    up_ref,
    up_t_ref,
    down_ref,
    down_t_ref,
    out_ref,
    dt_ref,
    z_ref,
    g_ref,
    g_vec_ref,
    g_bias_ref,
    e_scr,
):
    _, total_rows, width, length = xt_ref.shape
    head = width // heads
    scaling = 1.0 / math.sqrt(head)

    sums = (g_ref, g_vec_ref, g_bias_ref)
    place = {}
    for name in ("gate", "tri_out", "query", "key", "value", "gate2", "att_out"):
        place[name] = slice(len(place) * width, (len(place) + 1) * width)
    ups = slice(7 * width, 7 * width + up_ref.shape[1])
    downs = [
        slice(at, at + width) for at in range(ups.stop, ups.stop + up_ref.shape[1], width)
    ]

    @pl.when(pl.program_id(0) == 0)
    def _():
        for n, ref in enumerate(sums):
            ref[...] = before[n][...] if before else jnp.zeros(ref.shape, ref.dtype)

    per = length // 128
    mine = [slice(h * head, (h + 1) * head) for h in range(heads)]
    there = [slice(h * length, (h + 1) * length) for h in range(heads)]
    ones = jnp.ones((16, length), BF)
    parts = [slice(p * 128, (p + 1) * 128) for p in range(per)]

    def tiles(n, function, *items):
        results = [function(p, *[item[:, parts[p]] for item in items]) for p in range(per)]
        return [jnp.concatenate(list(column), axis=1) for column in zip(*results)]

    def step(at, carry):
        start = at * count
        rows = range(count)
        side = lambda items: jnp.concatenate(items, axis=1)
        x0, hat1, scale1, normed1, gate_raw = {}, {}, {}, {}, {}
        hat_t, scale_t, mixed, branch = {}, {}, {}, {}
        for n in rows:

            def first(p):
                tile = xt_ref[0, start + n, :, parts[p]].astype(F32)
                hat, scale = normalize(tile)
                return tile, hat, scale, (hat * vec_ref[0] + vec_ref[1]).astype(BF)

            x0[n], hat1[n], scale1[n], normed1[n] = tiles(n, first)
            gate_raw[n] = nn(gate_wt_ref[...], normed1[n])

            def second(p):
                hat, scale = normalize(t_ref[p, start + n])
                return hat, scale, (hat * vec_ref[2] + vec_ref[3]).astype(BF)

            hat_t[n], scale_t[n], mixed[n] = tiles(n, second)
            branch[n] = nn(tri_out_t_ref[...], mixed[n])

        gate1, x1, hat2, scale2, normed2, hidden, kv_tok = {}, {}, {}, {}, {}, {}, {}
        for n in rows:

            def join(p, before, raw, add):
                gate = sigmoid(raw)
                after = before + gate * add
                hat, scale = normalize(after)
                return gate, after, hat, scale, (hat * vec_ref[4] + vec_ref[5]).astype(BF)

            gate1[n], x1[n], hat2[n], scale2[n], normed2[n] = tiles(
                n, join, x0[n], gate_raw[n], branch[n]
            )
            hidden[n] = nn(att_t_ref[...], normed2[n])
            kv_tok[n] = nn(normed2[n].T, att_kv_ref[...])

        query, key, value, gate2 = {}, {}, {}, {}
        for n in rows:

            def split(p, tile):
                gate = sigmoid(tile[3 * width :].astype(BF).astype(F32))
                asked = (tile[:width] * (scaling * LOG2E)).astype(BF)
                return asked, tile[width : 2 * width].astype(BF), tile[2 * width : 3 * width].astype(BF), gate

            query[n], key[n], value[n], gate2[n] = tiles(n, split, hidden[n])
            kv_tok[n] = kv_tok[n].astype(BF)

        pairs = [(n, h) for n in rows for h in range(heads)]

        def scores(n, h):
            return nn(kv_tok[n][:, :width] * lane_ref[h], query[n])

        outs, inverses = {}, {}

        def mix(n, h):
            both = nn(jnp.concatenate([value[n][mine[h]], ones], axis=0), e_scr[n, :, there[h]])
            inverses[n, h] = 1.0 / both[head : head + 1]
            outs[n, h] = both[:head] * inverses[n, h]

        coming = scores(*pairs[0])
        for at_pair, (n, h) in enumerate(pairs):
            score = coming
            if at_pair + 1 < len(pairs):
                coming = scores(*pairs[at_pair + 1])
            score = score + bias_ref[h]
            peak = jnp.max(score, axis=0, keepdims=True)
            e_scr[n, :, there[h]] = jnp.exp2(score - peak).astype(BF)
            if at_pair:
                mix(*pairs[at_pair - 1])
        mix(*pairs[-1])

        attended, gated, x2 = {}, {}, {}
        for n in rows:
            attended[n] = jnp.concatenate([outs[n, h] for h in range(heads)], axis=0)
            (gated[n],) = tiles(n, lambda p, gate, out: ((gate * out).astype(BF),), gate2[n], attended[n])
            x2[n] = nn(att_out_t_ref[...], gated[n])
        hat3, scale3, normed3, up, cot_tok, cot_low, grad_act = {}, {}, {}, {}, {}, {}, {}
        for n in rows:

            def third(p, before, add):
                after = before + add
                hat, scale = normalize(after)
                return after, hat, scale, (hat * vec_ref[6] + vec_ref[7]).astype(BF)

            x2[n], hat3[n], scale3[n], normed3[n] = tiles(n, third, x1[n], x2[n])
            up[n] = nn(up_t_ref[...], normed3[n])
            cot_tok[n] = load_tokens(cot_ref, start + n, order).astype(BF)
            cot_low[n] = cot_tok[n].T
            grad_act[n] = nn(down_ref[...], cot_low[n])
        act, down, grad_up, grad3 = {}, {}, {}, {}
        for n in rows:

            def silu(p, raw, grad):
                gate = sigmoid(raw)
                return (raw * gate).astype(BF), (grad * (gate * (1.0 + raw * (1.0 - gate)))).astype(BF)

            act[n], grad_up[n] = tiles(n, silu, up[n], grad_act[n])
            down[n] = nn(down_t_ref[...], act[n])
            grad3[n] = nn(up_ref[...], grad_up[n])
        grad = nn(side([act[n] for n in rows]), jnp.concatenate([cot_tok[n] for n in rows], axis=0))
        for n, part in enumerate(downs):
            g_ref[:, part] += grad[n * width : (n + 1) * width]
        g_ref[:, ups] += nt(side([normed3[n] for n in rows]), side([grad_up[n] for n in rows]))

        grad_x2, grad_x2_low, grad_gated = {}, {}, {}
        for n in rows:

            def third_back(p, grad_out, grad, hat, scale):
                g_vec_ref[6] += grad * hat
                g_vec_ref[7] += grad
                grad = grad_out.astype(F32) + normalize_back(grad, vec_ref[6], hat, scale)
                return grad, grad.astype(BF)

            grad_x2[n], grad_x2_low[n] = tiles(n, third_back, cot_low[n], grad3[n], hat3[n], scale3[n])
            grad_gated[n] = nn(att_out_ref[...], grad_x2_low[n])
            (out,) = tiles(n, lambda p, one, two: ((one + two).astype(BF),), x2[n], down[n])
            store_tokens(out_ref, start + n, order, out.T.astype(F32))
        g_ref[:, place["att_out"]] += nt(
            side([gated[n] for n in rows]), side([grad_x2_low[n] for n in rows])
        )
        grad_gate2, grad_out, center = {}, {}, {}
        for n in rows:

            def gate_back(p, grad, gate, out):
                mixed_grad = grad * gate
                scaled = [mixed_grad[mine[h]] * inverses[n, h][:, parts[p]] for h in range(heads)]
                low = jnp.concatenate(scaled, axis=0).astype(BF)
                product = low.astype(F32) * out
                centers = [jnp.sum(product[mine[h]], axis=0, keepdims=True) for h in range(heads)]
                return ((mixed_grad * out * (1.0 - gate)).astype(BF), low, *centers)

            grad_gate2[n], grad_out[n], *centers = tiles(n, gate_back, grad_gated[n], gate2[n], attended[n])
            for h in range(heads):
                center[n, h] = centers[h]

        grad_queries, grad_keys, grad_values = {}, {}, {}

        def probs(n, h):
            return nn(kv_tok[n][:, width:] * lane_ref[h], grad_out[n])

        def spread(n, h, grad_score):
            both = nn(jnp.concatenate([key[n][mine[h]], chain_ref[...]], axis=0), grad_score)
            grad_queries[n, h] = (both[:head] * scaling).astype(BF)
            g_bias_ref[h] += both[head:]
            grad_keys[n, h] = (nt(query[n][mine[h]], grad_score) * LN2).astype(BF)

        coming, behind = probs(*pairs[0]), None
        for at_pair, (n, h) in enumerate(pairs):
            grad_prob = coming
            if at_pair + 1 < len(pairs):
                coming = probs(*pairs[at_pair + 1])
            expon = e_scr[n, :, there[h]]
            grad_score = (expon.astype(F32) * (grad_prob - center[n, h])).astype(BF)
            grad_values[n, h] = nt(grad_out[n][mine[h]], expon).astype(BF)
            if behind is not None:
                spread(*behind)
            behind = (n, h, grad_score)
        spread(*behind)

        grad_hidden, grad2 = {}, {}
        for n in rows:
            blocks = [items[n, h] for items in (grad_queries, grad_keys, grad_values) for h in range(heads)]
            grad_hidden[n] = jnp.concatenate(blocks + [grad_gate2[n]], axis=0)
            grad2[n] = nn(att_ref[...], grad_hidden[n])
        g_ref[:, place["query"].start : place["gate2"].stop] += nt(
            side([normed2[n] for n in rows]), side([grad_hidden[n] for n in rows])
        )
        grad_x1, grad_branch, grad_gate1, grad_mix, grad1 = {}, {}, {}, {}, {}
        for n in rows:

            def second_back(p, grad_after, grad, hat, scale, gate, added):
                g_vec_ref[4] += grad * hat
                g_vec_ref[5] += grad
                grad = grad_after + normalize_back(grad, vec_ref[4], hat, scale)
                gated_grad = grad * gate
                return grad, gated_grad.astype(BF), (gated_grad * added * (1.0 - gate)).astype(BF)

            grad_x1[n], grad_branch[n], grad_gate1[n] = tiles(
                n, second_back, grad_x2[n], grad2[n], hat2[n], scale2[n], gate1[n], branch[n]
            )
            grad_mix[n] = nn(tri_out_ref[...], grad_branch[n])
            grad1[n] = nn(gate_w_ref[...], grad_gate1[n])
        g_ref[:, place["tri_out"]] += nt(
            side([mixed[n] for n in rows]), side([grad_branch[n] for n in rows])
        )
        g_ref[:, place["gate"]] += nt(
            side([normed1[n] for n in rows]), side([grad_gate1[n] for n in rows])
        )
        for n in rows:
            for p, part in enumerate(parts):
                grad, hat, scale = grad_mix[n][:, part], hat_t[n][:, part], scale_t[n][:, part]
                g_vec_ref[2] += grad * hat
                g_vec_ref[3] += grad
                dt_ref[p, start + n] = normalize_back(grad, vec_ref[2], hat, scale)
                grad, hat, scale = grad1[n][:, part], hat1[n][:, part], scale1[n][:, part]
                g_vec_ref[0] += grad * hat
                g_vec_ref[1] += grad
                grad = grad_x1[n][:, part] + normalize_back(grad, vec_ref[0], hat, scale)
                z_ref[start + n, :, part] = grad
        return carry

    lax.fori_loop(0, total_rows // count, step, 0)


def rows_pass(c, chunks, half, before, t, xt, cot_rows, order, bias, chain, lane, vecs, weights, heads):
    _, all_rows, width, length = xt.shape
    blocks, pieces, sub, tokens, _ = cot_rows.shape
    rows = blocks * sub
    some, count = 4, 4
    inner = sub // some
    full = lambda item: pl.BlockSpec(item.shape, lambda at, half: (0,) * item.ndim)
    of_all = pl.BlockSpec((some, width, length), lambda at, half: (c * (rows // some) + at, 0, 0))
    xt_some = pl.BlockSpec(
        (1, some, width, length), lambda at, half: (half[0], c * (rows // some) + at, 0, 0)
    )
    t_some = pl.BlockSpec(
        (length // 128, some, width, 128), lambda at, half: (0, c * (rows // some) + at, 0, 0)
    )
    dt_some = pl.BlockSpec((length // 128, some, width, 128), lambda at, half: (0, at, 0, 0))
    by_piece = pl.BlockSpec(
        (1, pieces, some, tokens, width), lambda at, half: (at // inner, 0, at % inner, 0, 0)
    )
    consts = (bias, chain, lane, vecs) + weights
    wide = weights[-1].shape[1]
    sum_shapes = [
        jax.ShapeDtypeStruct(shape, F32)
        for shape in ((width, 7 * width + 2 * wide), (8, width, 128), (heads, 16, length))
    ]
    before_specs = [full(item) for item in before[:3]]
    before_specs += [pl.BlockSpec(memory_space=pl.ANY)] * len(before[3:])
    return pl.pallas_call(
        functools.partial(rows_kernel, count, heads, order, c == 0),
        grid_spec=pltpu.PrefetchScalarGridSpec(
            num_scalar_prefetch=1,
            grid=(rows // some,),
            in_specs=before_specs + [t_some, xt_some, by_piece] + [full(item) for item in consts],
            out_specs=[by_piece, dt_some, of_all] + [full(item) for item in sum_shapes],
            scratch_shapes=[
                pltpu.VMEM((count, length, heads * length), BF),
            ],
        ),
        out_shape=[
            jax.ShapeDtypeStruct(cot_rows.shape, BF),
            by_halves(rows, width, length),
            jax.ShapeDtypeStruct((all_rows, width, length), F32),
        ]
        + sum_shapes,
        input_output_aliases={4: 2} if before else {},
        compiler_params=pltpu.CompilerParams(vmem_limit_bytes=VMEM_LIMIT),
        cost_estimate=cost(1.2e11),
        name="rows",
    )(half, *before, t, xt, cot_rows, *consts)


def edges_back_kernel(
    order, half_ref, xt_ref, z_ref, da_ref, db_ref, wt_ref, w_ref, gain_ref, shift_ref, out_ref, g_w_ref, g_vec_ref
):
    _, rows, width, length = xt_ref.shape
    count = 4

    @pl.when(pl.program_id(0) == 0)
    def _():
        g_w_ref[...] = jnp.zeros(g_w_ref.shape, F32)
        g_vec_ref[...] = jnp.zeros(g_vec_ref.shape, F32)

    def step(at, carry):
        start = at * count
        x0 = stacked(xt_ref.at[0], start, count).astype(F32)
        lanes = x0.shape[1]
        gain = widen(gain_ref[...], lanes)
        hat, scale = normalize(x0)
        normed = (hat * gain + widen(shift_ref[...], lanes)).astype(BF)
        proj = nn(wt_ref[...], normed)
        pa, pag = proj[:width], proj[width : 2 * width]
        pb, pbg = proj[2 * width : 3 * width], proj[3 * width :]
        halves = [(n, half) for n in range(count) for half in range(da_ref.shape[0])]
        da = jnp.concatenate([da_ref[half, start + n] for n, half in halves], axis=1)
        db = jnp.concatenate([db_ref[half, start + n] for n, half in halves], axis=1)
        sa, sb = sigmoid(pag), sigmoid(pbg)
        dsa, dsb = da * sa, db * sb
        grads = jnp.concatenate(
            [
                dsa.astype(BF),
                (dsa * pa * (1.0 - sa)).astype(BF),
                dsb.astype(BF),
                (dsb * pb * (1.0 - sb)).astype(BF),
            ],
            axis=0,
        )
        g_w_ref[...] += nt(normed, grads)
        grad = nn(w_ref[...], grads)
        g_vec_ref[0] += fold(grad * hat)
        g_vec_ref[1] += fold(grad)
        out = stacked(z_ref, start, count) + normalize_back(grad, gain, hat, scale)
        out = out.astype(BF)
        for n in range(count):
            store_tokens(out_ref, start + n, order, out[:, n * length : (n + 1) * length].T.astype(F32))
        return carry

    lax.fori_loop(0, rows // count, step, 0)


def edges_back(half, xt, z, da, db, order, weight_t, weight, gain, shift, shape):
    _, rows, width, length = xt.shape
    blocks, pieces, sub, tokens, _ = shape
    chunks = order[2]
    some = sub // chunks
    step = 16 // some
    inner = blocks // step
    full = lambda item: pl.BlockSpec(item.shape, lambda at, half: (0,) * item.ndim)
    xt_row = pl.BlockSpec((1, 16, width, length), lambda at, half: (half[0], at, 0, 0))
    by_row = pl.BlockSpec((16, width, length), lambda at, half: (at, 0, 0))
    by_half = pl.BlockSpec((length // 128, 16, width, 128), lambda at, half: (0, at, 0, 0))
    sum_shapes = [
        jax.ShapeDtypeStruct(weight.shape, F32),
        jax.ShapeDtypeStruct((2, width, 128), F32),
    ]
    by_piece = pl.BlockSpec(
        (step, pieces, some, tokens, width), lambda at, half: (at % inner, 0, at // inner, 0, 0)
    )
    return pl.pallas_call(
        functools.partial(edges_back_kernel, order),
        grid_spec=pltpu.PrefetchScalarGridSpec(
            num_scalar_prefetch=1,
            grid=(chunks * inner,),
            in_specs=[xt_row, by_row] + [by_half] * 2 + [full(item) for item in (weight_t, weight, gain, shift)],
            out_specs=[by_piece] + [full(item) for item in sum_shapes],
        ),
        out_shape=[jax.ShapeDtypeStruct(shape, BF)] + sum_shapes,
        compiler_params=pltpu.CompilerParams(vmem_limit_bytes=VMEM_LIMIT),
        cost_estimate=cost(4.0e10),
        name="edges_back",
    )(half, xt, z, da, db, weight_t, weight, gain, shift)


def shards(
    row_size,
    col_size,
    pair_state,
    cotangent,
    chain_lengths,
    tri_gain,
    tri_shift,
    tri_weight,
    mix_gain,
    mix_shift,
    tri_out,
    att_gain,
    att_shift,
    att_weight,
    chain_bias,
    att_out,
    trans_gain,
    trans_shift,
    up_weight,
    down_weight,
):
    heads = HEADS
    crops, own_rows, tokens, width = pair_state.shape
    length = col_size * tokens
    chunks = CHUNKS
    some = own_rows // (col_size * chunks)
    axes = ("row", "col")
    group = row_size * col_size
    order = (row_size, col_size, chunks)
    shape = (row_size, col_size, some, tokens, width)

    def swap(values):
        return lax.all_to_all(values, axes, split_axis=0, concat_axis=0, tiled=True)

    def cut(values):
        parts = values.reshape(group, chunks, some, tokens, width)
        return [parts[:, c] for c in range(chunks)]

    def join(parts):
        return jnp.stack(parts, axis=1).reshape(crops, own_rows, tokens, width)

    def across(values, bit):
        return lax.ppermute(values, "col", [(q, q ^ bit) for q in range(col_size)])

    bits = [1 << n for n in range(col_size.bit_length() - 1)]

    def doubled(items, axis, size, bits):
        for bit in bits:
            lows = [values.astype(sent) for values, sent in items]
            others = [lax.ppermute(low, axis, [(q, q ^ bit) for q in range(size)]) for low in lows]
            others = lax.optimization_barrier(tuple(others))
            items = [
                (low.astype(F32) + other.astype(F32), sent)
                for low, other, (_, sent) in zip(lows, others, items)
            ]
        return items

    whole = (row_size, col_size, some * chunks, tokens, width)
    cot_parts = cut(cotangent)

    wide = lambda item: jnp.broadcast_to(item[:, None], (width, 128))
    vecs = jnp.stack(
        [
            wide(item)
            for item in (
                tri_gain,
                tri_shift,
                mix_gain,
                mix_shift,
                att_gain,
                att_shift,
                trans_gain,
                trans_shift,
            )
        ]
    )
    edge_w = tri_weight[:, : 4 * width]
    edge_wt = edge_w.T
    gate_w = tri_weight[:, 4 * width :]
    lengths = lax.dynamic_index_in_dim(chain_lengths, lax.axis_index("row"), 0, keepdims=False)
    ends = jnp.cumsum(lengths)
    places = jnp.arange(length, dtype=jnp.int32)
    places = places.reshape(order + (some,)).transpose(1, 2, 0, 3).reshape(length)
    chain = jnp.sum((places[:, None] >= ends[None, :]).astype(jnp.int32), axis=-1)
    same = (chain[:, None] == chain[None, :]).astype(F32)
    bias = (LOG2E * chain_bias)[:, None, None] * same[None]
    which = (jnp.arange(16, dtype=jnp.int32)[:, None] == chain[None, :]).astype(F32)
    head_of = jnp.arange(width, dtype=jnp.int32) // (width // heads)
    lane = (jnp.arange(heads, dtype=jnp.int32)[:, None] == head_of[None, :]).astype(BF)
    lane = jnp.broadcast_to(lane[:, None, :], (heads, length, width))
    me = lax.axis_index("col")
    own = own_rows
    far_bit = col_size // 2
    half, core = me // far_bit, me % far_bit
    token_place = jnp.stack([(me ^ m) * tokens for m in range(col_size)])
    place = [(s * far_bit + (core ^ k)) * own for s in range(2) for k in range(2)]
    place = jnp.stack(place + [half])
    here = (core * own).reshape(1)
    half_at = half.reshape(1)
    weights = (
        gate_w,
        gate_w.T,
        tri_out,
        tri_out.T,
        att_weight.T,
        att_weight[:, width : 3 * width],
        att_weight,
        att_out,
        att_out.T,
        up_weight,
        up_weight.T,
        down_weight,
        down_weight.T,
    )
    chain_rows = which.astype(BF)

    groups = pair_state.reshape(crops, 2, far_bit, own_rows // col_size, tokens, width)
    lefts, rights, xt, cot_rows, waits = [], [], [], [], []
    for s in range(2):
        pieces = []
        for k in range(2):
            part = lax.dynamic_index_in_dim(groups[:, s], core ^ k, 1, keepdims=False)
            if len(waits) > 1:
                part = after(part, waits[-2])
            part = lax.all_to_all(part, "row", split_axis=0, concat_axis=0, tiled=True)
            waits.append(across(part, far_bit ^ k))
            pieces += [waits[-1], across(part, 1)] if k else [part, waits[-1]]
        if s:
            held = after(cot_parts[0], waits[-2], lefts[0])
            cot_rows.append(swap(held).reshape(shape))
        own_part, far, far_other, near_other = pieces
        pieces = [own_part, near_other, far, far_other]
        left, right, *xt = edges(token_place, s, pieces, xt, order, edge_wt, vecs[0], vecs[1])
        lefts.append(left)
        rights += [right, across(right, 1)]
    (xt,) = xt
    t = triangle(place, lefts, rights)
    lefts = [item for left in lefts for item in (left, across(left, 1))]
    for part in cot_parts[1:]:
        cot_rows.append(swap(after(part, t)).reshape(shape))
    state, outs, dts, sent = [], [], [], []
    pairs = [[q, q + far_bit] for q in range(far_bit)]
    for c in range(chunks):
        out, dt, z, *sums = rows_pass(
            c, chunks, half_at, state, t, xt, cot_rows[c], order, bias, chain_rows, lane, vecs, weights, heads
        )
        state = sums + [z]
        dt = turn(dt, outs)
        if c < chunks - 1:
            dts.append(dt)
            outs.append(swap(out.reshape(group, some, tokens, width)))
            near = lax.dynamic_index_in_dim(dt, half, 0, keepdims=False)
            sent.append((near, across(lax.dynamic_index_in_dim(dt, 1 - half, 0, keepdims=False), far_bit)))
    dts.append(dt)
    crossed = []
    for near, far in sent:
        crossed.append(jnp.where(half == 0, jnp.stack([near, far]), jnp.stack([far, near])))
    crossed.append(
        lax.all_to_all(dt, "col", split_axis=0, concat_axis=0, axis_index_groups=pairs, tiled=True)
    )
    g_rows, g_vec, g_bias = sums
    row_bits = [1 << n for n in range(row_size.bit_length() - 1)]
    ((g_rows, _),) = doubled([(g_rows, BF)], "row", row_size, row_bits[:1])
    da = left_back(place, dts, rights, g_rows)
    ((g_rows, _),) = doubled([(g_rows, BF)], "row", row_size, row_bits[1:])
    grads = [[item, across(item, 1)] for item in crossed[:-1]]
    grads.append([crossed[-1], across(crossed[-1], 1)])
    outs.append(swap(out.reshape(group, some, tokens, width)))
    pair_out = join(outs)
    db = right_back(here, grads, lefts, g_rows)
    back, g_edge, g_vec_edge = edges_back(
        half_at, xt, z, da, db, order, edge_wt, edge_w, vecs[0], vecs[1], whole
    )
    g_vec = jnp.sum(g_vec, axis=-1)
    g_vec_edge = jnp.sum(g_vec_edge, axis=-1)
    g_chain = jnp.sum(g_bias * which[None], axis=(1, 2))
    small = jnp.concatenate(
        [g_vec[:2] + g_vec_edge, g_vec[2:], jnp.pad(g_chain, (0, width - heads))[None]], axis=0
    )
    items = doubled([(g_edge, BF), (small, F32)], "row", row_size, row_bits)
    grad_pair = swap(back.reshape(group, some * chunks, tokens, width))
    grad_pair = grad_pair.reshape(crops, own_rows, tokens, width)
    items = doubled(items + [(g_rows, BF)], "col", col_size, bits[::-1])
    t_edge, small, total = [values for values, _ in items]
    column = lambda at, n=1: total[:, at * width : (at + n) * width]
    ff = up_weight.shape[1] // width
    t_gate, t_tri_out, t_att = column(0), column(1), column(2, 4)
    t_att_out, t_up = column(6), column(7, ff)
    t_down = jnp.concatenate([column(7 + ff + n) for n in range(ff)], axis=0)
    return (
        pair_out,
        grad_pair,
        small[0],
        small[1],
        jnp.concatenate([t_edge, t_gate], axis=1),
        small[2],
        small[3],
        t_tri_out,
        small[4],
        small[5],
        t_att,
        small[8, :heads],
        t_att_out,
        small[6],
        small[7],
        t_up,
        t_down,
    )


def solution(mesh):
    pair = P("dp", "row", "col", None)
    vector, matrix = P("dp"), P("dp", None)
    return jax.shard_map(
        functools.partial(shards, mesh.shape["row"], mesh.shape["col"]),
        mesh=mesh,
        in_specs=(pair, pair, P("dp", None)) + (P(),) * 15,
        out_specs=(
            pair,
            pair,
            vector,
            vector,
            matrix,
            vector,
            vector,
            matrix,
            vector,
            vector,
            matrix,
            vector,
            matrix,
            vector,
            vector,
            matrix,
            matrix,
        ),
        check_vma=False,
    )
```

```python
import functools
import math

import jax
import jax.numpy as jnp
from jax import lax
from jax.experimental import pallas as pl
from jax.experimental.pallas import tpu as pltpu
from jax.sharding import PartitionSpec as P

HEADS = 4
EPS = 1e-05
LOG2E = math.log2(math.e)
LN2 = math.log(2.0)
CHUNKS = 2
VMEM_LIMIT = 56 * 1024 * 1024
BF = jnp.bfloat16
F32 = jnp.float32


def nn(left, right):
    return lax.dot_general(left, right, (((1,), (0,)), ((), ())), preferred_element_type=F32)


def nt(left, right):
    return lax.dot_general(left, right, (((1,), (1,)), ((), ())), preferred_element_type=F32)


def tn(left, right):
    return lax.dot_general(left, right, (((0,), (0,)), ((), ())), preferred_element_type=F32)


def cost(flops, size=0):
    return pl.CostEstimate(flops=int(flops), bytes_accessed=int(size), transcendentals=0)


def sigmoid(values):
    return 0.5 * jnp.tanh(0.5 * values) + 0.5


def normalize(values):
    center = values - jnp.mean(values, axis=0, keepdims=True)
    spread = jnp.mean(center * center, axis=0, keepdims=True)
    scale = lax.rsqrt(spread + EPS)
    return center * scale, scale


def normalize_back(grads, gain, hat, scale):
    grad_hat = grads * gain
    first = jnp.mean(grad_hat, axis=0, keepdims=True)
    second = jnp.mean(grad_hat * hat, axis=0, keepdims=True)
    return scale * (grad_hat - first - hat * second)


def widen(column, lanes):
    return jnp.concatenate([column] * (lanes // column.shape[1]), axis=1)


def fold(values):
    parts = [values[:, at : at + 128] for at in range(0, values.shape[1], 128)]
    return functools.reduce(lambda one, two: one + two, parts)


def to_order(flat, order):
    length, width = flat.shape
    flat = flat.reshape(order + (length // math.prod(order), width))
    return flat.transpose(1, 2, 0, 3, 4).reshape(length, width)


def load_tokens(ref, row, order):
    _, pieces, some, tokens, width = ref.shape
    flat = ref[row // some, :, row % some, :, :].astype(F32)
    return to_order(flat.reshape(pieces * tokens, width), order)


def store_tokens(ref, row, order, values):
    _, pieces, some, tokens, width = ref.shape
    back = (order[1], order[2], order[0])
    flat = values.reshape(back + (pieces * tokens // math.prod(order), width))
    flat = flat.transpose(2, 0, 1, 3, 4).reshape(pieces, tokens, width)
    ref[row // some, :, row % some, :, :] = flat.astype(ref.dtype)


def stacked(ref, start, count):
    return jnp.concatenate([ref[start + n] for n in range(count)], axis=1)


def spread_out(ref, start, count, values):
    length = values.shape[1] // count
    for n in range(count):
        ref[start + n] = values[:, n * length : (n + 1) * length].astype(ref.dtype)


def no_op(*refs):
    pass


def tip(values):
    return values[(0,) * (values.ndim - 2)][:16, :128]


def after(values, *others):
    others = [tip(item) for item in others]
    anywhere = pl.BlockSpec(memory_space=pltpu.HBM)
    return pl.pallas_call(
        no_op,
        in_specs=[anywhere] * (1 + len(others)),
        out_specs=anywhere,
        out_shape=jax.ShapeDtypeStruct(values.shape, values.dtype),
        input_output_aliases={0: 0},
        cost_estimate=cost(0),
        name="after",
    )(values, *others)


def edges_kernel(order, place_ref, *refs):
    x_refs, (w_ref, gain_ref, shift_ref), rest = refs[:4], refs[4:7], refs[-6:]
    a_ref, b_ref, xt_ref, a_scr, b_scr, x_scr = rest
    width, rows, length = a_ref.shape
    pitch = a_scr.shape[1] // rows
    count = x_scr.shape[0]
    _, some, tokens, _ = x_refs[0].shape

    def step(at, carry):
        start = at * count
        turned = []
        for n in range(count):
            row = start + n
            for m, ref in enumerate(x_refs):
                there = pl.ds(pl.multiple_of(place_ref[m], tokens), tokens)
                x_scr[n, there, :] = ref[row // some, row % some].astype(F32)
            turned.append(to_order(x_scr[n], order).astype(BF).T)
        x0 = jnp.concatenate(turned, axis=1)
        for n in range(count):
            xt_ref[0, start + n] = turned[n]
        hat, _ = normalize(x0.astype(F32))
        lanes = x0.shape[1]
        normed = (hat * widen(gain_ref[...], lanes) + widen(shift_ref[...], lanes)).astype(BF)
        proj = nn(w_ref[...], normed)
        left = sigmoid(proj[width : 2 * width]) * proj[:width]
        right = sigmoid(proj[3 * width : 4 * width]) * proj[2 * width : 3 * width]
        for n in range(count):
            base = pl.multiple_of((start + n) * pitch, 8)
            for half in range(length // 128):
                part = slice(n * length + half * 128, n * length + half * 128 + 128)
                a_scr[half, pl.ds(base, width), :] = left[:, part]
                b_scr[half, pl.ds(base, width), :] = right[:, part]
        return carry

    lax.fori_loop(0, rows // count, step, 0)

    def turn(at, carry):
        for n in range(8):
            e = at * 8 + n
            for scr, out in ((a_scr, a_ref), (b_scr, b_ref)):
                halves = [scr[h, pl.ds(e, rows, stride=pitch), :] for h in range(scr.shape[0])]
                out[e] = jnp.concatenate(halves, axis=1).astype(BF)
        return carry

    lax.fori_loop(0, width // 8, turn, 0)


def edges(place, half, x_pieces, before, order, weight, gain, shift):
    blocks, rows_there, tokens, width = x_pieces[0].shape
    length = len(x_pieces) * tokens
    chunks = order[2]
    some = rows_there // chunks
    step = 16 // some
    inner = blocks // step
    rows = blocks * some * chunks
    const = lambda at, place: (0, 0)
    pitch = width + 8
    low = pl.BlockSpec((width, 16, length), lambda at, place: (0, at, 0))
    spec = pl.BlockSpec(
        (step, some, tokens, width),
        lambda at, place: (at % inner, at // inner, 0, 0),
    )
    return pl.pallas_call(
        functools.partial(edges_kernel, order),
        grid_spec=pltpu.PrefetchScalarGridSpec(
            num_scalar_prefetch=1,
            grid=(chunks * inner,),
            in_specs=[spec] * 4
            + [
                pl.BlockSpec(weight.shape, const),
                pl.BlockSpec(gain.shape, const),
                pl.BlockSpec(shift.shape, const),
            ]
            + [pl.BlockSpec(memory_space=pl.ANY)] * len(before),
            out_specs=[low, low, pl.BlockSpec((1, 16, width, length), lambda at, place: (half, at, 0, 0))],
            scratch_shapes=[
                pltpu.VMEM((length // 128, 16 * pitch, 128), F32),
                pltpu.VMEM((length // 128, 16 * pitch, 128), F32),
                pltpu.VMEM((4, length, width), F32),
            ],
        ),
        out_shape=[jax.ShapeDtypeStruct((width, rows, length), BF)] * 2
        + [jax.ShapeDtypeStruct((2, rows, width, length), BF)],
        input_output_aliases={8: 2} if before else {},
        compiler_params=pltpu.CompilerParams(vmem_limit_bytes=VMEM_LIMIT),
        cost_estimate=cost(3.0e9),
        name="edges",
    )(place, *x_pieces, weight, gain, shift, *before)


def gather_pieces(place_ref, rights, e, scr):
    for n, piece in enumerate(rights):
        rows = piece.shape[1]
        scr[e, pl.ds(pl.multiple_of(place_ref[n], rows), rows), :] = piece[e]


def by_channel(ref):
    halves, rows, some, lanes = ref.shape
    return ref.reshape(halves, rows * some, lanes)


def put_channel(ref, e, values):
    halves, rows, some, lanes = ref.shape
    flat = by_channel(ref)
    for half in range(halves):
        flat[half, pl.ds(e, rows, stride=some), :] = values[:, half * lanes : (half + 1) * lanes]


def ahead(first, count, begin, end):
    coming = begin(first)
    for e in range(first, first + count):
        here = coming
        if e + 1 < first + count:
            coming = begin(e + 1)
        end(e, here)


SOME = 16


def cut_refs(refs, *counts):
    parts = []
    for count in counts:
        parts.append(refs[:count])
        refs = refs[count:]
    return parts + list(refs)


def triangle_kernel(place_ref, *refs):
    lefts, rights, _, t_ref, scr, own_scr = cut_refs(refs, 2, 4, 1)
    for half, left in enumerate(lefts):

        @pl.when(place_ref[4] == half)
        def _():
            own_scr[...] = left[...]

    def begin(e):
        gather_pieces(place_ref, rights, e, scr)
        return nt(own_scr[e], scr[e])

    ahead(0, SOME, begin, functools.partial(put_channel, t_ref))


def high_spec(rows, length):
    return pl.BlockSpec((length // 128, rows, SOME, 128), lambda at, place: (0, 0, at, 0))


def low_spec(rows, lanes):
    return pl.BlockSpec((SOME, rows, lanes), lambda at, place: (at, 0, 0))


def by_halves(rows, width, length):
    return jax.ShapeDtypeStruct((length // 128, rows, width, 128), F32)


def channel_call(kernel, name, flops, scalar, ins, in_specs, out_specs, out_shape, scratch=()):
    return pl.pallas_call(
        kernel,
        grid_spec=pltpu.PrefetchScalarGridSpec(
            num_scalar_prefetch=1,
            grid=(ins[0].shape[0 if ins[0].ndim == 3 else 2] // SOME,),
            in_specs=in_specs,
            out_specs=out_specs,
            scratch_shapes=scratch,
        ),
        out_shape=out_shape,
        compiler_params=pltpu.CompilerParams(vmem_limit_bytes=VMEM_LIMIT),
        cost_estimate=cost(flops),
        name=name,
    )(scalar, *ins)


def triangle(place, lefts, rights, other):
    width, rows, length = lefts[0].shape
    return channel_call(
        triangle_kernel,
        "triangle",
        3.0e9,
        place,
        (*lefts, *rights, tip(other)),
        [low_spec(rows, length)] * 6 + [pl.BlockSpec(memory_space=pltpu.HBM)],
        high_spec(rows, length),
        by_halves(rows, width, length),
        [pltpu.VMEM((SOME, length, length), BF), pltpu.VMEM((SOME, rows, length), BF)],
    )


def turn_kernel(grad_ref, *refs):
    out_ref = refs[-1]
    halves, rows, some, _ = grad_ref.shape
    flat = by_channel(grad_ref)
    for e in range(some):
        for half in range(halves):
            out_ref[half, e] = flat[half, pl.ds(e, rows, stride=some), :].astype(BF)


def turn(grad, others):
    halves, rows, width, lanes = grad.shape
    some = 32
    return pl.pallas_call(
        turn_kernel,
        grid=(width // some,),
        in_specs=[pl.BlockSpec((halves, rows, some, lanes), lambda at: (0, 0, at, 0))]
        + [pl.BlockSpec(memory_space=pltpu.HBM)] * len(others),
        out_specs=pl.BlockSpec((halves, some, rows, lanes), lambda at: (0, at, 0, 0)),
        out_shape=jax.ShapeDtypeStruct((halves, width, rows, lanes), BF),
        compiler_params=pltpu.CompilerParams(vmem_limit_bytes=VMEM_LIMIT),
        cost_estimate=cost(5.0e9),
        name="turn",
    )(grad, *[tip(item) for item in others])


def right_back_kernel(chunks, here_ref, *refs):
    lefts, grads, _, db_ref, scr = cut_refs(refs, 4, 2 * chunks, 1)
    rows = db_ref.shape[1]

    def begin(e):
        pairs = [(s, k) for s in range(2) for k in range(2)]
        grad = [grads[2 * c + k][s, e] for s, k in pairs for c in range(chunks)]
        left = [lefts[2 * s + k][e] for s, k in pairs]
        return tn(jnp.concatenate(grad, axis=0), jnp.concatenate(left, axis=0))

    def end(e, db):
        scr[e] = db
        put_channel(db_ref, e, scr[e, pl.ds(pl.multiple_of(here_ref[0], rows), rows), :])

    ahead(0, SOME, begin, end)


def right_back(here, grads, lefts, other):
    width, rows, length = lefts[0].shape
    chunks = len(grads)
    _, _, some, part = grads[0][0].shape
    both = pl.BlockSpec((2, SOME, some, part), lambda at, here: (0, at, 0, 0))
    return channel_call(
        functools.partial(right_back_kernel, chunks),
        "right_back",
        2.2e10,
        here,
        [*lefts] + [item for chunk in grads for item in chunk] + [tip(other)],
        [low_spec(rows, length)] * 4 + [both] * (2 * chunks) + [pl.BlockSpec(memory_space=pltpu.HBM)],
        high_spec(rows, length),
        by_halves(rows, width, length),
        [pltpu.VMEM((SOME, part, length), F32)],
    )


def left_back_kernel(chunks, place_ref, *refs):
    rights, grads, da_ref, scr = cut_refs(refs, 4, chunks)

    def begin(e):
        gather_pieces(place_ref, rights, e, scr)
        grad = [jnp.concatenate([ref[0, e], ref[1, e]], axis=1) for ref in grads]
        return nn(jnp.concatenate(grad, axis=0), scr[e])

    ahead(0, SOME, begin, functools.partial(put_channel, da_ref))


def left_back(place, grads, rights):
    _, width, some, part = grads[0].shape
    _, rows, length = rights[0].shape
    both = pl.BlockSpec((2, SOME, some, part), lambda at, place: (0, at, 0, 0))
    return channel_call(
        functools.partial(left_back_kernel, len(grads)),
        "left_back",
        2.0e10,
        place,
        (*rights, *grads),
        [low_spec(rows, length)] * 4 + [both] * len(grads),
        high_spec(rows, length),
        by_halves(rows, width, length),
        [pltpu.VMEM((SOME, length, length), BF)],
    )


def rows_kernel(count, heads, order, first, half_ref, *refs):
    before = []
    if not first:
        before, refs = refs[:3], refs[4:]
    rows_body(count, heads, order, before, *refs)


def rows_body(
    count,
    heads,
    order,
    before,
    t_ref,
    xt_ref,
    cot_ref,
    bias_ref,
    chain_ref,
    lane_ref,
    vec_ref,
    gate_w_ref,
    gate_wt_ref,
    tri_out_ref,
    tri_out_t_ref,
    att_t_ref,
    att_kv_ref,
    att_ref,
    att_out_ref,
    att_out_t_ref,
    up_ref,
    up_t_ref,
    down_ref,
    down_t_ref,
    out_ref,
    dt_ref,
    z_ref,
    g_ref,
    g_vec_ref,
    g_bias_ref,
    e_scr,
):
    _, total_rows, width, length = xt_ref.shape
    head = width // heads
    scaling = 1.0 / math.sqrt(head)

    sums = (g_ref, g_vec_ref, g_bias_ref)
    place = {}
    for name in ("gate", "tri_out", "query", "key", "value", "gate2", "att_out"):
        place[name] = slice(len(place) * width, (len(place) + 1) * width)
    ups = slice(7 * width, 7 * width + up_ref.shape[1])
    downs = [
        slice(at, at + width) for at in range(ups.stop, ups.stop + up_ref.shape[1], width)
    ]

    @pl.when(pl.program_id(0) == 0)
    def _():
        for n, ref in enumerate(sums):
            ref[...] = before[n][...] if before else jnp.zeros(ref.shape, ref.dtype)

    per = length // 128
    mine = [slice(h * head, (h + 1) * head) for h in range(heads)]
    there = [slice(h * length, (h + 1) * length) for h in range(heads)]
    ones = jnp.ones((16, length), BF)
    parts = [slice(p * 128, (p + 1) * 128) for p in range(per)]

    def tiles(n, function, *items):
        results = [function(p, *[item[:, parts[p]] for item in items]) for p in range(per)]
        return [jnp.concatenate(list(column), axis=1) for column in zip(*results)]

    def step(at, carry):
        start = at * count
        rows = range(count)
        side = lambda items: jnp.concatenate(items, axis=1)
        x0, hat1, scale1, normed1, gate_raw = {}, {}, {}, {}, {}
        hat_t, scale_t, mixed, branch = {}, {}, {}, {}
        for n in rows:

            def first(p):
                tile = xt_ref[0, start + n, :, parts[p]].astype(F32)
                hat, scale = normalize(tile)
                return tile, hat, scale, (hat * vec_ref[0] + vec_ref[1]).astype(BF)

            x0[n], hat1[n], scale1[n], normed1[n] = tiles(n, first)
            gate_raw[n] = nn(gate_wt_ref[...], normed1[n])

            def second(p):
                hat, scale = normalize(t_ref[p, start + n])
                return hat, scale, (hat * vec_ref[2] + vec_ref[3]).astype(BF)

            hat_t[n], scale_t[n], mixed[n] = tiles(n, second)
            branch[n] = nn(tri_out_t_ref[...], mixed[n])

        gate1, x1, hat2, scale2, normed2, hidden, kv_tok = {}, {}, {}, {}, {}, {}, {}
        for n in rows:

            def join(p, before, raw, add):
                gate = sigmoid(raw)
                after = before + gate * add
                hat, scale = normalize(after)
                return gate, after, hat, scale, (hat * vec_ref[4] + vec_ref[5]).astype(BF)

            gate1[n], x1[n], hat2[n], scale2[n], normed2[n] = tiles(
                n, join, x0[n], gate_raw[n], branch[n]
            )
            hidden[n] = nn(att_t_ref[...], normed2[n])
            kv_tok[n] = nn(normed2[n].T, att_kv_ref[...])

        query, key, value, gate2 = {}, {}, {}, {}
        for n in rows:

            def split(p, tile):
                gate = sigmoid(tile[3 * width :].astype(BF).astype(F32))
                asked = (tile[:width] * (scaling * LOG2E)).astype(BF)
                return asked, tile[width : 2 * width].astype(BF), tile[2 * width : 3 * width].astype(BF), gate

            query[n], key[n], value[n], gate2[n] = tiles(n, split, hidden[n])
            kv_tok[n] = kv_tok[n].astype(BF)

        pairs = [(n, h) for n in rows for h in range(heads)]

        def scores(n, h):
            return nn(kv_tok[n][:, :width] * lane_ref[h], query[n])

        outs, inverses = {}, {}

        def mix(n, h):
            both = nn(jnp.concatenate([value[n][mine[h]], ones], axis=0), e_scr[n, :, there[h]])
            inverses[n, h] = 1.0 / both[head : head + 1]
            outs[n, h] = both[:head] * inverses[n, h]

        coming = scores(*pairs[0])
        for at_pair, (n, h) in enumerate(pairs):
            score = coming
            if at_pair + 1 < len(pairs):
                coming = scores(*pairs[at_pair + 1])
            score = score + bias_ref[h]
            peak = jnp.max(score, axis=0, keepdims=True)
            e_scr[n, :, there[h]] = jnp.exp2(score - peak).astype(BF)
            if at_pair:
                mix(*pairs[at_pair - 1])
        mix(*pairs[-1])

        attended, gated, x2 = {}, {}, {}
        for n in rows:
            attended[n] = jnp.concatenate([outs[n, h] for h in range(heads)], axis=0)
            (gated[n],) = tiles(n, lambda p, gate, out: ((gate * out).astype(BF),), gate2[n], attended[n])
            x2[n] = nn(att_out_t_ref[...], gated[n])
        hat3, scale3, normed3, up, cot_tok, cot_low, grad_act = {}, {}, {}, {}, {}, {}, {}
        for n in rows:

            def third(p, before, add):
                after = before + add
                hat, scale = normalize(after)
                return after, hat, scale, (hat * vec_ref[6] + vec_ref[7]).astype(BF)

            x2[n], hat3[n], scale3[n], normed3[n] = tiles(n, third, x1[n], x2[n])
            up[n] = nn(up_t_ref[...], normed3[n])
            cot_tok[n] = load_tokens(cot_ref, start + n, order).astype(BF)
            cot_low[n] = cot_tok[n].T
            grad_act[n] = nn(down_ref[...], cot_low[n])
        act, down, grad_up, grad3 = {}, {}, {}, {}
        for n in rows:

            def silu(p, raw, grad):
                gate = sigmoid(raw)
                return (raw * gate).astype(BF), (grad * (gate * (1.0 + raw * (1.0 - gate)))).astype(BF)

            act[n], grad_up[n] = tiles(n, silu, up[n], grad_act[n])
            down[n] = nn(down_t_ref[...], act[n])
            grad3[n] = nn(up_ref[...], grad_up[n])
        grad = nn(side([act[n] for n in rows]), jnp.concatenate([cot_tok[n] for n in rows], axis=0))
        for n, part in enumerate(downs):
            g_ref[:, part] += grad[n * width : (n + 1) * width]
        g_ref[:, ups] += nt(side([normed3[n] for n in rows]), side([grad_up[n] for n in rows]))

        grad_x2, grad_x2_low, grad_gated = {}, {}, {}
        for n in rows:

            def third_back(p, grad_out, grad, hat, scale):
                g_vec_ref[6] += grad * hat
                g_vec_ref[7] += grad
                grad = grad_out.astype(F32) + normalize_back(grad, vec_ref[6], hat, scale)
                return grad, grad.astype(BF)

            grad_x2[n], grad_x2_low[n] = tiles(n, third_back, cot_low[n], grad3[n], hat3[n], scale3[n])
            grad_gated[n] = nn(att_out_ref[...], grad_x2_low[n])
            (out,) = tiles(n, lambda p, one, two: ((one + two).astype(BF),), x2[n], down[n])
            store_tokens(out_ref, start + n, order, out.T.astype(F32))
        g_ref[:, place["att_out"]] += nt(
            side([gated[n] for n in rows]), side([grad_x2_low[n] for n in rows])
        )
        grad_gate2, grad_out, center = {}, {}, {}
        for n in rows:

            def gate_back(p, grad, gate, out):
                mixed_grad = grad * gate
                scaled = [mixed_grad[mine[h]] * inverses[n, h][:, parts[p]] for h in range(heads)]
                low = jnp.concatenate(scaled, axis=0).astype(BF)
                product = low.astype(F32) * out
                centers = [jnp.sum(product[mine[h]], axis=0, keepdims=True) for h in range(heads)]
                return ((mixed_grad * out * (1.0 - gate)).astype(BF), low, *centers)

            grad_gate2[n], grad_out[n], *centers = tiles(n, gate_back, grad_gated[n], gate2[n], attended[n])
            for h in range(heads):
                center[n, h] = centers[h]

        grad_queries, grad_keys, grad_values = {}, {}, {}

        def probs(n, h):
            return nn(kv_tok[n][:, width:] * lane_ref[h], grad_out[n])

        def spread(n, h, grad_score):
            both = nn(jnp.concatenate([key[n][mine[h]], chain_ref[...]], axis=0), grad_score)
            grad_queries[n, h] = (both[:head] * scaling).astype(BF)
            g_bias_ref[h] += both[head:]
            grad_keys[n, h] = (nt(query[n][mine[h]], grad_score) * LN2).astype(BF)

        coming, behind = probs(*pairs[0]), None
        for at_pair, (n, h) in enumerate(pairs):
            grad_prob = coming
            if at_pair + 1 < len(pairs):
                coming = probs(*pairs[at_pair + 1])
            expon = e_scr[n, :, there[h]]
            grad_score = (expon.astype(F32) * (grad_prob - center[n, h])).astype(BF)
            grad_values[n, h] = nt(grad_out[n][mine[h]], expon).astype(BF)
            if behind is not None:
                spread(*behind)
            behind = (n, h, grad_score)
        spread(*behind)

        grad_hidden, grad2 = {}, {}
        for n in rows:
            blocks = [items[n, h] for items in (grad_queries, grad_keys, grad_values) for h in range(heads)]
            grad_hidden[n] = jnp.concatenate(blocks + [grad_gate2[n]], axis=0)
            grad2[n] = nn(att_ref[...], grad_hidden[n])
        g_ref[:, place["query"].start : place["gate2"].stop] += nt(
            side([normed2[n] for n in rows]), side([grad_hidden[n] for n in rows])
        )
        grad_x1, grad_branch, grad_gate1, grad_mix, grad1 = {}, {}, {}, {}, {}
        for n in rows:

            def second_back(p, grad_after, grad, hat, scale, gate, added):
                g_vec_ref[4] += grad * hat
                g_vec_ref[5] += grad
                grad = grad_after + normalize_back(grad, vec_ref[4], hat, scale)
                gated_grad = grad * gate
                return grad, gated_grad.astype(BF), (gated_grad * added * (1.0 - gate)).astype(BF)

            grad_x1[n], grad_branch[n], grad_gate1[n] = tiles(
                n, second_back, grad_x2[n], grad2[n], hat2[n], scale2[n], gate1[n], branch[n]
            )
            grad_mix[n] = nn(tri_out_ref[...], grad_branch[n])
            grad1[n] = nn(gate_w_ref[...], grad_gate1[n])
        g_ref[:, place["tri_out"]] += nt(
            side([mixed[n] for n in rows]), side([grad_branch[n] for n in rows])
        )
        g_ref[:, place["gate"]] += nt(
            side([normed1[n] for n in rows]), side([grad_gate1[n] for n in rows])
        )
        for n in rows:
            for p, part in enumerate(parts):
                grad, hat, scale = grad_mix[n][:, part], hat_t[n][:, part], scale_t[n][:, part]
                g_vec_ref[2] += grad * hat
                g_vec_ref[3] += grad
                dt_ref[p, start + n] = normalize_back(grad, vec_ref[2], hat, scale)
                grad, hat, scale = grad1[n][:, part], hat1[n][:, part], scale1[n][:, part]
                g_vec_ref[0] += grad * hat
                g_vec_ref[1] += grad
                grad = grad_x1[n][:, part] + normalize_back(grad, vec_ref[0], hat, scale)
                z_ref[start + n, :, part] = grad
        return carry

    lax.fori_loop(0, total_rows // count, step, 0)


def rows_pass(c, chunks, half, before, t, xt, cot_rows, order, bias, chain, lane, vecs, weights, heads):
    _, all_rows, width, length = xt.shape
    blocks, pieces, sub, tokens, _ = cot_rows.shape
    rows = blocks * sub
    some, count = 4, 4
    inner = sub // some
    full = lambda item: pl.BlockSpec(item.shape, lambda at, half: (0,) * item.ndim)
    of_all = pl.BlockSpec((some, width, length), lambda at, half: (c * (rows // some) + at, 0, 0))
    xt_some = pl.BlockSpec(
        (1, some, width, length), lambda at, half: (half[0], c * (rows // some) + at, 0, 0)
    )
    t_some = pl.BlockSpec(
        (length // 128, some, width, 128), lambda at, half: (0, c * (rows // some) + at, 0, 0)
    )
    dt_some = pl.BlockSpec((length // 128, some, width, 128), lambda at, half: (0, at, 0, 0))
    by_piece = pl.BlockSpec(
        (1, pieces, some, tokens, width), lambda at, half: (at // inner, 0, at % inner, 0, 0)
    )
    consts = (bias, chain, lane, vecs) + weights
    wide = weights[-1].shape[1]
    sum_shapes = [
        jax.ShapeDtypeStruct(shape, F32)
        for shape in ((width, 7 * width + 2 * wide), (8, width, 128), (heads, 16, length))
    ]
    before_specs = [full(item) for item in before[:3]]
    before_specs += [pl.BlockSpec(memory_space=pl.ANY)] * len(before[3:])
    return pl.pallas_call(
        functools.partial(rows_kernel, count, heads, order, c == 0),
        grid_spec=pltpu.PrefetchScalarGridSpec(
            num_scalar_prefetch=1,
            grid=(rows // some,),
            in_specs=before_specs + [t_some, xt_some, by_piece] + [full(item) for item in consts],
            out_specs=[by_piece, dt_some, of_all] + [full(item) for item in sum_shapes],
            scratch_shapes=[
                pltpu.VMEM((count, length, heads * length), BF),
            ],
        ),
        out_shape=[
            jax.ShapeDtypeStruct(cot_rows.shape, BF),
            by_halves(rows, width, length),
            jax.ShapeDtypeStruct((all_rows, width, length), F32),
        ]
        + sum_shapes,
        input_output_aliases={4: 2} if before else {},
        compiler_params=pltpu.CompilerParams(vmem_limit_bytes=VMEM_LIMIT),
        cost_estimate=cost(1.2e11),
        name="rows",
    )(half, *before, t, xt, cot_rows, *consts)


def edges_back_kernel(
    order, half_ref, xt_ref, z_ref, da_ref, db_ref, wt_ref, w_ref, gain_ref, shift_ref, out_ref, g_w_ref, g_vec_ref
):
    _, rows, width, length = xt_ref.shape
    count = 4

    @pl.when(pl.program_id(0) == 0)
    def _():
        g_w_ref[...] = jnp.zeros(g_w_ref.shape, F32)
        g_vec_ref[...] = jnp.zeros(g_vec_ref.shape, F32)

    def step(at, carry):
        start = at * count
        x0 = stacked(xt_ref.at[0], start, count).astype(F32)
        lanes = x0.shape[1]
        gain = widen(gain_ref[...], lanes)
        hat, scale = normalize(x0)
        normed = (hat * gain + widen(shift_ref[...], lanes)).astype(BF)
        proj = nn(wt_ref[...], normed)
        pa, pag = proj[:width], proj[width : 2 * width]
        pb, pbg = proj[2 * width : 3 * width], proj[3 * width :]
        halves = [(n, half) for n in range(count) for half in range(da_ref.shape[0])]
        da = jnp.concatenate([da_ref[half, start + n] for n, half in halves], axis=1)
        db = jnp.concatenate([db_ref[half, start + n] for n, half in halves], axis=1)
        sa, sb = sigmoid(pag), sigmoid(pbg)
        dsa, dsb = da * sa, db * sb
        grads = jnp.concatenate(
            [
                dsa.astype(BF),
                (dsa * pa * (1.0 - sa)).astype(BF),
                dsb.astype(BF),
                (dsb * pb * (1.0 - sb)).astype(BF),
            ],
            axis=0,
        )
        g_w_ref[...] += nt(normed, grads)
        grad = nn(w_ref[...], grads)
        g_vec_ref[0] += fold(grad * hat)
        g_vec_ref[1] += fold(grad)
        out = stacked(z_ref, start, count) + normalize_back(grad, gain, hat, scale)
        out = out.astype(BF)
        for n in range(count):
            store_tokens(out_ref, start + n, order, out[:, n * length : (n + 1) * length].T.astype(F32))
        return carry

    lax.fori_loop(0, rows // count, step, 0)


def edges_back(half, xt, z, da, db, order, weight_t, weight, gain, shift, shape):
    _, rows, width, length = xt.shape
    blocks, pieces, sub, tokens, _ = shape
    chunks = order[2]
    some = sub // chunks
    step = 16 // some
    inner = blocks // step
    full = lambda item: pl.BlockSpec(item.shape, lambda at, half: (0,) * item.ndim)
    xt_row = pl.BlockSpec((1, 16, width, length), lambda at, half: (half[0], at, 0, 0))
    by_row = pl.BlockSpec((16, width, length), lambda at, half: (at, 0, 0))
    by_half = pl.BlockSpec((length // 128, 16, width, 128), lambda at, half: (0, at, 0, 0))
    sum_shapes = [
        jax.ShapeDtypeStruct(weight.shape, F32),
        jax.ShapeDtypeStruct((2, width, 128), F32),
    ]
    by_piece = pl.BlockSpec(
        (step, pieces, some, tokens, width), lambda at, half: (at % inner, 0, at // inner, 0, 0)
    )
    return pl.pallas_call(
        functools.partial(edges_back_kernel, order),
        grid_spec=pltpu.PrefetchScalarGridSpec(
            num_scalar_prefetch=1,
            grid=(chunks * inner,),
            in_specs=[xt_row, by_row] + [by_half] * 2 + [full(item) for item in (weight_t, weight, gain, shift)],
            out_specs=[by_piece] + [full(item) for item in sum_shapes],
        ),
        out_shape=[jax.ShapeDtypeStruct(shape, BF)] + sum_shapes,
        compiler_params=pltpu.CompilerParams(vmem_limit_bytes=VMEM_LIMIT),
        cost_estimate=cost(4.0e10),
        name="edges_back",
    )(half, xt, z, da, db, weight_t, weight, gain, shift)


def shards(
    row_size,
    col_size,
    pair_state,
    cotangent,
    chain_lengths,
    tri_gain,
    tri_shift,
    tri_weight,
    mix_gain,
    mix_shift,
    tri_out,
    att_gain,
    att_shift,
    att_weight,
    chain_bias,
    att_out,
    trans_gain,
    trans_shift,
    up_weight,
    down_weight,
):
    heads = HEADS
    crops, own_rows, tokens, width = pair_state.shape
    length = col_size * tokens
    chunks = CHUNKS
    some = own_rows // (col_size * chunks)
    axes = ("row", "col")
    group = row_size * col_size
    order = (row_size, col_size, chunks)
    shape = (row_size, col_size, some, tokens, width)

    def swap(values):
        return lax.all_to_all(values, axes, split_axis=0, concat_axis=0, tiled=True)

    def cut(values):
        parts = values.reshape(group, chunks, some, tokens, width)
        return [parts[:, c] for c in range(chunks)]

    def join(parts):
        return jnp.stack(parts, axis=1).reshape(crops, own_rows, tokens, width)

    def across(values, bit):
        return lax.ppermute(values, "col", [(q, q ^ bit) for q in range(col_size)])

    bits = [1 << n for n in range(col_size.bit_length() - 1)]

    def doubled(items, axis, size, bits):
        for bit in bits:
            lows = [values.astype(sent) for values, sent in items]
            others = [lax.ppermute(low, axis, [(q, q ^ bit) for q in range(size)]) for low in lows]
            others = lax.optimization_barrier(tuple(others))
            items = [
                (low.astype(F32) + other.astype(F32), sent)
                for low, other, (_, sent) in zip(lows, others, items)
            ]
        return items

    def summed_over_rows(values, sent):
        low = values.astype(sent)
        terms = [low.astype(F32)]
        for m in range(1, row_size):
            other = lax.ppermute(low, "row", [(r, r ^ m) for r in range(row_size)])
            terms.append(other.astype(F32))
        while len(terms) > 1:
            terms = [terms[n] + terms[n + 1] for n in range(0, len(terms), 2)]
        return terms[0]

    whole = (row_size, col_size, some * chunks, tokens, width)
    cot_parts = cut(cotangent)

    wide = lambda item: jnp.broadcast_to(item[:, None], (width, 128))
    vecs = jnp.stack(
        [
            wide(item)
            for item in (
                tri_gain,
                tri_shift,
                mix_gain,
                mix_shift,
                att_gain,
                att_shift,
                trans_gain,
                trans_shift,
            )
        ]
    )
    edge_w = tri_weight[:, : 4 * width]
    edge_wt = edge_w.T
    gate_w = tri_weight[:, 4 * width :]
    lengths = lax.dynamic_index_in_dim(chain_lengths, lax.axis_index("row"), 0, keepdims=False)
    ends = jnp.cumsum(lengths)
    places = jnp.arange(length, dtype=jnp.int32)
    places = places.reshape(order + (some,)).transpose(1, 2, 0, 3).reshape(length)
    chain = jnp.sum((places[:, None] >= ends[None, :]).astype(jnp.int32), axis=-1)
    same = (chain[:, None] == chain[None, :]).astype(F32)
    bias = (LOG2E * chain_bias)[:, None, None] * same[None]
    which = (jnp.arange(16, dtype=jnp.int32)[:, None] == chain[None, :]).astype(F32)
    head_of = jnp.arange(width, dtype=jnp.int32) // (width // heads)
    lane = (jnp.arange(heads, dtype=jnp.int32)[:, None] == head_of[None, :]).astype(BF)
    lane = jnp.broadcast_to(lane[:, None, :], (heads, length, width))
    me = lax.axis_index("col")
    own = own_rows
    far_bit = col_size // 2
    half, core = me // far_bit, me % far_bit
    token_place = jnp.stack([(me ^ m) * tokens for m in range(col_size)])
    place = [(s * far_bit + (core ^ k)) * own for s in range(2) for k in range(2)]
    place = jnp.stack(place + [half])
    here = (core * own).reshape(1)
    half_at = half.reshape(1)
    weights = (
        gate_w,
        gate_w.T,
        tri_out,
        tri_out.T,
        att_weight.T,
        att_weight[:, width : 3 * width],
        att_weight,
        att_out,
        att_out.T,
        up_weight,
        up_weight.T,
        down_weight,
        down_weight.T,
    )
    chain_rows = which.astype(BF)

    groups = pair_state.reshape(crops, 2, far_bit, own_rows // col_size, tokens, width)
    lefts, rights, xt, cot_rows, waits = [], [], [], [], []
    for s in range(2):
        pieces = []
        for k in range(2):
            part = lax.dynamic_index_in_dim(groups[:, s], core ^ k, 1, keepdims=False)
            if len(waits) > 1:
                part = after(part, waits[-2])
            part = lax.all_to_all(part, "row", split_axis=0, concat_axis=0, tiled=True)
            waits.append(across(part, far_bit ^ k))
            pieces += [waits[-1], across(part, 1)] if k else [part, waits[-1]]
        if s:
            cot_rows.append(swap(cot_parts[0]).reshape(shape))
        own_part, far, far_other, near_other = pieces
        pieces = [own_part, near_other, far, far_other]
        left, right, *xt = edges(token_place, s, pieces, xt, order, edge_wt, vecs[0], vecs[1])
        lefts.append(left)
        rights += [right, across(right, 1)]
    (xt,) = xt
    t = triangle(place, lefts, rights, cot_rows[0])
    lefts = [item for left in lefts for item in (left, across(left, 1))]
    for part in cot_parts[1:]:
        cot_rows.append(swap(part).reshape(shape))
    state, outs, dts, sent = [], [], [], []
    pairs = [[q, q + far_bit] for q in range(far_bit)]
    for c in range(chunks):
        out, dt, z, *sums = rows_pass(
            c, chunks, half_at, state, t, xt, cot_rows[c], order, bias, chain_rows, lane, vecs, weights, heads
        )
        state = sums + [z]
        dt = turn(dt, outs)
        if c < chunks - 1:
            dts.append(dt)
            outs.append(swap(out.reshape(group, some, tokens, width)))
            near = lax.dynamic_index_in_dim(dt, half, 0, keepdims=False)
            sent.append((near, across(lax.dynamic_index_in_dim(dt, 1 - half, 0, keepdims=False), far_bit)))
    dts.append(dt)
    crossed = []
    for near, far in sent:
        crossed.append(jnp.where(half == 0, jnp.stack([near, far]), jnp.stack([far, near])))
    crossed.append(
        lax.all_to_all(dt, "col", split_axis=0, concat_axis=0, axis_index_groups=pairs, tiled=True)
    )
    g_rows, g_vec, g_bias = sums
    row_bits = [1 << n for n in range(row_size.bit_length() - 1)]
    ((g_rows, _),) = doubled([(g_rows, BF)], "row", row_size, row_bits[:1])
    da = left_back(place, dts, rights)
    ((g_rows, _),) = doubled([(g_rows, BF)], "row", row_size, row_bits[1:])
    grads = [[item, across(item, 1)] for item in crossed[:-1]]
    crossed[-1] = after(crossed[-1], da)
    grads.append([crossed[-1], across(crossed[-1], 1)])
    outs.append(swap(out.reshape(group, some, tokens, width)))
    pair_out = join(outs)
    db = right_back(here, grads, lefts, g_rows)
    back, g_edge, g_vec_edge = edges_back(
        half_at, xt, z, da, db, order, edge_wt, edge_w, vecs[0], vecs[1], whole
    )
    g_vec = jnp.sum(g_vec, axis=-1)
    g_vec_edge = jnp.sum(g_vec_edge, axis=-1)
    g_chain = jnp.sum(g_bias * which[None], axis=(1, 2))
    small = jnp.concatenate(
        [g_vec[:2] + g_vec_edge, g_vec[2:], jnp.pad(g_chain, (0, width - heads))[None]], axis=0
    )
    grad_pair = swap(back.reshape(group, some * chunks, tokens, width))
    grad_pair = grad_pair.reshape(crops, own_rows, tokens, width)
    g_rows = after(g_rows, pair_out, back)
    ((total, _),) = doubled([(g_rows, BF)], "col", col_size, bits[::-1])
    items = [(summed_over_rows(g_edge, BF), BF), (summed_over_rows(small, F32), F32)]
    t_edge, small = [values for values, _ in doubled(items, "col", col_size, bits[::-1])]
    column = lambda at, n=1: total[:, at * width : (at + n) * width]
    ff = up_weight.shape[1] // width
    t_gate, t_tri_out, t_att = column(0), column(1), column(2, 4)
    t_att_out, t_up = column(6), column(7, ff)
    t_down = jnp.concatenate([column(7 + ff + n) for n in range(ff)], axis=0)
    return (
        pair_out,
        grad_pair,
        small[0],
        small[1],
        jnp.concatenate([t_edge, t_gate], axis=1),
        small[2],
        small[3],
        t_tri_out,
        small[4],
        small[5],
        t_att,
        small[8, :heads],
        t_att_out,
        small[6],
        small[7],
        t_up,
        t_down,
    )


def solution(mesh):
    pair = P("dp", "row", "col", None)
    vector, matrix = P("dp"), P("dp", None)
    return jax.shard_map(
        functools.partial(shards, mesh.shape["row"], mesh.shape["col"]),
        mesh=mesh,
        in_specs=(pair, pair, P("dp", None)) + (P(),) * 15,
        out_specs=(
            pair,
            pair,
            vector,
            vector,
            matrix,
            vector,
            vector,
            matrix,
            vector,
            vector,
            matrix,
            vector,
            matrix,
            vector,
            vector,
            matrix,
            matrix,
        ),
        check_vma=False,
    )
```

```python
import functools
import math

import jax
import jax.numpy as jnp
from jax import lax
from jax.experimental import pallas as pl
from jax.experimental.pallas import tpu as pltpu
from jax.sharding import PartitionSpec as P

HEADS = 4
EPS = 1e-05
LOG2E = math.log2(math.e)
LN2 = math.log(2.0)
CHUNKS = 2
VMEM_LIMIT = 56 * 1024 * 1024
BF = jnp.bfloat16
F32 = jnp.float32


def nn(left, right):
    return lax.dot_general(left, right, (((1,), (0,)), ((), ())), preferred_element_type=F32)


def nt(left, right):
    return lax.dot_general(left, right, (((1,), (1,)), ((), ())), preferred_element_type=F32)


def tn(left, right):
    return lax.dot_general(left, right, (((0,), (0,)), ((), ())), preferred_element_type=F32)


def cost(flops, size=0):
    return pl.CostEstimate(flops=int(flops), bytes_accessed=int(size), transcendentals=0)


def sigmoid(values):
    return 0.5 * jnp.tanh(0.5 * values) + 0.5


def normalize(values):
    center = values - jnp.mean(values, axis=0, keepdims=True)
    spread = jnp.mean(center * center, axis=0, keepdims=True)
    scale = lax.rsqrt(spread + EPS)
    return center * scale, scale


def normalize_back(grads, gain, hat, scale):
    grad_hat = grads * gain
    first = jnp.mean(grad_hat, axis=0, keepdims=True)
    second = jnp.mean(grad_hat * hat, axis=0, keepdims=True)
    return scale * (grad_hat - first - hat * second)


def widen(column, lanes):
    return jnp.concatenate([column] * (lanes // column.shape[1]), axis=1)


def fold(values):
    parts = [values[:, at : at + 128] for at in range(0, values.shape[1], 128)]
    return functools.reduce(lambda one, two: one + two, parts)


def to_order(flat, order):
    length, width = flat.shape
    flat = flat.reshape(order + (length // math.prod(order), width))
    return flat.transpose(1, 2, 0, 3, 4).reshape(length, width)


def load_tokens(ref, row, order):
    _, pieces, some, tokens, width = ref.shape
    flat = ref[row // some, :, row % some, :, :].astype(F32)
    return to_order(flat.reshape(pieces * tokens, width), order)


def store_tokens(ref, row, order, values):
    _, pieces, some, tokens, width = ref.shape
    back = (order[1], order[2], order[0])
    flat = values.reshape(back + (pieces * tokens // math.prod(order), width))
    flat = flat.transpose(2, 0, 1, 3, 4).reshape(pieces, tokens, width)
    ref[row // some, :, row % some, :, :] = flat.astype(ref.dtype)


def stacked(ref, start, count):
    return jnp.concatenate([ref[start + n] for n in range(count)], axis=1)


def spread_out(ref, start, count, values):
    length = values.shape[1] // count
    for n in range(count):
        ref[start + n] = values[:, n * length : (n + 1) * length].astype(ref.dtype)


def no_op(*refs):
    pass


def tip(values):
    return values[(0,) * (values.ndim - 2)][:16, :128]


def after(values, *others):
    others = [tip(item) for item in others]
    anywhere = pl.BlockSpec(memory_space=pltpu.HBM)
    return pl.pallas_call(
        no_op,
        in_specs=[anywhere] * (1 + len(others)),
        out_specs=anywhere,
        out_shape=jax.ShapeDtypeStruct(values.shape, values.dtype),
        input_output_aliases={0: 0},
        cost_estimate=cost(0),
        name="after",
    )(values, *others)


def edges_kernel(order, place_ref, *refs):
    x_refs, (w_ref, gain_ref, shift_ref), rest = refs[:4], refs[4:7], refs[-6:]
    a_ref, b_ref, xt_ref, a_scr, b_scr, x_scr = rest
    width, rows, length = a_ref.shape
    pitch = a_scr.shape[1] // rows
    count = x_scr.shape[0]
    _, some, tokens, _ = x_refs[0].shape

    def step(at, carry):
        start = at * count
        turned = []
        for n in range(count):
            row = start + n
            for m, ref in enumerate(x_refs):
                there = pl.ds(pl.multiple_of(place_ref[m], tokens), tokens)
                x_scr[n, there, :] = ref[row // some, row % some].astype(F32)
            turned.append(to_order(x_scr[n], order).astype(BF).T)
        x0 = jnp.concatenate(turned, axis=1)
        for n in range(count):
            xt_ref[0, start + n] = turned[n]
        hat, _ = normalize(x0.astype(F32))
        lanes = x0.shape[1]
        normed = (hat * widen(gain_ref[...], lanes) + widen(shift_ref[...], lanes)).astype(BF)
        proj = nn(w_ref[...], normed)
        left = sigmoid(proj[width : 2 * width]) * proj[:width]
        right = sigmoid(proj[3 * width : 4 * width]) * proj[2 * width : 3 * width]
        for n in range(count):
            base = pl.multiple_of((start + n) * pitch, 8)
            for half in range(length // 128):
                part = slice(n * length + half * 128, n * length + half * 128 + 128)
                a_scr[half, pl.ds(base, width), :] = left[:, part]
                b_scr[half, pl.ds(base, width), :] = right[:, part]
        return carry

    lax.fori_loop(0, rows // count, step, 0)

    def turn(at, carry):
        for n in range(8):
            e = at * 8 + n
            for scr, out in ((a_scr, a_ref), (b_scr, b_ref)):
                halves = [scr[h, pl.ds(e, rows, stride=pitch), :] for h in range(scr.shape[0])]
                out[e] = jnp.concatenate(halves, axis=1).astype(BF)
        return carry

    lax.fori_loop(0, width // 8, turn, 0)


def edges(place, half, x_pieces, before, others, order, weight, gain, shift):
    blocks, rows_there, tokens, width = x_pieces[0].shape
    length = len(x_pieces) * tokens
    chunks = order[2]
    some = rows_there // chunks
    step = 16 // some
    inner = blocks // step
    rows = blocks * some * chunks
    const = lambda at, place: (0, 0)
    pitch = width + 8
    low = pl.BlockSpec((width, 16, length), lambda at, place: (0, at, 0))
    spec = pl.BlockSpec(
        (step, some, tokens, width),
        lambda at, place: (at % inner, at // inner, 0, 0),
    )
    return pl.pallas_call(
        functools.partial(edges_kernel, order),
        grid_spec=pltpu.PrefetchScalarGridSpec(
            num_scalar_prefetch=1,
            grid=(chunks * inner,),
            in_specs=[spec] * 4
            + [
                pl.BlockSpec(weight.shape, const),
                pl.BlockSpec(gain.shape, const),
                pl.BlockSpec(shift.shape, const),
            ]
            + [pl.BlockSpec(memory_space=pl.ANY)] * len(before)
            + [pl.BlockSpec(memory_space=pltpu.HBM)] * len(others),
            out_specs=[low, low, pl.BlockSpec((1, 16, width, length), lambda at, place: (half, at, 0, 0))],
            scratch_shapes=[
                pltpu.VMEM((length // 128, 16 * pitch, 128), F32),
                pltpu.VMEM((length // 128, 16 * pitch, 128), F32),
                pltpu.VMEM((4, length, width), F32),
            ],
        ),
        out_shape=[jax.ShapeDtypeStruct((width, rows, length), BF)] * 2
        + [jax.ShapeDtypeStruct((2, rows, width, length), BF)],
        input_output_aliases={8: 2} if before else {},
        compiler_params=pltpu.CompilerParams(vmem_limit_bytes=VMEM_LIMIT),
        cost_estimate=cost(3.0e9),
        name="edges",
    )(place, *x_pieces, weight, gain, shift, *before, *[tip(item) for item in others])


def gather_pieces(place_ref, rights, e, scr):
    for n, piece in enumerate(rights):
        rows = piece.shape[1]
        scr[e, pl.ds(pl.multiple_of(place_ref[n], rows), rows), :] = piece[e]


def by_channel(ref):
    halves, rows, some, lanes = ref.shape
    return ref.reshape(halves, rows * some, lanes)


def put_channel(ref, e, values):
    halves, rows, some, lanes = ref.shape
    flat = by_channel(ref)
    for half in range(halves):
        flat[half, pl.ds(e, rows, stride=some), :] = values[:, half * lanes : (half + 1) * lanes]


def ahead(first, count, begin, end):
    coming = begin(first)
    for e in range(first, first + count):
        here = coming
        if e + 1 < first + count:
            coming = begin(e + 1)
        end(e, here)


SOME = 16


def cut_refs(refs, *counts):
    parts = []
    for count in counts:
        parts.append(refs[:count])
        refs = refs[count:]
    return parts + list(refs)


def triangle_kernel(place_ref, *refs):
    lefts, rights, t_ref, scr, own_scr = cut_refs(refs, 2, 4)
    for half, left in enumerate(lefts):

        @pl.when(place_ref[4] == half)
        def _():
            own_scr[...] = left[...]

    def begin(e):
        gather_pieces(place_ref, rights, e, scr)
        return nt(own_scr[e], scr[e])

    ahead(0, SOME, begin, functools.partial(put_channel, t_ref))


def high_spec(rows, length):
    return pl.BlockSpec((length // 128, rows, SOME, 128), lambda at, place: (0, 0, at, 0))


def low_spec(rows, lanes):
    return pl.BlockSpec((SOME, rows, lanes), lambda at, place: (at, 0, 0))


def by_halves(rows, width, length):
    return jax.ShapeDtypeStruct((length // 128, rows, width, 128), F32)


def channel_call(kernel, name, flops, scalar, ins, in_specs, out_specs, out_shape, scratch=()):
    return pl.pallas_call(
        kernel,
        grid_spec=pltpu.PrefetchScalarGridSpec(
            num_scalar_prefetch=1,
            grid=(ins[0].shape[0 if ins[0].ndim == 3 else 2] // SOME,),
            in_specs=in_specs,
            out_specs=out_specs,
            scratch_shapes=scratch,
        ),
        out_shape=out_shape,
        compiler_params=pltpu.CompilerParams(vmem_limit_bytes=VMEM_LIMIT),
        cost_estimate=cost(flops),
        name=name,
    )(scalar, *ins)


def triangle(place, lefts, rights):
    width, rows, length = lefts[0].shape
    return channel_call(
        triangle_kernel,
        "triangle",
        3.0e9,
        place,
        (*lefts, *rights),
        [low_spec(rows, length)] * 6,
        high_spec(rows, length),
        by_halves(rows, width, length),
        [pltpu.VMEM((SOME, length, length), BF), pltpu.VMEM((SOME, rows, length), BF)],
    )


def turn_kernel(grad_ref, *refs):
    out_ref = refs[-1]
    halves, rows, some, _ = grad_ref.shape
    flat = by_channel(grad_ref)
    for e in range(some):
        for half in range(halves):
            out_ref[half, e] = flat[half, pl.ds(e, rows, stride=some), :].astype(BF)


def turn(grad, others):
    halves, rows, width, lanes = grad.shape
    some = 32
    return pl.pallas_call(
        turn_kernel,
        grid=(width // some,),
        in_specs=[pl.BlockSpec((halves, rows, some, lanes), lambda at: (0, 0, at, 0))]
        + [pl.BlockSpec(memory_space=pltpu.HBM)] * len(others),
        out_specs=pl.BlockSpec((halves, some, rows, lanes), lambda at: (0, at, 0, 0)),
        out_shape=jax.ShapeDtypeStruct((halves, width, rows, lanes), BF),
        compiler_params=pltpu.CompilerParams(vmem_limit_bytes=VMEM_LIMIT),
        cost_estimate=cost(5.0e9),
        name="turn",
    )(grad, *[tip(item) for item in others])


def right_back_kernel(chunks, here_ref, *refs):
    lefts, grads, _, db_ref, scr = cut_refs(refs, 4, 2 * chunks, 1)
    rows = db_ref.shape[1]

    def begin(e):
        pairs = [(s, k) for s in range(2) for k in range(2)]
        grad = [grads[2 * c + k][s, e] for s, k in pairs for c in range(chunks)]
        left = [lefts[2 * s + k][e] for s, k in pairs]
        return tn(jnp.concatenate(grad, axis=0), jnp.concatenate(left, axis=0))

    def end(e, db):
        scr[e] = db
        put_channel(db_ref, e, scr[e, pl.ds(pl.multiple_of(here_ref[0], rows), rows), :])

    ahead(0, SOME, begin, end)


def right_back(here, grads, lefts, other):
    width, rows, length = lefts[0].shape
    chunks = len(grads)
    _, _, some, part = grads[0][0].shape
    both = pl.BlockSpec((2, SOME, some, part), lambda at, here: (0, at, 0, 0))
    return channel_call(
        functools.partial(right_back_kernel, chunks),
        "right_back",
        2.2e10,
        here,
        [*lefts] + [item for chunk in grads for item in chunk] + [tip(other)],
        [low_spec(rows, length)] * 4 + [both] * (2 * chunks) + [pl.BlockSpec(memory_space=pltpu.HBM)],
        high_spec(rows, length),
        by_halves(rows, width, length),
        [pltpu.VMEM((SOME, part, length), F32)],
    )


def left_back_kernel(chunks, place_ref, *refs):
    rights, grads, _, da_ref, scr = cut_refs(refs, 4, chunks, 1)

    def begin(e):
        gather_pieces(place_ref, rights, e, scr)
        grad = [jnp.concatenate([ref[0, e], ref[1, e]], axis=1) for ref in grads]
        return nn(jnp.concatenate(grad, axis=0), scr[e])

    ahead(0, SOME, begin, functools.partial(put_channel, da_ref))


def left_back(place, grads, rights, other):
    _, width, some, part = grads[0].shape
    _, rows, length = rights[0].shape
    both = pl.BlockSpec((2, SOME, some, part), lambda at, place: (0, at, 0, 0))
    return channel_call(
        functools.partial(left_back_kernel, len(grads)),
        "left_back",
        2.0e10,
        place,
        (*rights, *grads, tip(other)),
        [low_spec(rows, length)] * 4 + [both] * len(grads) + [pl.BlockSpec(memory_space=pltpu.HBM)],
        high_spec(rows, length),
        by_halves(rows, width, length),
        [pltpu.VMEM((SOME, length, length), BF)],
    )


def rows_kernel(count, heads, order, first, half_ref, *refs):
    before = []
    if not first:
        before, refs = refs[:3], refs[4:]
    rows_body(count, heads, order, before, *refs)


def rows_body(
    count,
    heads,
    order,
    before,
    t_ref,
    xt_ref,
    cot_ref,
    bias_ref,
    chain_ref,
    lane_ref,
    vec_ref,
    gate_w_ref,
    gate_wt_ref,
    tri_out_ref,
    tri_out_t_ref,
    att_t_ref,
    att_kv_ref,
    att_ref,
    att_out_ref,
    att_out_t_ref,
    up_ref,
    up_t_ref,
    down_ref,
    down_t_ref,
    out_ref,
    dt_ref,
    z_ref,
    g_ref,
    g_vec_ref,
    g_bias_ref,
    e_scr,
):
    _, total_rows, width, length = xt_ref.shape
    head = width // heads
    scaling = 1.0 / math.sqrt(head)

    sums = (g_ref, g_vec_ref, g_bias_ref)
    place = {}
    for name in ("gate", "tri_out", "query", "key", "value", "gate2", "att_out"):
        place[name] = slice(len(place) * width, (len(place) + 1) * width)
    ups = slice(7 * width, 7 * width + up_ref.shape[1])
    downs = [
        slice(at, at + width) for at in range(ups.stop, ups.stop + up_ref.shape[1], width)
    ]

    @pl.when(pl.program_id(0) == 0)
    def _():
        for n, ref in enumerate(sums):
            ref[...] = before[n][...] if before else jnp.zeros(ref.shape, ref.dtype)

    per = length // 128
    mine = [slice(h * head, (h + 1) * head) for h in range(heads)]
    there = [slice(h * length, (h + 1) * length) for h in range(heads)]
    ones = jnp.ones((16, length), BF)
    parts = [slice(p * 128, (p + 1) * 128) for p in range(per)]

    def tiles(n, function, *items):
        results = [function(p, *[item[:, parts[p]] for item in items]) for p in range(per)]
        return [jnp.concatenate(list(column), axis=1) for column in zip(*results)]

    def step(at, carry):
        start = at * count
        rows = range(count)
        side = lambda items: jnp.concatenate(items, axis=1)
        x0, hat1, scale1, normed1, gate_raw = {}, {}, {}, {}, {}
        hat_t, scale_t, mixed, branch = {}, {}, {}, {}
        for n in rows:

            def first(p):
                tile = xt_ref[0, start + n, :, parts[p]].astype(F32)
                hat, scale = normalize(tile)
                return tile, hat, scale, (hat * vec_ref[0] + vec_ref[1]).astype(BF)

            x0[n], hat1[n], scale1[n], normed1[n] = tiles(n, first)
            gate_raw[n] = nn(gate_wt_ref[...], normed1[n])

            def second(p):
                hat, scale = normalize(t_ref[p, start + n])
                return hat, scale, (hat * vec_ref[2] + vec_ref[3]).astype(BF)

            hat_t[n], scale_t[n], mixed[n] = tiles(n, second)
            branch[n] = nn(tri_out_t_ref[...], mixed[n])

        gate1, x1, hat2, scale2, normed2, hidden, kv_tok = {}, {}, {}, {}, {}, {}, {}
        for n in rows:

            def join(p, before, raw, add):
                gate = sigmoid(raw)
                after = before + gate * add
                hat, scale = normalize(after)
                return gate, after, hat, scale, (hat * vec_ref[4] + vec_ref[5]).astype(BF)

            gate1[n], x1[n], hat2[n], scale2[n], normed2[n] = tiles(
                n, join, x0[n], gate_raw[n], branch[n]
            )
            hidden[n] = nn(att_t_ref[...], normed2[n])
            kv_tok[n] = nn(normed2[n].T, att_kv_ref[...])

        query, key, value, gate2 = {}, {}, {}, {}
        for n in rows:

            def split(p, tile):
                gate = sigmoid(tile[3 * width :].astype(BF).astype(F32))
                asked = (tile[:width] * (scaling * LOG2E)).astype(BF)
                return asked, tile[width : 2 * width].astype(BF), tile[2 * width : 3 * width].astype(BF), gate

            query[n], key[n], value[n], gate2[n] = tiles(n, split, hidden[n])
            kv_tok[n] = kv_tok[n].astype(BF)

        pairs = [(n, h) for n in rows for h in range(heads)]

        def scores(n, h):
            return nn(kv_tok[n][:, :width] * lane_ref[h], query[n])

        outs, inverses = {}, {}

        def mix(n, h):
            both = nn(jnp.concatenate([value[n][mine[h]], ones], axis=0), e_scr[n, :, there[h]])
            inverses[n, h] = 1.0 / both[head : head + 1]
            outs[n, h] = both[:head] * inverses[n, h]

        coming = scores(*pairs[0])
        for at_pair, (n, h) in enumerate(pairs):
            score = coming
            if at_pair + 1 < len(pairs):
                coming = scores(*pairs[at_pair + 1])
            score = score + bias_ref[h]
            peak = jnp.max(score, axis=0, keepdims=True)
            e_scr[n, :, there[h]] = jnp.exp2(score - peak).astype(BF)
            if at_pair:
                mix(*pairs[at_pair - 1])
        mix(*pairs[-1])

        attended, gated, x2 = {}, {}, {}
        for n in rows:
            attended[n] = jnp.concatenate([outs[n, h] for h in range(heads)], axis=0)
            (gated[n],) = tiles(n, lambda p, gate, out: ((gate * out).astype(BF),), gate2[n], attended[n])
            x2[n] = nn(att_out_t_ref[...], gated[n])
        hat3, scale3, normed3, up, cot_tok, cot_low, grad_act = {}, {}, {}, {}, {}, {}, {}
        for n in rows:

            def third(p, before, add):
                after = before + add
                hat, scale = normalize(after)
                return after, hat, scale, (hat * vec_ref[6] + vec_ref[7]).astype(BF)

            x2[n], hat3[n], scale3[n], normed3[n] = tiles(n, third, x1[n], x2[n])
            up[n] = nn(up_t_ref[...], normed3[n])
            cot_tok[n] = load_tokens(cot_ref, start + n, order).astype(BF)
            cot_low[n] = cot_tok[n].T
            grad_act[n] = nn(down_ref[...], cot_low[n])
        act, down, grad_up, grad3 = {}, {}, {}, {}
        for n in rows:

            def silu(p, raw, grad):
                gate = sigmoid(raw)
                return (raw * gate).astype(BF), (grad * (gate * (1.0 + raw * (1.0 - gate)))).astype(BF)

            act[n], grad_up[n] = tiles(n, silu, up[n], grad_act[n])
            down[n] = nn(down_t_ref[...], act[n])
            grad3[n] = nn(up_ref[...], grad_up[n])
        grad = nn(side([act[n] for n in rows]), jnp.concatenate([cot_tok[n] for n in rows], axis=0))
        for n, part in enumerate(downs):
            g_ref[:, part] += grad[n * width : (n + 1) * width]
        g_ref[:, ups] += nt(side([normed3[n] for n in rows]), side([grad_up[n] for n in rows]))

        grad_x2, grad_x2_low, grad_gated = {}, {}, {}
        for n in rows:

            def third_back(p, grad_out, grad, hat, scale):
                g_vec_ref[6] += grad * hat
                g_vec_ref[7] += grad
                grad = grad_out.astype(F32) + normalize_back(grad, vec_ref[6], hat, scale)
                return grad, grad.astype(BF)

            grad_x2[n], grad_x2_low[n] = tiles(n, third_back, cot_low[n], grad3[n], hat3[n], scale3[n])
            grad_gated[n] = nn(att_out_ref[...], grad_x2_low[n])
            (out,) = tiles(n, lambda p, one, two: ((one + two).astype(BF),), x2[n], down[n])
            store_tokens(out_ref, start + n, order, out.T.astype(F32))
        g_ref[:, place["att_out"]] += nt(
            side([gated[n] for n in rows]), side([grad_x2_low[n] for n in rows])
        )
        grad_gate2, grad_out, center = {}, {}, {}
        for n in rows:

            def gate_back(p, grad, gate, out):
                mixed_grad = grad * gate
                scaled = [mixed_grad[mine[h]] * inverses[n, h][:, parts[p]] for h in range(heads)]
                low = jnp.concatenate(scaled, axis=0).astype(BF)
                product = low.astype(F32) * out
                centers = [jnp.sum(product[mine[h]], axis=0, keepdims=True) for h in range(heads)]
                return ((mixed_grad * out * (1.0 - gate)).astype(BF), low, *centers)

            grad_gate2[n], grad_out[n], *centers = tiles(n, gate_back, grad_gated[n], gate2[n], attended[n])
            for h in range(heads):
                center[n, h] = centers[h]

        grad_queries, grad_keys, grad_values = {}, {}, {}

        def probs(n, h):
            return nn(kv_tok[n][:, width:] * lane_ref[h], grad_out[n])

        def spread(n, h, grad_score):
            both = nn(jnp.concatenate([key[n][mine[h]], chain_ref[...]], axis=0), grad_score)
            grad_queries[n, h] = (both[:head] * scaling).astype(BF)
            g_bias_ref[h] += both[head:]
            grad_keys[n, h] = (nt(query[n][mine[h]], grad_score) * LN2).astype(BF)

        coming, behind = probs(*pairs[0]), None
        for at_pair, (n, h) in enumerate(pairs):
            grad_prob = coming
            if at_pair + 1 < len(pairs):
                coming = probs(*pairs[at_pair + 1])
            expon = e_scr[n, :, there[h]]
            grad_score = (expon.astype(F32) * (grad_prob - center[n, h])).astype(BF)
            grad_values[n, h] = nt(grad_out[n][mine[h]], expon).astype(BF)
            if behind is not None:
                spread(*behind)
            behind = (n, h, grad_score)
        spread(*behind)

        grad_hidden, grad2 = {}, {}
        for n in rows:
            blocks = [items[n, h] for items in (grad_queries, grad_keys, grad_values) for h in range(heads)]
            grad_hidden[n] = jnp.concatenate(blocks + [grad_gate2[n]], axis=0)
            grad2[n] = nn(att_ref[...], grad_hidden[n])
        g_ref[:, place["query"].start : place["gate2"].stop] += nt(
            side([normed2[n] for n in rows]), side([grad_hidden[n] for n in rows])
        )
        grad_x1, grad_branch, grad_gate1, grad_mix, grad1 = {}, {}, {}, {}, {}
        for n in rows:

            def second_back(p, grad_after, grad, hat, scale, gate, added):
                g_vec_ref[4] += grad * hat
                g_vec_ref[5] += grad
                grad = grad_after + normalize_back(grad, vec_ref[4], hat, scale)
                gated_grad = grad * gate
                return grad, gated_grad.astype(BF), (gated_grad * added * (1.0 - gate)).astype(BF)

            grad_x1[n], grad_branch[n], grad_gate1[n] = tiles(
                n, second_back, grad_x2[n], grad2[n], hat2[n], scale2[n], gate1[n], branch[n]
            )
            grad_mix[n] = nn(tri_out_ref[...], grad_branch[n])
            grad1[n] = nn(gate_w_ref[...], grad_gate1[n])
        g_ref[:, place["tri_out"]] += nt(
            side([mixed[n] for n in rows]), side([grad_branch[n] for n in rows])
        )
        g_ref[:, place["gate"]] += nt(
            side([normed1[n] for n in rows]), side([grad_gate1[n] for n in rows])
        )
        for n in rows:
            for p, part in enumerate(parts):
                grad, hat, scale = grad_mix[n][:, part], hat_t[n][:, part], scale_t[n][:, part]
                g_vec_ref[2] += grad * hat
                g_vec_ref[3] += grad
                dt_ref[p, start + n] = normalize_back(grad, vec_ref[2], hat, scale)
                grad, hat, scale = grad1[n][:, part], hat1[n][:, part], scale1[n][:, part]
                g_vec_ref[0] += grad * hat
                g_vec_ref[1] += grad
                grad = grad_x1[n][:, part] + normalize_back(grad, vec_ref[0], hat, scale)
                z_ref[start + n, :, part] = grad
        return carry

    lax.fori_loop(0, total_rows // count, step, 0)


def rows_pass(c, chunks, half, before, t, xt, cot_rows, order, bias, chain, lane, vecs, weights, heads):
    _, all_rows, width, length = xt.shape
    blocks, pieces, sub, tokens, _ = cot_rows.shape
    rows = blocks * sub
    some, count = 4, 4
    inner = sub // some
    full = lambda item: pl.BlockSpec(item.shape, lambda at, half: (0,) * item.ndim)
    of_all = pl.BlockSpec((some, width, length), lambda at, half: (c * (rows // some) + at, 0, 0))
    xt_some = pl.BlockSpec(
        (1, some, width, length), lambda at, half: (half[0], c * (rows // some) + at, 0, 0)
    )
    t_some = pl.BlockSpec(
        (length // 128, some, width, 128), lambda at, half: (0, c * (rows // some) + at, 0, 0)
    )
    dt_some = pl.BlockSpec((length // 128, some, width, 128), lambda at, half: (0, at, 0, 0))
    by_piece = pl.BlockSpec(
        (1, pieces, some, tokens, width), lambda at, half: (at // inner, 0, at % inner, 0, 0)
    )
    consts = (bias, chain, lane, vecs) + weights
    wide = weights[-1].shape[1]
    sum_shapes = [
        jax.ShapeDtypeStruct(shape, F32)
        for shape in ((width, 7 * width + 2 * wide), (8, width, 128), (heads, 16, length))
    ]
    before_specs = [full(item) for item in before[:3]]
    before_specs += [pl.BlockSpec(memory_space=pl.ANY)] * len(before[3:])
    return pl.pallas_call(
        functools.partial(rows_kernel, count, heads, order, c == 0),
        grid_spec=pltpu.PrefetchScalarGridSpec(
            num_scalar_prefetch=1,
            grid=(rows // some,),
            in_specs=before_specs + [t_some, xt_some, by_piece] + [full(item) for item in consts],
            out_specs=[by_piece, dt_some, of_all] + [full(item) for item in sum_shapes],
            scratch_shapes=[
                pltpu.VMEM((count, length, heads * length), BF),
            ],
        ),
        out_shape=[
            jax.ShapeDtypeStruct(cot_rows.shape, BF),
            by_halves(rows, width, length),
            jax.ShapeDtypeStruct((all_rows, width, length), F32),
        ]
        + sum_shapes,
        input_output_aliases={4: 2} if before else {},
        compiler_params=pltpu.CompilerParams(vmem_limit_bytes=VMEM_LIMIT),
        cost_estimate=cost(1.2e11),
        name="rows",
    )(half, *before, t, xt, cot_rows, *consts)


def edges_back_kernel(
    order, half_ref, xt_ref, z_ref, da_ref, db_ref, wt_ref, w_ref, gain_ref, shift_ref, out_ref, g_w_ref, g_vec_ref
):
    _, rows, width, length = xt_ref.shape
    count = 4

    @pl.when(pl.program_id(0) == 0)
    def _():
        g_w_ref[...] = jnp.zeros(g_w_ref.shape, F32)
        g_vec_ref[...] = jnp.zeros(g_vec_ref.shape, F32)

    def step(at, carry):
        start = at * count
        x0 = stacked(xt_ref.at[0], start, count).astype(F32)
        lanes = x0.shape[1]
        gain = widen(gain_ref[...], lanes)
        hat, scale = normalize(x0)
        normed = (hat * gain + widen(shift_ref[...], lanes)).astype(BF)
        proj = nn(wt_ref[...], normed)
        pa, pag = proj[:width], proj[width : 2 * width]
        pb, pbg = proj[2 * width : 3 * width], proj[3 * width :]
        halves = [(n, half) for n in range(count) for half in range(da_ref.shape[0])]
        da = jnp.concatenate([da_ref[half, start + n] for n, half in halves], axis=1)
        db = jnp.concatenate([db_ref[half, start + n] for n, half in halves], axis=1)
        sa, sb = sigmoid(pag), sigmoid(pbg)
        dsa, dsb = da * sa, db * sb
        grads = jnp.concatenate(
            [
                dsa.astype(BF),
                (dsa * pa * (1.0 - sa)).astype(BF),
                dsb.astype(BF),
                (dsb * pb * (1.0 - sb)).astype(BF),
            ],
            axis=0,
        )
        g_w_ref[...] += nt(normed, grads)
        grad = nn(w_ref[...], grads)
        g_vec_ref[0] += fold(grad * hat)
        g_vec_ref[1] += fold(grad)
        out = stacked(z_ref, start, count) + normalize_back(grad, gain, hat, scale)
        out = out.astype(BF)
        for n in range(count):
            store_tokens(out_ref, start + n, order, out[:, n * length : (n + 1) * length].T.astype(F32))
        return carry

    lax.fori_loop(0, rows // count, step, 0)


def edges_back(half, xt, z, da, db, order, weight_t, weight, gain, shift, shape):
    _, rows, width, length = xt.shape
    blocks, pieces, sub, tokens, _ = shape
    chunks = order[2]
    some = sub // chunks
    step = 16 // some
    inner = blocks // step
    full = lambda item: pl.BlockSpec(item.shape, lambda at, half: (0,) * item.ndim)
    xt_row = pl.BlockSpec((1, 16, width, length), lambda at, half: (half[0], at, 0, 0))
    by_row = pl.BlockSpec((16, width, length), lambda at, half: (at, 0, 0))
    by_half = pl.BlockSpec((length // 128, 16, width, 128), lambda at, half: (0, at, 0, 0))
    sum_shapes = [
        jax.ShapeDtypeStruct(weight.shape, F32),
        jax.ShapeDtypeStruct((2, width, 128), F32),
    ]
    by_piece = pl.BlockSpec(
        (step, pieces, some, tokens, width), lambda at, half: (at % inner, 0, at // inner, 0, 0)
    )
    return pl.pallas_call(
        functools.partial(edges_back_kernel, order),
        grid_spec=pltpu.PrefetchScalarGridSpec(
            num_scalar_prefetch=1,
            grid=(chunks * inner,),
            in_specs=[xt_row, by_row] + [by_half] * 2 + [full(item) for item in (weight_t, weight, gain, shift)],
            out_specs=[by_piece] + [full(item) for item in sum_shapes],
        ),
        out_shape=[jax.ShapeDtypeStruct(shape, BF)] + sum_shapes,
        compiler_params=pltpu.CompilerParams(vmem_limit_bytes=VMEM_LIMIT),
        cost_estimate=cost(4.0e10),
        name="edges_back",
    )(half, xt, z, da, db, weight_t, weight, gain, shift)


def shards(
    row_size,
    col_size,
    pair_state,
    cotangent,
    chain_lengths,
    tri_gain,
    tri_shift,
    tri_weight,
    mix_gain,
    mix_shift,
    tri_out,
    att_gain,
    att_shift,
    att_weight,
    chain_bias,
    att_out,
    trans_gain,
    trans_shift,
    up_weight,
    down_weight,
):
    heads = HEADS
    crops, own_rows, tokens, width = pair_state.shape
    length = col_size * tokens
    chunks = CHUNKS
    some = own_rows // (col_size * chunks)
    axes = ("row", "col")
    group = row_size * col_size
    order = (row_size, col_size, chunks)
    shape = (row_size, col_size, some, tokens, width)

    def swap(values):
        return lax.all_to_all(values, axes, split_axis=0, concat_axis=0, tiled=True)

    def cut(values):
        parts = values.reshape(group, chunks, some, tokens, width)
        return [parts[:, c] for c in range(chunks)]

    def join(parts):
        return jnp.stack(parts, axis=1).reshape(crops, own_rows, tokens, width)

    def across(values, bit):
        return lax.ppermute(values, "col", [(q, q ^ bit) for q in range(col_size)])

    bits = [1 << n for n in range(col_size.bit_length() - 1)]

    def doubled(items, axis, size, bits):
        for bit in bits:
            lows = [values.astype(sent) for values, sent in items]
            others = [lax.ppermute(low, axis, [(q, q ^ bit) for q in range(size)]) for low in lows]
            others = lax.optimization_barrier(tuple(others))
            items = [
                (low.astype(F32) + other.astype(F32), sent)
                for low, other, (_, sent) in zip(lows, others, items)
            ]
        return items

    whole = (row_size, col_size, some * chunks, tokens, width)
    cot_parts = cut(cotangent)

    wide = lambda item: jnp.broadcast_to(item[:, None], (width, 128))
    vecs = jnp.stack(
        [
            wide(item)
            for item in (
                tri_gain,
                tri_shift,
                mix_gain,
                mix_shift,
                att_gain,
                att_shift,
                trans_gain,
                trans_shift,
            )
        ]
    )
    edge_w = tri_weight[:, : 4 * width]
    edge_wt = edge_w.T
    gate_w = tri_weight[:, 4 * width :]
    lengths = lax.dynamic_index_in_dim(chain_lengths, lax.axis_index("row"), 0, keepdims=False)
    ends = jnp.cumsum(lengths)
    places = jnp.arange(length, dtype=jnp.int32)
    places = places.reshape(order + (some,)).transpose(1, 2, 0, 3).reshape(length)
    chain = jnp.sum((places[:, None] >= ends[None, :]).astype(jnp.int32), axis=-1)
    same = (chain[:, None] == chain[None, :]).astype(F32)
    bias = (LOG2E * chain_bias)[:, None, None] * same[None]
    which = (jnp.arange(16, dtype=jnp.int32)[:, None] == chain[None, :]).astype(F32)
    head_of = jnp.arange(width, dtype=jnp.int32) // (width // heads)
    lane = (jnp.arange(heads, dtype=jnp.int32)[:, None] == head_of[None, :]).astype(BF)
    lane = jnp.broadcast_to(lane[:, None, :], (heads, length, width))
    me = lax.axis_index("col")
    own = own_rows
    far_bit = col_size // 2
    half, core = me // far_bit, me % far_bit
    token_place = jnp.stack([(me ^ m) * tokens for m in range(col_size)])
    place = [(s * far_bit + (core ^ k)) * own for s in range(2) for k in range(2)]
    place = jnp.stack(place + [half])
    here = (core * own).reshape(1)
    half_at = half.reshape(1)
    weights = (
        gate_w,
        gate_w.T,
        tri_out,
        tri_out.T,
        att_weight.T,
        att_weight[:, width : 3 * width],
        att_weight,
        att_out,
        att_out.T,
        up_weight,
        up_weight.T,
        down_weight,
        down_weight.T,
    )
    chain_rows = which.astype(BF)

    groups = pair_state.reshape(crops, 2, far_bit, own_rows // col_size, tokens, width)
    x_pieces, crossings = [], []
    for s in range(2):
        pieces = []
        for k in range(2):
            part = lax.dynamic_index_in_dim(groups[:, s], core ^ k, 1, keepdims=False)
            if len(crossings) > 1:
                part = after(part, crossings[-2])
            part = lax.all_to_all(part, "row", split_axis=0, concat_axis=0, tiled=True)
            crossings.append(across(part, far_bit ^ k))
            pieces += [crossings[-1], across(part, 1)] if k else [part, crossings[-1]]
        own_part, far, far_other, near_other = pieces
        x_pieces.append([own_part, near_other, far, far_other])
    cot_rows, before = [], part
    for held in cot_parts:
        before = swap(after(held, before))
        cot_rows.append(before.reshape(shape))
    lefts, rights, xt = [], [], []
    for s, pieces in enumerate(x_pieces):
        others = [] if s else [crossings[2], cot_parts[0]]
        left, right, *xt = edges(
            token_place, s, pieces, xt, others, order, edge_wt, vecs[0], vecs[1]
        )
        lefts.append(left)
        rights += [right, across(right, 1)]
    (xt,) = xt
    t = triangle(place, lefts, rights)
    lefts = [item for left in lefts for item in (left, across(left, 1))]
    state, outs, dts, sent = [], [], [], []
    pairs = [[q, q + far_bit] for q in range(far_bit)]
    for c in range(chunks):
        out, dt, z, *sums = rows_pass(
            c, chunks, half_at, state, t, xt, cot_rows[c], order, bias, chain_rows, lane, vecs, weights, heads
        )
        state = sums + [z]
        dt = turn(dt, outs)
        if c < chunks - 1:
            dts.append(dt)
            outs.append(swap(out.reshape(group, some, tokens, width)))
            near = lax.dynamic_index_in_dim(dt, half, 0, keepdims=False)
            sent.append((near, across(lax.dynamic_index_in_dim(dt, 1 - half, 0, keepdims=False), far_bit)))
    dts.append(dt)
    crossed = []
    for near, far in sent:
        crossed.append(jnp.where(half == 0, jnp.stack([near, far]), jnp.stack([far, near])))
    crossed.append(
        lax.all_to_all(dt, "col", split_axis=0, concat_axis=0, axis_index_groups=pairs, tiled=True)
    )
    g_rows, g_vec, g_bias = sums
    row_bits = [1 << n for n in range(row_size.bit_length() - 1)]
    ((g_rows, _),) = doubled([(g_rows, BF)], "row", row_size, row_bits[:1])
    da = left_back(place, dts, rights, g_rows)
    ((g_rows, _),) = doubled([(g_rows, BF)], "row", row_size, row_bits[1:])
    grads = [[item, across(item, 1)] for item in crossed[:-1]]
    crossed[-1] = after(crossed[-1], da)
    grads.append([crossed[-1], across(crossed[-1], 1)])
    outs.append(swap(out.reshape(group, some, tokens, width)))
    pair_out = join(outs)
    db = right_back(here, grads, lefts, g_rows)
    back, g_edge, g_vec_edge = edges_back(
        half_at, xt, z, da, db, order, edge_wt, edge_w, vecs[0], vecs[1], whole
    )
    g_vec = jnp.sum(g_vec, axis=-1)
    g_vec_edge = jnp.sum(g_vec_edge, axis=-1)
    g_chain = jnp.sum(g_bias * which[None], axis=(1, 2))
    small = jnp.concatenate(
        [g_vec[:2] + g_vec_edge, g_vec[2:], jnp.pad(g_chain, (0, width - heads))[None]], axis=0
    )
    items = doubled([(g_edge, BF), (small, F32)], "row", row_size, row_bits)
    back = after(back, *[values for values, _ in items])
    grad_pair = swap(back.reshape(group, some * chunks, tokens, width))
    grad_pair = grad_pair.reshape(crops, own_rows, tokens, width)
    g_rows = after(g_rows, pair_out, back)
    items = doubled(items + [(g_rows, BF)], "col", col_size, bits[::-1])
    t_edge, small, total = [values for values, _ in items]
    column = lambda at, n=1: total[:, at * width : (at + n) * width]
    ff = up_weight.shape[1] // width
    t_gate, t_tri_out, t_att = column(0), column(1), column(2, 4)
    t_att_out, t_up = column(6), column(7, ff)
    t_down = jnp.concatenate([column(7 + ff + n) for n in range(ff)], axis=0)
    return (
        pair_out,
        grad_pair,
        small[0],
        small[1],
        jnp.concatenate([t_edge, t_gate], axis=1),
        small[2],
        small[3],
        t_tri_out,
        small[4],
        small[5],
        t_att,
        small[8, :heads],
        t_att_out,
        small[6],
        small[7],
        t_up,
        t_down,
    )


def solution(mesh):
    pair = P("dp", "row", "col", None)
    vector, matrix = P("dp"), P("dp", None)
    return jax.shard_map(
        functools.partial(shards, mesh.shape["row"], mesh.shape["col"]),
        mesh=mesh,
        in_specs=(pair, pair, P("dp", None)) + (P(),) * 15,
        out_specs=(
            pair,
            pair,
            vector,
            vector,
            matrix,
            vector,
            vector,
            matrix,
            vector,
            vector,
            matrix,
            vector,
            matrix,
            vector,
            vector,
            matrix,
            matrix,
        ),
        check_vma=False,
    )
```

```python
import functools
import math

import jax
import jax.numpy as jnp
from jax import lax
from jax.experimental import pallas as pl
from jax.experimental.pallas import tpu as pltpu
from jax.sharding import PartitionSpec as P

HEADS = 4
EPS = 1e-05
LOG2E = math.log2(math.e)
LN2 = math.log(2.0)
CHUNKS = 2
VMEM_LIMIT = 56 * 1024 * 1024
BF = jnp.bfloat16
F32 = jnp.float32


def nn(left, right):
    return lax.dot_general(left, right, (((1,), (0,)), ((), ())), preferred_element_type=F32)


def nt(left, right):
    return lax.dot_general(left, right, (((1,), (1,)), ((), ())), preferred_element_type=F32)


def tn(left, right):
    return lax.dot_general(left, right, (((0,), (0,)), ((), ())), preferred_element_type=F32)


def cost(flops, size=0):
    return pl.CostEstimate(flops=int(flops), bytes_accessed=int(size), transcendentals=0)


def sigmoid(values):
    return 0.5 * jnp.tanh(0.5 * values) + 0.5


def normalize(values):
    center = values - jnp.mean(values, axis=0, keepdims=True)
    spread = jnp.mean(center * center, axis=0, keepdims=True)
    scale = lax.rsqrt(spread + EPS)
    return center * scale, scale


def normalize_back(grads, gain, hat, scale):
    grad_hat = grads * gain
    first = jnp.mean(grad_hat, axis=0, keepdims=True)
    second = jnp.mean(grad_hat * hat, axis=0, keepdims=True)
    return scale * (grad_hat - first - hat * second)


def widen(column, lanes):
    return jnp.concatenate([column] * (lanes // column.shape[1]), axis=1)


def fold(values):
    parts = [values[:, at : at + 128] for at in range(0, values.shape[1], 128)]
    return functools.reduce(lambda one, two: one + two, parts)


def to_order(flat, order):
    length, width = flat.shape
    flat = flat.reshape(order + (length // math.prod(order), width))
    return flat.transpose(1, 2, 0, 3, 4).reshape(length, width)


def load_tokens(ref, row, order):
    _, pieces, some, tokens, width = ref.shape
    flat = ref[row // some, :, row % some, :, :].astype(F32)
    return to_order(flat.reshape(pieces * tokens, width), order)


def store_tokens(ref, row, order, values):
    _, pieces, some, tokens, width = ref.shape
    back = (order[1], order[2], order[0])
    flat = values.reshape(back + (pieces * tokens // math.prod(order), width))
    flat = flat.transpose(2, 0, 1, 3, 4).reshape(pieces, tokens, width)
    ref[row // some, :, row % some, :, :] = flat.astype(ref.dtype)


def stacked(ref, start, count):
    return jnp.concatenate([ref[start + n] for n in range(count)], axis=1)


def spread_out(ref, start, count, values):
    length = values.shape[1] // count
    for n in range(count):
        ref[start + n] = values[:, n * length : (n + 1) * length].astype(ref.dtype)


def no_op(*refs):
    pass


def tip(values):
    return values[(0,) * (values.ndim - 2)][:16, :128]


def after(values, *others):
    others = [tip(item) for item in others]
    anywhere = pl.BlockSpec(memory_space=pltpu.HBM)
    return pl.pallas_call(
        no_op,
        in_specs=[anywhere] * (1 + len(others)),
        out_specs=anywhere,
        out_shape=jax.ShapeDtypeStruct(values.shape, values.dtype),
        input_output_aliases={0: 0},
        cost_estimate=cost(0),
        name="after",
    )(values, *others)


def edges_kernel(order, place_ref, *refs):
    x_refs, (w_ref, gain_ref, shift_ref), rest = refs[:4], refs[4:7], refs[-6:]
    a_ref, b_ref, xt_ref, a_scr, b_scr, x_scr = rest
    width, rows, length = a_ref.shape
    pitch = a_scr.shape[1] // rows
    count = x_scr.shape[0]
    _, some, tokens, _ = x_refs[0].shape

    def step(at, carry):
        start = at * count
        turned = []
        for n in range(count):
            row = start + n
            for m, ref in enumerate(x_refs):
                there = pl.ds(pl.multiple_of(place_ref[m], tokens), tokens)
                x_scr[n, there, :] = ref[row // some, row % some].astype(F32)
            turned.append(to_order(x_scr[n], order).astype(BF).T)
        x0 = jnp.concatenate(turned, axis=1)
        for n in range(count):
            xt_ref[0, start + n] = turned[n]
        hat, _ = normalize(x0.astype(F32))
        lanes = x0.shape[1]
        normed = (hat * widen(gain_ref[...], lanes) + widen(shift_ref[...], lanes)).astype(BF)
        proj = nn(w_ref[...], normed)
        left = sigmoid(proj[width : 2 * width]) * proj[:width]
        right = sigmoid(proj[3 * width : 4 * width]) * proj[2 * width : 3 * width]
        for n in range(count):
            base = pl.multiple_of((start + n) * pitch, 8)
            for half in range(length // 128):
                part = slice(n * length + half * 128, n * length + half * 128 + 128)
                a_scr[half, pl.ds(base, width), :] = left[:, part]
                b_scr[half, pl.ds(base, width), :] = right[:, part]
        return carry

    lax.fori_loop(0, rows // count, step, 0)

    def turn(at, carry):
        for n in range(8):
            e = at * 8 + n
            for scr, out in ((a_scr, a_ref), (b_scr, b_ref)):
                halves = [scr[h, pl.ds(e, rows, stride=pitch), :] for h in range(scr.shape[0])]
                out[e] = jnp.concatenate(halves, axis=1).astype(BF)
        return carry

    lax.fori_loop(0, width // 8, turn, 0)


def edges(place, half, x_pieces, before, others, order, weight, gain, shift):
    blocks, rows_there, tokens, width = x_pieces[0].shape
    length = len(x_pieces) * tokens
    chunks = order[2]
    some = rows_there // chunks
    step = 16 // some
    inner = blocks // step
    rows = blocks * some * chunks
    const = lambda at, place: (0, 0)
    pitch = width + 8
    low = pl.BlockSpec((width, 16, length), lambda at, place: (0, at, 0))
    spec = pl.BlockSpec(
        (step, some, tokens, width),
        lambda at, place: (at % inner, at // inner, 0, 0),
    )
    return pl.pallas_call(
        functools.partial(edges_kernel, order),
        grid_spec=pltpu.PrefetchScalarGridSpec(
            num_scalar_prefetch=1,
            grid=(chunks * inner,),
            in_specs=[spec] * 4
            + [
                pl.BlockSpec(weight.shape, const),
                pl.BlockSpec(gain.shape, const),
                pl.BlockSpec(shift.shape, const),
            ]
            + [pl.BlockSpec(memory_space=pl.ANY)] * len(before)
            + [pl.BlockSpec(memory_space=pltpu.HBM)] * len(others),
            out_specs=[low, low, pl.BlockSpec((1, 16, width, length), lambda at, place: (half, at, 0, 0))],
            scratch_shapes=[
                pltpu.VMEM((length // 128, 16 * pitch, 128), F32),
                pltpu.VMEM((length // 128, 16 * pitch, 128), F32),
                pltpu.VMEM((4, length, width), F32),
            ],
        ),
        out_shape=[jax.ShapeDtypeStruct((width, rows, length), BF)] * 2
        + [jax.ShapeDtypeStruct((2, rows, width, length), BF)],
        input_output_aliases={8: 2} if before else {},
        compiler_params=pltpu.CompilerParams(vmem_limit_bytes=VMEM_LIMIT),
        cost_estimate=cost(3.0e9),
        name="edges",
    )(place, *x_pieces, weight, gain, shift, *before, *[tip(item) for item in others])


def gather_pieces(place_ref, rights, e, scr):
    for n, piece in enumerate(rights):
        rows = piece.shape[1]
        scr[e, pl.ds(pl.multiple_of(place_ref[n], rows), rows), :] = piece[e]


def by_channel(ref):
    halves, rows, some, lanes = ref.shape
    return ref.reshape(halves, rows * some, lanes)


def put_channel(ref, e, values):
    halves, rows, some, lanes = ref.shape
    flat = by_channel(ref)
    for half in range(halves):
        flat[half, pl.ds(e, rows, stride=some), :] = values[:, half * lanes : (half + 1) * lanes]


def ahead(first, count, begin, end):
    coming = begin(first)
    for e in range(first, first + count):
        here = coming
        if e + 1 < first + count:
            coming = begin(e + 1)
        end(e, here)


SOME = 16


def cut_refs(refs, *counts):
    parts = []
    for count in counts:
        parts.append(refs[:count])
        refs = refs[count:]
    return parts + list(refs)


def triangle_kernel(place_ref, *refs):
    lefts, rights, t_ref, scr, own_scr = cut_refs(refs, 2, 4)
    for half, left in enumerate(lefts):

        @pl.when(place_ref[4] == half)
        def _():
            own_scr[...] = left[...]

    def begin(e):
        gather_pieces(place_ref, rights, e, scr)
        return nt(own_scr[e], scr[e])

    ahead(0, SOME, begin, functools.partial(put_channel, t_ref))


def high_spec(rows, length):
    return pl.BlockSpec((length // 128, rows, SOME, 128), lambda at, place: (0, 0, at, 0))


def low_spec(rows, lanes):
    return pl.BlockSpec((SOME, rows, lanes), lambda at, place: (at, 0, 0))


def by_halves(rows, width, length):
    return jax.ShapeDtypeStruct((length // 128, rows, width, 128), F32)


def channel_call(kernel, name, flops, scalar, ins, in_specs, out_specs, out_shape, scratch=()):
    return pl.pallas_call(
        kernel,
        grid_spec=pltpu.PrefetchScalarGridSpec(
            num_scalar_prefetch=1,
            grid=(ins[0].shape[0 if ins[0].ndim == 3 else 2] // SOME,),
            in_specs=in_specs,
            out_specs=out_specs,
            scratch_shapes=scratch,
        ),
        out_shape=out_shape,
        compiler_params=pltpu.CompilerParams(vmem_limit_bytes=VMEM_LIMIT),
        cost_estimate=cost(flops),
        name=name,
    )(scalar, *ins)


def triangle(place, lefts, rights):
    width, rows, length = lefts[0].shape
    return channel_call(
        triangle_kernel,
        "triangle",
        3.0e9,
        place,
        (*lefts, *rights),
        [low_spec(rows, length)] * 6,
        high_spec(rows, length),
        by_halves(rows, width, length),
        [pltpu.VMEM((SOME, length, length), BF), pltpu.VMEM((SOME, rows, length), BF)],
    )


def turn_kernel(grad_ref, *refs):
    out_ref = refs[-1]
    halves, rows, some, _ = grad_ref.shape
    flat = by_channel(grad_ref)
    for e in range(some):
        for half in range(halves):
            out_ref[half, e] = flat[half, pl.ds(e, rows, stride=some), :].astype(BF)


def turn(grad, others):
    halves, rows, width, lanes = grad.shape
    some = 32
    return pl.pallas_call(
        turn_kernel,
        grid=(width // some,),
        in_specs=[pl.BlockSpec((halves, rows, some, lanes), lambda at: (0, 0, at, 0))]
        + [pl.BlockSpec(memory_space=pltpu.HBM)] * len(others),
        out_specs=pl.BlockSpec((halves, some, rows, lanes), lambda at: (0, at, 0, 0)),
        out_shape=jax.ShapeDtypeStruct((halves, width, rows, lanes), BF),
        compiler_params=pltpu.CompilerParams(vmem_limit_bytes=VMEM_LIMIT),
        cost_estimate=cost(5.0e9),
        name="turn",
    )(grad, *[tip(item) for item in others])


def right_back_kernel(chunks, here_ref, *refs):
    lefts, grads, db_ref, scr = cut_refs(refs, 4, 2 * chunks)
    rows = db_ref.shape[1]

    def begin(e):
        pairs = [(s, k) for s in range(2) for k in range(2)]
        grad = [grads[2 * c + k][s, e] for s, k in pairs for c in range(chunks)]
        left = [lefts[2 * s + k][e] for s, k in pairs]
        return tn(jnp.concatenate(grad, axis=0), jnp.concatenate(left, axis=0))

    def end(e, db):
        scr[e] = db
        put_channel(db_ref, e, scr[e, pl.ds(pl.multiple_of(here_ref[0], rows), rows), :])

    ahead(0, SOME, begin, end)


def right_back(here, grads, lefts):
    width, rows, length = lefts[0].shape
    chunks = len(grads)
    _, _, some, part = grads[0][0].shape
    both = pl.BlockSpec((2, SOME, some, part), lambda at, here: (0, at, 0, 0))
    return channel_call(
        functools.partial(right_back_kernel, chunks),
        "right_back",
        2.2e10,
        here,
        [*lefts] + [item for chunk in grads for item in chunk],
        [low_spec(rows, length)] * 4 + [both] * (2 * chunks),
        high_spec(rows, length),
        by_halves(rows, width, length),
        [pltpu.VMEM((SOME, part, length), F32)],
    )


def left_back_kernel(chunks, place_ref, *refs):
    rights, grads, _, da_ref, scr = cut_refs(refs, 4, chunks, 1)

    def begin(e):
        gather_pieces(place_ref, rights, e, scr)
        grad = [jnp.concatenate([ref[0, e], ref[1, e]], axis=1) for ref in grads]
        return nn(jnp.concatenate(grad, axis=0), scr[e])

    ahead(0, SOME, begin, functools.partial(put_channel, da_ref))


def left_back(place, grads, rights, other):
    _, width, some, part = grads[0].shape
    _, rows, length = rights[0].shape
    both = pl.BlockSpec((2, SOME, some, part), lambda at, place: (0, at, 0, 0))
    return channel_call(
        functools.partial(left_back_kernel, len(grads)),
        "left_back",
        2.0e10,
        place,
        (*rights, *grads, tip(other)),
        [low_spec(rows, length)] * 4 + [both] * len(grads) + [pl.BlockSpec(memory_space=pltpu.HBM)],
        high_spec(rows, length),
        by_halves(rows, width, length),
        [pltpu.VMEM((SOME, length, length), BF)],
    )


def rows_kernel(count, heads, order, first, half_ref, other_ref, *refs):
    before = []
    if not first:
        before, refs = refs[:3], refs[4:]
    rows_body(count, heads, order, before, *refs)


def rows_body(
    count,
    heads,
    order,
    before,
    t_ref,
    xt_ref,
    cot_ref,
    bias_ref,
    chain_ref,
    lane_ref,
    vec_ref,
    gate_w_ref,
    gate_wt_ref,
    tri_out_ref,
    tri_out_t_ref,
    att_t_ref,
    att_kv_ref,
    att_ref,
    att_out_ref,
    att_out_t_ref,
    up_ref,
    up_t_ref,
    down_ref,
    down_t_ref,
    out_ref,
    dt_ref,
    z_ref,
    g_ref,
    g_vec_ref,
    g_bias_ref,
    e_scr,
):
    _, total_rows, width, length = xt_ref.shape
    head = width // heads
    scaling = 1.0 / math.sqrt(head)

    sums = (g_ref, g_vec_ref, g_bias_ref)
    place = {}
    for name in ("gate", "tri_out", "query", "key", "value", "gate2", "att_out"):
        place[name] = slice(len(place) * width, (len(place) + 1) * width)
    ups = slice(7 * width, 7 * width + up_ref.shape[1])
    downs = [
        slice(at, at + width) for at in range(ups.stop, ups.stop + up_ref.shape[1], width)
    ]

    @pl.when(pl.program_id(0) == 0)
    def _():
        for n, ref in enumerate(sums):
            ref[...] = before[n][...] if before else jnp.zeros(ref.shape, ref.dtype)

    per = length // 128
    mine = [slice(h * head, (h + 1) * head) for h in range(heads)]
    there = [slice(h * length, (h + 1) * length) for h in range(heads)]
    ones = jnp.ones((16, length), BF)
    parts = [slice(p * 128, (p + 1) * 128) for p in range(per)]

    def tiles(n, function, *items):
        results = [function(p, *[item[:, parts[p]] for item in items]) for p in range(per)]
        return [jnp.concatenate(list(column), axis=1) for column in zip(*results)]

    def step(at, carry):
        start = at * count
        rows = range(count)
        side = lambda items: jnp.concatenate(items, axis=1)
        x0, hat1, scale1, normed1, gate_raw = {}, {}, {}, {}, {}
        hat_t, scale_t, mixed, branch = {}, {}, {}, {}
        for n in rows:

            def first(p):
                tile = xt_ref[0, start + n, :, parts[p]].astype(F32)
                hat, scale = normalize(tile)
                return tile, hat, scale, (hat * vec_ref[0] + vec_ref[1]).astype(BF)

            x0[n], hat1[n], scale1[n], normed1[n] = tiles(n, first)
            gate_raw[n] = nn(gate_wt_ref[...], normed1[n])

            def second(p):
                hat, scale = normalize(t_ref[p, start + n])
                return hat, scale, (hat * vec_ref[2] + vec_ref[3]).astype(BF)

            hat_t[n], scale_t[n], mixed[n] = tiles(n, second)
            branch[n] = nn(tri_out_t_ref[...], mixed[n])

        gate1, x1, hat2, scale2, normed2, hidden, kv_tok = {}, {}, {}, {}, {}, {}, {}
        for n in rows:

            def join(p, before, raw, add):
                gate = sigmoid(raw)
                after = before + gate * add
                hat, scale = normalize(after)
                return gate, after, hat, scale, (hat * vec_ref[4] + vec_ref[5]).astype(BF)

            gate1[n], x1[n], hat2[n], scale2[n], normed2[n] = tiles(
                n, join, x0[n], gate_raw[n], branch[n]
            )
            hidden[n] = nn(att_t_ref[...], normed2[n])
            kv_tok[n] = nn(normed2[n].T, att_kv_ref[...])

        query, key, value, gate2 = {}, {}, {}, {}
        for n in rows:

            def split(p, tile):
                gate = sigmoid(tile[3 * width :].astype(BF).astype(F32))
                asked = (tile[:width] * (scaling * LOG2E)).astype(BF)
                return asked, tile[width : 2 * width].astype(BF), tile[2 * width : 3 * width].astype(BF), gate

            query[n], key[n], value[n], gate2[n] = tiles(n, split, hidden[n])
            kv_tok[n] = kv_tok[n].astype(BF)

        pairs = [(n, h) for n in rows for h in range(heads)]

        def scores(n, h):
            return nn(kv_tok[n][:, :width] * lane_ref[h], query[n])

        outs, inverses = {}, {}

        def mix(n, h):
            both = nn(jnp.concatenate([value[n][mine[h]], ones], axis=0), e_scr[n, :, there[h]])
            inverses[n, h] = 1.0 / both[head : head + 1]
            outs[n, h] = both[:head] * inverses[n, h]

        coming = scores(*pairs[0])
        for at_pair, (n, h) in enumerate(pairs):
            score = coming
            if at_pair + 1 < len(pairs):
                coming = scores(*pairs[at_pair + 1])
            score = score + bias_ref[h]
            peak = jnp.max(score, axis=0, keepdims=True)
            e_scr[n, :, there[h]] = jnp.exp2(score - peak).astype(BF)
            if at_pair:
                mix(*pairs[at_pair - 1])
        mix(*pairs[-1])

        attended, gated, x2 = {}, {}, {}
        for n in rows:
            attended[n] = jnp.concatenate([outs[n, h] for h in range(heads)], axis=0)
            (gated[n],) = tiles(n, lambda p, gate, out: ((gate * out).astype(BF),), gate2[n], attended[n])
            x2[n] = nn(att_out_t_ref[...], gated[n])
        hat3, scale3, normed3, up, cot_tok, cot_low, grad_act = {}, {}, {}, {}, {}, {}, {}
        for n in rows:

            def third(p, before, add):
                after = before + add
                hat, scale = normalize(after)
                return after, hat, scale, (hat * vec_ref[6] + vec_ref[7]).astype(BF)

            x2[n], hat3[n], scale3[n], normed3[n] = tiles(n, third, x1[n], x2[n])
            up[n] = nn(up_t_ref[...], normed3[n])
            cot_tok[n] = load_tokens(cot_ref, start + n, order).astype(BF)
            cot_low[n] = cot_tok[n].T
            grad_act[n] = nn(down_ref[...], cot_low[n])
        act, down, grad_up, grad3 = {}, {}, {}, {}
        for n in rows:

            def silu(p, raw, grad):
                gate = sigmoid(raw)
                return (raw * gate).astype(BF), (grad * (gate * (1.0 + raw * (1.0 - gate)))).astype(BF)

            act[n], grad_up[n] = tiles(n, silu, up[n], grad_act[n])
            down[n] = nn(down_t_ref[...], act[n])
            grad3[n] = nn(up_ref[...], grad_up[n])
        grad = nn(side([act[n] for n in rows]), jnp.concatenate([cot_tok[n] for n in rows], axis=0))
        for n, part in enumerate(downs):
            g_ref[:, part] += grad[n * width : (n + 1) * width]
        g_ref[:, ups] += nt(side([normed3[n] for n in rows]), side([grad_up[n] for n in rows]))

        grad_x2, grad_x2_low, grad_gated = {}, {}, {}
        for n in rows:

            def third_back(p, grad_out, grad, hat, scale):
                g_vec_ref[6] += grad * hat
                g_vec_ref[7] += grad
                grad = grad_out.astype(F32) + normalize_back(grad, vec_ref[6], hat, scale)
                return grad, grad.astype(BF)

            grad_x2[n], grad_x2_low[n] = tiles(n, third_back, cot_low[n], grad3[n], hat3[n], scale3[n])
            grad_gated[n] = nn(att_out_ref[...], grad_x2_low[n])
            (out,) = tiles(n, lambda p, one, two: ((one + two).astype(BF),), x2[n], down[n])
            store_tokens(out_ref, start + n, order, out.T.astype(F32))
        g_ref[:, place["att_out"]] += nt(
            side([gated[n] for n in rows]), side([grad_x2_low[n] for n in rows])
        )
        grad_gate2, grad_out, center = {}, {}, {}
        for n in rows:

            def gate_back(p, grad, gate, out):
                mixed_grad = grad * gate
                scaled = [mixed_grad[mine[h]] * inverses[n, h][:, parts[p]] for h in range(heads)]
                low = jnp.concatenate(scaled, axis=0).astype(BF)
                product = low.astype(F32) * out
                centers = [jnp.sum(product[mine[h]], axis=0, keepdims=True) for h in range(heads)]
                return ((mixed_grad * out * (1.0 - gate)).astype(BF), low, *centers)

            grad_gate2[n], grad_out[n], *centers = tiles(n, gate_back, grad_gated[n], gate2[n], attended[n])
            for h in range(heads):
                center[n, h] = centers[h]

        grad_queries, grad_keys, grad_values = {}, {}, {}

        def probs(n, h):
            return nn(kv_tok[n][:, width:] * lane_ref[h], grad_out[n])

        def spread(n, h, grad_score):
            both = nn(jnp.concatenate([key[n][mine[h]], chain_ref[...]], axis=0), grad_score)
            grad_queries[n, h] = (both[:head] * scaling).astype(BF)
            g_bias_ref[h] += both[head:]
            grad_keys[n, h] = (nt(query[n][mine[h]], grad_score) * LN2).astype(BF)

        coming, behind = probs(*pairs[0]), None
        for at_pair, (n, h) in enumerate(pairs):
            grad_prob = coming
            if at_pair + 1 < len(pairs):
                coming = probs(*pairs[at_pair + 1])
            expon = e_scr[n, :, there[h]]
            grad_score = (expon.astype(F32) * (grad_prob - center[n, h])).astype(BF)
            grad_values[n, h] = nt(grad_out[n][mine[h]], expon).astype(BF)
            if behind is not None:
                spread(*behind)
            behind = (n, h, grad_score)
        spread(*behind)

        grad_hidden, grad2 = {}, {}
        for n in rows:
            blocks = [items[n, h] for items in (grad_queries, grad_keys, grad_values) for h in range(heads)]
            grad_hidden[n] = jnp.concatenate(blocks + [grad_gate2[n]], axis=0)
            grad2[n] = nn(att_ref[...], grad_hidden[n])
        g_ref[:, place["query"].start : place["gate2"].stop] += nt(
            side([normed2[n] for n in rows]), side([grad_hidden[n] for n in rows])
        )
        grad_x1, grad_branch, grad_gate1, grad_mix, grad1 = {}, {}, {}, {}, {}
        for n in rows:

            def second_back(p, grad_after, grad, hat, scale, gate, added):
                g_vec_ref[4] += grad * hat
                g_vec_ref[5] += grad
                grad = grad_after + normalize_back(grad, vec_ref[4], hat, scale)
                gated_grad = grad * gate
                return grad, gated_grad.astype(BF), (gated_grad * added * (1.0 - gate)).astype(BF)

            grad_x1[n], grad_branch[n], grad_gate1[n] = tiles(
                n, second_back, grad_x2[n], grad2[n], hat2[n], scale2[n], gate1[n], branch[n]
            )
            grad_mix[n] = nn(tri_out_ref[...], grad_branch[n])
            grad1[n] = nn(gate_w_ref[...], grad_gate1[n])
        g_ref[:, place["tri_out"]] += nt(
            side([mixed[n] for n in rows]), side([grad_branch[n] for n in rows])
        )
        g_ref[:, place["gate"]] += nt(
            side([normed1[n] for n in rows]), side([grad_gate1[n] for n in rows])
        )
        for n in rows:
            for p, part in enumerate(parts):
                grad, hat, scale = grad_mix[n][:, part], hat_t[n][:, part], scale_t[n][:, part]
                g_vec_ref[2] += grad * hat
                g_vec_ref[3] += grad
                dt_ref[p, start + n] = normalize_back(grad, vec_ref[2], hat, scale)
                grad, hat, scale = grad1[n][:, part], hat1[n][:, part], scale1[n][:, part]
                g_vec_ref[0] += grad * hat
                g_vec_ref[1] += grad
                grad = grad_x1[n][:, part] + normalize_back(grad, vec_ref[0], hat, scale)
                z_ref[start + n, :, part] = grad
        return carry

    lax.fori_loop(0, total_rows // count, step, 0)


def rows_pass(c, chunks, half, other, before, t, xt, cot_rows, order, bias, chain, lane, vecs, weights, heads):
    _, all_rows, width, length = xt.shape
    blocks, pieces, sub, tokens, _ = cot_rows.shape
    rows = blocks * sub
    some, count = 4, 4
    inner = sub // some
    full = lambda item: pl.BlockSpec(item.shape, lambda at, half: (0,) * item.ndim)
    of_all = pl.BlockSpec((some, width, length), lambda at, half: (c * (rows // some) + at, 0, 0))
    xt_some = pl.BlockSpec(
        (1, some, width, length), lambda at, half: (half[0], c * (rows // some) + at, 0, 0)
    )
    t_some = pl.BlockSpec(
        (length // 128, some, width, 128), lambda at, half: (0, c * (rows // some) + at, 0, 0)
    )
    dt_some = pl.BlockSpec((length // 128, some, width, 128), lambda at, half: (0, at, 0, 0))
    by_piece = pl.BlockSpec(
        (1, pieces, some, tokens, width), lambda at, half: (at // inner, 0, at % inner, 0, 0)
    )
    consts = (bias, chain, lane, vecs) + weights
    wide = weights[-1].shape[1]
    sum_shapes = [
        jax.ShapeDtypeStruct(shape, F32)
        for shape in ((width, 7 * width + 2 * wide), (8, width, 128), (heads, 16, length))
    ]
    before_specs = [full(item) for item in before[:3]]
    before_specs += [pl.BlockSpec(memory_space=pl.ANY)] * len(before[3:])
    return pl.pallas_call(
        functools.partial(rows_kernel, count, heads, order, c == 0),
        grid_spec=pltpu.PrefetchScalarGridSpec(
            num_scalar_prefetch=1,
            grid=(rows // some,),
            in_specs=[pl.BlockSpec(memory_space=pltpu.HBM)]
            + before_specs
            + [t_some, xt_some, by_piece] + [full(item) for item in consts],
            out_specs=[by_piece, dt_some, of_all] + [full(item) for item in sum_shapes],
            scratch_shapes=[
                pltpu.VMEM((count, length, heads * length), BF),
            ],
        ),
        out_shape=[
            jax.ShapeDtypeStruct(cot_rows.shape, BF),
            by_halves(rows, width, length),
            jax.ShapeDtypeStruct((all_rows, width, length), F32),
        ]
        + sum_shapes,
        input_output_aliases={5: 2} if before else {},
        compiler_params=pltpu.CompilerParams(vmem_limit_bytes=VMEM_LIMIT),
        cost_estimate=cost(1.2e11),
        name="rows",
    )(half, other, *before, t, xt, cot_rows, *consts)


def edges_back_kernel(
    order, half_ref, xt_ref, z_ref, da_ref, db_ref, wt_ref, w_ref, gain_ref, shift_ref, out_ref, g_w_ref, g_vec_ref
):
    _, rows, width, length = xt_ref.shape
    count = 4

    @pl.when(pl.program_id(0) == 0)
    def _():
        g_w_ref[...] = jnp.zeros(g_w_ref.shape, F32)
        g_vec_ref[...] = jnp.zeros(g_vec_ref.shape, F32)

    def step(at, carry):
        start = at * count
        x0 = stacked(xt_ref.at[0], start, count).astype(F32)
        lanes = x0.shape[1]
        gain = widen(gain_ref[...], lanes)
        hat, scale = normalize(x0)
        normed = (hat * gain + widen(shift_ref[...], lanes)).astype(BF)
        proj = nn(wt_ref[...], normed)
        pa, pag = proj[:width], proj[width : 2 * width]
        pb, pbg = proj[2 * width : 3 * width], proj[3 * width :]
        halves = [(n, half) for n in range(count) for half in range(da_ref.shape[0])]
        da = jnp.concatenate([da_ref[half, start + n] for n, half in halves], axis=1)
        db = jnp.concatenate([db_ref[half, start + n] for n, half in halves], axis=1)
        sa, sb = sigmoid(pag), sigmoid(pbg)
        dsa, dsb = da * sa, db * sb
        grads = jnp.concatenate(
            [
                dsa.astype(BF),
                (dsa * pa * (1.0 - sa)).astype(BF),
                dsb.astype(BF),
                (dsb * pb * (1.0 - sb)).astype(BF),
            ],
            axis=0,
        )
        g_w_ref[...] += nt(normed, grads)
        grad = nn(w_ref[...], grads)
        g_vec_ref[0] += fold(grad * hat)
        g_vec_ref[1] += fold(grad)
        out = stacked(z_ref, start, count) + normalize_back(grad, gain, hat, scale)
        out = out.astype(BF)
        for n in range(count):
            store_tokens(out_ref, start + n, order, out[:, n * length : (n + 1) * length].T.astype(F32))
        return carry

    lax.fori_loop(0, rows // count, step, 0)


def edges_back(half, xt, z, da, db, order, weight_t, weight, gain, shift, shape):
    _, rows, width, length = xt.shape
    blocks, pieces, sub, tokens, _ = shape
    chunks = order[2]
    some = sub // chunks
    step = 16 // some
    inner = blocks // step
    full = lambda item: pl.BlockSpec(item.shape, lambda at, half: (0,) * item.ndim)
    xt_row = pl.BlockSpec((1, 16, width, length), lambda at, half: (half[0], at, 0, 0))
    by_row = pl.BlockSpec((16, width, length), lambda at, half: (at, 0, 0))
    by_half = pl.BlockSpec((length // 128, 16, width, 128), lambda at, half: (0, at, 0, 0))
    sum_shapes = [
        jax.ShapeDtypeStruct(weight.shape, F32),
        jax.ShapeDtypeStruct((2, width, 128), F32),
    ]
    by_piece = pl.BlockSpec(
        (step, pieces, some, tokens, width), lambda at, half: (at % inner, 0, at // inner, 0, 0)
    )
    return pl.pallas_call(
        functools.partial(edges_back_kernel, order),
        grid_spec=pltpu.PrefetchScalarGridSpec(
            num_scalar_prefetch=1,
            grid=(chunks * inner,),
            in_specs=[xt_row, by_row] + [by_half] * 2 + [full(item) for item in (weight_t, weight, gain, shift)],
            out_specs=[by_piece] + [full(item) for item in sum_shapes],
        ),
        out_shape=[jax.ShapeDtypeStruct(shape, BF)] + sum_shapes,
        compiler_params=pltpu.CompilerParams(vmem_limit_bytes=VMEM_LIMIT),
        cost_estimate=cost(4.0e10),
        name="edges_back",
    )(half, xt, z, da, db, weight_t, weight, gain, shift)


def shards(
    row_size,
    col_size,
    pair_state,
    cotangent,
    chain_lengths,
    tri_gain,
    tri_shift,
    tri_weight,
    mix_gain,
    mix_shift,
    tri_out,
    att_gain,
    att_shift,
    att_weight,
    chain_bias,
    att_out,
    trans_gain,
    trans_shift,
    up_weight,
    down_weight,
):
    heads = HEADS
    crops, own_rows, tokens, width = pair_state.shape
    length = col_size * tokens
    chunks = CHUNKS
    some = own_rows // (col_size * chunks)
    axes = ("row", "col")
    group = row_size * col_size
    order = (row_size, col_size, chunks)
    shape = (row_size, col_size, some, tokens, width)

    def swap(values):
        return lax.all_to_all(values, axes, split_axis=0, concat_axis=0, tiled=True)

    def cut(values):
        parts = values.reshape(group, chunks, some, tokens, width)
        return [parts[:, c] for c in range(chunks)]

    def join(parts):
        return jnp.stack(parts, axis=1).reshape(crops, own_rows, tokens, width)

    def across(values, bit):
        return lax.ppermute(values, "col", [(q, q ^ bit) for q in range(col_size)])

    bits = [1 << n for n in range(col_size.bit_length() - 1)]

    def doubled(items, axis, size, bits):
        for bit in bits:
            lows = [values.astype(sent) for values, sent in items]
            others = [lax.ppermute(low, axis, [(q, q ^ bit) for q in range(size)]) for low in lows]
            others = lax.optimization_barrier(tuple(others))
            items = [
                (low.astype(F32) + other.astype(F32), sent)
                for low, other, (_, sent) in zip(lows, others, items)
            ]
        return items

    def summed_over_rows(values, sent):
        low = values.astype(sent)
        terms = [low.astype(F32)]
        for m in range(1, row_size):
            other = lax.ppermute(low, "row", [(r, r ^ m) for r in range(row_size)])
            terms.append(other.astype(F32))
        while len(terms) > 1:
            terms = [terms[n] + terms[n + 1] for n in range(0, len(terms), 2)]
        return terms[0]

    whole = (row_size, col_size, some * chunks, tokens, width)
    cot_parts = cut(cotangent)

    wide = lambda item: jnp.broadcast_to(item[:, None], (width, 128))
    vecs = jnp.stack(
        [
            wide(item)
            for item in (
                tri_gain,
                tri_shift,
                mix_gain,
                mix_shift,
                att_gain,
                att_shift,
                trans_gain,
                trans_shift,
            )
        ]
    )
    edge_w = tri_weight[:, : 4 * width]
    edge_wt = edge_w.T
    gate_w = tri_weight[:, 4 * width :]
    lengths = lax.dynamic_index_in_dim(chain_lengths, lax.axis_index("row"), 0, keepdims=False)
    ends = jnp.cumsum(lengths)
    places = jnp.arange(length, dtype=jnp.int32)
    places = places.reshape(order + (some,)).transpose(1, 2, 0, 3).reshape(length)
    chain = jnp.sum((places[:, None] >= ends[None, :]).astype(jnp.int32), axis=-1)
    same = (chain[:, None] == chain[None, :]).astype(F32)
    bias = (LOG2E * chain_bias)[:, None, None] * same[None]
    which = (jnp.arange(16, dtype=jnp.int32)[:, None] == chain[None, :]).astype(F32)
    head_of = jnp.arange(width, dtype=jnp.int32) // (width // heads)
    lane = (jnp.arange(heads, dtype=jnp.int32)[:, None] == head_of[None, :]).astype(BF)
    lane = jnp.broadcast_to(lane[:, None, :], (heads, length, width))
    me = lax.axis_index("col")
    own = own_rows
    far_bit = col_size // 2
    half, core = me // far_bit, me % far_bit
    token_place = jnp.stack([(me ^ m) * tokens for m in range(col_size)])
    place = [(s * far_bit + (core ^ k)) * own for s in range(2) for k in range(2)]
    place = jnp.stack(place + [half])
    here = (core * own).reshape(1)
    half_at = half.reshape(1)
    weights = (
        gate_w,
        gate_w.T,
        tri_out,
        tri_out.T,
        att_weight.T,
        att_weight[:, width : 3 * width],
        att_weight,
        att_out,
        att_out.T,
        up_weight,
        up_weight.T,
        down_weight,
        down_weight.T,
    )
    chain_rows = which.astype(BF)

    groups = pair_state.reshape(crops, 2, far_bit, own_rows // col_size, tokens, width)
    x_pieces, crossings = [], []
    for s in range(2):
        pieces = []
        for k in range(2):
            part = lax.dynamic_index_in_dim(groups[:, s], core ^ k, 1, keepdims=False)
            if len(crossings) > 1:
                part = after(part, crossings[-2])
            part = lax.all_to_all(part, "row", split_axis=0, concat_axis=0, tiled=True)
            crossings.append(across(part, far_bit ^ k))
            pieces += [crossings[-1], across(part, 1)] if k else [part, crossings[-1]]
        own_part, far, far_other, near_other = pieces
        x_pieces.append([own_part, near_other, far, far_other])
    cot_rows, before = [], part
    for held in cot_parts:
        before = swap(after(held, before))
        cot_rows.append(before.reshape(shape))
    lefts, rights, xt = [], [], []
    for s, pieces in enumerate(x_pieces):
        others = [] if s else [crossings[2], cot_parts[0]]
        left, right, *xt = edges(
            token_place, s, pieces, xt, others, order, edge_wt, vecs[0], vecs[1]
        )
        lefts.append(left)
        rights += [right, across(right, 1)]
    (xt,) = xt
    t = triangle(place, lefts, rights)
    tips = [across(tip(cot_rows[0]), 1), tip(cot_rows[1])]
    lefts = [item for left in lefts for item in (left, across(left, 1))]
    state, outs, dts, sent = [], [], [], []
    pairs = [[q, q + far_bit] for q in range(far_bit)]
    for c in range(chunks):
        out, dt, z, *sums = rows_pass(
            c, chunks, half_at, tips[c], state, t, xt, cot_rows[c], order, bias, chain_rows, lane, vecs, weights, heads
        )
        state = sums + [z]
        dt = turn(dt, outs)
        if c < chunks - 1:
            dts.append(dt)
            outs.append(swap(out.reshape(group, some, tokens, width)))
            near = lax.dynamic_index_in_dim(dt, half, 0, keepdims=False)
            sent.append((near, across(lax.dynamic_index_in_dim(dt, 1 - half, 0, keepdims=False), far_bit)))
    dts.append(dt)
    crossed = []
    for near, far in sent:
        crossed.append(jnp.where(half == 0, jnp.stack([near, far]), jnp.stack([far, near])))
    crossed.append(
        lax.all_to_all(dt, "col", split_axis=0, concat_axis=0, axis_index_groups=pairs, tiled=True)
    )
    g_rows, g_vec, g_bias = sums
    row_bits = [1 << n for n in range(row_size.bit_length() - 1)]
    g_rows = summed_over_rows(g_rows, BF)
    da = left_back(place, dts, rights, g_rows)
    grads = [[item, across(item, 1)] for item in crossed[:-1]]
    crossed[-1] = after(crossed[-1], da)
    grads.append([crossed[-1], across(crossed[-1], 1)])
    outs.append(swap(out.reshape(group, some, tokens, width)))
    pair_out = join(outs)
    db = right_back(here, grads, lefts)
    back, g_edge, g_vec_edge = edges_back(
        half_at, xt, z, da, db, order, edge_wt, edge_w, vecs[0], vecs[1], whole
    )
    g_vec = jnp.sum(g_vec, axis=-1)
    g_vec_edge = jnp.sum(g_vec_edge, axis=-1)
    g_chain = jnp.sum(g_bias * which[None], axis=(1, 2))
    small = jnp.concatenate(
        [g_vec[:2] + g_vec_edge, g_vec[2:], jnp.pad(g_chain, (0, width - heads))[None]], axis=0
    )
    items = doubled([(g_edge, BF), (small, F32)], "row", row_size, row_bits)
    back = after(back, *[values for values, _ in items])
    grad_pair = swap(back.reshape(group, some * chunks, tokens, width))
    grad_pair = grad_pair.reshape(crops, own_rows, tokens, width)
    g_rows = after(g_rows, pair_out, back)
    items = doubled(items + [(g_rows, BF)], "col", col_size, bits[::-1])
    t_edge, small, total = [values for values, _ in items]
    column = lambda at, n=1: total[:, at * width : (at + n) * width]
    ff = up_weight.shape[1] // width
    t_gate, t_tri_out, t_att = column(0), column(1), column(2, 4)
    t_att_out, t_up = column(6), column(7, ff)
    t_down = jnp.concatenate([column(7 + ff + n) for n in range(ff)], axis=0)
    return (
        pair_out,
        grad_pair,
        small[0],
        small[1],
        jnp.concatenate([t_edge, t_gate], axis=1),
        small[2],
        small[3],
        t_tri_out,
        small[4],
        small[5],
        t_att,
        small[8, :heads],
        t_att_out,
        small[6],
        small[7],
        t_up,
        t_down,
    )


def solution(mesh):
    pair = P("dp", "row", "col", None)
    vector, matrix = P("dp"), P("dp", None)
    return jax.shard_map(
        functools.partial(shards, mesh.shape["row"], mesh.shape["col"]),
        mesh=mesh,
        in_specs=(pair, pair, P("dp", None)) + (P(),) * 15,
        out_specs=(
            pair,
            pair,
            vector,
            vector,
            matrix,
            vector,
            vector,
            matrix,
            vector,
            vector,
            matrix,
            vector,
            matrix,
            vector,
            vector,
            matrix,
            matrix,
        ),
        check_vma=False,
    )
```

```python
import functools
import math

import jax
import jax.numpy as jnp
from jax import lax
from jax.experimental import pallas as pl
from jax.experimental.pallas import tpu as pltpu
from jax.sharding import PartitionSpec as P

HEADS = 4
EPS = 1e-05
LOG2E = math.log2(math.e)
LN2 = math.log(2.0)
CHUNKS = 2
VMEM_LIMIT = 56 * 1024 * 1024
BF = jnp.bfloat16
F32 = jnp.float32


def nn(left, right):
    return lax.dot_general(left, right, (((1,), (0,)), ((), ())), preferred_element_type=F32)


def nt(left, right):
    return lax.dot_general(left, right, (((1,), (1,)), ((), ())), preferred_element_type=F32)


def tn(left, right):
    return lax.dot_general(left, right, (((0,), (0,)), ((), ())), preferred_element_type=F32)


def cost(flops, size=0):
    return pl.CostEstimate(flops=int(flops), bytes_accessed=int(size), transcendentals=0)


def sigmoid(values):
    return 0.5 * jnp.tanh(0.5 * values) + 0.5


def normalize(values):
    center = values - jnp.mean(values, axis=0, keepdims=True)
    spread = jnp.mean(center * center, axis=0, keepdims=True)
    scale = lax.rsqrt(spread + EPS)
    return center * scale, scale


def normalize_back(grads, gain, hat, scale):
    grad_hat = grads * gain
    first = jnp.mean(grad_hat, axis=0, keepdims=True)
    second = jnp.mean(grad_hat * hat, axis=0, keepdims=True)
    return scale * (grad_hat - first - hat * second)


def widen(column, lanes):
    return jnp.concatenate([column] * (lanes // column.shape[1]), axis=1)


def fold(values):
    parts = [values[:, at : at + 128] for at in range(0, values.shape[1], 128)]
    return functools.reduce(lambda one, two: one + two, parts)


def to_order(flat, order):
    length, width = flat.shape
    flat = flat.reshape(order + (length // math.prod(order), width))
    return flat.transpose(1, 2, 0, 3, 4).reshape(length, width)


def load_tokens(ref, row, order):
    _, pieces, some, tokens, width = ref.shape
    flat = ref[row // some, :, row % some, :, :].astype(F32)
    return to_order(flat.reshape(pieces * tokens, width), order)


def store_tokens(ref, row, order, values):
    _, pieces, some, tokens, width = ref.shape
    back = (order[1], order[2], order[0])
    flat = values.reshape(back + (pieces * tokens // math.prod(order), width))
    flat = flat.transpose(2, 0, 1, 3, 4).reshape(pieces, tokens, width)
    ref[row // some, :, row % some, :, :] = flat.astype(ref.dtype)


def stacked(ref, start, count):
    return jnp.concatenate([ref[start + n] for n in range(count)], axis=1)


def spread_out(ref, start, count, values):
    length = values.shape[1] // count
    for n in range(count):
        ref[start + n] = values[:, n * length : (n + 1) * length].astype(ref.dtype)


def no_op(*refs):
    pass


def tip(values):
    return values[(0,) * (values.ndim - 2)][:16, :128]


def after(values, *others):
    others = [tip(item) for item in others]
    anywhere = pl.BlockSpec(memory_space=pltpu.HBM)
    return pl.pallas_call(
        no_op,
        in_specs=[anywhere] * (1 + len(others)),
        out_specs=anywhere,
        out_shape=jax.ShapeDtypeStruct(values.shape, values.dtype),
        input_output_aliases={0: 0},
        cost_estimate=cost(0),
        name="after",
    )(values, *others)


def edges_kernel(order, place_ref, *refs):
    x_refs, (w_ref, gain_ref, shift_ref), rest = refs[:4], refs[4:7], refs[-6:]
    a_ref, b_ref, xt_ref, a_scr, b_scr, x_scr = rest
    width, rows, length = a_ref.shape
    pitch = a_scr.shape[1] // rows
    count = x_scr.shape[0]
    _, some, tokens, _ = x_refs[0].shape

    def step(at, carry):
        start = at * count
        turned = []
        for n in range(count):
            row = start + n
            for m, ref in enumerate(x_refs):
                there = pl.ds(pl.multiple_of(place_ref[m], tokens), tokens)
                x_scr[n, there, :] = ref[row // some, row % some].astype(F32)
            turned.append(to_order(x_scr[n], order).astype(BF).T)
        x0 = jnp.concatenate(turned, axis=1)
        for n in range(count):
            xt_ref[0, start + n] = turned[n]
        hat, _ = normalize(x0.astype(F32))
        lanes = x0.shape[1]
        normed = (hat * widen(gain_ref[...], lanes) + widen(shift_ref[...], lanes)).astype(BF)
        proj = nn(w_ref[...], normed)
        left = sigmoid(proj[width : 2 * width]) * proj[:width]
        right = sigmoid(proj[3 * width : 4 * width]) * proj[2 * width : 3 * width]
        for n in range(count):
            base = pl.multiple_of((start + n) * pitch, 8)
            for half in range(length // 128):
                part = slice(n * length + half * 128, n * length + half * 128 + 128)
                a_scr[half, pl.ds(base, width), :] = left[:, part]
                b_scr[half, pl.ds(base, width), :] = right[:, part]
        return carry

    lax.fori_loop(0, rows // count, step, 0)

    def turn(at, carry):
        for n in range(8):
            e = at * 8 + n
            for scr, out in ((a_scr, a_ref), (b_scr, b_ref)):
                halves = [scr[h, pl.ds(e, rows, stride=pitch), :] for h in range(scr.shape[0])]
                out[e] = jnp.concatenate(halves, axis=1).astype(BF)
        return carry

    lax.fori_loop(0, width // 8, turn, 0)


def edges(place, half, x_pieces, before, others, order, weight, gain, shift):
    blocks, rows_there, tokens, width = x_pieces[0].shape
    length = len(x_pieces) * tokens
    chunks = order[2]
    some = rows_there // chunks
    step = 16 // some
    inner = blocks // step
    rows = blocks * some * chunks
    const = lambda at, place: (0, 0)
    pitch = width + 8
    low = pl.BlockSpec((width, 16, length), lambda at, place: (0, at, 0))
    spec = pl.BlockSpec(
        (step, some, tokens, width),
        lambda at, place: (at % inner, at // inner, 0, 0),
    )
    return pl.pallas_call(
        functools.partial(edges_kernel, order),
        grid_spec=pltpu.PrefetchScalarGridSpec(
            num_scalar_prefetch=1,
            grid=(chunks * inner,),
            in_specs=[spec] * 4
            + [
                pl.BlockSpec(weight.shape, const),
                pl.BlockSpec(gain.shape, const),
                pl.BlockSpec(shift.shape, const),
            ]
            + [pl.BlockSpec(memory_space=pl.ANY)] * len(before)
            + [pl.BlockSpec(memory_space=pltpu.HBM)] * len(others),
            out_specs=[low, low, pl.BlockSpec((1, 16, width, length), lambda at, place: (half, at, 0, 0))],
            scratch_shapes=[
                pltpu.VMEM((length // 128, 16 * pitch, 128), F32),
                pltpu.VMEM((length // 128, 16 * pitch, 128), F32),
                pltpu.VMEM((4, length, width), F32),
            ],
        ),
        out_shape=[jax.ShapeDtypeStruct((width, rows, length), BF)] * 2
        + [jax.ShapeDtypeStruct((2, rows, width, length), BF)],
        input_output_aliases={8: 2} if before else {},
        compiler_params=pltpu.CompilerParams(vmem_limit_bytes=VMEM_LIMIT),
        cost_estimate=cost(3.0e9),
        name="edges",
    )(place, *x_pieces, weight, gain, shift, *before, *[tip(item) for item in others])


def gather_pieces(place_ref, rights, e, scr):
    for n, piece in enumerate(rights):
        rows = piece.shape[1]
        scr[e, pl.ds(pl.multiple_of(place_ref[n], rows), rows), :] = piece[e]


def by_channel(ref):
    halves, rows, some, lanes = ref.shape
    return ref.reshape(halves, rows * some, lanes)


def put_channel(ref, e, values):
    halves, rows, some, lanes = ref.shape
    flat = by_channel(ref)
    for half in range(halves):
        flat[half, pl.ds(e, rows, stride=some), :] = values[:, half * lanes : (half + 1) * lanes]


def ahead(first, count, begin, end):
    coming = begin(first)
    for e in range(first, first + count):
        here = coming
        if e + 1 < first + count:
            coming = begin(e + 1)
        end(e, here)


SOME = 16


def cut_refs(refs, *counts):
    parts = []
    for count in counts:
        parts.append(refs[:count])
        refs = refs[count:]
    return parts + list(refs)


def triangle_kernel(place_ref, *refs):
    lefts, rights, t_ref, scr, own_scr = cut_refs(refs, 2, 4)
    for half, left in enumerate(lefts):

        @pl.when(place_ref[4] == half)
        def _():
            own_scr[...] = left[...]

    def begin(e):
        gather_pieces(place_ref, rights, e, scr)
        return nt(own_scr[e], scr[e])

    ahead(0, SOME, begin, functools.partial(put_channel, t_ref))


def high_spec(rows, length):
    return pl.BlockSpec((length // 128, rows, SOME, 128), lambda at, place: (0, 0, at, 0))


def low_spec(rows, lanes):
    return pl.BlockSpec((SOME, rows, lanes), lambda at, place: (at, 0, 0))


def by_halves(rows, width, length):
    return jax.ShapeDtypeStruct((length // 128, rows, width, 128), F32)


def channel_call(kernel, name, flops, scalar, ins, in_specs, out_specs, out_shape, scratch=()):
    return pl.pallas_call(
        kernel,
        grid_spec=pltpu.PrefetchScalarGridSpec(
            num_scalar_prefetch=1,
            grid=(ins[0].shape[0 if ins[0].ndim == 3 else 2] // SOME,),
            in_specs=in_specs,
            out_specs=out_specs,
            scratch_shapes=scratch,
        ),
        out_shape=out_shape,
        compiler_params=pltpu.CompilerParams(vmem_limit_bytes=VMEM_LIMIT),
        cost_estimate=cost(flops),
        name=name,
    )(scalar, *ins)


def triangle(place, lefts, rights):
    width, rows, length = lefts[0].shape
    return channel_call(
        triangle_kernel,
        "triangle",
        3.0e9,
        place,
        (*lefts, *rights),
        [low_spec(rows, length)] * 6,
        high_spec(rows, length),
        by_halves(rows, width, length),
        [pltpu.VMEM((SOME, length, length), BF), pltpu.VMEM((SOME, rows, length), BF)],
    )


def turn_kernel(grad_ref, *refs):
    out_ref = refs[-1]
    halves, rows, some, _ = grad_ref.shape
    flat = by_channel(grad_ref)
    for e in range(some):
        for half in range(halves):
            out_ref[half, e] = flat[half, pl.ds(e, rows, stride=some), :].astype(BF)


def turn(grad, others):
    halves, rows, width, lanes = grad.shape
    some = 32
    return pl.pallas_call(
        turn_kernel,
        grid=(width // some,),
        in_specs=[pl.BlockSpec((halves, rows, some, lanes), lambda at: (0, 0, at, 0))]
        + [pl.BlockSpec(memory_space=pltpu.HBM)] * len(others),
        out_specs=pl.BlockSpec((halves, some, rows, lanes), lambda at: (0, at, 0, 0)),
        out_shape=jax.ShapeDtypeStruct((halves, width, rows, lanes), BF),
        compiler_params=pltpu.CompilerParams(vmem_limit_bytes=VMEM_LIMIT),
        cost_estimate=cost(5.0e9),
        name="turn",
    )(grad, *[tip(item) for item in others])


def right_back_kernel(chunks, here_ref, *refs):
    lefts, grads, db_ref, scr = cut_refs(refs, 4, 2 * chunks)
    rows = db_ref.shape[1]

    def begin(e):
        pairs = [(s, k) for s in range(2) for k in range(2)]
        grad = [grads[2 * c + k][s, e] for s, k in pairs for c in range(chunks)]
        left = [lefts[2 * s + k][e] for s, k in pairs]
        return tn(jnp.concatenate(grad, axis=0), jnp.concatenate(left, axis=0))

    def end(e, db):
        scr[e] = db
        put_channel(db_ref, e, scr[e, pl.ds(pl.multiple_of(here_ref[0], rows), rows), :])

    ahead(0, SOME, begin, end)


def right_back(here, grads, lefts):
    width, rows, length = lefts[0].shape
    chunks = len(grads)
    _, _, some, part = grads[0][0].shape
    both = pl.BlockSpec((2, SOME, some, part), lambda at, here: (0, at, 0, 0))
    return channel_call(
        functools.partial(right_back_kernel, chunks),
        "right_back",
        2.2e10,
        here,
        [*lefts] + [item for chunk in grads for item in chunk],
        [low_spec(rows, length)] * 4 + [both] * (2 * chunks),
        high_spec(rows, length),
        by_halves(rows, width, length),
        [pltpu.VMEM((SOME, part, length), F32)],
    )


def left_back_kernel(chunks, place_ref, *refs):
    rights, grads, da_ref, scr = cut_refs(refs, 4, chunks)

    def begin(e):
        gather_pieces(place_ref, rights, e, scr)
        grad = [jnp.concatenate([ref[0, e], ref[1, e]], axis=1) for ref in grads]
        return nn(jnp.concatenate(grad, axis=0), scr[e])

    ahead(0, SOME, begin, functools.partial(put_channel, da_ref))


def left_back(place, grads, rights):
    _, width, some, part = grads[0].shape
    _, rows, length = rights[0].shape
    both = pl.BlockSpec((2, SOME, some, part), lambda at, place: (0, at, 0, 0))
    return channel_call(
        functools.partial(left_back_kernel, len(grads)),
        "left_back",
        2.0e10,
        place,
        (*rights, *grads),
        [low_spec(rows, length)] * 4 + [both] * len(grads),
        high_spec(rows, length),
        by_halves(rows, width, length),
        [pltpu.VMEM((SOME, length, length), BF)],
    )


def rows_kernel(count, heads, order, first, half_ref, other_ref, *refs):
    before = []
    if not first:
        before, refs = refs[:3], refs[4:]
    rows_body(count, heads, order, before, *refs)


def rows_body(
    count,
    heads,
    order,
    before,
    t_ref,
    xt_ref,
    cot_ref,
    bias_ref,
    chain_ref,
    lane_ref,
    vec_ref,
    gate_w_ref,
    gate_wt_ref,
    tri_out_ref,
    tri_out_t_ref,
    att_t_ref,
    att_kv_ref,
    att_ref,
    att_out_ref,
    att_out_t_ref,
    up_ref,
    up_t_ref,
    down_ref,
    down_t_ref,
    out_ref,
    dt_ref,
    z_ref,
    g_ref,
    g_vec_ref,
    g_bias_ref,
    e_scr,
):
    _, total_rows, width, length = xt_ref.shape
    head = width // heads
    scaling = 1.0 / math.sqrt(head)

    sums = (g_ref, g_vec_ref, g_bias_ref)
    place = {}
    for name in ("gate", "tri_out", "query", "key", "value", "gate2", "att_out"):
        place[name] = slice(len(place) * width, (len(place) + 1) * width)
    ups = slice(7 * width, 7 * width + up_ref.shape[1])
    downs = [
        slice(at, at + width) for at in range(ups.stop, ups.stop + up_ref.shape[1], width)
    ]

    @pl.when(pl.program_id(0) == 0)
    def _():
        for n, ref in enumerate(sums):
            ref[...] = before[n][...] if before else jnp.zeros(ref.shape, ref.dtype)

    per = length // 128
    mine = [slice(h * head, (h + 1) * head) for h in range(heads)]
    there = [slice(h * length, (h + 1) * length) for h in range(heads)]
    ones = jnp.ones((16, length), BF)
    parts = [slice(p * 128, (p + 1) * 128) for p in range(per)]

    def tiles(n, function, *items):
        results = [function(p, *[item[:, parts[p]] for item in items]) for p in range(per)]
        return [jnp.concatenate(list(column), axis=1) for column in zip(*results)]

    def step(at, carry):
        start = at * count
        rows = range(count)
        side = lambda items: jnp.concatenate(items, axis=1)
        x0, hat1, scale1, normed1, gate_raw = {}, {}, {}, {}, {}
        hat_t, scale_t, mixed, branch = {}, {}, {}, {}
        for n in rows:

            def first(p):
                tile = xt_ref[0, start + n, :, parts[p]].astype(F32)
                hat, scale = normalize(tile)
                return tile, hat, scale, (hat * vec_ref[0] + vec_ref[1]).astype(BF)

            x0[n], hat1[n], scale1[n], normed1[n] = tiles(n, first)
            gate_raw[n] = nn(gate_wt_ref[...], normed1[n])

            def second(p):
                hat, scale = normalize(t_ref[p, start + n])
                return hat, scale, (hat * vec_ref[2] + vec_ref[3]).astype(BF)

            hat_t[n], scale_t[n], mixed[n] = tiles(n, second)
            branch[n] = nn(tri_out_t_ref[...], mixed[n])

        gate1, x1, hat2, scale2, normed2, hidden, kv_tok = {}, {}, {}, {}, {}, {}, {}
        for n in rows:

            def join(p, before, raw, add):
                gate = sigmoid(raw)
                after = before + gate * add
                hat, scale = normalize(after)
                return gate, after, hat, scale, (hat * vec_ref[4] + vec_ref[5]).astype(BF)

            gate1[n], x1[n], hat2[n], scale2[n], normed2[n] = tiles(
                n, join, x0[n], gate_raw[n], branch[n]
            )
            hidden[n] = nn(att_t_ref[...], normed2[n])
            kv_tok[n] = nn(normed2[n].T, att_kv_ref[...])

        query, key, value, gate2 = {}, {}, {}, {}
        for n in rows:

            def split(p, tile):
                gate = sigmoid(tile[3 * width :].astype(BF).astype(F32))
                asked = (tile[:width] * (scaling * LOG2E)).astype(BF)
                return asked, tile[width : 2 * width].astype(BF), tile[2 * width : 3 * width].astype(BF), gate

            query[n], key[n], value[n], gate2[n] = tiles(n, split, hidden[n])
            kv_tok[n] = kv_tok[n].astype(BF)

        pairs = [(n, h) for n in rows for h in range(heads)]

        def scores(n, h):
            return nn(kv_tok[n][:, :width] * lane_ref[h], query[n])

        outs, inverses = {}, {}

        def mix(n, h):
            both = nn(jnp.concatenate([value[n][mine[h]], ones], axis=0), e_scr[n, :, there[h]])
            inverses[n, h] = 1.0 / both[head : head + 1]
            outs[n, h] = both[:head] * inverses[n, h]

        coming = scores(*pairs[0])
        for at_pair, (n, h) in enumerate(pairs):
            score = coming
            if at_pair + 1 < len(pairs):
                coming = scores(*pairs[at_pair + 1])
            score = score + bias_ref[h]
            peak = jnp.max(score, axis=0, keepdims=True)
            e_scr[n, :, there[h]] = jnp.exp2(score - peak).astype(BF)
            if at_pair:
                mix(*pairs[at_pair - 1])
        mix(*pairs[-1])

        attended, gated, x2 = {}, {}, {}
        for n in rows:
            attended[n] = jnp.concatenate([outs[n, h] for h in range(heads)], axis=0)
            (gated[n],) = tiles(n, lambda p, gate, out: ((gate * out).astype(BF),), gate2[n], attended[n])
            x2[n] = nn(att_out_t_ref[...], gated[n])
        hat3, scale3, normed3, up, cot_tok, cot_low, grad_act = {}, {}, {}, {}, {}, {}, {}
        for n in rows:

            def third(p, before, add):
                after = before + add
                hat, scale = normalize(after)
                return after, hat, scale, (hat * vec_ref[6] + vec_ref[7]).astype(BF)

            x2[n], hat3[n], scale3[n], normed3[n] = tiles(n, third, x1[n], x2[n])
            up[n] = nn(up_t_ref[...], normed3[n])
            cot_tok[n] = load_tokens(cot_ref, start + n, order).astype(BF)
            cot_low[n] = cot_tok[n].T
            grad_act[n] = nn(down_ref[...], cot_low[n])
        act, down, grad_up, grad3 = {}, {}, {}, {}
        for n in rows:

            def silu(p, raw, grad):
                gate = sigmoid(raw)
                return (raw * gate).astype(BF), (grad * (gate * (1.0 + raw * (1.0 - gate)))).astype(BF)

            act[n], grad_up[n] = tiles(n, silu, up[n], grad_act[n])
            down[n] = nn(down_t_ref[...], act[n])
            grad3[n] = nn(up_ref[...], grad_up[n])
        grad = nn(side([act[n] for n in rows]), jnp.concatenate([cot_tok[n] for n in rows], axis=0))
        for n, part in enumerate(downs):
            g_ref[:, part] += grad[n * width : (n + 1) * width]
        g_ref[:, ups] += nt(side([normed3[n] for n in rows]), side([grad_up[n] for n in rows]))

        grad_x2, grad_x2_low, grad_gated = {}, {}, {}
        for n in rows:

            def third_back(p, grad_out, grad, hat, scale):
                g_vec_ref[6] += grad * hat
                g_vec_ref[7] += grad
                grad = grad_out.astype(F32) + normalize_back(grad, vec_ref[6], hat, scale)
                return grad, grad.astype(BF)

            grad_x2[n], grad_x2_low[n] = tiles(n, third_back, cot_low[n], grad3[n], hat3[n], scale3[n])
            grad_gated[n] = nn(att_out_ref[...], grad_x2_low[n])
            (out,) = tiles(n, lambda p, one, two: ((one + two).astype(BF),), x2[n], down[n])
            store_tokens(out_ref, start + n, order, out.T.astype(F32))
        g_ref[:, place["att_out"]] += nt(
            side([gated[n] for n in rows]), side([grad_x2_low[n] for n in rows])
        )
        grad_gate2, grad_out, center = {}, {}, {}
        for n in rows:

            def gate_back(p, grad, gate, out):
                mixed_grad = grad * gate
                scaled = [mixed_grad[mine[h]] * inverses[n, h][:, parts[p]] for h in range(heads)]
                low = jnp.concatenate(scaled, axis=0).astype(BF)
                product = low.astype(F32) * out
                centers = [jnp.sum(product[mine[h]], axis=0, keepdims=True) for h in range(heads)]
                return ((mixed_grad * out * (1.0 - gate)).astype(BF), low, *centers)

            grad_gate2[n], grad_out[n], *centers = tiles(n, gate_back, grad_gated[n], gate2[n], attended[n])
            for h in range(heads):
                center[n, h] = centers[h]

        grad_queries, grad_keys, grad_values = {}, {}, {}

        def probs(n, h):
            return nn(kv_tok[n][:, width:] * lane_ref[h], grad_out[n])

        def spread(n, h, grad_score):
            both = nn(jnp.concatenate([key[n][mine[h]], chain_ref[...]], axis=0), grad_score)
            grad_queries[n, h] = (both[:head] * scaling).astype(BF)
            g_bias_ref[h] += both[head:]
            grad_keys[n, h] = (nt(query[n][mine[h]], grad_score) * LN2).astype(BF)

        coming, behind = probs(*pairs[0]), None
        for at_pair, (n, h) in enumerate(pairs):
            grad_prob = coming
            if at_pair + 1 < len(pairs):
                coming = probs(*pairs[at_pair + 1])
            expon = e_scr[n, :, there[h]]
            grad_score = (expon.astype(F32) * (grad_prob - center[n, h])).astype(BF)
            grad_values[n, h] = nt(grad_out[n][mine[h]], expon).astype(BF)
            if behind is not None:
                spread(*behind)
            behind = (n, h, grad_score)
        spread(*behind)

        grad_hidden, grad2 = {}, {}
        for n in rows:
            blocks = [items[n, h] for items in (grad_queries, grad_keys, grad_values) for h in range(heads)]
            grad_hidden[n] = jnp.concatenate(blocks + [grad_gate2[n]], axis=0)
            grad2[n] = nn(att_ref[...], grad_hidden[n])
        g_ref[:, place["query"].start : place["gate2"].stop] += nt(
            side([normed2[n] for n in rows]), side([grad_hidden[n] for n in rows])
        )
        grad_x1, grad_branch, grad_gate1, grad_mix, grad1 = {}, {}, {}, {}, {}
        for n in rows:

            def second_back(p, grad_after, grad, hat, scale, gate, added):
                g_vec_ref[4] += grad * hat
                g_vec_ref[5] += grad
                grad = grad_after + normalize_back(grad, vec_ref[4], hat, scale)
                gated_grad = grad * gate
                return grad, gated_grad.astype(BF), (gated_grad * added * (1.0 - gate)).astype(BF)

            grad_x1[n], grad_branch[n], grad_gate1[n] = tiles(
                n, second_back, grad_x2[n], grad2[n], hat2[n], scale2[n], gate1[n], branch[n]
            )
            grad_mix[n] = nn(tri_out_ref[...], grad_branch[n])
            grad1[n] = nn(gate_w_ref[...], grad_gate1[n])
        g_ref[:, place["tri_out"]] += nt(
            side([mixed[n] for n in rows]), side([grad_branch[n] for n in rows])
        )
        g_ref[:, place["gate"]] += nt(
            side([normed1[n] for n in rows]), side([grad_gate1[n] for n in rows])
        )
        for n in rows:
            for p, part in enumerate(parts):
                grad, hat, scale = grad_mix[n][:, part], hat_t[n][:, part], scale_t[n][:, part]
                g_vec_ref[2] += grad * hat
                g_vec_ref[3] += grad
                dt_ref[p, start + n] = normalize_back(grad, vec_ref[2], hat, scale)
                grad, hat, scale = grad1[n][:, part], hat1[n][:, part], scale1[n][:, part]
                g_vec_ref[0] += grad * hat
                g_vec_ref[1] += grad
                grad = grad_x1[n][:, part] + normalize_back(grad, vec_ref[0], hat, scale)
                z_ref[start + n, :, part] = grad
        return carry

    lax.fori_loop(0, total_rows // count, step, 0)


def rows_pass(c, chunks, half, other, before, t, xt, cot_rows, order, bias, chain, lane, vecs, weights, heads):
    _, all_rows, width, length = xt.shape
    blocks, pieces, sub, tokens, _ = cot_rows.shape
    rows = blocks * sub
    some, count = 4, 4
    inner = sub // some
    full = lambda item: pl.BlockSpec(item.shape, lambda at, half: (0,) * item.ndim)
    of_all = pl.BlockSpec((some, width, length), lambda at, half: (c * (rows // some) + at, 0, 0))
    xt_some = pl.BlockSpec(
        (1, some, width, length), lambda at, half: (half[0], c * (rows // some) + at, 0, 0)
    )
    t_some = pl.BlockSpec(
        (length // 128, some, width, 128), lambda at, half: (0, c * (rows // some) + at, 0, 0)
    )
    dt_some = pl.BlockSpec((length // 128, some, width, 128), lambda at, half: (0, at, 0, 0))
    by_piece = pl.BlockSpec(
        (1, pieces, some, tokens, width), lambda at, half: (at // inner, 0, at % inner, 0, 0)
    )
    consts = (bias, chain, lane, vecs) + weights
    wide = weights[-1].shape[1]
    sum_shapes = [
        jax.ShapeDtypeStruct(shape, F32)
        for shape in ((width, 7 * width + 2 * wide), (8, width, 128), (heads, 16, length))
    ]
    before_specs = [full(item) for item in before[:3]]
    before_specs += [pl.BlockSpec(memory_space=pl.ANY)] * len(before[3:])
    return pl.pallas_call(
        functools.partial(rows_kernel, count, heads, order, c == 0),
        grid_spec=pltpu.PrefetchScalarGridSpec(
            num_scalar_prefetch=1,
            grid=(rows // some,),
            in_specs=[pl.BlockSpec(memory_space=pltpu.HBM)]
            + before_specs
            + [t_some, xt_some, by_piece] + [full(item) for item in consts],
            out_specs=[by_piece, dt_some, of_all] + [full(item) for item in sum_shapes],
            scratch_shapes=[
                pltpu.VMEM((count, length, heads * length), BF),
            ],
        ),
        out_shape=[
            jax.ShapeDtypeStruct(cot_rows.shape, BF),
            by_halves(rows, width, length),
            jax.ShapeDtypeStruct((all_rows, width, length), F32),
        ]
        + sum_shapes,
        input_output_aliases={5: 2} if before else {},
        compiler_params=pltpu.CompilerParams(vmem_limit_bytes=VMEM_LIMIT),
        cost_estimate=cost(1.2e11),
        name="rows",
    )(half, other, *before, t, xt, cot_rows, *consts)


def edges_back_kernel(
    order, half_ref, xt_ref, z_ref, da_ref, db_ref, wt_ref, w_ref, gain_ref, shift_ref, out_ref, g_w_ref, g_vec_ref
):
    _, rows, width, length = xt_ref.shape
    count = 4

    @pl.when(pl.program_id(0) == 0)
    def _():
        g_w_ref[...] = jnp.zeros(g_w_ref.shape, F32)
        g_vec_ref[...] = jnp.zeros(g_vec_ref.shape, F32)

    def step(at, carry):
        start = at * count
        x0 = stacked(xt_ref.at[0], start, count).astype(F32)
        lanes = x0.shape[1]
        gain = widen(gain_ref[...], lanes)
        hat, scale = normalize(x0)
        normed = (hat * gain + widen(shift_ref[...], lanes)).astype(BF)
        proj = nn(wt_ref[...], normed)
        pa, pag = proj[:width], proj[width : 2 * width]
        pb, pbg = proj[2 * width : 3 * width], proj[3 * width :]
        halves = [(n, half) for n in range(count) for half in range(da_ref.shape[0])]
        da = jnp.concatenate([da_ref[half, start + n] for n, half in halves], axis=1)
        db = jnp.concatenate([db_ref[half, start + n] for n, half in halves], axis=1)
        sa, sb = sigmoid(pag), sigmoid(pbg)
        dsa, dsb = da * sa, db * sb
        grads = jnp.concatenate(
            [
                dsa.astype(BF),
                (dsa * pa * (1.0 - sa)).astype(BF),
                dsb.astype(BF),
                (dsb * pb * (1.0 - sb)).astype(BF),
            ],
            axis=0,
        )
        g_w_ref[...] += nt(normed, grads)
        grad = nn(w_ref[...], grads)
        g_vec_ref[0] += fold(grad * hat)
        g_vec_ref[1] += fold(grad)
        out = stacked(z_ref, start, count) + normalize_back(grad, gain, hat, scale)
        out = out.astype(BF)
        for n in range(count):
            store_tokens(out_ref, start + n, order, out[:, n * length : (n + 1) * length].T.astype(F32))
        return carry

    lax.fori_loop(0, rows // count, step, 0)


def edges_back(half, xt, z, da, db, order, weight_t, weight, gain, shift, shape):
    _, rows, width, length = xt.shape
    blocks, pieces, sub, tokens, _ = shape
    chunks = order[2]
    some = sub // chunks
    step = 16 // some
    inner = blocks // step
    full = lambda item: pl.BlockSpec(item.shape, lambda at, half: (0,) * item.ndim)
    xt_row = pl.BlockSpec((1, 16, width, length), lambda at, half: (half[0], at, 0, 0))
    by_row = pl.BlockSpec((16, width, length), lambda at, half: (at, 0, 0))
    by_half = pl.BlockSpec((length // 128, 16, width, 128), lambda at, half: (0, at, 0, 0))
    sum_shapes = [
        jax.ShapeDtypeStruct(weight.shape, F32),
        jax.ShapeDtypeStruct((2, width, 128), F32),
    ]
    by_piece = pl.BlockSpec(
        (step, pieces, some, tokens, width), lambda at, half: (at % inner, 0, at // inner, 0, 0)
    )
    return pl.pallas_call(
        functools.partial(edges_back_kernel, order),
        grid_spec=pltpu.PrefetchScalarGridSpec(
            num_scalar_prefetch=1,
            grid=(chunks * inner,),
            in_specs=[xt_row, by_row] + [by_half] * 2 + [full(item) for item in (weight_t, weight, gain, shift)],
            out_specs=[by_piece] + [full(item) for item in sum_shapes],
        ),
        out_shape=[jax.ShapeDtypeStruct(shape, BF)] + sum_shapes,
        compiler_params=pltpu.CompilerParams(vmem_limit_bytes=VMEM_LIMIT),
        cost_estimate=cost(4.0e10),
        name="edges_back",
    )(half, xt, z, da, db, weight_t, weight, gain, shift)


def shards(
    row_size,
    col_size,
    pair_state,
    cotangent,
    chain_lengths,
    tri_gain,
    tri_shift,
    tri_weight,
    mix_gain,
    mix_shift,
    tri_out,
    att_gain,
    att_shift,
    att_weight,
    chain_bias,
    att_out,
    trans_gain,
    trans_shift,
    up_weight,
    down_weight,
):
    heads = HEADS
    crops, own_rows, tokens, width = pair_state.shape
    length = col_size * tokens
    chunks = CHUNKS
    some = own_rows // (col_size * chunks)
    axes = ("row", "col")
    group = row_size * col_size
    order = (row_size, col_size, chunks)
    shape = (row_size, col_size, some, tokens, width)

    def swap(values):
        return lax.all_to_all(values, axes, split_axis=0, concat_axis=0, tiled=True)

    def cut(values):
        parts = values.reshape(group, chunks, some, tokens, width)
        return [parts[:, c] for c in range(chunks)]

    def join(parts):
        return jnp.stack(parts, axis=1).reshape(crops, own_rows, tokens, width)

    def across(values, bit):
        return lax.ppermute(values, "col", [(q, q ^ bit) for q in range(col_size)])

    bits = [1 << n for n in range(col_size.bit_length() - 1)]

    def doubled(items, axis, size, bits):
        for bit in bits:
            lows = [values.astype(sent) for values, sent in items]
            others = [lax.ppermute(low, axis, [(q, q ^ bit) for q in range(size)]) for low in lows]
            others = lax.optimization_barrier(tuple(others))
            items = [
                (low.astype(F32) + other.astype(F32), sent)
                for low, other, (_, sent) in zip(lows, others, items)
            ]
        return items

    def summed_over_rows(values, sent):
        low = values.astype(sent)
        terms = [low.astype(F32)]
        for m in range(1, row_size):
            other = lax.ppermute(low, "row", [(r, r ^ m) for r in range(row_size)])
            terms.append(other.astype(F32))
        while len(terms) > 1:
            terms = [terms[n] + terms[n + 1] for n in range(0, len(terms), 2)]
        return terms[0]

    whole = (row_size, col_size, some * chunks, tokens, width)
    cot_parts = cut(cotangent)

    wide = lambda item: jnp.broadcast_to(item[:, None], (width, 128))
    vecs = jnp.stack(
        [
            wide(item)
            for item in (
                tri_gain,
                tri_shift,
                mix_gain,
                mix_shift,
                att_gain,
                att_shift,
                trans_gain,
                trans_shift,
            )
        ]
    )
    edge_w = tri_weight[:, : 4 * width]
    edge_wt = edge_w.T
    gate_w = tri_weight[:, 4 * width :]
    lengths = lax.dynamic_index_in_dim(chain_lengths, lax.axis_index("row"), 0, keepdims=False)
    ends = jnp.cumsum(lengths)
    places = jnp.arange(length, dtype=jnp.int32)
    places = places.reshape(order + (some,)).transpose(1, 2, 0, 3).reshape(length)
    chain = jnp.sum((places[:, None] >= ends[None, :]).astype(jnp.int32), axis=-1)
    same = (chain[:, None] == chain[None, :]).astype(F32)
    bias = (LOG2E * chain_bias)[:, None, None] * same[None]
    which = (jnp.arange(16, dtype=jnp.int32)[:, None] == chain[None, :]).astype(F32)
    head_of = jnp.arange(width, dtype=jnp.int32) // (width // heads)
    lane = (jnp.arange(heads, dtype=jnp.int32)[:, None] == head_of[None, :]).astype(BF)
    lane = jnp.broadcast_to(lane[:, None, :], (heads, length, width))
    me = lax.axis_index("col")
    own = own_rows
    far_bit = col_size // 2
    half, core = me // far_bit, me % far_bit
    token_place = jnp.stack([(me ^ m) * tokens for m in range(col_size)])
    place = [(s * far_bit + (core ^ k)) * own for s in range(2) for k in range(2)]
    place = jnp.stack(place + [half])
    here = (core * own).reshape(1)
    half_at = half.reshape(1)
    weights = (
        gate_w,
        gate_w.T,
        tri_out,
        tri_out.T,
        att_weight.T,
        att_weight[:, width : 3 * width],
        att_weight,
        att_out,
        att_out.T,
        up_weight,
        up_weight.T,
        down_weight,
        down_weight.T,
    )
    chain_rows = which.astype(BF)

    some_rows = own_rows // col_size
    x_pieces, crossings = [], []
    for s in range(2):
        pieces = []
        for k in range(2):
            start = (s * far_bit + (core ^ k)) * some_rows
            part = lax.dynamic_slice_in_dim(pair_state, start, some_rows, axis=1)
            if len(crossings) > 1:
                part = after(part, crossings[-2])
            part = lax.all_to_all(part, "row", split_axis=0, concat_axis=0, tiled=True)
            crossings.append(across(part, far_bit ^ k))
            pieces += [crossings[-1], across(part, 1)] if k else [part, crossings[-1]]
        own_part, far, far_other, near_other = pieces
        x_pieces.append([own_part, near_other, far, far_other])
    cot_rows, before = [], part
    for held in cot_parts:
        before = swap(after(held, before))
        cot_rows.append(before.reshape(shape))
    lefts, rights, xt = [], [], []
    for s, pieces in enumerate(x_pieces):
        others = [] if s else [crossings[2], cot_parts[0]]
        left, right, *xt = edges(
            token_place, s, pieces, xt, others, order, edge_wt, vecs[0], vecs[1]
        )
        lefts.append(left)
        rights += [right, across(right, 1)]
    (xt,) = xt
    t = triangle(place, lefts, rights)
    tips = [across(tip(cot_rows[0]), 1), tip(cot_rows[1])]
    lefts = [item for left in lefts for item in (left, across(left, 1))]
    state, outs, dts, sent = [], [], [], []
    pairs = [[q, q + far_bit] for q in range(far_bit)]
    for c in range(chunks):
        out, dt, z, *sums = rows_pass(
            c, chunks, half_at, tips[c], state, t, xt, cot_rows[c], order, bias, chain_rows, lane, vecs, weights, heads
        )
        state = sums + [z]
        dt = turn(dt, outs)
        if c < chunks - 1:
            dts.append(dt)
            outs.append(swap(out.reshape(group, some, tokens, width)))
            near = lax.dynamic_index_in_dim(dt, half, 0, keepdims=False)
            sent.append((near, across(lax.dynamic_index_in_dim(dt, 1 - half, 0, keepdims=False), far_bit)))
    dts.append(dt)
    crossed = []
    for near, far in sent:
        crossed.append(jnp.where(half == 0, jnp.stack([near, far]), jnp.stack([far, near])))
    crossed.append(
        lax.all_to_all(dt, "col", split_axis=0, concat_axis=0, axis_index_groups=pairs, tiled=True)
    )
    g_rows, g_vec, g_bias = sums
    row_bits = [1 << n for n in range(row_size.bit_length() - 1)]
    g_rows = summed_over_rows(g_rows, BF)
    da = left_back(place, dts, rights)
    grads = [[item, across(item, 1)] for item in crossed[:-1]]
    crossed[-1] = after(crossed[-1], da)
    grads.append([crossed[-1], across(crossed[-1], 1)])
    outs.append(swap(after(out.reshape(group, some, tokens, width), g_rows, crossed[-1])))
    pair_out = join(outs)
    db = right_back(here, grads, lefts)
    back, g_edge, g_vec_edge = edges_back(
        half_at, xt, z, da, db, order, edge_wt, edge_w, vecs[0], vecs[1], whole
    )
    g_vec = jnp.sum(g_vec, axis=-1)
    g_vec_edge = jnp.sum(g_vec_edge, axis=-1)
    g_chain = jnp.sum(g_bias * which[None], axis=(1, 2))
    small = jnp.concatenate(
        [g_vec[:2] + g_vec_edge, g_vec[2:], jnp.pad(g_chain, (0, width - heads))[None]], axis=0
    )
    items = doubled([(g_edge, BF), (small, F32)], "row", row_size, row_bits)
    back = after(back, *[values for values, _ in items])
    grad_pair = swap(back.reshape(group, some * chunks, tokens, width))
    grad_pair = grad_pair.reshape(crops, own_rows, tokens, width)
    g_rows = after(g_rows, pair_out, back)
    items = doubled(items + [(g_rows, BF)], "col", col_size, bits[::-1])
    t_edge, small, total = [values for values, _ in items]
    column = lambda at, n=1: total[:, at * width : (at + n) * width]
    ff = up_weight.shape[1] // width
    t_gate, t_tri_out, t_att = column(0), column(1), column(2, 4)
    t_att_out, t_up = column(6), column(7, ff)
    t_down = jnp.concatenate([column(7 + ff + n) for n in range(ff)], axis=0)
    return (
        pair_out,
        grad_pair,
        small[0],
        small[1],
        jnp.concatenate([t_edge, t_gate], axis=1),
        small[2],
        small[3],
        t_tri_out,
        small[4],
        small[5],
        t_att,
        small[8, :heads],
        t_att_out,
        small[6],
        small[7],
        t_up,
        t_down,
    )


def solution(mesh):
    pair = P("dp", "row", "col", None)
    vector, matrix = P("dp"), P("dp", None)
    return jax.shard_map(
        functools.partial(shards, mesh.shape["row"], mesh.shape["col"]),
        mesh=mesh,
        in_specs=(pair, pair, P("dp", None)) + (P(),) * 15,
        out_specs=(
            pair,
            pair,
            vector,
            vector,
            matrix,
            vector,
            vector,
            matrix,
            vector,
            vector,
            matrix,
            vector,
            matrix,
            vector,
            vector,
            matrix,
            matrix,
        ),
        check_vma=False,
    )
```

```python
import functools
import math

import jax
import jax.numpy as jnp
from jax import lax
from jax.experimental import pallas as pl
from jax.experimental.pallas import tpu as pltpu
from jax.sharding import PartitionSpec as P

HEADS = 4
EPS = 1e-05
LOG2E = math.log2(math.e)
LN2 = math.log(2.0)
CHUNKS = 2
VMEM_LIMIT = 56 * 1024 * 1024
BF = jnp.bfloat16
F32 = jnp.float32


def nn(left, right):
    return lax.dot_general(left, right, (((1,), (0,)), ((), ())), preferred_element_type=F32)


def nt(left, right):
    return lax.dot_general(left, right, (((1,), (1,)), ((), ())), preferred_element_type=F32)


def tn(left, right):
    return lax.dot_general(left, right, (((0,), (0,)), ((), ())), preferred_element_type=F32)


def cost(flops, size=0):
    return pl.CostEstimate(flops=int(flops), bytes_accessed=int(size), transcendentals=0)


def sigmoid(values):
    return 0.5 * jnp.tanh(0.5 * values) + 0.5


def normalize(values):
    center = values - jnp.mean(values, axis=0, keepdims=True)
    spread = jnp.mean(center * center, axis=0, keepdims=True)
    scale = lax.rsqrt(spread + EPS)
    return center * scale, scale


def normalize_back(grads, gain, hat, scale):
    grad_hat = grads * gain
    first = jnp.mean(grad_hat, axis=0, keepdims=True)
    second = jnp.mean(grad_hat * hat, axis=0, keepdims=True)
    return scale * (grad_hat - first - hat * second)


def widen(column, lanes):
    return jnp.concatenate([column] * (lanes // column.shape[1]), axis=1)


def fold(values):
    parts = [values[:, at : at + 128] for at in range(0, values.shape[1], 128)]
    return functools.reduce(lambda one, two: one + two, parts)


def to_order(flat, order):
    length, width = flat.shape
    flat = flat.reshape(order + (length // math.prod(order), width))
    return flat.transpose(1, 2, 0, 3, 4).reshape(length, width)


def load_tokens(ref, row, order):
    _, pieces, some, tokens, width = ref.shape
    flat = ref[row // some, :, row % some, :, :].astype(F32)
    return to_order(flat.reshape(pieces * tokens, width), order)


def store_tokens(ref, row, order, values):
    _, pieces, some, tokens, width = ref.shape
    back = (order[1], order[2], order[0])
    flat = values.reshape(back + (pieces * tokens // math.prod(order), width))
    flat = flat.transpose(2, 0, 1, 3, 4).reshape(pieces, tokens, width)
    ref[row // some, :, row % some, :, :] = flat.astype(ref.dtype)


def stacked(ref, start, count):
    return jnp.concatenate([ref[start + n] for n in range(count)], axis=1)


def spread_out(ref, start, count, values):
    length = values.shape[1] // count
    for n in range(count):
        ref[start + n] = values[:, n * length : (n + 1) * length].astype(ref.dtype)


def no_op(*refs):
    pass


def tip(values):
    return values[(0,) * (values.ndim - 2)][:16, :128]


def after(values, *others):
    others = [tip(item) for item in others]
    anywhere = pl.BlockSpec(memory_space=pltpu.HBM)
    return pl.pallas_call(
        no_op,
        in_specs=[anywhere] * (1 + len(others)),
        out_specs=anywhere,
        out_shape=jax.ShapeDtypeStruct(values.shape, values.dtype),
        input_output_aliases={0: 0},
        cost_estimate=cost(0),
        name="after",
    )(values, *others)


def edges_kernel(order, place_ref, *refs):
    x_refs, (w_ref, gain_ref, shift_ref), rest = refs[:4], refs[4:7], refs[-6:]
    a_ref, b_ref, xt_ref, a_scr, b_scr, x_scr = rest
    width, rows, length = a_ref.shape
    pitch = a_scr.shape[1] // rows
    count = x_scr.shape[0]
    _, some, tokens, _ = x_refs[0].shape

    def step(at, carry):
        start = at * count
        turned = []
        for n in range(count):
            row = start + n
            for m, ref in enumerate(x_refs):
                there = pl.ds(pl.multiple_of(place_ref[m], tokens), tokens)
                x_scr[n, there, :] = ref[row // some, row % some].astype(F32)
            turned.append(to_order(x_scr[n], order).astype(BF).T)
        x0 = jnp.concatenate(turned, axis=1)
        for n in range(count):
            xt_ref[0, start + n] = turned[n]
        hat, _ = normalize(x0.astype(F32))
        lanes = x0.shape[1]
        normed = (hat * widen(gain_ref[...], lanes) + widen(shift_ref[...], lanes)).astype(BF)
        proj = nn(w_ref[...], normed)
        left = sigmoid(proj[width : 2 * width]) * proj[:width]
        right = sigmoid(proj[3 * width : 4 * width]) * proj[2 * width : 3 * width]
        for n in range(count):
            base = pl.multiple_of((start + n) * pitch, 8)
            for half in range(length // 128):
                part = slice(n * length + half * 128, n * length + half * 128 + 128)
                a_scr[half, pl.ds(base, width), :] = left[:, part]
                b_scr[half, pl.ds(base, width), :] = right[:, part]
        return carry

    lax.fori_loop(0, rows // count, step, 0)

    def turn(at, carry):
        for n in range(8):
            e = at * 8 + n
            for scr, out in ((a_scr, a_ref), (b_scr, b_ref)):
                halves = [scr[h, pl.ds(e, rows, stride=pitch), :] for h in range(scr.shape[0])]
                out[e] = jnp.concatenate(halves, axis=1).astype(BF)
        return carry

    lax.fori_loop(0, width // 8, turn, 0)


def edges(place, half, x_pieces, before, others, order, weight, gain, shift):
    blocks, rows_there, tokens, width = x_pieces[0].shape
    length = len(x_pieces) * tokens
    chunks = order[2]
    some = rows_there // chunks
    step = 16 // some
    inner = blocks // step
    rows = blocks * some * chunks
    const = lambda at, place: (0, 0)
    pitch = width + 8
    low = pl.BlockSpec((width, 16, length), lambda at, place: (0, at, 0))
    spec = pl.BlockSpec(
        (step, some, tokens, width),
        lambda at, place: (at % inner, at // inner, 0, 0),
    )
    return pl.pallas_call(
        functools.partial(edges_kernel, order),
        grid_spec=pltpu.PrefetchScalarGridSpec(
            num_scalar_prefetch=1,
            grid=(chunks * inner,),
            in_specs=[spec] * 4
            + [
                pl.BlockSpec(weight.shape, const),
                pl.BlockSpec(gain.shape, const),
                pl.BlockSpec(shift.shape, const),
            ]
            + [pl.BlockSpec(memory_space=pl.ANY)] * len(before)
            + [pl.BlockSpec(memory_space=pltpu.HBM)] * len(others),
            out_specs=[low, low, pl.BlockSpec((1, 16, width, length), lambda at, place: (half, at, 0, 0))],
            scratch_shapes=[
                pltpu.VMEM((length // 128, 16 * pitch, 128), F32),
                pltpu.VMEM((length // 128, 16 * pitch, 128), F32),
                pltpu.VMEM((4, length, width), F32),
            ],
        ),
        out_shape=[jax.ShapeDtypeStruct((width, rows, length), BF)] * 2
        + [jax.ShapeDtypeStruct((2, rows, width, length), BF)],
        input_output_aliases={8: 2} if before else {},
        compiler_params=pltpu.CompilerParams(vmem_limit_bytes=VMEM_LIMIT),
        cost_estimate=cost(3.0e9),
        name="edges",
    )(place, *x_pieces, weight, gain, shift, *before, *[tip(item) for item in others])


def gather_pieces(place_ref, rights, e, scr):
    for n, piece in enumerate(rights):
        rows = piece.shape[1]
        scr[e, pl.ds(pl.multiple_of(place_ref[n], rows), rows), :] = piece[e]


def by_channel(ref):
    halves, rows, some, lanes = ref.shape
    return ref.reshape(halves, rows * some, lanes)


def put_channel(ref, e, values):
    halves, rows, some, lanes = ref.shape
    flat = by_channel(ref)
    for half in range(halves):
        flat[half, pl.ds(e, rows, stride=some), :] = values[:, half * lanes : (half + 1) * lanes]


def ahead(first, count, begin, end):
    coming = begin(first)
    for e in range(first, first + count):
        here = coming
        if e + 1 < first + count:
            coming = begin(e + 1)
        end(e, here)


SOME = 16


def cut_refs(refs, *counts):
    parts = []
    for count in counts:
        parts.append(refs[:count])
        refs = refs[count:]
    return parts + list(refs)


def triangle_kernel(place_ref, *refs):
    lefts, rights, t_ref, scr, own_scr = cut_refs(refs, 2, 4)
    for half, left in enumerate(lefts):

        @pl.when(place_ref[4] == half)
        def _():
            own_scr[...] = left[...]

    def begin(e):
        gather_pieces(place_ref, rights, e, scr)
        return nt(own_scr[e], scr[e])

    ahead(0, SOME, begin, functools.partial(put_channel, t_ref))


def high_spec(rows, length):
    return pl.BlockSpec((length // 128, rows, SOME, 128), lambda at, place: (0, 0, at, 0))


def low_spec(rows, lanes):
    return pl.BlockSpec((SOME, rows, lanes), lambda at, place: (at, 0, 0))


def by_halves(rows, width, length):
    return jax.ShapeDtypeStruct((length // 128, rows, width, 128), F32)


def channel_call(kernel, name, flops, scalar, ins, in_specs, out_specs, out_shape, scratch=()):
    return pl.pallas_call(
        kernel,
        grid_spec=pltpu.PrefetchScalarGridSpec(
            num_scalar_prefetch=1,
            grid=(ins[0].shape[0 if ins[0].ndim == 3 else 2] // SOME,),
            in_specs=in_specs,
            out_specs=out_specs,
            scratch_shapes=scratch,
        ),
        out_shape=out_shape,
        compiler_params=pltpu.CompilerParams(vmem_limit_bytes=VMEM_LIMIT),
        cost_estimate=cost(flops),
        name=name,
    )(scalar, *ins)


def triangle(place, lefts, rights):
    width, rows, length = lefts[0].shape
    return channel_call(
        triangle_kernel,
        "triangle",
        3.0e9,
        place,
        (*lefts, *rights),
        [low_spec(rows, length)] * 6,
        high_spec(rows, length),
        by_halves(rows, width, length),
        [pltpu.VMEM((SOME, length, length), BF), pltpu.VMEM((SOME, rows, length), BF)],
    )


def turn_kernel(grad_ref, *refs):
    out_ref = refs[-1]
    halves, rows, some, _ = grad_ref.shape
    flat = by_channel(grad_ref)
    for e in range(some):
        for half in range(halves):
            out_ref[half, e] = flat[half, pl.ds(e, rows, stride=some), :].astype(BF)


def turn(grad, others):
    halves, rows, width, lanes = grad.shape
    some = 32
    return pl.pallas_call(
        turn_kernel,
        grid=(width // some,),
        in_specs=[pl.BlockSpec((halves, rows, some, lanes), lambda at: (0, 0, at, 0))]
        + [pl.BlockSpec(memory_space=pltpu.HBM)] * len(others),
        out_specs=pl.BlockSpec((halves, some, rows, lanes), lambda at: (0, at, 0, 0)),
        out_shape=jax.ShapeDtypeStruct((halves, width, rows, lanes), BF),
        compiler_params=pltpu.CompilerParams(vmem_limit_bytes=VMEM_LIMIT),
        cost_estimate=cost(5.0e9),
        name="turn",
    )(grad, *[tip(item) for item in others])


def right_back_kernel(chunks, here_ref, *refs):
    lefts, grads, db_ref, scr = cut_refs(refs, 4, 2 * chunks)
    rows = db_ref.shape[1]

    def begin(e):
        pairs = [(s, k) for s in range(2) for k in range(2)]
        grad = [grads[2 * c + k][s, e] for s, k in pairs for c in range(chunks)]
        left = [lefts[2 * s + k][e] for s, k in pairs]
        return tn(jnp.concatenate(grad, axis=0), jnp.concatenate(left, axis=0))

    def end(e, db):
        scr[e] = db
        put_channel(db_ref, e, scr[e, pl.ds(pl.multiple_of(here_ref[0], rows), rows), :])

    ahead(0, SOME, begin, end)


def right_back(here, grads, lefts):
    width, rows, length = lefts[0].shape
    chunks = len(grads)
    _, _, some, part = grads[0][0].shape
    both = pl.BlockSpec((2, SOME, some, part), lambda at, here: (0, at, 0, 0))
    return channel_call(
        functools.partial(right_back_kernel, chunks),
        "right_back",
        2.2e10,
        here,
        [*lefts] + [item for chunk in grads for item in chunk],
        [low_spec(rows, length)] * 4 + [both] * (2 * chunks),
        high_spec(rows, length),
        by_halves(rows, width, length),
        [pltpu.VMEM((SOME, part, length), F32)],
    )


def left_back_kernel(chunks, place_ref, *refs):
    rights, grads, da_ref, scr = cut_refs(refs, 4, chunks)

    def begin(e):
        gather_pieces(place_ref, rights, e, scr)
        grad = [jnp.concatenate([ref[0, e], ref[1, e]], axis=1) for ref in grads]
        return nn(jnp.concatenate(grad, axis=0), scr[e])

    ahead(0, SOME, begin, functools.partial(put_channel, da_ref))


def left_back(place, grads, rights):
    _, width, some, part = grads[0].shape
    _, rows, length = rights[0].shape
    both = pl.BlockSpec((2, SOME, some, part), lambda at, place: (0, at, 0, 0))
    return channel_call(
        functools.partial(left_back_kernel, len(grads)),
        "left_back",
        2.0e10,
        place,
        (*rights, *grads),
        [low_spec(rows, length)] * 4 + [both] * len(grads),
        high_spec(rows, length),
        by_halves(rows, width, length),
        [pltpu.VMEM((SOME, length, length), BF)],
    )


def rows_kernel(count, heads, order, first, half_ref, other_ref, *refs):
    before = []
    if not first:
        before, refs = refs[:3], refs[4:]
    rows_body(count, heads, order, before, *refs)


def rows_body(
    count,
    heads,
    order,
    before,
    t_ref,
    xt_ref,
    cot_ref,
    bias_ref,
    chain_ref,
    lane_ref,
    vec_ref,
    gate_w_ref,
    gate_wt_ref,
    tri_out_ref,
    tri_out_t_ref,
    att_t_ref,
    att_kv_ref,
    att_ref,
    att_out_ref,
    att_out_t_ref,
    up_ref,
    up_t_ref,
    down_ref,
    down_t_ref,
    out_ref,
    dt_ref,
    z_ref,
    g_ref,
    g_vec_ref,
    g_bias_ref,
    e_scr,
):
    _, total_rows, width, length = xt_ref.shape
    head = width // heads
    scaling = 1.0 / math.sqrt(head)

    sums = (g_ref, g_vec_ref, g_bias_ref)
    place = {}
    for name in ("gate", "tri_out", "query", "key", "value", "gate2", "att_out"):
        place[name] = slice(len(place) * width, (len(place) + 1) * width)
    ups = slice(7 * width, 7 * width + up_ref.shape[1])
    downs = [
        slice(at, at + width) for at in range(ups.stop, ups.stop + up_ref.shape[1], width)
    ]

    @pl.when(pl.program_id(0) == 0)
    def _():
        for n, ref in enumerate(sums):
            ref[...] = before[n][...] if before else jnp.zeros(ref.shape, ref.dtype)

    per = length // 128
    mine = [slice(h * head, (h + 1) * head) for h in range(heads)]
    there = [slice(h * length, (h + 1) * length) for h in range(heads)]
    ones = jnp.ones((16, length), BF)
    parts = [slice(p * 128, (p + 1) * 128) for p in range(per)]

    def tiles(n, function, *items):
        results = [function(p, *[item[:, parts[p]] for item in items]) for p in range(per)]
        return [jnp.concatenate(list(column), axis=1) for column in zip(*results)]

    def step(at, carry):
        start = at * count
        rows = range(count)
        side = lambda items: jnp.concatenate(items, axis=1)
        x0, hat1, scale1, normed1, gate_raw = {}, {}, {}, {}, {}
        hat_t, scale_t, mixed, branch = {}, {}, {}, {}
        for n in rows:

            def first(p):
                tile = xt_ref[0, start + n, :, parts[p]].astype(F32)
                hat, scale = normalize(tile)
                return tile, hat, scale, (hat * vec_ref[0] + vec_ref[1]).astype(BF)

            x0[n], hat1[n], scale1[n], normed1[n] = tiles(n, first)
            gate_raw[n] = nn(gate_wt_ref[...], normed1[n])

            def second(p):
                hat, scale = normalize(t_ref[p, start + n])
                return hat, scale, (hat * vec_ref[2] + vec_ref[3]).astype(BF)

            hat_t[n], scale_t[n], mixed[n] = tiles(n, second)
            branch[n] = nn(tri_out_t_ref[...], mixed[n])

        gate1, x1, hat2, scale2, normed2, hidden, kv_tok = {}, {}, {}, {}, {}, {}, {}
        for n in rows:

            def join(p, before, raw, add):
                gate = sigmoid(raw)
                after = before + gate * add
                hat, scale = normalize(after)
                return gate, after, hat, scale, (hat * vec_ref[4] + vec_ref[5]).astype(BF)

            gate1[n], x1[n], hat2[n], scale2[n], normed2[n] = tiles(
                n, join, x0[n], gate_raw[n], branch[n]
            )
            hidden[n] = nn(att_t_ref[...], normed2[n])
            kv_tok[n] = nn(normed2[n].T, att_kv_ref[...])

        query, key, value, gate2 = {}, {}, {}, {}
        for n in rows:

            def split(p, tile):
                gate = sigmoid(tile[3 * width :].astype(BF).astype(F32))
                asked = (tile[:width] * (scaling * LOG2E)).astype(BF)
                return asked, tile[width : 2 * width].astype(BF), tile[2 * width : 3 * width].astype(BF), gate

            query[n], key[n], value[n], gate2[n] = tiles(n, split, hidden[n])
            kv_tok[n] = kv_tok[n].astype(BF)

        pairs = [(n, h) for n in rows for h in range(heads)]

        def scores(n, h):
            return nn(kv_tok[n][:, :width] * lane_ref[h], query[n])

        outs, inverses = {}, {}

        def mix(n, h):
            both = nn(jnp.concatenate([value[n][mine[h]], ones], axis=0), e_scr[n, :, there[h]])
            inverses[n, h] = 1.0 / both[head : head + 1]
            outs[n, h] = both[:head] * inverses[n, h]

        coming = scores(*pairs[0])
        for at_pair, (n, h) in enumerate(pairs):
            score = coming
            if at_pair + 1 < len(pairs):
                coming = scores(*pairs[at_pair + 1])
            score = score + bias_ref[h]
            peak = jnp.max(score, axis=0, keepdims=True)
            e_scr[n, :, there[h]] = jnp.exp2(score - peak).astype(BF)
            if at_pair:
                mix(*pairs[at_pair - 1])
        mix(*pairs[-1])

        attended, gated, x2 = {}, {}, {}
        for n in rows:
            attended[n] = jnp.concatenate([outs[n, h] for h in range(heads)], axis=0)
            (gated[n],) = tiles(n, lambda p, gate, out: ((gate * out).astype(BF),), gate2[n], attended[n])
            x2[n] = nn(att_out_t_ref[...], gated[n])
        hat3, scale3, normed3, up, cot_tok, cot_low, grad_act = {}, {}, {}, {}, {}, {}, {}
        for n in rows:

            def third(p, before, add):
                after = before + add
                hat, scale = normalize(after)
                return after, hat, scale, (hat * vec_ref[6] + vec_ref[7]).astype(BF)

            x2[n], hat3[n], scale3[n], normed3[n] = tiles(n, third, x1[n], x2[n])
            up[n] = nn(up_t_ref[...], normed3[n])
            cot_tok[n] = load_tokens(cot_ref, start + n, order).astype(BF)
            cot_low[n] = cot_tok[n].T
            grad_act[n] = nn(down_ref[...], cot_low[n])
        act, down, grad_up, grad3 = {}, {}, {}, {}
        for n in rows:

            def silu(p, raw, grad):
                gate = sigmoid(raw)
                return (raw * gate).astype(BF), (grad * (gate * (1.0 + raw * (1.0 - gate)))).astype(BF)

            act[n], grad_up[n] = tiles(n, silu, up[n], grad_act[n])
            down[n] = nn(down_t_ref[...], act[n])
            grad3[n] = nn(up_ref[...], grad_up[n])
        grad = nn(side([act[n] for n in rows]), jnp.concatenate([cot_tok[n] for n in rows], axis=0))
        for n, part in enumerate(downs):
            g_ref[:, part] += grad[n * width : (n + 1) * width]
        g_ref[:, ups] += nt(side([normed3[n] for n in rows]), side([grad_up[n] for n in rows]))

        grad_x2, grad_x2_low, grad_gated = {}, {}, {}
        for n in rows:

            def third_back(p, grad_out, grad, hat, scale):
                g_vec_ref[6] += grad * hat
                g_vec_ref[7] += grad
                grad = grad_out.astype(F32) + normalize_back(grad, vec_ref[6], hat, scale)
                return grad, grad.astype(BF)

            grad_x2[n], grad_x2_low[n] = tiles(n, third_back, cot_low[n], grad3[n], hat3[n], scale3[n])
            grad_gated[n] = nn(att_out_ref[...], grad_x2_low[n])
            (out,) = tiles(n, lambda p, one, two: ((one + two).astype(BF),), x2[n], down[n])
            store_tokens(out_ref, start + n, order, out.T.astype(F32))
        g_ref[:, place["att_out"]] += nt(
            side([gated[n] for n in rows]), side([grad_x2_low[n] for n in rows])
        )
        grad_gate2, grad_out, center = {}, {}, {}
        for n in rows:

            def gate_back(p, grad, gate, out):
                mixed_grad = grad * gate
                scaled = [mixed_grad[mine[h]] * inverses[n, h][:, parts[p]] for h in range(heads)]
                low = jnp.concatenate(scaled, axis=0).astype(BF)
                product = low.astype(F32) * out
                centers = [jnp.sum(product[mine[h]], axis=0, keepdims=True) for h in range(heads)]
                return ((mixed_grad * out * (1.0 - gate)).astype(BF), low, *centers)

            grad_gate2[n], grad_out[n], *centers = tiles(n, gate_back, grad_gated[n], gate2[n], attended[n])
            for h in range(heads):
                center[n, h] = centers[h]

        grad_queries, grad_keys, grad_values = {}, {}, {}

        def probs(n, h):
            return nn(kv_tok[n][:, width:] * lane_ref[h], grad_out[n])

        def spread(n, h, grad_score):
            both = nn(jnp.concatenate([key[n][mine[h]], chain_ref[...]], axis=0), grad_score)
            grad_queries[n, h] = (both[:head] * scaling).astype(BF)
            g_bias_ref[h] += both[head:]
            grad_keys[n, h] = (nt(query[n][mine[h]], grad_score) * LN2).astype(BF)

        coming, behind = probs(*pairs[0]), None
        for at_pair, (n, h) in enumerate(pairs):
            grad_prob = coming
            if at_pair + 1 < len(pairs):
                coming = probs(*pairs[at_pair + 1])
            expon = e_scr[n, :, there[h]]
            grad_score = (expon.astype(F32) * (grad_prob - center[n, h])).astype(BF)
            grad_values[n, h] = nt(grad_out[n][mine[h]], expon).astype(BF)
            if behind is not None:
                spread(*behind)
            behind = (n, h, grad_score)
        spread(*behind)

        grad_hidden, grad2 = {}, {}
        for n in rows:
            blocks = [items[n, h] for items in (grad_queries, grad_keys, grad_values) for h in range(heads)]
            grad_hidden[n] = jnp.concatenate(blocks + [grad_gate2[n]], axis=0)
            grad2[n] = nn(att_ref[...], grad_hidden[n])
        g_ref[:, place["query"].start : place["gate2"].stop] += nt(
            side([normed2[n] for n in rows]), side([grad_hidden[n] for n in rows])
        )
        grad_x1, grad_branch, grad_gate1, grad_mix, grad1 = {}, {}, {}, {}, {}
        for n in rows:

            def second_back(p, grad_after, grad, hat, scale, gate, added):
                g_vec_ref[4] += grad * hat
                g_vec_ref[5] += grad
                grad = grad_after + normalize_back(grad, vec_ref[4], hat, scale)
                gated_grad = grad * gate
                return grad, gated_grad.astype(BF), (gated_grad * added * (1.0 - gate)).astype(BF)

            grad_x1[n], grad_branch[n], grad_gate1[n] = tiles(
                n, second_back, grad_x2[n], grad2[n], hat2[n], scale2[n], gate1[n], branch[n]
            )
            grad_mix[n] = nn(tri_out_ref[...], grad_branch[n])
            grad1[n] = nn(gate_w_ref[...], grad_gate1[n])
        g_ref[:, place["tri_out"]] += nt(
            side([mixed[n] for n in rows]), side([grad_branch[n] for n in rows])
        )
        g_ref[:, place["gate"]] += nt(
            side([normed1[n] for n in rows]), side([grad_gate1[n] for n in rows])
        )
        for n in rows:
            for p, part in enumerate(parts):
                grad, hat, scale = grad_mix[n][:, part], hat_t[n][:, part], scale_t[n][:, part]
                g_vec_ref[2] += grad * hat
                g_vec_ref[3] += grad
                dt_ref[p, start + n] = normalize_back(grad, vec_ref[2], hat, scale)
                grad, hat, scale = grad1[n][:, part], hat1[n][:, part], scale1[n][:, part]
                g_vec_ref[0] += grad * hat
                g_vec_ref[1] += grad
                grad = grad_x1[n][:, part] + normalize_back(grad, vec_ref[0], hat, scale)
                z_ref[start + n, :, part] = grad
        return carry

    lax.fori_loop(0, total_rows // count, step, 0)


def rows_pass(c, chunks, half, other, before, t, xt, cot_rows, order, bias, chain, lane, vecs, weights, heads):
    _, all_rows, width, length = xt.shape
    blocks, pieces, sub, tokens, _ = cot_rows.shape
    rows = blocks * sub
    some, count = 4, 4
    inner = sub // some
    full = lambda item: pl.BlockSpec(item.shape, lambda at, half: (0,) * item.ndim)
    of_all = pl.BlockSpec((some, width, length), lambda at, half: (c * (rows // some) + at, 0, 0))
    xt_some = pl.BlockSpec(
        (1, some, width, length), lambda at, half: (half[0], c * (rows // some) + at, 0, 0)
    )
    t_some = pl.BlockSpec(
        (length // 128, some, width, 128), lambda at, half: (0, c * (rows // some) + at, 0, 0)
    )
    dt_some = pl.BlockSpec((length // 128, some, width, 128), lambda at, half: (0, at, 0, 0))
    by_piece = pl.BlockSpec(
        (1, pieces, some, tokens, width), lambda at, half: (at // inner, 0, at % inner, 0, 0)
    )
    consts = (bias, chain, lane, vecs) + weights
    wide = weights[-1].shape[1]
    sum_shapes = [
        jax.ShapeDtypeStruct(shape, F32)
        for shape in ((width, 7 * width + 2 * wide), (8, width, 128), (heads, 16, length))
    ]
    before_specs = [full(item) for item in before[:3]]
    before_specs += [pl.BlockSpec(memory_space=pl.ANY)] * len(before[3:])
    return pl.pallas_call(
        functools.partial(rows_kernel, count, heads, order, c == 0),
        grid_spec=pltpu.PrefetchScalarGridSpec(
            num_scalar_prefetch=1,
            grid=(rows // some,),
            in_specs=[pl.BlockSpec(memory_space=pltpu.HBM)]
            + before_specs
            + [t_some, xt_some, by_piece] + [full(item) for item in consts],
            out_specs=[by_piece, dt_some, of_all] + [full(item) for item in sum_shapes],
            scratch_shapes=[
                pltpu.VMEM((count, length, heads * length), BF),
            ],
        ),
        out_shape=[
            jax.ShapeDtypeStruct(cot_rows.shape, BF),
            by_halves(rows, width, length),
            jax.ShapeDtypeStruct((all_rows, width, length), F32),
        ]
        + sum_shapes,
        input_output_aliases={5: 2} if before else {},
        compiler_params=pltpu.CompilerParams(vmem_limit_bytes=VMEM_LIMIT),
        cost_estimate=cost(1.2e11),
        name="rows",
    )(half, other, *before, t, xt, cot_rows, *consts)


def edges_back_kernel(
    order, half_ref, xt_ref, z_ref, da_ref, db_ref, wt_ref, w_ref, gain_ref, shift_ref, out_ref, g_w_ref, g_vec_ref
):
    _, rows, width, length = xt_ref.shape
    count = 4

    @pl.when(pl.program_id(0) == 0)
    def _():
        g_w_ref[...] = jnp.zeros(g_w_ref.shape, F32)
        g_vec_ref[...] = jnp.zeros(g_vec_ref.shape, F32)

    def step(at, carry):
        start = at * count
        x0 = stacked(xt_ref.at[0], start, count).astype(F32)
        lanes = x0.shape[1]
        gain = widen(gain_ref[...], lanes)
        hat, scale = normalize(x0)
        normed = (hat * gain + widen(shift_ref[...], lanes)).astype(BF)
        proj = nn(wt_ref[...], normed)
        pa, pag = proj[:width], proj[width : 2 * width]
        pb, pbg = proj[2 * width : 3 * width], proj[3 * width :]
        halves = [(n, half) for n in range(count) for half in range(da_ref.shape[0])]
        da = jnp.concatenate([da_ref[half, start + n] for n, half in halves], axis=1)
        db = jnp.concatenate([db_ref[half, start + n] for n, half in halves], axis=1)
        sa, sb = sigmoid(pag), sigmoid(pbg)
        dsa, dsb = da * sa, db * sb
        grads = jnp.concatenate(
            [
                dsa.astype(BF),
                (dsa * pa * (1.0 - sa)).astype(BF),
                dsb.astype(BF),
                (dsb * pb * (1.0 - sb)).astype(BF),
            ],
            axis=0,
        )
        g_w_ref[...] += nt(normed, grads)
        grad = nn(w_ref[...], grads)
        g_vec_ref[0] += fold(grad * hat)
        g_vec_ref[1] += fold(grad)
        out = stacked(z_ref, start, count) + normalize_back(grad, gain, hat, scale)
        out = out.astype(BF)
        for n in range(count):
            store_tokens(out_ref, start + n, order, out[:, n * length : (n + 1) * length].T.astype(F32))
        return carry

    lax.fori_loop(0, rows // count, step, 0)


def edges_back(half, xt, z, da, db, order, weight_t, weight, gain, shift, shape):
    _, rows, width, length = xt.shape
    blocks, pieces, sub, tokens, _ = shape
    chunks = order[2]
    some = sub // chunks
    step = 16 // some
    inner = blocks // step
    full = lambda item: pl.BlockSpec(item.shape, lambda at, half: (0,) * item.ndim)
    xt_row = pl.BlockSpec((1, 16, width, length), lambda at, half: (half[0], at, 0, 0))
    by_row = pl.BlockSpec((16, width, length), lambda at, half: (at, 0, 0))
    by_half = pl.BlockSpec((length // 128, 16, width, 128), lambda at, half: (0, at, 0, 0))
    sum_shapes = [
        jax.ShapeDtypeStruct(weight.shape, F32),
        jax.ShapeDtypeStruct((2, width, 128), F32),
    ]
    by_piece = pl.BlockSpec(
        (step, pieces, some, tokens, width), lambda at, half: (at % inner, 0, at // inner, 0, 0)
    )
    return pl.pallas_call(
        functools.partial(edges_back_kernel, order),
        grid_spec=pltpu.PrefetchScalarGridSpec(
            num_scalar_prefetch=1,
            grid=(chunks * inner,),
            in_specs=[xt_row, by_row] + [by_half] * 2 + [full(item) for item in (weight_t, weight, gain, shift)],
            out_specs=[by_piece] + [full(item) for item in sum_shapes],
        ),
        out_shape=[jax.ShapeDtypeStruct(shape, BF)] + sum_shapes,
        compiler_params=pltpu.CompilerParams(vmem_limit_bytes=VMEM_LIMIT),
        cost_estimate=cost(4.0e10),
        name="edges_back",
    )(half, xt, z, da, db, weight_t, weight, gain, shift)


def shards(
    row_size,
    col_size,
    pair_state,
    cotangent,
    chain_lengths,
    tri_gain,
    tri_shift,
    tri_weight,
    mix_gain,
    mix_shift,
    tri_out,
    att_gain,
    att_shift,
    att_weight,
    chain_bias,
    att_out,
    trans_gain,
    trans_shift,
    up_weight,
    down_weight,
):
    heads = HEADS
    crops, own_rows, tokens, width = pair_state.shape
    length = col_size * tokens
    chunks = CHUNKS
    some = own_rows // (col_size * chunks)
    axes = ("row", "col")
    group = row_size * col_size
    order = (row_size, col_size, chunks)
    shape = (row_size, col_size, some, tokens, width)

    def swap(values):
        return lax.all_to_all(values, axes, split_axis=0, concat_axis=0, tiled=True)

    def cut(values):
        parts = values.reshape(group, chunks, some, tokens, width)
        return [parts[:, c] for c in range(chunks)]

    def join(parts):
        return jnp.stack(parts, axis=1).reshape(crops, own_rows, tokens, width)

    def across(values, bit):
        return lax.ppermute(values, "col", [(q, q ^ bit) for q in range(col_size)])

    bits = [1 << n for n in range(col_size.bit_length() - 1)]

    def doubled(items, axis, size, bits):
        for bit in bits:
            lows = [values.astype(sent) for values, sent in items]
            others = [lax.ppermute(low, axis, [(q, q ^ bit) for q in range(size)]) for low in lows]
            others = lax.optimization_barrier(tuple(others))
            items = [
                (low.astype(F32) + other.astype(F32), sent)
                for low, other, (_, sent) in zip(lows, others, items)
            ]
        return items

    def summed_over_rows(values, sent):
        low = values.astype(sent)
        terms = [low.astype(F32)]
        for m in range(1, row_size):
            other = lax.ppermute(low, "row", [(r, r ^ m) for r in range(row_size)])
            terms.append(other.astype(F32))
        while len(terms) > 1:
            terms = [terms[n] + terms[n + 1] for n in range(0, len(terms), 2)]
        return terms[0]

    whole = (row_size, col_size, some * chunks, tokens, width)
    cot_parts = cut(cotangent)

    wide = lambda item: jnp.broadcast_to(item[:, None], (width, 128))
    vecs = jnp.stack(
        [
            wide(item)
            for item in (
                tri_gain,
                tri_shift,
                mix_gain,
                mix_shift,
                att_gain,
                att_shift,
                trans_gain,
                trans_shift,
            )
        ]
    )
    edge_w = tri_weight[:, : 4 * width]
    edge_wt = edge_w.T
    gate_w = tri_weight[:, 4 * width :]
    lengths = lax.dynamic_index_in_dim(chain_lengths, lax.axis_index("row"), 0, keepdims=False)
    ends = jnp.cumsum(lengths)
    places = jnp.arange(length, dtype=jnp.int32)
    places = places.reshape(order + (some,)).transpose(1, 2, 0, 3).reshape(length)
    chain = jnp.sum((places[:, None] >= ends[None, :]).astype(jnp.int32), axis=-1)
    same = (chain[:, None] == chain[None, :]).astype(F32)
    bias = (LOG2E * chain_bias)[:, None, None] * same[None]
    which = (jnp.arange(16, dtype=jnp.int32)[:, None] == chain[None, :]).astype(F32)
    head_of = jnp.arange(width, dtype=jnp.int32) // (width // heads)
    lane = (jnp.arange(heads, dtype=jnp.int32)[:, None] == head_of[None, :]).astype(BF)
    lane = jnp.broadcast_to(lane[:, None, :], (heads, length, width))
    me = lax.axis_index("col")
    own = own_rows
    far_bit = col_size // 2
    half, core = me // far_bit, me % far_bit
    token_place = jnp.stack([(me ^ m) * tokens for m in range(col_size)])
    place = [(s * far_bit + (core ^ k)) * own for s in range(2) for k in range(2)]
    place = jnp.stack(place + [half])
    here = (core * own).reshape(1)
    half_at = half.reshape(1)
    weights = (
        gate_w,
        gate_w.T,
        tri_out,
        tri_out.T,
        att_weight.T,
        att_weight[:, width : 3 * width],
        att_weight,
        att_out,
        att_out.T,
        up_weight,
        up_weight.T,
        down_weight,
        down_weight.T,
    )
    chain_rows = which.astype(BF)

    some_rows = own_rows // col_size
    x_pieces, crossings = [], []
    for s in range(2):
        pieces = []
        for k in range(2):
            start = (s * far_bit + (core ^ k)) * some_rows
            part = lax.dynamic_slice_in_dim(pair_state, start, some_rows, axis=1)
            if len(crossings) > 1:
                part = after(part, crossings[-2])
            part = lax.all_to_all(part, "row", split_axis=0, concat_axis=0, tiled=True)
            crossings.append(across(part, far_bit ^ k))
            pieces += [crossings[-1], across(part, 1)] if k else [part, crossings[-1]]
        own_part, far, far_other, near_other = pieces
        x_pieces.append([own_part, near_other, far, far_other])
    cot_rows, before = [], part
    for held in cot_parts:
        before = swap(after(held, before))
        cot_rows.append(before.reshape(shape))
    lefts, rights, xt = [], [], []
    for s, pieces in enumerate(x_pieces):
        others = [] if s else [crossings[2], cot_parts[0]]
        left, right, *xt = edges(
            token_place, s, pieces, xt, others, order, edge_wt, vecs[0], vecs[1]
        )
        lefts.append(left)
        rights += [right, across(right, 1)]
    (xt,) = xt
    t = triangle(place, lefts, rights)
    tips = [across(tip(cot_rows[0]), 1), tip(cot_rows[1])]
    lefts = [item for left in lefts for item in (left, across(left, 1))]
    state, outs, dts, sent = [], [], [], []
    pairs = [[q, q + far_bit] for q in range(far_bit)]
    for c in range(chunks):
        out, dt, z, *sums = rows_pass(
            c, chunks, half_at, tips[c], state, t, xt, cot_rows[c], order, bias, chain_rows, lane, vecs, weights, heads
        )
        state = sums + [z]
        dt = turn(dt, outs)
        if c < chunks - 1:
            dts.append(dt)
            outs.append(swap(out.reshape(group, some, tokens, width)))
            near = lax.dynamic_index_in_dim(dt, half, 0, keepdims=False)
            sent.append((near, across(lax.dynamic_index_in_dim(dt, 1 - half, 0, keepdims=False), far_bit)))
    dts.append(dt)
    crossed = []
    for near, far in sent:
        crossed.append(jnp.where(half == 0, jnp.stack([near, far]), jnp.stack([far, near])))
    crossed.append(
        lax.all_to_all(dt, "col", split_axis=0, concat_axis=0, axis_index_groups=pairs, tiled=True)
    )
    g_rows, g_vec, g_bias = sums
    row_bits = [1 << n for n in range(row_size.bit_length() - 1)]
    g_rows = summed_over_rows(g_rows, BF)
    da = left_back(place, dts, rights)
    grads = [[item, across(item, 1)] for item in crossed[:-1]]
    crossed[-1] = after(crossed[-1], da, g_rows)
    grads.append([crossed[-1], across(crossed[-1], 1)])
    outs.append(swap(out.reshape(group, some, tokens, width)))
    pair_out = join(outs)
    db = right_back(here, grads, lefts)
    back, g_edge, g_vec_edge = edges_back(
        half_at, xt, z, da, db, order, edge_wt, edge_w, vecs[0], vecs[1], whole
    )
    g_vec = jnp.sum(g_vec, axis=-1)
    g_vec_edge = jnp.sum(g_vec_edge, axis=-1)
    g_chain = jnp.sum(g_bias * which[None], axis=(1, 2))
    small = jnp.concatenate(
        [g_vec[:2] + g_vec_edge, g_vec[2:], jnp.pad(g_chain, (0, width - heads))[None]], axis=0
    )
    items = doubled([(g_edge, BF), (small, F32)], "row", row_size, row_bits)
    back = after(back, *[values for values, _ in items])
    grad_pair = swap(back.reshape(group, some * chunks, tokens, width))
    grad_pair = grad_pair.reshape(crops, own_rows, tokens, width)
    g_rows = after(g_rows, pair_out, back)
    items = doubled(items + [(g_rows, BF)], "col", col_size, bits[::-1])
    t_edge, small, total = [values for values, _ in items]
    column = lambda at, n=1: total[:, at * width : (at + n) * width]
    ff = up_weight.shape[1] // width
    t_gate, t_tri_out, t_att = column(0), column(1), column(2, 4)
    t_att_out, t_up = column(6), column(7, ff)
    t_down = jnp.concatenate([column(7 + ff + n) for n in range(ff)], axis=0)
    return (
        pair_out,
        grad_pair,
        small[0],
        small[1],
        jnp.concatenate([t_edge, t_gate], axis=1),
        small[2],
        small[3],
        t_tri_out,
        small[4],
        small[5],
        t_att,
        small[8, :heads],
        t_att_out,
        small[6],
        small[7],
        t_up,
        t_down,
    )


def solution(mesh):
    pair = P("dp", "row", "col", None)
    vector, matrix = P("dp"), P("dp", None)
    return jax.shard_map(
        functools.partial(shards, mesh.shape["row"], mesh.shape["col"]),
        mesh=mesh,
        in_specs=(pair, pair, P("dp", None)) + (P(),) * 15,
        out_specs=(
            pair,
            pair,
            vector,
            vector,
            matrix,
            vector,
            vector,
            matrix,
            vector,
            vector,
            matrix,
            vector,
            matrix,
            vector,
            vector,
            matrix,
            matrix,
        ),
        check_vma=False,
    )
```
